32 devices in a mesh: dp: 8 (over z, x), fsdp: 4 (over y, core).
Axes of the slice: x: 2, y: 2, z: 4, core: 2. Of those that a mesh axis runs over, the one named last changes fastest.
Arguments:
- latents: int32 [512, 96, 32], P(('dp', 'fsdp')), may hold values from 0 to 31
- targets: int32 [512, 48, 32], P(('dp', 'fsdp')), may hold values from 0 to 31
- horizon: int32 [512], P(('dp', 'fsdp')), may hold values from 8 to 48, as said below
- memory_valid: int32 [512], P(('dp', 'fsdp')), may hold values 0 or 1
- embed: float32 [1024, 256], P('dp', 'fsdp'), may hold values from -1 to 1
- qkv_weight: float32 [3, 256, 768], P(None, 'fsdp', 'dp'), may hold values from -0.375 to 0.375
- out_weight: float32 [3, 256, 256], P(None, 'fsdp', 'dp'), may hold values from -2 to 2
- up_weight: float32 [3, 256, 1024], P(None, 'fsdp', 'dp'), may hold values from -0.375 to 0.375
- down_weight: float32 [3, 1024, 256], P(None, 'dp', 'fsdp'), may hold values from -0.1875 to 0.1875
- head_weight: float32 [256, 1024], P('fsdp', 'dp'), may hold values from -0.375 to 0.375
- gains: float32 [7, 256], replicated, may hold values from 0.4 to 2.2
- embed_rows: float32 [1024], P('dp'), may hold values from 9.6270915e-11 to 3.8508366e-10
- embed_cols: float32 [256], P('fsdp'), may hold values from 9.6270915e-11 to 3.8508366e-10
- qkv_rows: float32 [3, 256], P(None, 'fsdp'), may hold values from 9.6270915e-11 to 3.8508366e-10
- qkv_cols: float32 [3, 768], P(None, 'dp'), may hold values from 9.6270915e-11 to 3.8508366e-10
- out_rows: float32 [3, 256], P(None, 'fsdp'), may hold values from 9.6270915e-11 to 3.8508366e-10
- out_cols: float32 [3, 256], P(None, 'dp'), may hold values from 9.6270915e-11 to 3.8508366e-10
- up_rows: float32 [3, 256], P(None, 'fsdp'), may hold values from 9.6270915e-11 to 3.8508366e-10
- up_cols: float32 [3, 1024], P(None, 'dp'), may hold values from 9.6270915e-11 to 3.8508366e-10
- down_rows: float32 [3, 1024], P(None, 'dp'), may hold values from 9.6270915e-11 to 3.8508366e-10
- down_cols: float32 [3, 256], P(None, 'fsdp'), may hold values from 9.6270915e-11 to 3.8508366e-10
- head_rows: float32 [256], P('fsdp'), may hold values from 9.6270915e-11 to 3.8508366e-10
- head_cols: float32 [1024], P('dp'), may hold values from 9.6270915e-11 to 3.8508366e-10
- gain_second: float32 [7, 256], replicated, may hold values from 9.627091e-10 to 3.8508365e-09
Outputs:
- loss_sum: float32 [], replicated
- position_count: float32 [], replicated
- grad_norm: float32 [], replicated
- embed_new: float32 [1024, 256], P('dp', 'fsdp')
- embed_grad: float32 [1024, 256], P('dp', 'fsdp')
- embed_rows_new: float32 [1024], P('dp')
- embed_cols_new: float32 [256], P('fsdp')
- qkv_new: float32 [3, 256, 768], P(None, 'fsdp', 'dp')
- qkv_grad: float32 [3, 256, 768], P(None, 'fsdp', 'dp')
- qkv_rows_new: float32 [3, 256], P(None, 'fsdp')
- qkv_cols_new: float32 [3, 768], P(None, 'dp')
- out_new: float32 [3, 256, 256], P(None, 'fsdp', 'dp')
- out_grad: float32 [3, 256, 256], P(None, 'fsdp', 'dp')
- out_rows_new: float32 [3, 256], P(None, 'fsdp')
- out_cols_new: float32 [3, 256], P(None, 'dp')
- up_new: float32 [3, 256, 1024], P(None, 'fsdp', 'dp')
- up_grad: float32 [3, 256, 1024], P(None, 'fsdp', 'dp')
- up_rows_new: float32 [3, 256], P(None, 'fsdp')
- up_cols_new: float32 [3, 1024], P(None, 'dp')
- down_new: float32 [3, 1024, 256], P(None, 'dp', 'fsdp')
- down_grad: float32 [3, 1024, 256], P(None, 'dp', 'fsdp')
- down_rows_new: float32 [3, 1024], P(None, 'dp')
- down_cols_new: float32 [3, 256], P(None, 'fsdp')
- head_new: float32 [256, 1024], P('fsdp', 'dp')
- head_grad: float32 [256, 1024], P('fsdp', 'dp')
- head_rows_new: float32 [256], P('fsdp')
- head_cols_new: float32 [1024], P('dp')
- gains_new: float32 [7, 256], replicated
- gains_grad: float32 [7, 256], replicated
- gain_second_new: float32 [7, 256], replicated
The draws below stay inside these ranges and needn't reach their ends.
Inputs may be any that keep to these rules, and one draw needn't show every extreme that they name: `horizon`: some sample has all 48 positions counted.
All inputs are finite; a program needn't handle non-finite values. No bound on the sum of `memory_valid` on one device may be relied on, other than what follows from the above.
Results may differ from the reference program's by a relative error of at most 0.0095.
The reference program's roundings to bfloat16 on the way count: a program that leaves them out, or rounds other values in their place, can miss the bound.
Values may be sent and summed in bfloat16 or wider, within the bound.
No kernel may reach another device: no remote copies, remote signals or barrier semaphores. Data moves between devices by JAX's collectives and lax.ppermute only.
A program may use at most 192 MiB of HBM per device.

```python
import math
import jax
import jax.numpy as jnp
from jax import lax

D = 256
HEADS = 8
FF = 1024
CATS = 32
CLASSES = 32
LAYERS = 3
SEG = 48
MEM = 48
SEQ_DEV = 16
CTX = 96
VOCAB = 1024
HEAD_DIM = 32
GAINS = 7
SAMPLES = 512
N_DP = 8
N_FSDP = 4


def draw_horizon(key, part):
    key = jax.random.fold_in(key, 11)
    sample_ids = jnp.arange(SAMPLES, dtype=jnp.int32)
    device_ids = sample_ids // SEQ_DEV
    outer_index = device_ids // N_FSDP
    inner_index = device_ids % N_FSDP
    third = SEG // 3
    ceiling = third + third * outer_index // max(N_DP - 1, 1) + (SEG - 2 * third) * inner_index // max(N_FSDP - 1, 1)
    random_bits = jax.random.randint(key, (SAMPLES,), 0, 1 << 20)
    drawn = ceiling - random_bits % (ceiling - ceiling // 2 + 1)
    return jnp.where(sample_ids == SAMPLES - 1, SEG, drawn).astype(jnp.int32)


def draw_gains(key, part):
    key = jax.random.fold_in(key, 12)
    ramp = 0.6 + 1.2 * jnp.arange(D, dtype=jnp.float32) / max(D - 1, 1)
    jitter = jax.random.uniform(key, (GAINS, D), jnp.float32, 0.8, 1.2)
    return ramp[None, :] * jitter


def set_ends(array, rng, smallest, high):
    place = [jax.random.randint(jax.random.fold_in(rng, axis), (), 0, length) for axis, length in enumerate(array.shape)]
    main_axis = array.shape.index(max(array.shape))
    beside = place[:main_axis] + [(place[main_axis] + 1) % array.shape[main_axis]] + place[main_axis + 1:]
    return array.at[tuple(place)].set(smallest).at[tuple(beside)].set(high)


def levels(rng, dims, shards, least, largest):
    def one(position, parts):
        draws = jax.random.uniform(jax.random.fold_in(jax.random.fold_in(rng, 6), position), (parts,), jnp.float32, least / len(shards), largest / len(shards))
        return jnp.repeat(jnp.exp(draws), dims[position] // parts).reshape((-1,) + (1,) * (len(dims) - position - 1))

    gain = one(*shards[0])
    for cut in shards[1:]:
        gain = gain * one(*cut)
    return gain


def gaussian(stream_key, dims, deviation, reach, shards=(), kind=jnp.bfloat16):
    result = deviation * jax.random.normal(stream_key, dims, jnp.float32)
    if shards:
        result = result * levels(stream_key, dims, shards, -0.22, 0.18)
    return jnp.clip(result, -reach, reach).astype(kind)


def setup_inputs(seed: int = 0) -> dict:
    seeds = jax.random.split(jax.random.key(seed), 25)
    return {
        "latents": set_ends(jax.random.randint(seeds[0], (SAMPLES, CTX, CATS), 0, CLASSES), jax.random.fold_in(seeds[0], 1), 0, CLASSES - 1).astype(jnp.int32),
        "targets": set_ends(jax.random.randint(seeds[1], (SAMPLES, SEG, CATS), 0, CLASSES), jax.random.fold_in(seeds[1], 1), 0, CLASSES - 1).astype(jnp.int32),
        "horizon": draw_horizon(jax.random.fold_in(seeds[24], 71), 0),
        "memory_valid": set_ends((jax.random.randint(seeds[3], (SAMPLES,), 0, 4) < 3).astype(jnp.int32), jax.random.fold_in(seeds[3], 1), 0, 1),
        "embed": gaussian(seeds[4], (VOCAB, D), CATS ** -0.5, 1.0, ((0, 8), (1, 4)), jnp.float32),
        "qkv_weight": gaussian(seeds[5], (LAYERS, D, 3 * D), D ** -0.5, 0.375, ((1, 4), (2, 8)), jnp.float32),
        "out_weight": gaussian(seeds[6], (LAYERS, D, D), (D // 32) ** -0.5, 2.0, ((1, 4), (2, 8)), jnp.float32),
        "up_weight": gaussian(seeds[7], (LAYERS, D, FF), D ** -0.5, 0.375, ((1, 4), (2, 8)), jnp.float32),
        "down_weight": gaussian(seeds[8], (LAYERS, FF, D), FF ** -0.5, 0.1875, ((1, 8), (2, 4)), jnp.float32),
        "head_weight": gaussian(seeds[9], (D, VOCAB), D ** -0.5, 0.375, ((0, 4), (1, 8)), jnp.float32),
        "gains": draw_gains(jax.random.fold_in(seeds[24], 71), 0),
        "embed_rows": jnp.clip(jnp.exp(math.log(3.850836594043727e-10) - 1.3862944 * jax.random.uniform(seeds[11], (VOCAB,), jnp.float32) ** levels(seeds[11], (VOCAB,), ((0, 8),), -0.2, 0.2)), 9.627091485109318e-11, 3.850836594043727e-10),
        "embed_cols": jnp.clip(jnp.exp(math.log(3.850836594043727e-10) - 1.3862944 * jax.random.uniform(seeds[12], (D,), jnp.float32) ** levels(seeds[12], (D,), ((0, 4),), -0.2, 0.2)), 9.627091485109318e-11, 3.850836594043727e-10),
        "qkv_rows": jnp.clip(jnp.exp(math.log(3.850836594043727e-10) - 1.3862944 * jax.random.uniform(seeds[13], (LAYERS, D), jnp.float32) ** levels(seeds[13], (LAYERS, D), ((1, 4),), -0.2, 0.2)), 9.627091485109318e-11, 3.850836594043727e-10),
        "qkv_cols": jnp.clip(jnp.exp(math.log(3.850836594043727e-10) - 1.3862944 * jax.random.uniform(seeds[14], (LAYERS, 3 * D), jnp.float32) ** levels(seeds[14], (LAYERS, 3 * D), ((1, 8),), -0.2, 0.2)), 9.627091485109318e-11, 3.850836594043727e-10),
        "out_rows": jnp.clip(jnp.exp(math.log(3.850836594043727e-10) - 1.3862944 * jax.random.uniform(seeds[15], (LAYERS, D), jnp.float32) ** levels(seeds[15], (LAYERS, D), ((1, 4),), -0.2, 0.2)), 9.627091485109318e-11, 3.850836594043727e-10),
        "out_cols": jnp.clip(jnp.exp(math.log(3.850836594043727e-10) - 1.3862944 * jax.random.uniform(seeds[16], (LAYERS, D), jnp.float32) ** levels(seeds[16], (LAYERS, D), ((1, 8),), -0.2, 0.2)), 9.627091485109318e-11, 3.850836594043727e-10),
        "up_rows": jnp.clip(jnp.exp(math.log(3.850836594043727e-10) - 1.3862944 * jax.random.uniform(seeds[17], (LAYERS, D), jnp.float32) ** levels(seeds[17], (LAYERS, D), ((1, 4),), -0.2, 0.2)), 9.627091485109318e-11, 3.850836594043727e-10),
        "up_cols": jnp.clip(jnp.exp(math.log(3.850836594043727e-10) - 1.3862944 * jax.random.uniform(seeds[18], (LAYERS, FF), jnp.float32) ** levels(seeds[18], (LAYERS, FF), ((1, 8),), -0.2, 0.2)), 9.627091485109318e-11, 3.850836594043727e-10),
        "down_rows": jnp.clip(jnp.exp(math.log(3.850836594043727e-10) - 1.3862944 * jax.random.uniform(seeds[19], (LAYERS, FF), jnp.float32) ** levels(seeds[19], (LAYERS, FF), ((1, 8),), -0.2, 0.2)), 9.627091485109318e-11, 3.850836594043727e-10),
        "down_cols": jnp.clip(jnp.exp(math.log(3.850836594043727e-10) - 1.3862944 * jax.random.uniform(seeds[20], (LAYERS, D), jnp.float32) ** levels(seeds[20], (LAYERS, D), ((1, 4),), -0.2, 0.2)), 9.627091485109318e-11, 3.850836594043727e-10),
        "head_rows": jnp.clip(jnp.exp(math.log(3.850836594043727e-10) - 1.3862944 * jax.random.uniform(seeds[21], (D,), jnp.float32) ** levels(seeds[21], (D,), ((0, 4),), -0.2, 0.2)), 9.627091485109318e-11, 3.850836594043727e-10),
        "head_cols": jnp.clip(jnp.exp(math.log(3.850836594043727e-10) - 1.3862944 * jax.random.uniform(seeds[22], (VOCAB,), jnp.float32) ** levels(seeds[22], (VOCAB,), ((0, 8),), -0.2, 0.2)), 9.627091485109318e-11, 3.850836594043727e-10),
        "gain_second": jnp.clip(jnp.exp(jax.random.uniform(seeds[23], (GAINS, D), jnp.float32, math.log(9.62709134633144e-10), math.log(3.850836538532576e-09))), 9.62709134633144e-10, 3.850836538532576e-09),
    }


@jax.custom_vjp
def low(v):
    return lax.optimization_barrier(v.astype(jnp.bfloat16)).astype(jnp.float32)

@jax.custom_vjp
def low_back(v):
    return v

def low_keep(v):
    return (low(v), None)

def low_pass(kept, grad):
    return (grad,)

def back_keep(v):
    return (v, None)

def back_low(kept, grad):
    return (low(grad),)
low.defvjp(low_keep, low_pass)
low_back.defvjp(back_keep, back_low)
decay_two = 0.9
step_rate = 0.3
clip_limit = 0.05
tiny_term = 1e-30
norm_eps = 1e-06
masked_score = -1e+30
highest = lax.Precision.HIGHEST

def product(left, right):
    return jnp.dot(left, right, precision=highest, preferred_element_type=jnp.float32)

def rms_norm(values, gain_row):
    return values * lax.rsqrt(lax.optimization_barrier(jnp.mean(values * values, axis=-1, keepdims=True)) + norm_eps) * gain_row

def attend(queries, key_rows, value_rows, allowed):
    scores = jnp.einsum('sqhd,skhd->shqk', queries, key_rows, precision=highest) * HEAD_DIM ** (-0.5)
    scores = jnp.where(allowed, low_back(scores), masked_score)
    peak_score = lax.optimization_barrier(jnp.max(scores, axis=-1, keepdims=True))
    exponent = jnp.exp(scores - peak_score)
    probability = low(exponent / lax.optimization_barrier(jnp.sum(exponent, axis=-1, keepdims=True)))
    return jnp.einsum('shqk,skhd->sqhd', probability, value_rows, precision=highest)

def layer(hidden, w_qkv, w_out, w_up, w_down, gain_att, gain_ffn, allowed):
    number = hidden.shape[0] // CTX
    normed = low(rms_norm(hidden, gain_att))
    qkv = low(low_back(product(normed, w_qkv)))
    queries = qkv[:, :D].reshape(number, CTX, HEADS, HEAD_DIM)
    key_rows = qkv[:, D:2 * D].reshape(number, CTX, HEADS, HEAD_DIM)
    value_rows = qkv[:, 2 * D:].reshape(number, CTX, HEADS, HEAD_DIM)
    mixture = attend(queries, key_rows, value_rows, allowed).reshape(number * CTX, D)
    mixture = low(low_back(mixture))
    middle = hidden + low_back(product(mixture, w_out))
    normed_two = low(rms_norm(middle, gain_ffn))
    inner_pre = low_back(product(normed_two, w_up))
    activated = low(jax.nn.gelu(inner_pre))
    return middle + low_back(product(activated, w_down))

def segment_loss(weights, latent_ids, target_ids, horizon, memory_valid):
    embed, w_qkv, w_out, w_up, w_down, head, gains = weights
    number = latent_ids.shape[0]
    classes = jnp.arange(CLASSES, dtype=jnp.int32)
    one_hot = (latent_ids[..., None] == classes).astype(jnp.float32).reshape(number * CTX, VOCAB)
    hidden = low_back(product(one_hot, embed))
    positions = jnp.arange(CTX, dtype=jnp.int32)
    causal = positions[None, :] <= positions[:, None]
    crosses = (positions[:, None] >= MEM) & (positions[None, :] < MEM)
    allowed = causal[None, None] & jnp.logical_not(crosses[None, None] & (memory_valid[:, None, None, None] == 0))
    for layer_at in range(LAYERS):
        hidden = layer(hidden, w_qkv[layer_at], w_out[layer_at], w_up[layer_at], w_down[layer_at], gains[layer_at], gains[LAYERS + layer_at], allowed)
    latest = hidden.reshape(number, CTX, D)[:, MEM:].reshape(number * SEG, D)
    final = low(rms_norm(latest, gains[2 * LAYERS]))
    logits = low_back(product(final, head)).reshape(number, SEG, CATS, CLASSES)
    peak_logit = lax.optimization_barrier(jnp.max(logits, axis=-1, keepdims=True))
    log_total = peak_logit[..., 0] + jnp.log(lax.optimization_barrier(jnp.sum(jnp.exp(logits - peak_logit), axis=-1)))
    chosen = lax.optimization_barrier(jnp.sum(jnp.where(target_ids[..., None] == classes, logits, 0.0), axis=-1))
    per_position = lax.optimization_barrier(jnp.sum(log_total - chosen, axis=-1))
    counted = jnp.arange(SEG, dtype=jnp.int32)[None, :] < horizon[:, None]
    return jnp.sum(jnp.where(counted, per_position, 0.0))

def total_loss(weights, latents, targets, horizon, memory_valid):
    rounded = (low(weights[0]), low(weights[1]), low(weights[2]), low(weights[3]), low(weights[4]), low(weights[5]), weights[6])
    groups = latents.shape[0] // 32
    batches = (latents.reshape(groups, 32, CTX, CATS), targets.reshape(groups, 32, SEG, CATS), horizon.reshape(groups, 32), memory_valid.reshape(groups, 32))

    def add_group(carried, batch):
        return (carried + segment_loss(rounded, batch[0], batch[1], batch[2], batch[3]), None)
    summed, unused = lax.scan(jax.checkpoint(add_group), jnp.zeros((), jnp.float32), batches)
    return summed

def factored(weight, grad, row_stats, column_stats):
    square = grad * grad + tiny_term
    rows_new = decay_two * row_stats + (1 - decay_two) * lax.optimization_barrier(jnp.mean(square, axis=-1))
    columns_new = decay_two * column_stats + (1 - decay_two) * lax.optimization_barrier(jnp.mean(square, axis=-2))
    second = rows_new[..., :, None] * columns_new[..., None, :] / lax.optimization_barrier(jnp.mean(rows_new, axis=-1))[..., None, None]
    spread = jnp.sqrt(lax.optimization_barrier(jnp.mean(weight * weight, axis=(-2, -1))))[..., None, None]
    return (weight - step_rate * spread * grad * lax.rsqrt(second), grad, rows_new, columns_new)

def reference(latents, targets, horizon, memory_valid, embed, qkv_weight, out_weight, up_weight, down_weight, head_weight, gains, embed_rows, embed_cols, qkv_rows, qkv_cols, out_rows, out_cols, up_rows, up_cols, down_rows, down_cols, head_rows, head_cols, gain_second):

    def loss_of(e, q, o, u, w, h, g):
        return total_loss((e, q, o, u, w, h, g), latents, targets, horizon, memory_valid)
    loss_sum, pullback = jax.vjp(loss_of, embed, qkv_weight, out_weight, up_weight, down_weight, head_weight, gains)
    raw_grads = pullback(jnp.ones((), jnp.float32))
    position_count = jnp.sum(horizon).astype(jnp.float32)
    averaged = [grad / position_count for grad in raw_grads]
    square_total = jnp.zeros((), jnp.float32)
    for grad in averaged:
        square_total = square_total + jnp.sum(grad * grad)
    grad_norm = jnp.sqrt(square_total)
    clip_factor = jnp.minimum(1.0, clip_limit / grad_norm)
    clipped = [grad * clip_factor for grad in averaged]
    embed_out = factored(embed, clipped[0], embed_rows, embed_cols)
    qkv_out = factored(qkv_weight, clipped[1], qkv_rows, qkv_cols)
    out_out = factored(out_weight, clipped[2], out_rows, out_cols)
    up_out = factored(up_weight, clipped[3], up_rows, up_cols)
    down_out = factored(down_weight, clipped[4], down_rows, down_cols)
    head_out = factored(head_weight, clipped[5], head_rows, head_cols)
    gain_grad = clipped[6]
    gain_second_new = decay_two * gain_second + (1 - decay_two) * (gain_grad * gain_grad + tiny_term)
    gains_new = gains - step_rate * jnp.sqrt(lax.optimization_barrier(jnp.mean(gains * gains, axis=-1, keepdims=True))) * gain_grad * lax.rsqrt(gain_second_new)
    return (loss_sum, position_count, grad_norm, embed_out[0], embed_out[1], embed_out[2], embed_out[3], qkv_out[0], qkv_out[1], qkv_out[2], qkv_out[3], out_out[0], out_out[1], out_out[2], out_out[3], up_out[0], up_out[1], up_out[2], up_out[3], down_out[0], down_out[1], down_out[2], down_out[3], head_out[0], head_out[1], head_out[2], head_out[3], gains_new, gain_grad, gain_second_new)
```

```python
import jax
import jax.numpy as jnp
from jax import lax
from jax.sharding import PartitionSpec as P

D = 256
HEADS = 8
FF = 1024
CATS = 32
CLASSES = 32
LAYERS = 3
SEG = 48
MEM = 48
CTX = 96
VOCAB = 1024


decay_two = 0.9
step_rate = 0.3
clip_limit = 0.05
tiny_term = 1e-30
norm_eps = 1e-06
masked_score = -1e30


def matmul(left, right):
    return jnp.dot(left, right, preferred_element_type=jnp.float32)


def matmul_tn(left, right):
    return lax.dot_general(
        left, right, (((0,), (0,)), ((), ())), preferred_element_type=jnp.float32
    )


def matmul_nt(left, right):
    return lax.dot_general(
        left, right, (((1,), (1,)), ((), ())), preferred_element_type=jnp.float32
    )


def rms_norm(values, gain_row):
    return (
        values * lax.rsqrt(jnp.mean(values * values, axis=-1, keepdims=True) + norm_eps) * gain_row
    )


def in_blocks(array, block):
    return array.reshape((array.shape[0] // block, block) + array.shape[1:])


def split_qkv(qkv, samples, block):
    heads_of = [
        qkv[:, start * D : (start + 1) * D].reshape(samples, CTX, HEADS, D // HEADS)
        for start in range(3)
    ]
    return [in_blocks(piece, block) for piece in heads_of]


def block_scores(queries, key_rows, allowed):
    scores = jnp.einsum("bqhd,bkhd->bhqk", queries, key_rows, preferred_element_type=jnp.float32)
    return jnp.where(allowed, scores * queries.shape[-1] ** (-0.5), masked_score)


def attend_block(inputs):
    queries, key_rows, value_rows, allowed = inputs
    scores = block_scores(queries, key_rows, allowed)
    peak_score = jnp.max(scores, axis=-1, keepdims=True)
    exponent = jnp.exp(scores - peak_score)
    total = jnp.sum(exponent, axis=-1, keepdims=True)
    probability = (exponent / total).astype(jnp.bfloat16)
    mixture = jnp.einsum(
        "bhqk,bkhd->bqhd", probability, value_rows, preferred_element_type=jnp.float32
    )
    return (mixture, peak_score[..., 0] + jnp.log(total[..., 0]))


def attend_back(inputs):
    queries, key_rows, value_rows, allowed, upstream, log_total = inputs
    scale_factor = queries.shape[-1] ** (-0.5)
    probability = jnp.exp(block_scores(queries, key_rows, allowed) - log_total[..., None])
    dprob = jnp.einsum("bqhd,bkhd->bhqk", upstream, value_rows, preferred_element_type=jnp.float32)
    dscore = (probability * (dprob - jnp.sum(probability * dprob, axis=-1, keepdims=True))).astype(
        jnp.bfloat16
    )
    dvalues = jnp.einsum(
        "bhqk,bqhd->bkhd",
        probability.astype(jnp.bfloat16),
        upstream,
        preferred_element_type=jnp.float32,
    )
    dqueries = (
        jnp.einsum("bhqk,bkhd->bqhd", dscore, key_rows, preferred_element_type=jnp.float32)
        * scale_factor
    )
    dkeys = (
        jnp.einsum("bhqk,bqhd->bkhd", dscore, queries, preferred_element_type=jnp.float32)
        * scale_factor
    )
    return (dqueries, dkeys, dvalues)


def attention(qkv, allowed):
    samples = allowed.shape[0]
    block = min(samples, 8)
    queries, key_rows, value_rows = split_qkv(qkv, samples, block)
    mixture, log_total = lax.map(
        attend_block, (queries, key_rows, value_rows, in_blocks(allowed, block))
    )
    return (mixture.reshape(samples * CTX, D), log_total)


def attention_back(qkv, allowed, upstream, log_total):
    samples = allowed.shape[0]
    block = min(samples, 8)
    queries, key_rows, value_rows = split_qkv(qkv, samples, block)
    upstream_blocks = in_blocks(upstream.reshape(samples, CTX, HEADS, D // HEADS), block)
    dqueries, dkeys, dvalues = lax.map(
        attend_back,
        (queries, key_rows, value_rows, in_blocks(allowed, block), upstream_blocks, log_total),
    )
    return jnp.concatenate(
        [
            dqueries.reshape(samples * CTX, D),
            dkeys.reshape(samples * CTX, D),
            dvalues.reshape(samples * CTX, D),
        ],
        axis=1,
    )


def layer_forward(hidden, w_qkv, w_out, w_up, w_down, gain_att, gain_ffn, allowed):
    normed, att_pull = jax.vjp(rms_norm, hidden, gain_att)
    normed_low = normed.astype(jnp.bfloat16)
    qkv = matmul(normed_low, w_qkv).astype(jnp.bfloat16)
    mixture, log_total = attention(qkv, allowed)
    mixture = mixture.astype(jnp.bfloat16)
    middle = hidden + matmul(mixture, w_out)
    normed_two, ffn_pull = jax.vjp(rms_norm, middle, gain_ffn)
    normed_two = normed_two.astype(jnp.bfloat16)
    inner_act, gelu_pull = jax.vjp(jax.nn.gelu, matmul(normed_two, w_up))
    activated = inner_act.astype(jnp.bfloat16)
    output = middle + matmul(activated, w_down)
    return (
        output,
        (att_pull, normed_low, qkv, mixture, log_total, ffn_pull, normed_two, gelu_pull, activated),
    )


def layer_backward(saved, w_qkv, w_out, w_up, w_down, allowed, upstream):
    att_pull, normed_low, qkv, mixture, log_total, ffn_pull, normed_two, gelu_pull, activated = (
        saved
    )
    dout = upstream.astype(jnp.bfloat16)
    grad_down = matmul_tn(dout, activated)
    dinner = gelu_pull(matmul_nt(dout, w_down))[0].astype(jnp.bfloat16)
    grad_up = matmul_tn(normed_two, dinner)
    dmiddle_norm, dgain_ffn = ffn_pull(matmul_nt(dinner, w_up))
    dmiddle = upstream + dmiddle_norm
    dattend = dmiddle.astype(jnp.bfloat16)
    grad_out = matmul_tn(mixture, dattend)
    dmixture = matmul_nt(dattend, w_out).astype(jnp.bfloat16)
    dqkv = attention_back(qkv, allowed, dmixture, log_total).astype(jnp.bfloat16)
    grad_qkv = matmul_tn(normed_low, dqkv)
    dhidden_norm, dgain_att = att_pull(matmul_nt(dqkv, w_qkv))
    return (dmiddle + dhidden_norm, (grad_qkv, grad_out, grad_up, grad_down), dgain_att, dgain_ffn)


def axis_bits(axis):
    return [1 << bit for bit in range(lax.axis_size(axis).bit_length() - 1)]


def swap(value, axis, bit):
    pairs = [(place, place ^ bit) for place in range(lax.axis_size(axis))]
    return lax.ppermute(value, axis, pairs)


def gather_pieces(piece):
    outer = lax.axis_size("dp").bit_length() - 1
    inner = lax.axis_size("fsdp").bit_length() - 1
    held = piece.reshape((1,) * (outer + inner) + piece.shape)
    order = [("dp", bit) for bit in reversed(range(outer))] + [
        ("fsdp", bit) for bit in reversed(range(inner))
    ]
    for place, (axis, bit) in enumerate(order):
        other = swap(held, axis, 1 << bit)
        upper = (lax.axis_index(axis) >> bit) & 1 == 1
        held = jnp.where(
            upper,
            jnp.concatenate([other, held], axis=place),
            jnp.concatenate([held, other], axis=place),
        )
    return held.reshape((lax.axis_size("dp"), lax.axis_size("fsdp")) + piece.shape)


def scatter_pieces(blocks):
    outer = lax.axis_size("dp").bit_length() - 1
    inner = lax.axis_size("fsdp").bit_length() - 1
    rows, columns = blocks.shape[2:]
    held = blocks.reshape((2,) * (outer + inner) + (rows, columns))
    order = [("dp", bit) for bit in reversed(range(outer))] + [
        ("fsdp", bit) for bit in reversed(range(inner))
    ]
    places = {item: place for place, item in enumerate(order)}
    for axis, bit in [("fsdp", bit) for bit in range(inner)] + [("dp", bit) for bit in range(outer)]:
        place = places[(axis, bit)]
        upper = (lax.axis_index(axis) >> bit) & 1 == 1
        low = lax.slice_in_dim(held, 0, 1, axis=place)
        high = lax.slice_in_dim(held, 1, 2, axis=place)
        other = swap(jnp.where(upper, low, high).astype(jnp.bfloat16), axis, 1 << bit)
        held = jnp.where(upper, high, low) + other.astype(jnp.float32)
    return held.reshape(rows, columns)


def sum_over(value, axis):
    terms = [value] + [swap(value, axis, step) for step in range(1, lax.axis_size(axis))]
    while len(terms) > 1:
        terms = [terms[at] + terms[at + 1] for at in range(0, len(terms), 2)]
    return terms[0]


def flat(items):
    return jnp.concatenate([item.reshape(-1) for item in items])


def unflat(vector, items):
    found, at = [], 0
    for item in items:
        found.append(vector[at : at + item.size].reshape(item.shape))
        at += item.size
    return found


def spread_columns(gathered, start, stop):
    part = gathered[:, :, :, start:stop]
    return part.transpose(1, 2, 0, 3).reshape(-1, part.shape[0] * (stop - start))


def block_columns(matrix):
    outer, inner = lax.axis_size("dp"), lax.axis_size("fsdp")
    return matrix.reshape(inner, matrix.shape[0] // inner, outer, -1).transpose(2, 0, 1, 3)


def shards(
    latents,
    targets,
    horizon,
    memory_valid,
    embed,
    qkv_weight,
    out_weight,
    up_weight,
    down_weight,
    head_weight,
    gains,
    embed_rows,
    embed_cols,
    qkv_rows,
    qkv_cols,
    out_rows,
    out_cols,
    up_rows,
    up_cols,
    down_rows,
    down_cols,
    head_rows,
    head_cols,
    gain_second,
):
    samples = latents.shape[0]
    layer_parts = [
        jnp.concatenate(
            [qkv_weight[at], out_weight[at], up_weight[at], down_weight[at].T], axis=1
        ).astype(jnp.bfloat16)
        for at in range(LAYERS)
    ]
    table_part = jnp.concatenate([embed.T, head_weight], axis=1).astype(jnp.bfloat16)
    widths = [qkv_weight.shape[2], out_weight.shape[2], up_weight.shape[2], down_weight.shape[1]]
    cuts = [0, widths[0], sum(widths[:2]), sum(widths[:3]), sum(widths)]
    table_cut = embed.shape[0]
    tables = gather_pieces(table_part)
    embed_full = spread_columns(tables, 0, table_cut).T
    head_full = spread_columns(tables, table_cut, 2 * table_cut)
    layer_weights = []
    for at in range(LAYERS):
        gathered = gather_pieces(layer_parts[at])
        pieces = [spread_columns(gathered, cuts[which], cuts[which + 1]) for which in range(4)]
        layer_weights.append((pieces[0], pieces[1], pieces[2], pieces[3].T))

    classes = jnp.arange(CLASSES, dtype=jnp.int32)
    one_hot = (latents[..., None] == classes).astype(jnp.bfloat16).reshape(samples * CTX, VOCAB)
    positions = jnp.arange(CTX, dtype=jnp.int32)
    causal = positions[None, :] <= positions[:, None]
    crosses = (positions[:, None] >= MEM) & (positions[None, :] < MEM)
    allowed = causal[None, None] & jnp.logical_not(
        crosses[None, None] & (memory_valid[:, None, None, None] == 0)
    )
    hidden = matmul(one_hot, embed_full)
    saved = []
    for layer_at in range(LAYERS):
        hidden, kept = layer_forward(
            hidden, *layer_weights[layer_at], gains[layer_at], gains[LAYERS + layer_at], allowed
        )
        saved.append(kept)
    latest = hidden.reshape(samples, CTX, D)[:, MEM:].reshape(samples * SEG, D)
    final, final_pull = jax.vjp(rms_norm, latest, gains[2 * LAYERS])
    final_low = final.astype(jnp.bfloat16)
    logits = matmul(final_low, head_full).reshape(samples, SEG, CATS, CLASSES)
    peak_logit = jnp.max(logits, axis=-1, keepdims=True)
    shifted = jnp.exp(logits - peak_logit)
    total = jnp.sum(shifted, axis=-1, keepdims=True)
    log_total = peak_logit[..., 0] + jnp.log(total[..., 0])
    target_hot = targets[..., None] == classes
    chosen = jnp.sum(jnp.where(target_hot, logits, 0.0), axis=-1)
    counted = jnp.arange(SEG, dtype=jnp.int32)[None, :] < horizon[:, None]
    per_position = jnp.sum(log_total - chosen, axis=-1)
    loss_local = jnp.sum(jnp.where(counted, per_position, 0.0))
    count_local = jnp.sum(horizon).astype(jnp.float32)
    dlogits = (shifted / total - target_hot.astype(jnp.float32)) * counted[:, :, None, None].astype(
        jnp.float32
    )
    dlogits = dlogits.reshape(samples * SEG, VOCAB).astype(jnp.bfloat16)
    head_term = matmul_tn(final_low, dlogits)
    dlatest, dgain_final = final_pull(matmul_nt(dlogits, head_full))
    upstream = jnp.concatenate(
        [jnp.zeros((samples, MEM, D), jnp.float32), dlatest.reshape(samples, SEG, D)], axis=1
    )
    upstream = upstream.reshape(samples * CTX, D)
    layer_raws = [None] * LAYERS
    att_terms = [None] * LAYERS
    ffn_terms = [None] * LAYERS
    for layer_at in reversed(range(LAYERS)):
        upstream, terms, att_terms[layer_at], ffn_terms[layer_at] = layer_backward(
            saved[layer_at], *layer_weights[layer_at], allowed, upstream
        )
        layer_raws[layer_at] = scatter_pieces(
            jnp.concatenate([block_columns(term) for term in terms], axis=3)
        )
    embed_term = matmul_tn(upstream.astype(jnp.bfloat16), one_hot)
    table_raw = scatter_pieces(
        jnp.concatenate([block_columns(embed_term), block_columns(head_term)], axis=3)
    )
    gain_local = jnp.stack(att_terms + ffn_terms + [dgain_final])

    raws = [jnp.stack([raw[:, cuts[at] : cuts[at + 1]] for raw in layer_raws]) for at in range(4)]
    raws = raws + [table_raw[:, :table_cut], table_raw[:, table_cut:]]
    masters = [
        qkv_weight,
        out_weight,
        up_weight,
        down_weight.transpose(0, 2, 1),
        embed.T,
        head_weight,
    ]
    inner_old = [qkv_rows, out_rows, up_rows, down_cols, embed_cols, head_rows]
    outer_old = [qkv_cols, out_cols, up_cols, down_rows, embed_rows, head_cols]
    inner_is_row = [True, True, True, False, False, True]
    inner_part = [jnp.sum(raw * raw, axis=-1) for raw in raws]
    outer_part = [jnp.sum(raw * raw, axis=-2) for raw in raws]
    weight_square = [jnp.sum(master * master, axis=(-2, -1)) for master in masters]
    outer_row_sums = [
        jnp.sum(outer_old[at], axis=-1) for at in range(6) if not inner_is_row[at]
    ]
    inner_row_sums = [jnp.sum(inner_old[at], axis=-1) for at in range(6) if inner_is_row[at]]
    scalars = [loss_local, jnp.sum(horizon).astype(jnp.float32)]
    first = inner_part + outer_row_sums + weight_square + scalars + [gain_local]
    first_sum = unflat(sum_over(flat(first), "dp"), first)
    inner_global, first_sum = first_sum[:6], first_sum[6:]
    outer_row_sums, first_sum = first_sum[:2], first_sum[2:]
    entry_square = [jnp.sum(part, axis=-1) for part in inner_global]
    second = outer_part + inner_row_sums + entry_square + first_sum
    second_sum = unflat(sum_over(flat(second), "fsdp"), second)
    outer_global, second_sum = second_sum[:6], second_sum[6:]
    inner_row_sums, second_sum = second_sum[:4], second_sum[4:]
    entry_square, second_sum = second_sum[:6], second_sum[6:]
    weight_total, second_sum = second_sum[:6], second_sum[6:]
    loss_total, count_total, gain_sum = second_sum
    row_sums = inner_row_sums[:3] + outer_row_sums + inner_row_sums[3:]

    square_total = jnp.sum(gain_sum * gain_sum)
    for part in entry_square:
        square_total = square_total + jnp.sum(part)
    norm_value = jnp.sqrt(square_total) / count_total
    scaling = jnp.minimum(1.0, clip_limit / norm_value) / count_total
    found = []
    for at in range(6):
        inner_length = masters[at].shape[-2] * lax.axis_size("fsdp")
        outer_length = masters[at].shape[-1] * lax.axis_size("dp")
        row_length = inner_length if inner_is_row[at] else outer_length
        entries = inner_length * outer_length
        square_scale = scaling * scaling
        inner_new = decay_two * inner_old[at] + (1 - decay_two) * (
            square_scale * inner_global[at] / outer_length + tiny_term
        )
        outer_new = decay_two * outer_old[at] + (1 - decay_two) * (
            square_scale * outer_global[at] / inner_length + tiny_term
        )
        mean_rows = decay_two * (row_sums[at] / row_length) + (1 - decay_two) * (
            square_scale * entry_square[at] / entries + tiny_term
        )
        spread = jnp.sqrt(weight_total[at] / entries)
        grad = raws[at] * scaling
        scale_of = (step_rate * spread * jnp.sqrt(mean_rows))[..., None, None]
        updated = masters[at] - scale_of * grad * (
            lax.rsqrt(inner_new)[..., :, None] * lax.rsqrt(outer_new)[..., None, :]
        )
        found.append((updated, grad, inner_new, outer_new))
    results = [loss_total, count_total, norm_value]
    for at in [4, 0, 1, 2, 3, 5]:
        updated, grad, inner_new, outer_new = found[at]
        if inner_is_row[at]:
            results = results + [updated, grad, inner_new, outer_new]
        else:
            turned = [jnp.swapaxes(item, -1, -2) for item in (updated, grad)]
            results = results + turned + [outer_new, inner_new]
    gain_grad = gain_sum * scaling
    gain_second_new = decay_two * gain_second + (1 - decay_two) * (
        gain_grad * gain_grad + tiny_term
    )
    gains_new = gains - step_rate * jnp.sqrt(
        jnp.mean(gains * gains, axis=-1, keepdims=True)
    ) * gain_grad * lax.rsqrt(gain_second_new)
    results = results + [gains_new, gain_grad, gain_second_new]
    return tuple(results)


def solution(mesh):
    return jax.shard_map(
        shards,
        mesh=mesh,
        in_specs=(
            P(("dp", "fsdp"), None, None),
            P(("dp", "fsdp"), None, None),
            P(("dp", "fsdp")),
            P(("dp", "fsdp")),
            P("dp", "fsdp"),
            P(None, "fsdp", "dp"),
            P(None, "fsdp", "dp"),
            P(None, "fsdp", "dp"),
            P(None, "dp", "fsdp"),
            P("fsdp", "dp"),
            P(),
            P("dp"),
            P("fsdp"),
            P(None, "fsdp"),
            P(None, "dp"),
            P(None, "fsdp"),
            P(None, "dp"),
            P(None, "fsdp"),
            P(None, "dp"),
            P(None, "dp"),
            P(None, "fsdp"),
            P("fsdp"),
            P("dp"),
            P(),
        ),
        out_specs=(
            P(),
            P(),
            P(),
            P("dp", "fsdp"),
            P("dp", "fsdp"),
            P("dp"),
            P("fsdp"),
            P(None, "fsdp", "dp"),
            P(None, "fsdp", "dp"),
            P(None, "fsdp"),
            P(None, "dp"),
            P(None, "fsdp", "dp"),
            P(None, "fsdp", "dp"),
            P(None, "fsdp"),
            P(None, "dp"),
            P(None, "fsdp", "dp"),
            P(None, "fsdp", "dp"),
            P(None, "fsdp"),
            P(None, "dp"),
            P(None, "dp", "fsdp"),
            P(None, "dp", "fsdp"),
            P(None, "dp"),
            P(None, "fsdp"),
            P("fsdp", "dp"),
            P("fsdp", "dp"),
            P("fsdp"),
            P("dp"),
            P(),
            P(),
            P(),
        ),
        check_vma=False,
    )
```

```python
import functools

import jax
import jax.numpy as jnp
from jax import lax
from jax.experimental import pallas as pl
from jax.experimental.pallas import tpu as pltpu
from jax.sharding import PartitionSpec as P

D = 256
HEADS = 8
HEAD = D // HEADS
FF = 1024
CATS = 32
CLASSES = 32
LAYERS = 3
SEG = 48
MEM = 48
CTX = 96
VOCAB = 1024
GROUP = 4
ROWS = GROUP * CTX
SPREAD = HEADS * CTX
WIDE = 3 * D + D + FF + FF
CUT = [0, 3 * D, 4 * D, 4 * D + FF, WIDE]
VMEM_BYTES = 56 * 1024 * 1024

decay_two = 0.9
step_rate = 0.3
clip_limit = 0.05
tiny_term = 1e-30
norm_eps = 1e-06
masked_score = -1e30
log2_e = 1.4426950408889634
score_scale = HEAD ** (-0.5)
gelu_one = 0.7978845608028654
gelu_two = 0.044715


def dot_nn(left, right):
    return lax.dot_general(
        left, right, (((1,), (0,)), ((), ())), preferred_element_type=jnp.float32
    )


def dot_nt(left, right):
    return lax.dot_general(
        left, right, (((1,), (1,)), ((), ())), preferred_element_type=jnp.float32
    )


def dot_tn(left, right):
    return lax.dot_general(
        left, right, (((0,), (0,)), ((), ())), preferred_element_type=jnp.float32
    )


def inverse_rms(values):
    return lax.rsqrt(jnp.mean(values * values, axis=-1, keepdims=True) + norm_eps)


def rms_back(values, inverse, gain_row, upstream):
    normed = values * inverse
    scaled = upstream * gain_row
    inner = jnp.mean(scaled * normed, axis=-1, keepdims=True)
    return (
        inverse * (scaled - normed * inner),
        jnp.sum(upstream * normed, axis=0, keepdims=True),
    )


def head_masks():
    lane = lax.broadcasted_iota(jnp.int32, (1, D // 2), 1) // HEAD
    return [lane == head for head in range(HEADS // 2)]


def expand_heads(rows, masks):
    half = D // 2
    nothing = jnp.zeros((CTX, half), rows.dtype)
    pieces = []
    for head in range(HEADS):
        side, at = divmod(head, HEADS // 2)
        kept = rows[:, side * half : (side + 1) * half] * masks[at].astype(rows.dtype)
        pair = [kept, nothing] if side == 0 else [nothing, kept]
        pieces.append(jnp.concatenate(pair, axis=1))
    return jnp.concatenate(pieces, axis=0)


def collapse_heads(spread, rows, masks):
    half, span = D // 2, SPREAD // 2
    sides = []
    for side in range(2):
        product = dot_tn(
            spread[:, side * span : (side + 1) * span], rows[:, side * half : (side + 1) * half]
        )
        taken = product[(HEADS // 2 - 1) * CTX :]
        for at in range(HEADS // 2 - 1):
            taken = jnp.where(masks[at], product[at * CTX : (at + 1) * CTX], taken)
        sides.append(taken)
    return jnp.concatenate(sides, axis=1)


def fill_bias(bias_ref):
    key_at = lax.broadcasted_iota(jnp.int32, (CTX, SPREAD), 0)
    query_at = lax.broadcasted_iota(jnp.int32, (CTX, SPREAD), 1) % CTX
    later = key_at > query_at
    crosses = (query_at >= MEM) & (key_at < MEM)
    bias_ref[0] = jnp.where(later | crosses, masked_score, 0.0)
    bias_ref[1] = jnp.where(later, masked_score, 0.0)


def unpack_weights(gathered_ref, widths, start=0):
    count = gathered_ref.shape[0]
    found = []
    for width in widths:
        found.append(
            jnp.concatenate(
                [gathered_ref[at, :, start : start + width] for at in range(count)], axis=1
            )
        )
        start += width
    return found


def one_hot_rows(latent_rows):
    spot = lax.broadcasted_iota(jnp.int32, (CATS, VOCAB), 1) // CLASSES
    group = lax.broadcasted_iota(jnp.int32, (CATS, VOCAB), 0)
    spreader = jnp.where(spot == group, 1.0, 0.0).astype(jnp.bfloat16)
    classes = (lax.broadcasted_iota(jnp.int32, (1, VOCAB), 1) % CLASSES).astype(jnp.float32)
    drawn = dot_nn(latent_rows, spreader)
    return jnp.where(drawn == classes, 1.0, 0.0).astype(jnp.bfloat16)


def forward_kernel(layer, widths, first, *refs):
    if first:
        (latent_ref, gathered_ref, gains_ref, valid_ref, entry_ref) = refs[:5]
        refs = refs[5:]
    else:
        (entry_ref, gathered_ref, gains_ref, valid_ref) = refs[:4]
        refs = refs[4:]
    output_ref, middle_ref, qkv_ref, mix_ref, lse_ref, weight_ref, bias_ref, inner_ref = refs[:8]
    step = pl.program_id(0)

    @pl.when(step == 0)
    def _():
        fill_bias(bias_ref)
        pieces = unpack_weights(gathered_ref, widths)
        for at in range(4):
            weight_ref[:, CUT[at] : CUT[at + 1]] = pieces[at]
        if first:
            embed_ref = refs[8]
            span = gathered_ref.shape[2] - sum(widths)
            embed_ref[...] = unpack_weights(gathered_ref, [span], sum(widths))[0]

    if first:
        hidden = dot_nt(one_hot_rows(latent_ref[...]), refs[8][...])
        entry_ref[...] = hidden
    else:
        hidden = entry_ref[...]
    masks = head_masks()
    gain_att = gains_ref[layer : layer + 1, :]
    gain_ffn = gains_ref[LAYERS + layer : LAYERS + layer + 1, :]
    normed = (hidden * inverse_rms(hidden) * gain_att).astype(jnp.bfloat16)
    qkv_ref[...] = dot_nn(normed, weight_ref[:, CUT[0] : CUT[1]]).astype(jnp.bfloat16)
    for sample in range(GROUP):
        rows = slice(sample * CTX, (sample + 1) * CTX)
        queries = qkv_ref[rows, 0:D]
        keys = qkv_ref[rows, D : 2 * D]
        values = qkv_ref[rows, 2 * D : 3 * D]
        scores = dot_nt(keys, expand_heads(queries, masks))
        scores = scores + bias_ref[valid_ref[step * GROUP + sample]]
        peak = jnp.max(scores, axis=0, keepdims=True)
        exponent = jnp.exp2((scores - peak) * (score_scale * log2_e))
        total = jnp.sum(exponent, axis=0, keepdims=True)
        chance = (exponent * (1.0 / total)).astype(jnp.bfloat16)
        mix_ref[rows, :] = collapse_heads(chance, values, masks).astype(jnp.bfloat16)
        lse_ref[sample] = peak * (score_scale * log2_e) + jnp.log2(total)
    middle = hidden + dot_nn(mix_ref[...], weight_ref[:, CUT[1] : CUT[2]])
    middle_ref[...] = middle
    normed_two = (middle * inverse_rms(middle) * gain_ffn).astype(jnp.bfloat16)
    for part in range(FF // D):
        columns = slice(part * D, (part + 1) * D)
        inner = dot_nn(normed_two, weight_ref[:, CUT[2] + part * D : CUT[2] + (part + 1) * D])
        for sample in range(GROUP):
            rows = slice(sample * CTX, (sample + 1) * CTX)
            value = inner[rows]
            bend = jnp.tanh(value * (gelu_one + (gelu_one * gelu_two) * (value * value)))
            inner_ref[rows, columns] = ((0.5 * value) * (1.0 + bend)).astype(jnp.bfloat16)
    output_ref[...] = middle + dot_nt(inner_ref[...], weight_ref[:, CUT[3] : CUT[4]])


def row_spec(width):
    return pl.BlockSpec((ROWS, width), lambda step: (step, 0))


def whole_spec(shape):
    return pl.BlockSpec(shape, lambda step: (0,) * len(shape))


def smem_spec():
    return pl.BlockSpec(memory_space=pltpu.SMEM)


def run_forward(layer, widths, source, gathered, gains, valid):
    first = layer == 0
    tokens = source.shape[0]
    f32, b16 = jnp.float32, jnp.bfloat16
    shape = jax.ShapeDtypeStruct
    common = [whole_spec(gathered.shape), whole_spec(gains.shape), smem_spec()]
    outs = [
        (shape((tokens, D), f32), row_spec(D)),
        (shape((tokens, D), f32), row_spec(D)),
        (shape((tokens, 3 * D), b16), row_spec(3 * D)),
        (shape((tokens, D), b16), row_spec(D)),
        (
            shape((tokens // CTX, 1, SPREAD), f32),
            pl.BlockSpec((GROUP, 1, SPREAD), lambda step: (step, 0, 0)),
        ),
        (shape((D, WIDE), b16), whole_spec((D, WIDE))),
    ]
    scratch = [pltpu.VMEM((2, CTX, SPREAD), f32), pltpu.VMEM((ROWS, FF), b16)]
    if first:
        in_specs = [row_spec(CATS)] + common
        operands = (source, gathered, gains, valid)
        outs = [(shape((tokens, D), f32), row_spec(D))] + outs
        scratch = scratch + [pltpu.VMEM((D, VOCAB), b16)]
    else:
        in_specs = [row_spec(D)] + common
        operands = (source, gathered, gains, valid)
    found = pl.pallas_call(
        functools.partial(forward_kernel, layer, widths, first),
        grid=(tokens // ROWS,),
        in_specs=in_specs,
        out_specs=[spec for _, spec in outs],
        out_shape=[item for item, _ in outs],
        scratch_shapes=scratch,
        compiler_params=pltpu.CompilerParams(vmem_limit_bytes=VMEM_BYTES),
        cost_estimate=pl.CostEstimate(
            flops=2 * tokens * D * WIDE * (2 if first else 1),
            bytes_accessed=tokens * D * 16 + D * WIDE * 4,
            transcendentals=tokens * (FF + SPREAD),
        ),
        name="layer_forward",
    )(*operands)
    if first:
        return found[0], found[1:]
    return source, found


def head_kernel(start, hidden_ref, table_ref, targets_ref, counted_ref, gains_ref, *refs):
    dhidden_ref, head_grad_ref, gain_ref, loss_ref, turned_ref, final_ref, dlogits_ref = refs
    samples = hidden_ref.shape[0] // CTX
    count = table_ref.shape[0]
    width = head_grad_ref.shape[2]
    tokens = samples * SEG
    gain_row = gains_ref[2 * LAYERS : 2 * LAYERS + 1, :]
    head = unpack_weights(table_ref, [width], start)[0]
    turned_ref[...] = head.T
    for sample in range(samples):
        latest = hidden_ref[sample * CTX + MEM : (sample + 1) * CTX, :]
        final_ref[sample * SEG : (sample + 1) * SEG, :] = (
            latest * inverse_rms(latest) * gain_row
        ).astype(jnp.bfloat16)
    block = D
    loss = jnp.zeros((1, block), jnp.float32)
    spots = lax.broadcasted_iota(jnp.int32, (CLASSES, block), 0)
    for part in range(tokens // block):
        columns = slice(part * block, (part + 1) * block)
        counted = counted_ref[0:1, columns]
        final = final_ref[columns, :]
        for quarter in range(VOCAB // D):
            logits = dot_nt(turned_ref[quarter * D : (quarter + 1) * D, :], final)
            for inside in range(D // CLASSES):
                group = quarter * (D // CLASSES) + inside
                values = logits[inside * CLASSES : (inside + 1) * CLASSES]
                peak = jnp.max(values, axis=0, keepdims=True)
                shifted = values - peak
                exponent = jnp.exp2(shifted * log2_e)
                total = jnp.sum(exponent, axis=0, keepdims=True)
                hot = spots == targets_ref[group : group + 1, columns]
                chosen = jnp.sum(jnp.where(hot, shifted, 0.0), axis=0, keepdims=True)
                loss = loss + counted * (jnp.log(total) - chosen)
                chance = exponent * (1.0 / total)
                slope = (chance - jnp.where(hot, 1.0, 0.0)) * counted
                dlogits_ref[group * CLASSES : (group + 1) * CLASSES, columns] = slope.astype(
                    jnp.bfloat16
                )
    loss_ref[...] = jnp.sum(loss, axis=1, keepdims=True)
    head_grad = dot_nt(final_ref[...].T, dlogits_ref[...])
    for at in range(count):
        head_grad_ref[at] = head_grad[:, at * width : (at + 1) * width]
    dfinal = dot_nn(head, dlogits_ref[...]).T
    gain_sum = jnp.zeros((1, D), jnp.float32)
    for sample in range(samples):
        latest = hidden_ref[sample * CTX + MEM : (sample + 1) * CTX, :]
        slope, gain_part = rms_back(
            latest,
            inverse_rms(latest),
            gain_row,
            dfinal[sample * SEG : (sample + 1) * SEG, :],
        )
        gain_sum = gain_sum + gain_part
        dhidden_ref[sample * CTX : sample * CTX + MEM, :] = jnp.zeros((MEM, D), jnp.float32)
        dhidden_ref[sample * CTX + MEM : (sample + 1) * CTX, :] = slope
    gain_ref[...] = gain_sum


def run_head(hidden, table, start, targets, counted, gains):
    tokens = hidden.shape[0]
    counts = targets.shape[1]
    f32, b16 = jnp.float32, jnp.bfloat16
    shape = jax.ShapeDtypeStruct
    vmem = pl.BlockSpec(memory_space=pltpu.VMEM)
    return pl.pallas_call(
        functools.partial(head_kernel, start),
        in_specs=[vmem] * 5,
        out_specs=[vmem] * 4,
        out_shape=[
            shape((tokens, D), f32),
            shape(table.shape[:2] + (table.shape[2] - start,), f32),
            shape((1, D), f32),
            shape((1, 1), f32),
        ],
        scratch_shapes=[
            pltpu.VMEM((VOCAB, D), b16),
            pltpu.VMEM((counts, D), b16),
            pltpu.VMEM((VOCAB, counts), b16),
        ],
        compiler_params=pltpu.CompilerParams(vmem_limit_bytes=VMEM_BYTES),
        cost_estimate=pl.CostEstimate(
            flops=6 * counts * D * VOCAB,
            bytes_accessed=tokens * D * 8 + D * VOCAB * 6,
            transcendentals=counts * VOCAB,
        ),
        name="head_and_loss",
    )(hidden, table, targets, counted, gains)


def backward_kernel(layer, widths, first, *refs):
    (entry_ref, middle_ref, qkv_ref, mix_ref, lse_ref, up_ref, weight_ref, gains_ref, valid_ref) = (
        refs[:9]
    )
    refs = refs[9:]
    if first:
        latent_ref = refs[0]
        refs = refs[1:]
        grad_ref, gain_ref = refs[:2]
        refs = refs[2:]
    else:
        dentry_ref, grad_ref, gain_ref = refs[:3]
        refs = refs[3:]
    (
        bias_ref,
        normed_ref,
        normed_two_ref,
        inner_ref,
        dinner_ref,
        dout_ref,
        dmiddle_ref,
        dqkv_ref,
        mixes_ref,
    ) = refs[:9]
    step = pl.program_id(0)
    last = pl.num_programs(0) - 1
    here = pl.ds(pl.multiple_of(step * ROWS, ROWS), ROWS)

    @pl.when(step == 0)
    def _():
        fill_bias(bias_ref)
        gain_ref[...] = jnp.zeros_like(gain_ref)

    masks = head_masks()
    gain_att = gains_ref[layer : layer + 1, :]
    gain_ffn = gains_ref[LAYERS + layer : LAYERS + layer + 1, :]
    upstream = up_ref[...]
    dout = upstream.astype(jnp.bfloat16)
    dout_ref[here, :] = dout
    mixes_ref[here, :] = mix_ref[...]
    middle = middle_ref[...]
    inverse_two = inverse_rms(middle)
    normed_two = (middle * inverse_two * gain_ffn).astype(jnp.bfloat16)
    normed_two_ref[here, :] = normed_two
    for part in range(FF // D):
        columns = slice(part * D, (part + 1) * D)
        inner = dot_nn(normed_two, weight_ref[:, CUT[2] + part * D : CUT[2] + (part + 1) * D])
        dact = dot_nn(dout, weight_ref[:, CUT[3] + part * D : CUT[3] + (part + 1) * D])
        for sample in range(GROUP):
            rows = slice(sample * CTX, (sample + 1) * CTX)
            there = pl.ds(pl.multiple_of(step * ROWS + sample * CTX, CTX), CTX)
            value = inner[rows]
            square = value * value
            bend = jnp.tanh(value * (gelu_one + (gelu_one * gelu_two) * square))
            half_value = 0.5 * value
            inner_ref[there, columns] = (half_value * (1.0 + bend)).astype(jnp.bfloat16)
            slope = (0.5 + 0.5 * bend) + (half_value * (1.0 - bend * bend)) * (
                gelu_one + (3.0 * gelu_one * gelu_two) * square
            )
            dinner_ref[there, columns] = (dact[rows] * slope).astype(jnp.bfloat16)
    dnormed_two = dot_nt(dinner_ref[here, :], weight_ref[:, CUT[2] : CUT[3]])
    through, gain_part = rms_back(middle, inverse_two, gain_ffn, dnormed_two)
    gain_ref[1:2, :] += gain_part
    dmiddle = upstream + through
    dattend = dmiddle.astype(jnp.bfloat16)
    dmiddle_ref[here, :] = dattend
    dmix = dot_nt(dattend, weight_ref[:, CUT[1] : CUT[2]]).astype(jnp.bfloat16)
    for sample in range(GROUP):
        rows = slice(sample * CTX, (sample + 1) * CTX)
        there = pl.ds(pl.multiple_of(step * ROWS + sample * CTX, CTX), CTX)
        queries = expand_heads(qkv_ref[rows, 0:D], masks)
        keys = qkv_ref[rows, D : 2 * D]
        values = qkv_ref[rows, 2 * D : 3 * D]
        slopes = expand_heads(dmix[rows], masks)
        scores = dot_nt(keys, queries) + bias_ref[valid_ref[step * GROUP + sample]]
        chance = jnp.exp2(scores * (score_scale * log2_e) - lse_ref[sample])
        dchance = dot_nt(values, slopes)
        weighed = chance * dchance
        dscore = (weighed - chance * jnp.sum(weighed, axis=0, keepdims=True)).astype(jnp.bfloat16)
        dvalues = dot_nn(chance.astype(jnp.bfloat16), slopes)
        dkeys = dot_nn(dscore, queries) * score_scale
        dqueries = collapse_heads(dscore, keys, masks) * score_scale
        dqkv_ref[there, 0:D] = dqueries.astype(jnp.bfloat16)
        dqkv_ref[there, D : 2 * D] = dkeys.astype(jnp.bfloat16)
        dqkv_ref[there, 2 * D : 3 * D] = dvalues.astype(jnp.bfloat16)
    hidden = entry_ref[...]
    inverse = inverse_rms(hidden)
    normed_ref[here, :] = (hidden * inverse * gain_att).astype(jnp.bfloat16)
    dnormed = dot_nt(dqkv_ref[here, :], weight_ref[:, CUT[0] : CUT[1]])
    through, gain_part = rms_back(hidden, inverse, gain_att, dnormed)
    gain_ref[0:1, :] += gain_part
    dentry = dmiddle + through
    if first:
        dlow_ref, hot_ref = refs[9:11]
        dlow_ref[here, :] = dentry.astype(jnp.bfloat16)
        hot_ref[here, :] = one_hot_rows(latent_ref[...])
    else:
        dentry_ref[...] = dentry

    @pl.when(step == last)
    def _():
        count = grad_ref.shape[0]
        cuts = [0]
        for width in widths:
            cuts.append(cuts[-1] + width)
        pairs = [
            (normed_ref, dqkv_ref),
            (mixes_ref, dmiddle_ref),
            (normed_two_ref, dinner_ref),
            (dout_ref, inner_ref),
        ]
        for which, (left, right) in enumerate(pairs):
            turned = left[...].T
            grad = dot_nn(turned, right[...])
            for at in range(count):
                grad_ref[at, :, cuts[which] : cuts[which + 1]] = grad[
                    :, at * widths[which] : (at + 1) * widths[which]
                ]
        if first:
            grad = dot_nn(refs[9][...].T, refs[10][...])
            span = grad_ref.shape[2] - cuts[-1]
            for at in range(count):
                grad_ref[at, :, cuts[-1] :] = grad[:, at * span : (at + 1) * span]


def run_backward(layer, widths, count, saved, upstream, gains, valid, latents=None, span=0):
    first = layer == 0
    entry, (output, middle, qkv, mix, lse, weights) = saved
    tokens = upstream.shape[0]
    f32, b16 = jnp.float32, jnp.bfloat16
    shape = jax.ShapeDtypeStruct
    in_specs = [
        row_spec(D),
        row_spec(D),
        row_spec(3 * D),
        row_spec(D),
        pl.BlockSpec((GROUP, 1, SPREAD), lambda step: (step, 0, 0)),
        row_spec(D),
        whole_spec(weights.shape),
        whole_spec(gains.shape),
        smem_spec(),
    ]
    operands = [entry, middle, qkv, mix, lse, upstream, weights, gains, valid]
    across = sum(widths) + span
    outs = [
        (shape((count, D, across), f32), whole_spec((count, D, across))),
        (shape((2, D), f32), whole_spec((2, D))),
    ]
    scratch = [
        pltpu.VMEM((2, CTX, SPREAD), f32),
        pltpu.VMEM((tokens, D), b16),
        pltpu.VMEM((tokens, D), b16),
        pltpu.VMEM((tokens, FF), b16),
        pltpu.VMEM((tokens, FF), b16),
        pltpu.VMEM((tokens, D), b16),
        pltpu.VMEM((tokens, D), b16),
        pltpu.VMEM((tokens, 3 * D), b16),
        pltpu.VMEM((tokens, D), b16),
    ]
    if first:
        in_specs.append(row_spec(CATS))
        operands.append(latents)
        scratch = scratch + [pltpu.VMEM((tokens, D), b16), pltpu.VMEM((tokens, VOCAB), b16)]
    else:
        outs.insert(0, (shape((tokens, D), f32), row_spec(D)))
    return pl.pallas_call(
        functools.partial(backward_kernel, layer, widths, first),
        grid=(tokens // ROWS,),
        in_specs=in_specs,
        out_specs=[spec for _, spec in outs],
        out_shape=[item for item, _ in outs],
        scratch_shapes=scratch,
        compiler_params=pltpu.CompilerParams(vmem_limit_bytes=VMEM_BYTES),
        cost_estimate=pl.CostEstimate(
            flops=6 * tokens * D * WIDE,
            bytes_accessed=tokens * D * 24 + D * WIDE * 6,
            transcendentals=tokens * (FF + SPREAD),
        ),
        name="layer_backward",
    )(*operands)


def swap(value, axis, bit):
    pairs = [(place, place ^ bit) for place in range(lax.axis_size(axis))]
    return lax.ppermute(value, axis, pairs)


def gather_pieces(pieces):
    outer = lax.axis_size("dp").bit_length() - 1
    inner = lax.axis_size("fsdp").bit_length() - 1
    order = [("dp", bit) for bit in reversed(range(outer))] + [
        ("fsdp", bit) for bit in reversed(range(inner))
    ]
    done = [None] * len(order)
    found = []
    for piece in pieces:
        held = piece.reshape((1,) * (outer + inner) + piece.shape)
        for place, (axis, bit) in enumerate(order):
            if done[place] is not None:
                held, _ = lax.optimization_barrier((held, done[place]))
            other = swap(held, axis, 1 << bit)
            done[place] = other
            upper = (lax.axis_index(axis) >> bit) & 1 == 1
            held = jnp.where(
                upper,
                jnp.concatenate([other, held], axis=place),
                jnp.concatenate([held, other], axis=place),
            )
        found.append(
            held.reshape(lax.axis_size("dp"), lax.axis_size("fsdp") * piece.shape[0], piece.shape[1])
        )
    return found


def scatter_pieces(blocks):
    outer = lax.axis_size("dp").bit_length() - 1
    inner = lax.axis_size("fsdp").bit_length() - 1
    rows, columns = blocks.shape[1] >> inner, blocks.shape[2]
    held = blocks.reshape((2,) * (outer + inner) + (rows, columns))
    order = [("dp", bit) for bit in reversed(range(outer))] + [
        ("fsdp", bit) for bit in reversed(range(inner))
    ]
    places = {item: place for place, item in enumerate(order)}
    for axis, bit in [("fsdp", bit) for bit in range(inner)] + [("dp", bit) for bit in range(outer)]:
        place = places[(axis, bit)]
        upper = (lax.axis_index(axis) >> bit) & 1 == 1
        low = lax.slice_in_dim(held, 0, 1, axis=place)
        high = lax.slice_in_dim(held, 1, 2, axis=place)
        other = swap(jnp.where(upper, low, high).astype(jnp.bfloat16), axis, 1 << bit)
        held = jnp.where(upper, high, low) + other.astype(jnp.float32)
    return held.reshape(rows, columns)


def sum_over(value, axis):
    terms = [value] + [swap(value, axis, step) for step in range(1, lax.axis_size(axis))]
    while len(terms) > 1:
        terms = [terms[at] + terms[at + 1] for at in range(0, len(terms), 2)]
    return terms[0]


def flat(items):
    return jnp.concatenate([item.reshape(-1) for item in items])


def unflat(vector, items):
    found, at = [], 0
    for item in items:
        found.append(vector[at : at + item.size].reshape(item.shape))
        at += item.size
    return found


def shards(
    latents,
    targets,
    horizon,
    memory_valid,
    embed,
    qkv_weight,
    out_weight,
    up_weight,
    down_weight,
    head_weight,
    gains,
    embed_rows,
    embed_cols,
    qkv_rows,
    qkv_cols,
    out_rows,
    out_cols,
    up_rows,
    up_cols,
    down_rows,
    down_cols,
    head_rows,
    head_cols,
    gain_second,
):
    samples = latents.shape[0]
    count = lax.axis_size("dp")
    layer_parts = [
        jnp.concatenate(
            [qkv_weight[at], out_weight[at], up_weight[at], down_weight[at].T], axis=1
        ).astype(jnp.bfloat16)
        for at in range(LAYERS)
    ]
    widths = [qkv_weight.shape[2], out_weight.shape[2], up_weight.shape[2], down_weight.shape[1]]
    cuts = [0, widths[0], sum(widths[:2]), sum(widths[:3]), sum(widths)]
    span = embed.shape[0]
    layer_parts[0] = jnp.concatenate([layer_parts[0], embed.T.astype(jnp.bfloat16)], axis=1)
    layer_parts[-1] = jnp.concatenate([layer_parts[-1], head_weight.astype(jnp.bfloat16)], axis=1)
    gathered = gather_pieces(layer_parts)

    latent_rows = latents.astype(jnp.bfloat16).reshape(samples * CTX, CATS)
    target_rows = targets.transpose(2, 0, 1).reshape(CATS, samples * SEG)
    counted = jnp.arange(SEG, dtype=jnp.int32)[None, :] < horizon[:, None]
    counted = counted.astype(jnp.float32).reshape(1, samples * SEG)
    current = latent_rows
    saved = []
    for at in range(LAYERS):
        saved.append(run_forward(at, widths, current, gathered[at], gains, memory_valid))
        current = saved[-1][1][0]
    upstream, head_term, dgain_final, loss_local = run_head(
        current, gathered[-1], cuts[-1], target_rows, counted, gains
    )
    loss_local = loss_local[0, 0]
    head_raw = scatter_pieces(head_term)
    layer_raws = [None] * LAYERS
    att_terms = [None] * LAYERS
    ffn_terms = [None] * LAYERS
    for at in reversed(range(LAYERS)):
        found = run_backward(
            at,
            widths,
            count,
            saved[at],
            upstream,
            gains,
            memory_valid,
            latent_rows if at == 0 else None,
            span if at == 0 else 0,
        )
        if at:
            upstream = found[0]
        layer_raws[at] = scatter_pieces(found[-2])
        att_terms[at], ffn_terms[at] = found[-1][0], found[-1][1]
    embed_raw = layer_raws[0][:, cuts[-1] :]
    gain_local = jnp.stack(att_terms + ffn_terms + [dgain_final[0]])

    raws = [jnp.stack([raw[:, cuts[at] : cuts[at + 1]] for raw in layer_raws]) for at in range(4)]
    raws = raws + [embed_raw, head_raw]
    masters = [
        qkv_weight,
        out_weight,
        up_weight,
        down_weight.transpose(0, 2, 1),
        embed.T,
        head_weight,
    ]
    inner_old = [qkv_rows, out_rows, up_rows, down_cols, embed_cols, head_rows]
    outer_old = [qkv_cols, out_cols, up_cols, down_rows, embed_rows, head_cols]
    inner_is_row = [True, True, True, False, False, True]
    inner_part = [jnp.sum(raw * raw, axis=-1) for raw in raws]
    outer_part = [jnp.sum(raw * raw, axis=-2) for raw in raws]
    weight_square = [jnp.sum(master * master, axis=(-2, -1)) for master in masters]
    outer_row_sums = [
        jnp.sum(outer_old[at], axis=-1) for at in range(6) if not inner_is_row[at]
    ]
    inner_row_sums = [jnp.sum(inner_old[at], axis=-1) for at in range(6) if inner_is_row[at]]
    scalars = [loss_local, jnp.sum(horizon).astype(jnp.float32)]
    first = inner_part + outer_row_sums + weight_square + scalars + [gain_local]
    first_sum = unflat(sum_over(flat(first), "dp"), first)
    inner_global, first_sum = first_sum[:6], first_sum[6:]
    outer_row_sums, first_sum = first_sum[:2], first_sum[2:]
    entry_square = [jnp.sum(part, axis=-1) for part in inner_global]
    second = outer_part + inner_row_sums + entry_square + first_sum
    second_sum = unflat(sum_over(flat(second), "fsdp"), second)
    outer_global, second_sum = second_sum[:6], second_sum[6:]
    inner_row_sums, second_sum = second_sum[:4], second_sum[4:]
    entry_square, second_sum = second_sum[:6], second_sum[6:]
    weight_total, second_sum = second_sum[:6], second_sum[6:]
    loss_total, count_total, gain_sum = second_sum
    row_sums = inner_row_sums[:3] + outer_row_sums + inner_row_sums[3:]

    square_total = jnp.sum(gain_sum * gain_sum)
    for part in entry_square:
        square_total = square_total + jnp.sum(part)
    norm_value = jnp.sqrt(square_total) / count_total
    scaling = jnp.minimum(1.0, clip_limit / norm_value) / count_total
    found = []
    for at in range(6):
        inner_length = masters[at].shape[-2] * lax.axis_size("fsdp")
        outer_length = masters[at].shape[-1] * lax.axis_size("dp")
        row_length = inner_length if inner_is_row[at] else outer_length
        entries = inner_length * outer_length
        square_scale = scaling * scaling
        inner_new = decay_two * inner_old[at] + (1 - decay_two) * (
            square_scale * inner_global[at] / outer_length + tiny_term
        )
        outer_new = decay_two * outer_old[at] + (1 - decay_two) * (
            square_scale * outer_global[at] / inner_length + tiny_term
        )
        mean_rows = decay_two * (row_sums[at] / row_length) + (1 - decay_two) * (
            square_scale * entry_square[at] / entries + tiny_term
        )
        spread = jnp.sqrt(weight_total[at] / entries)
        grad = raws[at] * scaling
        scale_of = (step_rate * spread * jnp.sqrt(mean_rows))[..., None, None]
        updated = masters[at] - scale_of * grad * (
            lax.rsqrt(inner_new)[..., :, None] * lax.rsqrt(outer_new)[..., None, :]
        )
        found.append((updated, grad, inner_new, outer_new))
    results = [loss_total, count_total, norm_value]
    for at in [4, 0, 1, 2, 3, 5]:
        updated, grad, inner_new, outer_new = found[at]
        if inner_is_row[at]:
            results = results + [updated, grad, inner_new, outer_new]
        else:
            turned = [jnp.swapaxes(item, -1, -2) for item in (updated, grad)]
            results = results + turned + [outer_new, inner_new]
    gain_grad = gain_sum * scaling
    gain_second_new = decay_two * gain_second + (1 - decay_two) * (
        gain_grad * gain_grad + tiny_term
    )
    gains_new = gains - step_rate * jnp.sqrt(
        jnp.mean(gains * gains, axis=-1, keepdims=True)
    ) * gain_grad * lax.rsqrt(gain_second_new)
    results = results + [gains_new, gain_grad, gain_second_new]
    return tuple(results)


def solution(mesh):
    return jax.shard_map(
        shards,
        mesh=mesh,
        in_specs=(
            P(("dp", "fsdp"), None, None),
            P(("dp", "fsdp"), None, None),
            P(("dp", "fsdp")),
            P(("dp", "fsdp")),
            P("dp", "fsdp"),
            P(None, "fsdp", "dp"),
            P(None, "fsdp", "dp"),
            P(None, "fsdp", "dp"),
            P(None, "dp", "fsdp"),
            P("fsdp", "dp"),
            P(),
            P("dp"),
            P("fsdp"),
            P(None, "fsdp"),
            P(None, "dp"),
            P(None, "fsdp"),
            P(None, "dp"),
            P(None, "fsdp"),
            P(None, "dp"),
            P(None, "dp"),
            P(None, "fsdp"),
            P("fsdp"),
            P("dp"),
            P(),
        ),
        out_specs=(
            P(),
            P(),
            P(),
            P("dp", "fsdp"),
            P("dp", "fsdp"),
            P("dp"),
            P("fsdp"),
            P(None, "fsdp", "dp"),
            P(None, "fsdp", "dp"),
            P(None, "fsdp"),
            P(None, "dp"),
            P(None, "fsdp", "dp"),
            P(None, "fsdp", "dp"),
            P(None, "fsdp"),
            P(None, "dp"),
            P(None, "fsdp", "dp"),
            P(None, "fsdp", "dp"),
            P(None, "fsdp"),
            P(None, "dp"),
            P(None, "dp", "fsdp"),
            P(None, "dp", "fsdp"),
            P(None, "dp"),
            P(None, "fsdp"),
            P("fsdp", "dp"),
            P("fsdp", "dp"),
            P("fsdp"),
            P("dp"),
            P(),
            P(),
            P(),
        ),
        check_vma=False,
    )
```

```python
import functools

import jax
import jax.numpy as jnp
from jax import lax
from jax.experimental import pallas as pl
from jax.experimental.pallas import tpu as pltpu
from jax.sharding import PartitionSpec as P

D = 256
HEADS = 8
HEAD = D // HEADS
FF = 1024
CATS = 32
CLASSES = 32
LAYERS = 3
SEG = 48
MEM = 48
CTX = 96
VOCAB = 1024
GROUP = 4
ROWS = GROUP * CTX
SPREAD = HEADS * CTX
PARTS = [3 * D, D, FF, FF]
VMEM_BYTES = 56 * 1024 * 1024

decay_two = 0.9
step_rate = 0.3
clip_limit = 0.05
tiny_term = 1e-30
norm_eps = 1e-06
masked_score = -1e30
log2_e = 1.4426950408889634
score_scale = HEAD ** (-0.5)
gelu_one = 0.7978845608028654
gelu_two = 0.044715


def dot_nn(left, right):
    return lax.dot_general(
        left, right, (((1,), (0,)), ((), ())), preferred_element_type=jnp.float32
    )


def dot_nt(left, right):
    return lax.dot_general(
        left, right, (((1,), (1,)), ((), ())), preferred_element_type=jnp.float32
    )


def dot_tn(left, right):
    return lax.dot_general(
        left, right, (((0,), (0,)), ((), ())), preferred_element_type=jnp.float32
    )


def inverse_rms(values):
    return lax.rsqrt(jnp.mean(values * values, axis=-1, keepdims=True) + norm_eps)


def rms_back(values, inverse, gain_row, upstream):
    normed = values * inverse
    scaled = upstream * gain_row
    inner = jnp.mean(scaled * normed, axis=-1, keepdims=True)
    return (
        inverse * (scaled - normed * inner),
        jnp.sum(upstream * normed, axis=0, keepdims=True),
    )


def head_masks():
    lane = lax.broadcasted_iota(jnp.int32, (1, D // 2), 1) // HEAD
    return [lane == head for head in range(HEADS // 2)]


def expand_heads(rows, masks):
    half = D // 2
    nothing = jnp.zeros((rows.shape[0], half), rows.dtype)
    pieces = []
    for head in range(HEADS):
        side, at = divmod(head, HEADS // 2)
        kept = rows[:, side * half : (side + 1) * half] * masks[at].astype(rows.dtype)
        pair = [kept, nothing] if side == 0 else [nothing, kept]
        pieces.append(jnp.concatenate(pair, axis=1))
    return jnp.concatenate(pieces, axis=0)


def collapse_heads(spread, rows, masks):
    half, span = D // 2, spread.shape[1] // 2
    queries = span // (HEADS // 2)
    sides = []
    for side in range(2):
        product = dot_tn(
            spread[:, side * span : (side + 1) * span], rows[:, side * half : (side + 1) * half]
        )
        taken = product[(HEADS // 2 - 1) * queries :]
        for at in range(HEADS // 2 - 1):
            taken = jnp.where(masks[at], product[at * queries : (at + 1) * queries], taken)
        sides.append(taken)
    return jnp.concatenate(sides, axis=1)


def fill_bias(bias_ref):
    spread = bias_ref.shape[2]
    queries = spread // HEADS
    key_at = lax.broadcasted_iota(jnp.int32, (CTX, spread), 0)
    query_at = lax.broadcasted_iota(jnp.int32, (CTX, spread), 1) % queries + (CTX - queries)
    later = key_at > query_at
    crosses = (query_at >= MEM) & (key_at < MEM)
    bias_ref[0] = jnp.where(later | crosses, masked_score, 0.0)
    bias_ref[1] = jnp.where(later, masked_score, 0.0)


def block_place(outer_at, inner_high, outer_bits, inner_bits):
    place = 0
    for bit in range(outer_bits):
        place |= ((outer_at >> bit) & 1) << (outer_bits - 1 - bit)
    for bit in range(inner_bits - 1):
        place |= ((inner_high >> bit) & 1) << (outer_bits + inner_bits - 2 - bit)
    return place


def place_weights(targets, own_ref, other_ref, core, widths, bits, start=0):
    outer_bits, inner_bits = bits
    rows = own_ref.shape[1]
    for high in range(1 << (inner_bits - 1)):
        for source, side in ((own_ref, core), (other_ref, 1 - core)):
            here = pl.ds(pl.multiple_of((2 * high + side) * rows, rows), rows)
            at = start
            for (target, column), width in zip(targets, widths):
                block = [
                    source[block_place(outer, high, outer_bits, inner_bits), :, at : at + width]
                    for outer in range(1 << outer_bits)
                ]
                target[here, column : column + (width << outer_bits)] = jnp.concatenate(
                    block, axis=1
                )
                at += width


def write_blocks(send_ref, keep_ref, sum_ref, core, widths, bits):
    outer_bits, inner_bits = bits
    rows = keep_ref.shape[1]
    for high in range(1 << (inner_bits - 1)):
        for target, side in ((keep_ref, core), (send_ref, 1 - core)):
            here = pl.ds(pl.multiple_of((2 * high + side) * rows, rows), rows)
            taken = sum_ref[here, :]
            for outer in range(1 << outer_bits):
                block, column = [], 0
                for width in widths:
                    block.append(taken[:, column + outer * width : column + (outer + 1) * width])
                    column += width << outer_bits
                target[block_place(outer, high, outer_bits, inner_bits)] = jnp.concatenate(
                    block, axis=1
                ).astype(target.dtype)


def one_hot_rows(latent_rows):
    spot = lax.broadcasted_iota(jnp.int32, (CATS, VOCAB), 1) // CLASSES
    group = lax.broadcasted_iota(jnp.int32, (CATS, VOCAB), 0)
    spreader = jnp.where(spot == group, 1.0, 0.0).astype(jnp.bfloat16)
    classes = (lax.broadcasted_iota(jnp.int32, (1, VOCAB), 1) % CLASSES).astype(jnp.float32)
    drawn = dot_nn(latent_rows, spreader)
    return jnp.where(drawn == classes, 1.0, 0.0).astype(jnp.bfloat16)


def tail_rows(values, queries):
    if queries == CTX:
        return values
    return jnp.concatenate(
        [
            values[(sample + 1) * CTX - queries : (sample + 1) * CTX]
            for sample in range(values.shape[0] // CTX)
        ],
        axis=0,
    )


def attend_forward(step, hidden, gain_row, weight_ref, valid_ref, bias_ref, masks, refs):
    middle_ref, qkv_ref, mix_ref, lse_ref = refs
    queries = lse_ref.shape[2] // HEADS
    normed = (hidden * inverse_rms(hidden) * gain_row).astype(jnp.bfloat16)
    qkv_ref[...] = dot_nn(normed, weight_ref[:, 0 : 3 * D]).astype(jnp.bfloat16)
    for sample in range(GROUP):
        rows = slice(sample * CTX, (sample + 1) * CTX)
        spread = expand_heads(qkv_ref[(sample + 1) * CTX - queries : (sample + 1) * CTX, 0:D], masks)
        scores = dot_nt(qkv_ref[rows, D : 2 * D], spread)
        scores = scores + bias_ref[valid_ref[step * GROUP + sample]]
        peak = jnp.max(scores, axis=0, keepdims=True)
        exponent = jnp.exp2((scores - peak) * (score_scale * log2_e))
        total = jnp.sum(exponent, axis=0, keepdims=True)
        chance = (exponent * (1.0 / total)).astype(jnp.bfloat16)
        mix_ref[sample * queries : (sample + 1) * queries, :] = collapse_heads(
            chance, qkv_ref[rows, 2 * D : 3 * D], masks
        ).astype(jnp.bfloat16)
        lse_ref[sample] = peak * (score_scale * log2_e) + jnp.log2(total)
    middle_ref[...] = tail_rows(hidden, queries) + dot_nn(
        mix_ref[...], weight_ref[:, 3 * D : 4 * D]
    )


def gelu_bend(value, square):
    return jnp.tanh(value * (gelu_one + (gelu_one * gelu_two) * square))


def gelu_slope(half_value, bend, square):
    return (0.5 + 0.5 * bend) + (half_value * (1.0 - bend * bend)) * (
        gelu_one + (3.0 * gelu_one * gelu_two) * square
    )


def feed_forward(middle, gain_row, weight_ref, inner_ref):
    normed = (middle * inverse_rms(middle) * gain_row).astype(jnp.bfloat16)
    for part in range(FF // D):
        columns = slice(part * D, (part + 1) * D)
        inner = dot_nn(normed, weight_ref[:, columns])
        for sample in range(GROUP):
            rows = slice(sample * CTX, (sample + 1) * CTX)
            value = inner[rows]
            bend = gelu_bend(value, value * value)
            inner_ref[rows, columns] = ((0.5 * value) * (1.0 + bend)).astype(jnp.bfloat16)
    return middle + dot_nt(inner_ref[...], weight_ref[:, FF : 2 * FF])


def feed_back(here, upstream, middle, gain_row, weight_ref, refs):
    normed_ref, inner_ref, dinner_ref, dout_ref = refs
    dout = upstream.astype(jnp.bfloat16)
    dout_ref[here(0, ROWS), :] = dout
    inverse = inverse_rms(middle)
    normed = (middle * inverse * gain_row).astype(jnp.bfloat16)
    normed_ref[here(0, ROWS), :] = normed
    for part in range(FF // D):
        columns = slice(part * D, (part + 1) * D)
        inner = dot_nn(normed, weight_ref[:, columns])
        dact = dot_nn(dout, weight_ref[:, FF + part * D : FF + (part + 1) * D])
        for sample in range(GROUP):
            rows = slice(sample * CTX, (sample + 1) * CTX)
            there = here(sample * CTX, CTX)
            value = inner[rows]
            square = value * value
            bend = gelu_bend(value, square)
            half_value = 0.5 * value
            inner_ref[there, columns] = (half_value * (1.0 + bend)).astype(jnp.bfloat16)
            dinner_ref[there, columns] = (
                dact[rows] * gelu_slope(half_value, bend, square)
            ).astype(jnp.bfloat16)
    dnormed = dot_nt(dinner_ref[here(0, ROWS), :], weight_ref[:, 0:FF])
    through, gain_part = rms_back(middle, inverse, gain_row, dnormed)
    return upstream + through, gain_part


def attend_back(step, here, saved, dmiddle, gain_row, weight_ref, valid_ref, bias_ref, masks, refs):
    hidden, qkv_ref, mix_ref, lse_ref = saved
    normed_ref, dmiddle_ref, dqkv_ref, mixes_ref = refs
    queries = lse_ref.shape[2] // HEADS
    short = here(0, GROUP * queries, queries)
    dattend = dmiddle.astype(jnp.bfloat16)
    dmiddle_ref[short, :] = dattend
    mixes_ref[short, :] = mix_ref[...]
    dmix = dot_nt(dattend, weight_ref[:, 3 * D : 4 * D]).astype(jnp.bfloat16)
    for sample in range(GROUP):
        rows = slice(sample * CTX, (sample + 1) * CTX)
        there = here(sample * CTX, CTX)
        spread = expand_heads(qkv_ref[(sample + 1) * CTX - queries : (sample + 1) * CTX, 0:D], masks)
        keys = qkv_ref[rows, D : 2 * D]
        slopes = expand_heads(dmix[sample * queries : (sample + 1) * queries], masks)
        scores = dot_nt(keys, spread) + bias_ref[valid_ref[step * GROUP + sample]]
        chance = jnp.exp2(scores * (score_scale * log2_e) - lse_ref[sample])
        dchance = dot_nt(qkv_ref[rows, 2 * D : 3 * D], slopes)
        weighed = chance * dchance
        dscore = (weighed - chance * jnp.sum(weighed, axis=0, keepdims=True)).astype(jnp.bfloat16)
        dvalues = dot_nn(chance.astype(jnp.bfloat16), slopes)
        dkeys = dot_nn(dscore, spread) * score_scale
        dqueries = (collapse_heads(dscore, keys, masks) * score_scale).astype(jnp.bfloat16)
        if queries < CTX:
            nothing = jnp.zeros((CTX - queries, D), jnp.bfloat16)
            dqueries = jnp.concatenate([nothing, dqueries], axis=0)
        dqkv_ref[there, 0:D] = dqueries
        dqkv_ref[there, D : 2 * D] = dkeys.astype(jnp.bfloat16)
        dqkv_ref[there, 2 * D : 3 * D] = dvalues.astype(jnp.bfloat16)
    inverse = inverse_rms(hidden)
    normed_ref[here(0, ROWS), :] = (hidden * inverse * gain_row).astype(jnp.bfloat16)
    dnormed = dot_nt(dqkv_ref[here(0, ROWS), :], weight_ref[:, 0 : 3 * D])
    through, gain_part = rms_back(hidden, inverse, gain_row, dnormed)
    if queries < CTX:
        nothing = jnp.zeros((CTX - queries, D), jnp.float32)
        pieces = []
        for sample in range(GROUP):
            pieces = pieces + [nothing, dmiddle[sample * queries : (sample + 1) * queries]]
        dmiddle = jnp.concatenate(pieces, axis=0)
    return dmiddle + through, gain_part


def row_spec(width, rows=ROWS):
    return pl.BlockSpec((rows, width), lambda step: (step, 0))


def lse_spec(queries):
    return pl.BlockSpec((GROUP, 1, HEADS * queries), lambda step: (step, 0, 0))


def whole_spec(shape):
    return pl.BlockSpec(shape, lambda step: (0,) * len(shape))


def smem_spec():
    return pl.BlockSpec(memory_space=pltpu.SMEM)


def forward_kernel(layer, widths, bits, source_ref, own_ref, other_ref, gains_ref, valid_ref, core_ref, *refs):
    entry_ref, att_ref, before_ref, bias_ref = refs[0], refs[5], refs[6], refs[7]
    step = pl.program_id(0)

    @pl.when(step == 0)
    def _():
        fill_bias(bias_ref)
        att = [(att_ref, 0), (att_ref, 3 * D)]
        before = [(before_ref, 0)] if layer == 0 else [(before_ref, 0), (before_ref, FF)]
        targets = att + before if layer == 0 else before + att
        place_weights(targets, own_ref, other_ref, core_ref[0], widths[: len(targets)], bits)

    if layer == 0:
        hidden = dot_nt(one_hot_rows(source_ref[...]), before_ref[...])
    else:
        gain_ffn = gains_ref[LAYERS + layer - 1 : LAYERS + layer, :]
        hidden = feed_forward(source_ref[...], gain_ffn, before_ref, refs[8])
    entry_ref[...] = hidden
    attend_forward(
        step,
        hidden,
        gains_ref[layer : layer + 1, :],
        att_ref,
        valid_ref,
        bias_ref,
        head_masks(),
        refs[1:5],
    )


def run_forward(layer, widths, bits, source, own, other, gains, valid, core):
    tokens = source.shape[0]
    queries = SEG if layer == LAYERS - 1 else CTX
    f32, b16 = jnp.float32, jnp.bfloat16
    shape = jax.ShapeDtypeStruct
    short = tokens // CTX * queries
    outs = [
        (shape((tokens, D), f32), row_spec(D)),
        (shape((short, D), f32), row_spec(D, GROUP * queries)),
        (shape((tokens, 3 * D), b16), row_spec(3 * D)),
        (shape((short, D), b16), row_spec(D, GROUP * queries)),
        (shape((tokens // CTX, 1, HEADS * queries), f32), lse_spec(queries)),
        (shape((D, 4 * D), b16), whole_spec((D, 4 * D))),
    ]
    scratch = [pltpu.VMEM((2, CTX, HEADS * queries), f32)]
    if layer == 0:
        scratch = [pltpu.VMEM((D, VOCAB), b16)] + scratch
    else:
        outs.append((shape((D, 2 * FF), b16), whole_spec((D, 2 * FF))))
        scratch.append(pltpu.VMEM((ROWS, FF), b16))
    return pl.pallas_call(
        functools.partial(forward_kernel, layer, widths, bits),
        grid=(tokens // ROWS,),
        in_specs=[
            row_spec(source.shape[1]),
            whole_spec(own.shape),
            whole_spec(other.shape),
            whole_spec(gains.shape),
            smem_spec(),
            smem_spec(),
        ],
        out_specs=[spec for _, spec in outs],
        out_shape=[item for item, _ in outs],
        scratch_shapes=scratch,
        compiler_params=pltpu.CompilerParams(vmem_limit_bytes=VMEM_BYTES),
        cost_estimate=pl.CostEstimate(
            flops=2 * tokens * D * 12 * D,
            bytes_accessed=tokens * D * 16 + D * 12 * D * 4,
            transcendentals=tokens * (FF + HEADS * CTX),
        ),
        name="forward_part",
    )(source, own, other, gains, valid, core)


def top_kernel(widths, bits, start, middle_ref, own_ref, other_ref, targets_ref, counted_ref, gains_ref, core_ref, *refs):
    dmiddle_ref, send_ref, keep_ref, gain_ref, loss_ref = refs[:5]
    weight_ref, head_ref, turned_ref, final_ref, dlogits_ref = refs[5:10]
    normed_ref, inner_ref, slope_ref, dinner_ref, dout_ref, last_ref, sum_ref = refs[10:]
    tokens = middle_ref.shape[0]
    gain_final = gains_ref[2 * LAYERS : 2 * LAYERS + 1, :]
    gain_ffn = gains_ref[2 * LAYERS - 1 : 2 * LAYERS, :]
    place_weights(
        [(weight_ref, 0), (weight_ref, FF), (head_ref, 0)],
        own_ref,
        other_ref,
        core_ref[0],
        widths,
        bits,
        start,
    )
    turned_ref[...] = head_ref[...].T
    for block in range(tokens // ROWS):
        rows = slice(block * ROWS, (block + 1) * ROWS)
        middle = middle_ref[rows, :]
        normed = (middle * inverse_rms(middle) * gain_ffn).astype(jnp.bfloat16)
        normed_ref[rows, :] = normed
        for part in range(FF // D):
            columns = slice(part * D, (part + 1) * D)
            inner = dot_nn(normed, weight_ref[:, columns])
            for piece in range(GROUP):
                value = inner[piece * CTX : (piece + 1) * CTX]
                there = slice(block * ROWS + piece * CTX, block * ROWS + (piece + 1) * CTX)
                square = value * value
                bend = gelu_bend(value, square)
                half_value = 0.5 * value
                inner_ref[there, columns] = (half_value * (1.0 + bend)).astype(jnp.bfloat16)
                slope_ref[there, columns] = gelu_slope(half_value, bend, square)
        last = middle + dot_nt(inner_ref[rows, :], weight_ref[:, FF : 2 * FF])
        last_ref[rows, :] = last
        final_ref[rows, :] = (last * inverse_rms(last) * gain_final).astype(jnp.bfloat16)
    span = D
    loss = jnp.zeros((1, span), jnp.float32)
    spots = lax.broadcasted_iota(jnp.int32, (CLASSES, span), 0)
    for part in range(tokens // span):
        columns = slice(part * span, (part + 1) * span)
        counted = counted_ref[0:1, columns]
        final = final_ref[columns, :]
        for quarter in range(VOCAB // D):
            logits = dot_nt(turned_ref[quarter * D : (quarter + 1) * D, :], final)
            for inside in range(D // CLASSES):
                group = quarter * (D // CLASSES) + inside
                values = logits[inside * CLASSES : (inside + 1) * CLASSES]
                shifted = values - jnp.max(values, axis=0, keepdims=True)
                exponent = jnp.exp2(shifted * log2_e)
                total = jnp.sum(exponent, axis=0, keepdims=True)
                hot = spots == targets_ref[group : group + 1, columns]
                chosen = jnp.sum(jnp.where(hot, shifted, 0.0), axis=0, keepdims=True)
                loss = loss + counted * (jnp.log(total) - chosen)
                chance = exponent * (1.0 / total)
                slope = (chance - jnp.where(hot, 1.0, 0.0)) * counted
                dlogits_ref[group * CLASSES : (group + 1) * CLASSES, columns] = slope.astype(
                    jnp.bfloat16
                )
    loss_ref[...] = jnp.sum(loss, axis=1, keepdims=True)
    sum_ref[:, 2 * FF :] = dot_nt(final_ref[...].T, dlogits_ref[...])
    dfinal = dot_nn(head_ref[...], dlogits_ref[...]).T
    last = last_ref[...]
    dlast, gain_part = rms_back(last, inverse_rms(last), gain_final, dfinal)
    gain_ref[1:2, :] = gain_part
    last_ref[...] = dlast
    gain_sum = jnp.zeros((1, D), jnp.float32)
    for block in range(tokens // ROWS):
        rows = slice(block * ROWS, (block + 1) * ROWS)
        upstream = last_ref[rows, :]
        dout = upstream.astype(jnp.bfloat16)
        dout_ref[rows, :] = dout
        for part in range(FF // D):
            columns = slice(part * D, (part + 1) * D)
            dact = dot_nn(dout, weight_ref[:, FF + part * D : FF + (part + 1) * D])
            dinner_ref[rows, columns] = (dact * slope_ref[rows, columns]).astype(jnp.bfloat16)
        dnormed = dot_nt(dinner_ref[rows, :], weight_ref[:, 0:FF])
        middle = middle_ref[rows, :]
        through, gain_part = rms_back(middle, inverse_rms(middle), gain_ffn, dnormed)
        gain_sum = gain_sum + gain_part
        dmiddle_ref[rows, :] = upstream + through
    gain_ref[0:1, :] = gain_sum
    sum_ref[:, 0:FF] = dot_nn(normed_ref[...].T, dinner_ref[...])
    sum_ref[:, FF : 2 * FF] = dot_nn(dout_ref[...].T, inner_ref[...])
    write_blocks(send_ref, keep_ref, sum_ref, core_ref[0], widths, bits)


def block_outs(own, widths):
    shape = jax.ShapeDtypeStruct
    blocks = own.shape[:2] + (sum(widths),)
    return [shape(blocks, jnp.bfloat16), shape(blocks, jnp.float32)]


def run_top(widths, bits, start, middle, own, other, targets, counted, gains, core):
    tokens = middle.shape[0]
    f32, b16 = jnp.float32, jnp.bfloat16
    shape = jax.ShapeDtypeStruct
    vmem = pl.BlockSpec(memory_space=pltpu.VMEM)
    return pl.pallas_call(
        functools.partial(top_kernel, widths, bits, start),
        in_specs=[vmem] * 6 + [smem_spec()],
        out_specs=[vmem] * 5,
        out_shape=[shape((tokens, D), f32)]
        + block_outs(own, widths)
        + [shape((2, D), f32), shape((1, 1), f32)],
        scratch_shapes=[
            pltpu.VMEM((D, 2 * FF), b16),
            pltpu.VMEM((D, VOCAB), b16),
            pltpu.VMEM((VOCAB, D), b16),
            pltpu.VMEM((tokens, D), b16),
            pltpu.VMEM((VOCAB, tokens), b16),
            pltpu.VMEM((tokens, D), b16),
            pltpu.VMEM((tokens, FF), b16),
            pltpu.VMEM((tokens, FF), f32),
            pltpu.VMEM((tokens, FF), b16),
            pltpu.VMEM((tokens, D), b16),
            pltpu.VMEM((tokens, D), f32),
            pltpu.VMEM((D, 2 * FF + VOCAB), f32),
        ],
        compiler_params=pltpu.CompilerParams(vmem_limit_bytes=VMEM_BYTES),
        cost_estimate=pl.CostEstimate(
            flops=6 * tokens * D * 3 * FF,
            bytes_accessed=tokens * D * 8 + D * 3 * FF * 10,
            transcendentals=tokens * (FF + VOCAB),
        ),
        name="loss_part",
    )(middle, own, other, targets, counted, gains, core)


def backward_kernel(layer, widths, bits, *refs):
    entry_ref, qkv_ref, mix_ref, lse_ref, dmiddle_ref, att_ref = refs[:6]
    gains_ref, valid_ref, core_ref = refs[6:9]
    if layer == 0:
        latent_ref, send_ref, keep_ref, gain_ref, bias_ref = refs[9:14]
        att_kept, before_kept, sum_ref = refs[14:18], refs[18:20], refs[20]
    else:
        before_ref, ffn_ref, out_ref, send_ref, keep_ref, gain_ref, bias_ref = refs[9:16]
        att_kept, before_kept, sum_ref = refs[16:20], refs[20:24], refs[24]
    step = pl.program_id(0)

    def here(start, length, unit=CTX):
        base = step * (GROUP * unit)
        return pl.ds(pl.multiple_of(base + start, 16), length)

    @pl.when(step == 0)
    def _():
        fill_bias(bias_ref)
        gain_ref[...] = jnp.zeros_like(gain_ref)

    dentry, gain_part = attend_back(
        step,
        here,
        (entry_ref[...], qkv_ref, mix_ref, lse_ref),
        dmiddle_ref[...],
        gains_ref[layer : layer + 1, :],
        att_ref,
        valid_ref,
        bias_ref,
        head_masks(),
        att_kept,
    )
    gain_ref[0:1, :] += gain_part
    if layer == 0:
        before_kept[0][here(0, ROWS), :] = dentry.astype(jnp.bfloat16)
        before_kept[1][here(0, ROWS), :] = one_hot_rows(latent_ref[...])
    else:
        dbefore, gain_part = feed_back(
            here,
            dentry,
            before_ref[...],
            gains_ref[LAYERS + layer - 1 : LAYERS + layer, :],
            ffn_ref,
            before_kept,
        )
        out_ref[...] = dbefore
        gain_ref[1:2, :] += gain_part

    @pl.when(step == pl.num_programs(0) - 1)
    def _():
        normed_ref, dattend_ref, dqkv_ref, mixes_ref = att_kept
        att = [(normed_ref, dqkv_ref), (mixes_ref, dattend_ref)]
        if layer == 0:
            pairs = att + [(before_kept[0], before_kept[1])]
        else:
            normed_two_ref, inner_ref, dinner_ref, dout_ref = before_kept
            pairs = [(normed_two_ref, dinner_ref), (dout_ref, inner_ref)] + att
        column = 0
        for left, right in pairs:
            wide = right.shape[1]
            sum_ref[:, column : column + wide] = dot_nn(left[...].T, right[...])
            column += wide
        write_blocks(send_ref, keep_ref, sum_ref, core_ref[0], widths, bits)


def run_backward(layer, widths, bits, blocks_like, saved, dmiddle, gains, valid, core, before):
    entry, _, qkv, mix, lse, weights = saved[:6]
    tokens = entry.shape[0]
    queries = lse.shape[2] // HEADS
    short = tokens // CTX * queries
    f32, b16 = jnp.float32, jnp.bfloat16
    shape = jax.ShapeDtypeStruct
    in_specs = [
        row_spec(D),
        row_spec(3 * D),
        row_spec(D, GROUP * queries),
        lse_spec(queries),
        row_spec(D, GROUP * queries),
        whole_spec(weights.shape),
        whole_spec(gains.shape),
        smem_spec(),
        smem_spec(),
    ]
    operands = [entry, qkv, mix, lse, dmiddle, weights, gains, valid, core]
    blocks = block_outs(blocks_like, widths)
    outs = [(item, whole_spec(item.shape)) for item in blocks]
    outs.append((shape((2, D), f32), whole_spec((2, D))))
    scratch = [
        pltpu.VMEM((2, CTX, HEADS * queries), f32),
        pltpu.VMEM((tokens, D), b16),
        pltpu.VMEM((short, D), b16),
        pltpu.VMEM((tokens, 3 * D), b16),
        pltpu.VMEM((short, D), b16),
    ]
    if layer == 0:
        in_specs.append(row_spec(CATS))
        operands.append(before)
        scratch = scratch + [pltpu.VMEM((tokens, D), b16), pltpu.VMEM((tokens, VOCAB), b16)]
        wide = 4 * D + VOCAB
    else:
        in_specs = in_specs + [row_spec(D), whole_spec(before[1].shape)]
        operands = operands + list(before)
        outs.insert(0, (shape((tokens, D), f32), row_spec(D)))
        scratch = scratch + [
            pltpu.VMEM((tokens, D), b16),
            pltpu.VMEM((tokens, FF), b16),
            pltpu.VMEM((tokens, FF), b16),
            pltpu.VMEM((tokens, D), b16),
        ]
        wide = 4 * D + 2 * FF
    return pl.pallas_call(
        functools.partial(backward_kernel, layer, widths, bits),
        grid=(tokens // ROWS,),
        in_specs=in_specs,
        out_specs=[spec for _, spec in outs],
        out_shape=[item for item, _ in outs],
        scratch_shapes=scratch + [pltpu.VMEM((D, wide), f32)],
        compiler_params=pltpu.CompilerParams(vmem_limit_bytes=VMEM_BYTES),
        cost_estimate=pl.CostEstimate(
            flops=6 * tokens * D * wide,
            bytes_accessed=tokens * D * 24 + D * wide * 6,
            transcendentals=tokens * (FF + HEADS * CTX),
        ),
        name="backward_part",
    )(*operands)


def matrix_plan(widths):
    order = [
        (2, 2), (3, 2), (5, 0), (2, 1), (3, 1), (0, 2), (1, 2),
        (2, 0), (3, 0), (0, 1), (1, 1), (0, 0), (1, 0), (4, 0),
    ]
    plan, column = {}, 0
    for which, layer in order:
        plan[(which, layer)] = (column, widths[which])
        column += widths[which]
    return plan, column


def matrix_list():
    return [(which, layer) for which in range(4) for layer in range(LAYERS)] + [(4, 0), (5, 0)]


MATRICES = 4 * LAYERS + 2
LANES = 128
INNER_ROWS = 16
COMMON_ROWS = 16
ROW_IS_INNER = [True, True, True, False, False, True]


def master_of(masters, which, layer):
    if which == 1:
        return masters[1][layer].T
    return masters[which][layer] if which < 4 else masters[which][...]


def old_row(refs, which, layer):
    return refs[which][layer : layer + 1, :] if which < 4 else refs[which][...]


def stats_kernel(widths, *refs):
    raw_early, raw_late, masters, row_refs = refs[0], refs[1], refs[2:8], refs[8:14]
    gains_at, loss_ref, counted_ref, packet_ref = refs[14:18], refs[18], refs[19], refs[20]
    plan, total = matrix_plan(widths)
    square = jnp.concatenate([raw_early[...] * raw_early[...], raw_late[...] * raw_late[...]], axis=1)
    rows = square.shape[0]
    one = lambda value: jnp.sum(jnp.sum(value, axis=1, keepdims=True), axis=0, keepdims=True)
    inner, weights, entries, row_sums = [], [], [], []
    for which, layer in matrix_list():
        column, width = plan[(which, layer)]
        inner.append(jnp.sum(square[:, column : column + width], axis=1, keepdims=True))
        entries.append(jnp.sum(inner[-1], axis=0, keepdims=True))
        master = master_of(masters, which, layer)
        weights.append(one(master * master))
        row_sums.append(one(old_row(row_refs, which, layer)))
    packet_ref[...] = jnp.zeros_like(packet_ref)
    inner.append(jnp.zeros((rows, LANES - MATRICES), jnp.float32))
    packet_ref[0:INNER_ROWS, 0:rows] = jnp.concatenate(inner, axis=1).T[0:INNER_ROWS, :]
    top, two, one_at, zero = [ref[...] for ref in gains_at]
    gain = jnp.concatenate(
        [zero[0:1], one_at[0:1], two[0:1], one_at[1:2], two[1:2], top[0:1], top[1:2]], axis=0
    )
    scalars = [loss_ref[...], one(counted_ref[...])] + weights + entries + row_sums
    scalars.append(jnp.zeros((1, LANES - len(scalars)), jnp.float32))
    at = INNER_ROWS
    packet_ref[at : at + 7, :] = gain[:, 0:LANES]
    packet_ref[at + 7 : at + 8, :] = jnp.concatenate(scalars, axis=1)
    packet_ref[at + 8 : at + 15, :] = gain[:, LANES:]
    outer = jnp.sum(square, axis=0, keepdims=True)
    at = INNER_ROWS + COMMON_ROWS
    for row, start in enumerate(range(0, total, LANES)):
        stop = min(start + LANES, total)
        packet_ref[at + row : at + row + 1, 0 : stop - start] = outer[:, start:stop]


def outer_rows(widths):
    _, total = matrix_plan(widths)
    return -(-total // (8 * LANES)) * 8


def run_stats(widths, raw_early, raw_late, masters, rows, gain_parts, loss, counted):
    vmem = pl.BlockSpec(memory_space=pltpu.VMEM)
    operands = [raw_early, raw_late] + masters + rows + gain_parts + [loss, counted]
    packet = (INNER_ROWS + COMMON_ROWS + outer_rows(widths), LANES)
    return pl.pallas_call(
        functools.partial(stats_kernel, widths),
        in_specs=[vmem] * len(operands),
        out_specs=vmem,
        out_shape=jax.ShapeDtypeStruct(packet, jnp.float32),
        name="statistics",
    )(*operands)


def update_kernel(widths, sizes, *refs):
    across_ref, along_ref, raw_early, raw_late = refs[:4]
    masters, inner_refs, outer_refs = refs[4:10], refs[10:16], refs[16:22]
    gains_ref, second_ref = refs[22:24]
    outs = refs[24:]
    outer_count, inner_count = sizes
    plan, total = matrix_plan(widths)
    rows = raw_early.shape[0]
    scalars = along_ref[7:8, :]
    pick = lambda at: scalars[:, at : at + 1]
    gain_sum = jnp.concatenate([along_ref[0:7, :], along_ref[8:15, :]], axis=1)
    gain_square = jnp.sum(jnp.sum(gain_sum * gain_sum, axis=1, keepdims=True), axis=0, keepdims=True)
    square_total = gain_square
    for at in range(MATRICES):
        square_total = square_total + pick(2 + MATRICES + at)
    count_total = pick(1)
    norm_value = jnp.sqrt(square_total) / count_total
    scaling = jnp.minimum(1.0, clip_limit / norm_value) / count_total
    square_scale = scaling * scaling
    outer_total = jnp.concatenate(
        [
            along_ref[COMMON_ROWS + row : COMMON_ROWS + row + 1, 0 : min(LANES, total - row * LANES)]
            for row in range(-(-total // LANES))
        ],
        axis=1,
    )
    inner_new = []
    for at, (which, layer) in enumerate(matrix_list()):
        outer_length = widths[which] * outer_count
        inner_new.append(
            decay_two * old_row(inner_refs, which, layer)
            + (1 - decay_two)
            * (square_scale * across_ref[at : at + 1, 0:rows] / outer_length + tiny_term)
        )
    stacked = jnp.concatenate(inner_new, axis=0)
    stacked = jnp.concatenate([stacked, jnp.ones((LANES - MATRICES, rows), jnp.float32)], axis=0)
    if rows < LANES:
        stacked = jnp.concatenate([stacked, jnp.ones((LANES, LANES - rows), jnp.float32)], axis=1)
    turned = lax.rsqrt(stacked).T
    outs[0][...] = pick(0)
    outs[1][...] = count_total
    outs[2][...] = norm_value
    first_out = {4: 3, 0: 7, 1: 11, 2: 15, 3: 19, 5: 23}
    for at, (which, layer) in enumerate(matrix_list()):
        column, width = plan[(which, layer)]
        outer_length, inner_length = width * outer_count, rows * inner_count
        row_length = inner_length if ROW_IS_INNER[which] else outer_length
        copies = outer_count if ROW_IS_INNER[which] else inner_count
        entries = outer_length * inner_length
        early = raw_early.shape[1]
        if column < early:
            raw = raw_early[:, column : column + width]
        else:
            raw = raw_late[:, column - early : column - early + width]
        outer_new = decay_two * old_row(outer_refs, which, layer) + (1 - decay_two) * (
            square_scale * outer_total[:, column : column + width] / inner_length + tiny_term
        )
        mean_rows = decay_two * (pick(2 + 2 * MATRICES + at) / (copies * row_length)) + (
            1 - decay_two
        ) * (square_scale * pick(2 + MATRICES + at) / entries + tiny_term)
        factor = step_rate * jnp.sqrt(pick(2 + at) / entries) * jnp.sqrt(mean_rows)
        grad = raw * scaling
        updated = master_of(masters, which, layer) - grad * (
            turned[0:rows, at : at + 1] * (factor * lax.rsqrt(outer_new))
        )
        first = first_out[which]
        row_new, column_new = (
            (inner_new[at], outer_new) if ROW_IS_INNER[which] else (outer_new, inner_new[at])
        )
        if which < 4:
            if which == 1:
                updated, grad = updated.T, grad.T
            outs[first][layer] = updated
            outs[first + 1][layer] = grad
            outs[first + 2][layer : layer + 1, :] = row_new
            outs[first + 3][layer : layer + 1, :] = column_new
        else:
            outs[first][...] = updated
            outs[first + 1][...] = grad
            outs[first + 2][...] = row_new
            outs[first + 3][...] = column_new
    gain_grad = gain_sum * scaling
    second_new = decay_two * second_ref[...] + (1 - decay_two) * (gain_grad * gain_grad + tiny_term)
    gains = gains_ref[...]
    spread = jnp.sqrt(jnp.mean(gains * gains, axis=-1, keepdims=True))
    outs[27][...] = gains - step_rate * spread * gain_grad * lax.rsqrt(second_new)
    outs[28][...] = gain_grad
    outs[29][...] = second_new


def run_update(widths, sizes, across, along, raw_early, raw_late, masters, inner, outer, gains, second):
    vmem = pl.BlockSpec(memory_space=pltpu.VMEM)
    operands = [across, along, raw_early, raw_late] + masters + inner + outer + [gains, second]
    shapes = [(1, 1)] * 3
    for which in [4, 0, 1, 2, 3, 5]:
        shapes = shapes + [masters[which].shape] * 2
        pair = [inner[which].shape, outer[which].shape]
        shapes = shapes + (pair if ROW_IS_INNER[which] else pair[::-1])
    shapes = shapes + [gains.shape] * 3
    return pl.pallas_call(
        functools.partial(update_kernel, widths, sizes),
        in_specs=[vmem] * len(operands),
        out_specs=[vmem] * len(shapes),
        out_shape=[jax.ShapeDtypeStruct(item, jnp.float32) for item in shapes],
        name="update",
    )(*operands)


def swap(value, axis, bit):
    pairs = [(place, place ^ bit) for place in range(lax.axis_size(axis))]
    return lax.ppermute(value, axis, pairs)


def tie(*values):
    return lax.optimization_barrier(values)


class Gather:
    def __init__(self, piece, steps):
        self.held, self.steps, self.at = piece[None], steps, 0

    def send(self):
        axis, bit = self.steps[self.at]
        self.other = swap(self.held, axis, 1 << bit)

    def join(self):
        axis, bit = self.steps[self.at]
        upper = (lax.axis_index(axis) >> bit) & 1 == 1
        self.held = jnp.where(
            upper,
            jnp.concatenate([self.other, self.held]),
            jnp.concatenate([self.held, self.other]),
        )
        self.at += 1

    def step(self, after=None):
        if after is not None:
            self.held, _ = tie(self.held, after.other)
        self.send()
        self.join()


class Scatter:
    def __init__(self, sent, kept, steps):
        self.sent, self.kept, self.steps, self.at = sent, kept, steps, 0

    def send(self):
        axis, bit = self.steps[self.at]
        self.other = swap(self.sent, axis, 1 << bit)

    def join(self):
        self.at += 1
        summed = self.kept + self.other.astype(jnp.float32)
        if self.at == len(self.steps):
            self.kept = summed
            return
        axis, bit = self.steps[self.at]
        side = (lax.axis_index(axis) >> bit) & 1
        half = summed.shape[0] // 2
        parts = summed.reshape((2, half) + summed.shape[1:])
        self.sent = jnp.where(side == 1, parts[0], parts[1]).astype(jnp.bfloat16)
        self.kept = jnp.where(side == 1, parts[1], parts[0])


def merged(parts):
    whole = Scatter(
        jnp.concatenate([part.sent for part in parts], axis=2),
        jnp.concatenate([part.kept for part in parts], axis=2),
        parts[0].steps,
    )
    whole.at = parts[0].at
    return whole


def shards(
    latents,
    targets,
    horizon,
    memory_valid,
    embed,
    qkv_weight,
    out_weight,
    up_weight,
    down_weight,
    head_weight,
    gains,
    embed_rows,
    embed_cols,
    qkv_rows,
    qkv_cols,
    out_rows,
    out_cols,
    up_rows,
    up_cols,
    down_rows,
    down_cols,
    head_rows,
    head_cols,
    gain_second,
):
    samples = latents.shape[0]
    sizes = (lax.axis_size("dp"), lax.axis_size("fsdp"))
    bits = (sizes[0].bit_length() - 1, sizes[1].bit_length() - 1)
    gather_steps = [("dp", bit) for bit in reversed(range(bits[0]))]
    gather_steps = gather_steps + [("fsdp", bit) for bit in reversed(range(bits[1]))]
    scatter_steps = gather_steps[::-1]
    core = (lax.axis_index("fsdp") & 1).astype(jnp.int32).reshape(1)

    low = lambda item: item.astype(jnp.bfloat16)
    out_turned = jnp.swapaxes(out_weight, 1, 2)
    down_turned = jnp.swapaxes(down_weight, 1, 2)
    masters = [qkv_weight, out_turned, up_weight, down_turned, embed.T, head_weight]
    widths = [qkv_weight.shape[2], out_weight.shape[2], up_weight.shape[2], down_weight.shape[1]]
    widths = widths + [embed.shape[0], head_weight.shape[1]]
    att_parts = [[qkv_weight[at], out_weight[at]] for at in range(LAYERS)]
    ffn_parts = [[up_weight[at], down_turned[at]] for at in range(LAYERS)]
    pieces = [
        att_parts[0] + [embed.T],
        ffn_parts[0] + att_parts[1],
        ffn_parts[1] + att_parts[2] + ffn_parts[2] + [head_weight],
    ]
    att_widths, ffn_widths = widths[0:2], widths[2:4]
    first, second, third = [
        Gather(low(jnp.concatenate(piece, axis=1)), gather_steps) for piece in pieces
    ]
    chunk_widths = [
        att_widths + widths[4:5],
        ffn_widths + att_widths,
        ffn_widths + att_widths + ffn_widths + widths[5:6],
    ]

    latent_rows = low(latents).reshape(samples * CTX, CATS)
    target_rows = targets.transpose(2, 0, 1).reshape(CATS, samples * SEG)
    counted = jnp.arange(SEG, dtype=jnp.int32)[None, :] < horizon[:, None]
    counted = counted.astype(jnp.float32).reshape(1, samples * SEG)
    shared = (gains, memory_valid, core)

    count = len(gather_steps)
    for at in range(count - 1):
        first.step()
        if at < count - 2:
            second.step(first)
        if at < count - 3:
            third.step(second)
    first.send()
    second.step(first)
    third.step(second)
    first.held, first.other, second.held, third.held = tie(
        first.held, first.other, second.held, third.held
    )
    second.send()
    third.send()
    kept = [run_forward(0, chunk_widths[0], bits, latent_rows, first.held, first.other, *shared)]
    middle, second.other, third.other = tie(kept[0][1], second.other, third.other)
    third.join()
    second.held, third.held = tie(second.held, third.held)
    third.send()
    kept.append(run_forward(1, chunk_widths[1], bits, middle, second.held, second.other, *shared))
    middle, third.other = tie(kept[1][1], third.other)
    kept.append(run_forward(2, chunk_widths[2], bits, middle, third.held, third.other, *shared))

    dmiddle, sent, held, gain_top, loss = run_top(
        ffn_widths + widths[5:6],
        bits,
        sum(ffn_widths + att_widths),
        kept[2][1],
        third.held,
        third.other,
        target_rows,
        counted,
        gains,
        core,
    )
    top = Scatter(sent, held, scatter_steps)
    top.send()
    like = first.held
    dmiddle, sent, held, gain_two = run_backward(
        2, chunk_widths[1], bits, like, kept[2], dmiddle, *shared, (kept[1][1], kept[2][6])
    )
    dmiddle, top.other = tie(dmiddle, top.other)
    top.join()
    two = Scatter(sent, held, scatter_steps)
    dmiddle, top.sent = tie(dmiddle, top.sent)
    top.send()
    two.send()
    dmiddle, sent, held, gain_one = run_backward(
        1, chunk_widths[1], bits, like, kept[1], dmiddle, *shared, (kept[0][1], kept[1][6])
    )
    dmiddle, top.other, two.other = tie(dmiddle, top.other, two.other)
    top.join()
    two.join()
    one = Scatter(sent, held, scatter_steps)
    dmiddle, top.sent, two.sent = tie(dmiddle, top.sent, two.sent)
    top.send()
    two.send()
    one.send()
    sent, held, gain_zero = run_backward(
        0, chunk_widths[0], bits, like, kept[0], dmiddle, *shared, latent_rows
    )
    sent, top.other, two.other, one.other = tie(sent, top.other, two.other, one.other)
    zero = Scatter(sent, held, scatter_steps)
    zero.send()
    two.join()
    two.send()
    one.join()
    one.send()
    top.join()
    zero.join()
    zero.send()
    one.join()
    one.send()
    two.join()
    zero.join()
    zero.send()
    one.join()
    early = merged([top, two, one])
    while early.at < count:
        early.send()
        early.join()
        zero.join()
        if zero.at < count:
            zero.send()
    while zero.at < count:
        zero.join()
        if zero.at < count:
            zero.send()
    raw_early, raw_late = early.kept[0], zero.kept[0]

    flat = lambda item: item if item.ndim == 2 else item.reshape(1, -1)
    inner = [flat(item) for item in (qkv_rows, out_rows, up_rows, down_cols, embed_cols, head_rows)]
    outer = [flat(item) for item in (qkv_cols, out_cols, up_cols, down_rows, embed_rows, head_cols)]
    row_stats = [inner[at] if ROW_IS_INNER[at] else outer[at] for at in range(6)]
    gain_parts = [gain_top, gain_two, gain_one, gain_zero]
    packet = run_stats(widths, raw_early, raw_late, masters, row_stats, gain_parts, loss, counted)
    edge = INNER_ROWS + COMMON_ROWS
    across = packet[:edge]
    for axis, bit in scatter_steps[bits[1] :]:
        across = across + swap(across, axis, 1 << bit)
    along = jnp.concatenate([across[INNER_ROWS:], packet[edge:]])
    for axis, bit in scatter_steps[: bits[1]][::-1]:
        along = along + swap(along, axis, 1 << bit)
    results = run_update(
        widths, sizes, across, along, raw_early, raw_late, masters, inner, outer, gains, gain_second
    )
    results = list(results)
    for at in range(3):
        results[at] = results[at].reshape(())
    for at in (3, 4, 11, 12, 19, 20):
        results[at] = jnp.swapaxes(results[at], -1, -2)
    for at in (5, 6, 25, 26):
        results[at] = results[at].reshape(-1)
    return tuple(results)


def solution(mesh):
    return jax.shard_map(
        shards,
        mesh=mesh,
        in_specs=(
            P(("dp", "fsdp"), None, None),
            P(("dp", "fsdp"), None, None),
            P(("dp", "fsdp")),
            P(("dp", "fsdp")),
            P("dp", "fsdp"),
            P(None, "fsdp", "dp"),
            P(None, "fsdp", "dp"),
            P(None, "fsdp", "dp"),
            P(None, "dp", "fsdp"),
            P("fsdp", "dp"),
            P(),
            P("dp"),
            P("fsdp"),
            P(None, "fsdp"),
            P(None, "dp"),
            P(None, "fsdp"),
            P(None, "dp"),
            P(None, "fsdp"),
            P(None, "dp"),
            P(None, "dp"),
            P(None, "fsdp"),
            P("fsdp"),
            P("dp"),
            P(),
        ),
        out_specs=(
            P(),
            P(),
            P(),
            P("dp", "fsdp"),
            P("dp", "fsdp"),
            P("dp"),
            P("fsdp"),
            P(None, "fsdp", "dp"),
            P(None, "fsdp", "dp"),
            P(None, "fsdp"),
            P(None, "dp"),
            P(None, "fsdp", "dp"),
            P(None, "fsdp", "dp"),
            P(None, "fsdp"),
            P(None, "dp"),
            P(None, "fsdp", "dp"),
            P(None, "fsdp", "dp"),
            P(None, "fsdp"),
            P(None, "dp"),
            P(None, "dp", "fsdp"),
            P(None, "dp", "fsdp"),
            P(None, "dp"),
            P(None, "fsdp"),
            P("fsdp", "dp"),
            P("fsdp", "dp"),
            P("fsdp"),
            P("dp"),
            P(),
            P(),
            P(),
        ),
        check_vma=False,
    )
```

```python
import functools

import jax
import jax.numpy as jnp
from jax import lax
from jax.experimental import pallas as pl
from jax.experimental.pallas import tpu as pltpu
from jax.sharding import PartitionSpec as P

D = 256
HEADS = 8
HEAD = D // HEADS
FF = 1024
CATS = 32
CLASSES = 32
LAYERS = 3
SEG = 48
MEM = 48
CTX = 96
VOCAB = 1024
GROUP = 4
ROWS = GROUP * CTX
SPREAD = HEADS * CTX
PARTS = [3 * D, D, FF, FF]
VMEM_BYTES = 56 * 1024 * 1024

decay_two = 0.9
step_rate = 0.3
clip_limit = 0.05
tiny_term = 1e-30
norm_eps = 1e-06
masked_score = -1e30
log2_e = 1.4426950408889634
score_scale = HEAD ** (-0.5)
gelu_one = 0.7978845608028654
gelu_two = 0.044715


def dot_nn(left, right):
    return lax.dot_general(
        left, right, (((1,), (0,)), ((), ())), preferred_element_type=jnp.float32
    )


def dot_nt(left, right):
    return lax.dot_general(
        left, right, (((1,), (1,)), ((), ())), preferred_element_type=jnp.float32
    )


def dot_tn(left, right):
    return lax.dot_general(
        left, right, (((0,), (0,)), ((), ())), preferred_element_type=jnp.float32
    )


def inverse_rms(values):
    return lax.rsqrt(jnp.mean(values * values, axis=-1, keepdims=True) + norm_eps)


def rms_back(values, inverse, gain_row, upstream):
    normed = values * inverse
    scaled = upstream * gain_row
    inner = jnp.mean(scaled * normed, axis=-1, keepdims=True)
    return (
        inverse * (scaled - normed * inner),
        jnp.sum(upstream * normed, axis=0, keepdims=True),
    )


def head_masks():
    lane = lax.broadcasted_iota(jnp.int32, (1, D // 2), 1) // HEAD
    return [lane == head for head in range(HEADS // 2)]


def expand_heads(rows, masks):
    half = D // 2
    nothing = jnp.zeros((rows.shape[0], half), rows.dtype)
    pieces = []
    for head in range(HEADS):
        side, at = divmod(head, HEADS // 2)
        kept = rows[:, side * half : (side + 1) * half] * masks[at].astype(rows.dtype)
        pair = [kept, nothing] if side == 0 else [nothing, kept]
        pieces.append(jnp.concatenate(pair, axis=1))
    return jnp.concatenate(pieces, axis=0)


def collapse_heads(spread, rows, masks):
    half, span = D // 2, spread.shape[1] // 2
    queries = span // (HEADS // 2)
    sides = []
    for side in range(2):
        product = dot_tn(
            spread[:, side * span : (side + 1) * span], rows[:, side * half : (side + 1) * half]
        )
        taken = product[(HEADS // 2 - 1) * queries :]
        for at in range(HEADS // 2 - 1):
            taken = jnp.where(masks[at], product[at * queries : (at + 1) * queries], taken)
        sides.append(taken)
    return jnp.concatenate(sides, axis=1)


def fill_bias(bias_ref):
    spread = bias_ref.shape[2]
    queries = spread // HEADS
    key_at = lax.broadcasted_iota(jnp.int32, (CTX, spread), 0)
    query_at = lax.broadcasted_iota(jnp.int32, (CTX, spread), 1) % queries + (CTX - queries)
    later = key_at > query_at
    crosses = (query_at >= MEM) & (key_at < MEM)
    bias_ref[0] = jnp.where(later | crosses, masked_score, 0.0)
    bias_ref[1] = jnp.where(later, masked_score, 0.0)


def block_place(outer_at, inner_high, outer_bits, inner_bits):
    place = outer_at
    for bit in range(inner_bits - 1):
        place |= ((inner_high >> bit) & 1) << (outer_bits + inner_bits - 2 - bit)
    return place


def place_weights(targets, own_ref, other_ref, core, widths, bits, start=0):
    outer_bits, inner_bits = bits
    rows = own_ref.shape[1]
    for high in range(1 << (inner_bits - 1)):
        for source, side in ((own_ref, core), (other_ref, 1 - core)):
            here = pl.ds(pl.multiple_of((2 * high + side) * rows, rows), rows)
            at = start
            for (target, column), width in zip(targets, widths):
                block = [
                    source[block_place(outer, high, outer_bits, inner_bits), :, at : at + width]
                    for outer in range(1 << outer_bits)
                ]
                target[here, column : column + (width << outer_bits)] = jnp.concatenate(
                    block, axis=1
                )
                at += width


def write_blocks(send_ref, keep_ref, sum_ref, core, widths, bits):
    outer_bits, inner_bits = bits
    rows = keep_ref.shape[1]
    for high in range(1 << (inner_bits - 1)):
        for target, side in ((keep_ref, core), (send_ref, 1 - core)):
            here = pl.ds(pl.multiple_of((2 * high + side) * rows, rows), rows)
            taken = sum_ref[here, :]
            for outer in range(1 << outer_bits):
                block, column = [], 0
                for width in widths:
                    block.append(taken[:, column + outer * width : column + (outer + 1) * width])
                    column += width << outer_bits
                target[block_place(outer, high, outer_bits, inner_bits)] = jnp.concatenate(
                    block, axis=1
                ).astype(target.dtype)


def one_hot_rows(latent_rows):
    spot = lax.broadcasted_iota(jnp.int32, (CATS, VOCAB), 1) // CLASSES
    group = lax.broadcasted_iota(jnp.int32, (CATS, VOCAB), 0)
    spreader = jnp.where(spot == group, 1.0, 0.0).astype(jnp.bfloat16)
    classes = (lax.broadcasted_iota(jnp.int32, (1, VOCAB), 1) % CLASSES).astype(jnp.float32)
    drawn = dot_nn(latent_rows, spreader)
    return jnp.where(drawn == classes, 1.0, 0.0).astype(jnp.bfloat16)


def tail_rows(values, queries):
    if queries == CTX:
        return values
    return jnp.concatenate(
        [
            values[(sample + 1) * CTX - queries : (sample + 1) * CTX]
            for sample in range(values.shape[0] // CTX)
        ],
        axis=0,
    )


def attend_forward(step, hidden, gain_row, weight_ref, valid_ref, bias_ref, masks, refs):
    middle_ref, qkv_ref, mix_ref, lse_ref = refs
    queries = lse_ref.shape[2] // HEADS
    normed = (hidden * inverse_rms(hidden) * gain_row).astype(jnp.bfloat16)
    qkv_ref[...] = dot_nn(normed, weight_ref[:, 0 : 3 * D]).astype(jnp.bfloat16)
    for sample in range(GROUP):
        rows = slice(sample * CTX, (sample + 1) * CTX)
        spread = expand_heads(qkv_ref[(sample + 1) * CTX - queries : (sample + 1) * CTX, 0:D], masks)
        scores = dot_nt(qkv_ref[rows, D : 2 * D], spread)
        scores = scores + bias_ref[valid_ref[step * GROUP + sample]]
        peak = jnp.max(scores, axis=0, keepdims=True)
        exponent = jnp.exp2((scores - peak) * (score_scale * log2_e))
        total = jnp.sum(exponent, axis=0, keepdims=True)
        chance = (exponent * (1.0 / total)).astype(jnp.bfloat16)
        mix_ref[sample * queries : (sample + 1) * queries, :] = collapse_heads(
            chance, qkv_ref[rows, 2 * D : 3 * D], masks
        ).astype(jnp.bfloat16)
        lse_ref[sample] = peak * (score_scale * log2_e) + jnp.log2(total)
    middle_ref[...] = tail_rows(hidden, queries) + dot_nn(
        mix_ref[...], weight_ref[:, 3 * D : 4 * D]
    )


def gelu_bend(value, square):
    return jnp.tanh(value * (gelu_one + (gelu_one * gelu_two) * square))


def gelu_slope(half_value, bend, square):
    return (0.5 + 0.5 * bend) + (half_value * (1.0 - bend * bend)) * (
        gelu_one + (3.0 * gelu_one * gelu_two) * square
    )


def feed_forward(middle, gain_row, weight_ref, inner_ref):
    normed = (middle * inverse_rms(middle) * gain_row).astype(jnp.bfloat16)
    for part in range(FF // D):
        columns = slice(part * D, (part + 1) * D)
        inner = dot_nn(normed, weight_ref[:, columns])
        for sample in range(GROUP):
            rows = slice(sample * CTX, (sample + 1) * CTX)
            value = inner[rows]
            bend = gelu_bend(value, value * value)
            inner_ref[rows, columns] = ((0.5 * value) * (1.0 + bend)).astype(jnp.bfloat16)
    return middle + dot_nt(inner_ref[...], weight_ref[:, FF : 2 * FF])


def feed_back(here, upstream, middle, gain_row, weight_ref, refs):
    normed_ref, inner_ref, dinner_ref, dout_ref = refs
    dout = upstream.astype(jnp.bfloat16)
    dout_ref[here(0, ROWS), :] = dout
    inverse = inverse_rms(middle)
    normed = (middle * inverse * gain_row).astype(jnp.bfloat16)
    normed_ref[here(0, ROWS), :] = normed
    for part in range(FF // D):
        columns = slice(part * D, (part + 1) * D)
        inner = dot_nn(normed, weight_ref[:, columns])
        dact = dot_nn(dout, weight_ref[:, FF + part * D : FF + (part + 1) * D])
        for sample in range(GROUP):
            rows = slice(sample * CTX, (sample + 1) * CTX)
            there = here(sample * CTX, CTX)
            value = inner[rows]
            square = value * value
            bend = gelu_bend(value, square)
            half_value = 0.5 * value
            inner_ref[there, columns] = (half_value * (1.0 + bend)).astype(jnp.bfloat16)
            dinner_ref[there, columns] = (
                dact[rows] * gelu_slope(half_value, bend, square)
            ).astype(jnp.bfloat16)
    dnormed = dot_nt(dinner_ref[here(0, ROWS), :], weight_ref[:, 0:FF])
    through, gain_part = rms_back(middle, inverse, gain_row, dnormed)
    return upstream + through, gain_part


def attend_back(step, here, saved, dmiddle, gain_row, weight_ref, valid_ref, bias_ref, masks, refs):
    hidden, qkv_ref, mix_ref, lse_ref = saved
    normed_ref, dmiddle_ref, dqkv_ref, mixes_ref = refs
    queries = lse_ref.shape[2] // HEADS
    short = here(0, GROUP * queries, queries)
    dattend = dmiddle.astype(jnp.bfloat16)
    dmiddle_ref[short, :] = dattend
    mixes_ref[short, :] = mix_ref[...]
    dmix = dot_nt(dattend, weight_ref[:, 3 * D : 4 * D]).astype(jnp.bfloat16)
    for sample in range(GROUP):
        rows = slice(sample * CTX, (sample + 1) * CTX)
        there = here(sample * CTX, CTX)
        spread = expand_heads(qkv_ref[(sample + 1) * CTX - queries : (sample + 1) * CTX, 0:D], masks)
        keys = qkv_ref[rows, D : 2 * D]
        slopes = expand_heads(dmix[sample * queries : (sample + 1) * queries], masks)
        scores = dot_nt(keys, spread) + bias_ref[valid_ref[step * GROUP + sample]]
        chance = jnp.exp2(scores * (score_scale * log2_e) - lse_ref[sample])
        dchance = dot_nt(qkv_ref[rows, 2 * D : 3 * D], slopes)
        weighed = chance * dchance
        dscore = (weighed - chance * jnp.sum(weighed, axis=0, keepdims=True)).astype(jnp.bfloat16)
        dvalues = dot_nn(chance.astype(jnp.bfloat16), slopes)
        dkeys = dot_nn(dscore, spread) * score_scale
        dqueries = (collapse_heads(dscore, keys, masks) * score_scale).astype(jnp.bfloat16)
        if queries < CTX:
            nothing = jnp.zeros((CTX - queries, D), jnp.bfloat16)
            dqueries = jnp.concatenate([nothing, dqueries], axis=0)
        dqkv_ref[there, 0:D] = dqueries
        dqkv_ref[there, D : 2 * D] = dkeys.astype(jnp.bfloat16)
        dqkv_ref[there, 2 * D : 3 * D] = dvalues.astype(jnp.bfloat16)
    inverse = inverse_rms(hidden)
    normed_ref[here(0, ROWS), :] = (hidden * inverse * gain_row).astype(jnp.bfloat16)
    dnormed = dot_nt(dqkv_ref[here(0, ROWS), :], weight_ref[:, 0 : 3 * D])
    through, gain_part = rms_back(hidden, inverse, gain_row, dnormed)
    if queries < CTX:
        nothing = jnp.zeros((CTX - queries, D), jnp.float32)
        pieces = []
        for sample in range(GROUP):
            pieces = pieces + [nothing, dmiddle[sample * queries : (sample + 1) * queries]]
        dmiddle = jnp.concatenate(pieces, axis=0)
    return dmiddle + through, gain_part


def row_spec(width, rows=ROWS):
    return pl.BlockSpec((rows, width), lambda step: (step, 0))


def lse_spec(queries):
    return pl.BlockSpec((GROUP, 1, HEADS * queries), lambda step: (step, 0, 0))


def whole_spec(shape):
    return pl.BlockSpec(shape, lambda step: (0,) * len(shape))


def smem_spec():
    return pl.BlockSpec(memory_space=pltpu.SMEM)


def forward_kernel(layer, widths, bits, source_ref, own_ref, other_ref, gains_ref, valid_ref, core_ref, *refs):
    entry_ref, att_ref, before_ref, bias_ref = refs[0], refs[5], refs[6], refs[7]
    step = pl.program_id(0)

    @pl.when(step == 0)
    def _():
        fill_bias(bias_ref)
        att = [(att_ref, 0), (att_ref, 3 * D)]
        before = [(before_ref, 0)] if layer == 0 else [(before_ref, 0), (before_ref, FF)]
        targets = att + before if layer == 0 else before + att
        place_weights(targets, own_ref, other_ref, core_ref[0], widths[: len(targets)], bits)

    if layer == 0:
        hidden = dot_nt(one_hot_rows(source_ref[...]), before_ref[...])
    else:
        gain_ffn = gains_ref[LAYERS + layer - 1 : LAYERS + layer, :]
        hidden = feed_forward(source_ref[...], gain_ffn, before_ref, refs[8])
    entry_ref[...] = hidden
    attend_forward(
        step,
        hidden,
        gains_ref[layer : layer + 1, :],
        att_ref,
        valid_ref,
        bias_ref,
        head_masks(),
        refs[1:5],
    )


def run_forward(layer, widths, bits, source, own, other, gains, valid, core):
    tokens = source.shape[0]
    queries = SEG if layer == LAYERS - 1 else CTX
    f32, b16 = jnp.float32, jnp.bfloat16
    shape = jax.ShapeDtypeStruct
    short = tokens // CTX * queries
    outs = [
        (shape((tokens, D), f32), row_spec(D)),
        (shape((short, D), f32), row_spec(D, GROUP * queries)),
        (shape((tokens, 3 * D), b16), row_spec(3 * D)),
        (shape((short, D), b16), row_spec(D, GROUP * queries)),
        (shape((tokens // CTX, 1, HEADS * queries), f32), lse_spec(queries)),
        (shape((D, 4 * D), b16), whole_spec((D, 4 * D))),
    ]
    scratch = [pltpu.VMEM((2, CTX, HEADS * queries), f32)]
    if layer == 0:
        scratch = [pltpu.VMEM((D, VOCAB), b16)] + scratch
    else:
        outs.append((shape((D, 2 * FF), b16), whole_spec((D, 2 * FF))))
        scratch.append(pltpu.VMEM((ROWS, FF), b16))
    return pl.pallas_call(
        functools.partial(forward_kernel, layer, widths, bits),
        grid=(tokens // ROWS,),
        in_specs=[
            row_spec(source.shape[1]),
            whole_spec(own.shape),
            whole_spec(other.shape),
            whole_spec(gains.shape),
            smem_spec(),
            smem_spec(),
        ],
        out_specs=[spec for _, spec in outs],
        out_shape=[item for item, _ in outs],
        scratch_shapes=scratch,
        compiler_params=pltpu.CompilerParams(vmem_limit_bytes=VMEM_BYTES),
        cost_estimate=pl.CostEstimate(
            flops=2 * tokens * D * 12 * D,
            bytes_accessed=tokens * D * 16 + D * 12 * D * 4,
            transcendentals=tokens * (FF + HEADS * CTX),
        ),
        name="forward_part",
    )(source, own, other, gains, valid, core)


def top_kernel(widths, bits, start, middle_ref, own_ref, other_ref, targets_ref, counted_ref, gains_ref, core_ref, *refs):
    dmiddle_ref, send_ref, keep_ref, gain_ref, loss_ref = refs[:5]
    weight_ref, head_ref, turned_ref, final_ref, dlogits_ref = refs[5:10]
    normed_ref, inner_ref, slope_ref, dinner_ref, dout_ref, last_ref, sum_ref = refs[10:]
    tokens = middle_ref.shape[0]
    gain_final = gains_ref[2 * LAYERS : 2 * LAYERS + 1, :]
    gain_ffn = gains_ref[2 * LAYERS - 1 : 2 * LAYERS, :]
    place_weights(
        [(weight_ref, 0), (weight_ref, FF), (head_ref, 0)],
        own_ref,
        other_ref,
        core_ref[0],
        widths,
        bits,
        start,
    )
    turned_ref[...] = head_ref[...].T
    for block in range(tokens // ROWS):
        rows = slice(block * ROWS, (block + 1) * ROWS)
        middle = middle_ref[rows, :]
        normed = (middle * inverse_rms(middle) * gain_ffn).astype(jnp.bfloat16)
        normed_ref[rows, :] = normed
        for part in range(FF // D):
            columns = slice(part * D, (part + 1) * D)
            inner = dot_nn(normed, weight_ref[:, columns])
            for piece in range(GROUP):
                value = inner[piece * CTX : (piece + 1) * CTX]
                there = slice(block * ROWS + piece * CTX, block * ROWS + (piece + 1) * CTX)
                square = value * value
                bend = gelu_bend(value, square)
                half_value = 0.5 * value
                inner_ref[there, columns] = (half_value * (1.0 + bend)).astype(jnp.bfloat16)
                slope_ref[there, columns] = gelu_slope(half_value, bend, square)
        last = middle + dot_nt(inner_ref[rows, :], weight_ref[:, FF : 2 * FF])
        last_ref[rows, :] = last
        final_ref[rows, :] = (last * inverse_rms(last) * gain_final).astype(jnp.bfloat16)
    span = D
    loss = jnp.zeros((1, span), jnp.float32)
    spots = lax.broadcasted_iota(jnp.int32, (CLASSES, span), 0)
    for part in range(tokens // span):
        columns = slice(part * span, (part + 1) * span)
        counted = counted_ref[0:1, columns]
        final = final_ref[columns, :]
        for quarter in range(VOCAB // D):
            logits = dot_nt(turned_ref[quarter * D : (quarter + 1) * D, :], final)
            for inside in range(D // CLASSES):
                group = quarter * (D // CLASSES) + inside
                values = logits[inside * CLASSES : (inside + 1) * CLASSES]
                shifted = values - jnp.max(values, axis=0, keepdims=True)
                exponent = jnp.exp2(shifted * log2_e)
                total = jnp.sum(exponent, axis=0, keepdims=True)
                hot = spots == targets_ref[group : group + 1, columns]
                chosen = jnp.sum(jnp.where(hot, shifted, 0.0), axis=0, keepdims=True)
                loss = loss + counted * (jnp.log(total) - chosen)
                chance = exponent * (1.0 / total)
                slope = (chance - jnp.where(hot, 1.0, 0.0)) * counted
                dlogits_ref[group * CLASSES : (group + 1) * CLASSES, columns] = slope.astype(
                    jnp.bfloat16
                )
    loss_ref[...] = jnp.sum(loss, axis=1, keepdims=True)
    sum_ref[:, 2 * FF :] = dot_nt(final_ref[...].T, dlogits_ref[...])
    dfinal = dot_nn(head_ref[...], dlogits_ref[...]).T
    last = last_ref[...]
    dlast, gain_part = rms_back(last, inverse_rms(last), gain_final, dfinal)
    gain_ref[1:2, :] = gain_part
    last_ref[...] = dlast
    gain_sum = jnp.zeros((1, D), jnp.float32)
    for block in range(tokens // ROWS):
        rows = slice(block * ROWS, (block + 1) * ROWS)
        upstream = last_ref[rows, :]
        dout = upstream.astype(jnp.bfloat16)
        dout_ref[rows, :] = dout
        for part in range(FF // D):
            columns = slice(part * D, (part + 1) * D)
            dact = dot_nn(dout, weight_ref[:, FF + part * D : FF + (part + 1) * D])
            dinner_ref[rows, columns] = (dact * slope_ref[rows, columns]).astype(jnp.bfloat16)
        dnormed = dot_nt(dinner_ref[rows, :], weight_ref[:, 0:FF])
        middle = middle_ref[rows, :]
        through, gain_part = rms_back(middle, inverse_rms(middle), gain_ffn, dnormed)
        gain_sum = gain_sum + gain_part
        dmiddle_ref[rows, :] = upstream + through
    gain_ref[0:1, :] = gain_sum
    sum_ref[:, 0:FF] = dot_nn(normed_ref[...].T, dinner_ref[...])
    sum_ref[:, FF : 2 * FF] = dot_nn(dout_ref[...].T, inner_ref[...])
    write_blocks(send_ref, keep_ref, sum_ref, core_ref[0], widths, bits)


def block_outs(own, widths):
    shape = jax.ShapeDtypeStruct
    blocks = own.shape[:2] + (sum(widths),)
    return [shape(blocks, jnp.bfloat16), shape(blocks, jnp.float32)]


def run_top(widths, bits, start, middle, own, other, targets, counted, gains, core):
    tokens = middle.shape[0]
    f32, b16 = jnp.float32, jnp.bfloat16
    shape = jax.ShapeDtypeStruct
    vmem = pl.BlockSpec(memory_space=pltpu.VMEM)
    return pl.pallas_call(
        functools.partial(top_kernel, widths, bits, start),
        in_specs=[vmem] * 6 + [smem_spec()],
        out_specs=[vmem] * 5,
        out_shape=[shape((tokens, D), f32)]
        + block_outs(own, widths)
        + [shape((2, D), f32), shape((1, 1), f32)],
        scratch_shapes=[
            pltpu.VMEM((D, 2 * FF), b16),
            pltpu.VMEM((D, VOCAB), b16),
            pltpu.VMEM((VOCAB, D), b16),
            pltpu.VMEM((tokens, D), b16),
            pltpu.VMEM((VOCAB, tokens), b16),
            pltpu.VMEM((tokens, D), b16),
            pltpu.VMEM((tokens, FF), b16),
            pltpu.VMEM((tokens, FF), f32),
            pltpu.VMEM((tokens, FF), b16),
            pltpu.VMEM((tokens, D), b16),
            pltpu.VMEM((tokens, D), f32),
            pltpu.VMEM((D, 2 * FF + VOCAB), f32),
        ],
        compiler_params=pltpu.CompilerParams(vmem_limit_bytes=VMEM_BYTES),
        cost_estimate=pl.CostEstimate(
            flops=6 * tokens * D * 3 * FF,
            bytes_accessed=tokens * D * 8 + D * 3 * FF * 10,
            transcendentals=tokens * (FF + VOCAB),
        ),
        name="loss_part",
    )(middle, own, other, targets, counted, gains, core)


def backward_kernel(layer, widths, bits, *refs):
    entry_ref, qkv_ref, mix_ref, lse_ref, dmiddle_ref, att_ref = refs[:6]
    gains_ref, valid_ref, core_ref = refs[6:9]
    if layer == 0:
        latent_ref, send_ref, keep_ref, gain_ref, bias_ref = refs[9:14]
        att_kept, before_kept, sum_ref = refs[14:18], refs[18:20], refs[20]
    else:
        before_ref, ffn_ref, out_ref, send_ref, keep_ref, gain_ref, bias_ref = refs[9:16]
        att_kept, before_kept, sum_ref = refs[16:20], refs[20:24], refs[24]
    step = pl.program_id(0)

    def here(start, length, unit=CTX):
        base = step * (GROUP * unit)
        return pl.ds(pl.multiple_of(base + start, 16), length)

    @pl.when(step == 0)
    def _():
        fill_bias(bias_ref)
        gain_ref[...] = jnp.zeros_like(gain_ref)

    dentry, gain_part = attend_back(
        step,
        here,
        (entry_ref[...], qkv_ref, mix_ref, lse_ref),
        dmiddle_ref[...],
        gains_ref[layer : layer + 1, :],
        att_ref,
        valid_ref,
        bias_ref,
        head_masks(),
        att_kept,
    )
    gain_ref[0:1, :] += gain_part
    if layer == 0:
        before_kept[0][here(0, ROWS), :] = dentry.astype(jnp.bfloat16)
        before_kept[1][here(0, ROWS), :] = one_hot_rows(latent_ref[...])
    else:
        dbefore, gain_part = feed_back(
            here,
            dentry,
            before_ref[...],
            gains_ref[LAYERS + layer - 1 : LAYERS + layer, :],
            ffn_ref,
            before_kept,
        )
        out_ref[...] = dbefore
        gain_ref[1:2, :] += gain_part

    @pl.when(step == pl.num_programs(0) - 1)
    def _():
        normed_ref, dattend_ref, dqkv_ref, mixes_ref = att_kept
        att = [(normed_ref, dqkv_ref), (mixes_ref, dattend_ref)]
        if layer == 0:
            pairs = att + [(before_kept[0], before_kept[1])]
        else:
            normed_two_ref, inner_ref, dinner_ref, dout_ref = before_kept
            pairs = [(normed_two_ref, dinner_ref), (dout_ref, inner_ref)] + att
        column = 0
        for left, right in pairs:
            wide = right.shape[1]
            sum_ref[:, column : column + wide] = dot_nn(left[...].T, right[...])
            column += wide
        write_blocks(send_ref, keep_ref, sum_ref, core_ref[0], widths, bits)


def run_backward(layer, widths, bits, blocks_like, saved, dmiddle, gains, valid, core, before):
    entry, _, qkv, mix, lse, weights = saved[:6]
    tokens = entry.shape[0]
    queries = lse.shape[2] // HEADS
    short = tokens // CTX * queries
    f32, b16 = jnp.float32, jnp.bfloat16
    shape = jax.ShapeDtypeStruct
    in_specs = [
        row_spec(D),
        row_spec(3 * D),
        row_spec(D, GROUP * queries),
        lse_spec(queries),
        row_spec(D, GROUP * queries),
        whole_spec(weights.shape),
        whole_spec(gains.shape),
        smem_spec(),
        smem_spec(),
    ]
    operands = [entry, qkv, mix, lse, dmiddle, weights, gains, valid, core]
    blocks = block_outs(blocks_like, widths)
    outs = [(item, whole_spec(item.shape)) for item in blocks]
    outs.append((shape((2, D), f32), whole_spec((2, D))))
    scratch = [
        pltpu.VMEM((2, CTX, HEADS * queries), f32),
        pltpu.VMEM((tokens, D), b16),
        pltpu.VMEM((short, D), b16),
        pltpu.VMEM((tokens, 3 * D), b16),
        pltpu.VMEM((short, D), b16),
    ]
    if layer == 0:
        in_specs.append(row_spec(CATS))
        operands.append(before)
        scratch = scratch + [pltpu.VMEM((tokens, D), b16), pltpu.VMEM((tokens, VOCAB), b16)]
        wide = 4 * D + VOCAB
    else:
        in_specs = in_specs + [row_spec(D), whole_spec(before[1].shape)]
        operands = operands + list(before)
        outs.insert(0, (shape((tokens, D), f32), row_spec(D)))
        scratch = scratch + [
            pltpu.VMEM((tokens, D), b16),
            pltpu.VMEM((tokens, FF), b16),
            pltpu.VMEM((tokens, FF), b16),
            pltpu.VMEM((tokens, D), b16),
        ]
        wide = 4 * D + 2 * FF
    return pl.pallas_call(
        functools.partial(backward_kernel, layer, widths, bits),
        grid=(tokens // ROWS,),
        in_specs=in_specs,
        out_specs=[spec for _, spec in outs],
        out_shape=[item for item, _ in outs],
        scratch_shapes=scratch + [pltpu.VMEM((D, wide), f32)],
        compiler_params=pltpu.CompilerParams(vmem_limit_bytes=VMEM_BYTES),
        cost_estimate=pl.CostEstimate(
            flops=6 * tokens * D * wide,
            bytes_accessed=tokens * D * 24 + D * wide * 6,
            transcendentals=tokens * (FF + HEADS * CTX),
        ),
        name="backward_part",
    )(*operands)


def matrix_plan(widths):
    order = [
        (2, 2), (3, 2), (5, 0), (2, 1), (3, 1), (0, 2), (1, 2),
        (2, 0), (3, 0), (0, 1), (1, 1), (0, 0), (1, 0), (4, 0),
    ]
    plan, column = {}, 0
    for which, layer in order:
        plan[(which, layer)] = (column, widths[which])
        column += widths[which]
    return plan, column


def matrix_list():
    return [(which, layer) for which in range(4) for layer in range(LAYERS)] + [(4, 0), (5, 0)]


MATRICES = 4 * LAYERS + 2
LANES = 128
INNER_ROWS = 16
COMMON_ROWS = 16
ROW_IS_INNER = [True, True, True, False, False, True]


def master_of(masters, which, layer):
    if which == 1:
        return masters[1][layer].T
    return masters[which][layer] if which < 4 else masters[which][...]


def old_row(refs, which, layer):
    return refs[which][layer : layer + 1, :] if which < 4 else refs[which][...]


def stats_kernel(widths, *refs):
    raw_early, raw_late, masters, row_refs = refs[0], refs[1], refs[2:8], refs[8:14]
    gains_at, loss_ref, counted_ref, packet_ref = refs[14:18], refs[18], refs[19], refs[20]
    plan, total = matrix_plan(widths)
    square = jnp.concatenate([raw_early[...] * raw_early[...], raw_late[...] * raw_late[...]], axis=1)
    rows = square.shape[0]
    one = lambda value: jnp.sum(jnp.sum(value, axis=1, keepdims=True), axis=0, keepdims=True)
    inner, weights, entries, row_sums = [], [], [], []
    for which, layer in matrix_list():
        column, width = plan[(which, layer)]
        inner.append(jnp.sum(square[:, column : column + width], axis=1, keepdims=True))
        entries.append(jnp.sum(inner[-1], axis=0, keepdims=True))
        master = master_of(masters, which, layer)
        weights.append(one(master * master))
        row_sums.append(one(old_row(row_refs, which, layer)))
    packet_ref[...] = jnp.zeros_like(packet_ref)
    inner.append(jnp.zeros((rows, LANES - MATRICES), jnp.float32))
    packet_ref[0:INNER_ROWS, 0:rows] = jnp.concatenate(inner, axis=1).T[0:INNER_ROWS, :]
    top, two, one_at, zero = [ref[...] for ref in gains_at]
    gain = jnp.concatenate(
        [zero[0:1], one_at[0:1], two[0:1], one_at[1:2], two[1:2], top[0:1], top[1:2]], axis=0
    )
    scalars = [loss_ref[...], one(counted_ref[...])] + weights + entries + row_sums
    scalars.append(jnp.zeros((1, LANES - len(scalars)), jnp.float32))
    at = INNER_ROWS
    packet_ref[at : at + 7, :] = gain[:, 0:LANES]
    packet_ref[at + 7 : at + 8, :] = jnp.concatenate(scalars, axis=1)
    packet_ref[at + 8 : at + 15, :] = gain[:, LANES:]
    outer = jnp.sum(square, axis=0, keepdims=True)
    at = INNER_ROWS + COMMON_ROWS
    for row, start in enumerate(range(0, total, LANES)):
        stop = min(start + LANES, total)
        packet_ref[at + row : at + row + 1, 0 : stop - start] = outer[:, start:stop]


def outer_rows(widths):
    _, total = matrix_plan(widths)
    return -(-total // (8 * LANES)) * 8


def run_stats(widths, raw_early, raw_late, masters, rows, gain_parts, loss, counted):
    vmem = pl.BlockSpec(memory_space=pltpu.VMEM)
    operands = [raw_early, raw_late] + masters + rows + gain_parts + [loss, counted]
    packet = (INNER_ROWS + COMMON_ROWS + outer_rows(widths), LANES)
    return pl.pallas_call(
        functools.partial(stats_kernel, widths),
        in_specs=[vmem] * len(operands),
        out_specs=vmem,
        out_shape=jax.ShapeDtypeStruct(packet, jnp.float32),
        name="statistics",
    )(*operands)


def update_kernel(widths, sizes, *refs):
    across_ref, along_ref, raw_early, raw_late = refs[:4]
    masters, inner_refs, outer_refs = refs[4:10], refs[10:16], refs[16:22]
    gains_ref, second_ref = refs[22:24]
    outs = refs[24:]
    outer_count, inner_count = sizes
    plan, total = matrix_plan(widths)
    rows = raw_early.shape[0]
    scalars = along_ref[7:8, :]
    pick = lambda at: scalars[:, at : at + 1]
    gain_sum = jnp.concatenate([along_ref[0:7, :], along_ref[8:15, :]], axis=1)
    gain_square = jnp.sum(jnp.sum(gain_sum * gain_sum, axis=1, keepdims=True), axis=0, keepdims=True)
    square_total = gain_square
    for at in range(MATRICES):
        square_total = square_total + pick(2 + MATRICES + at)
    count_total = pick(1)
    norm_value = jnp.sqrt(square_total) / count_total
    scaling = jnp.minimum(1.0, clip_limit / norm_value) / count_total
    square_scale = scaling * scaling
    outer_total = jnp.concatenate(
        [
            along_ref[COMMON_ROWS + row : COMMON_ROWS + row + 1, 0 : min(LANES, total - row * LANES)]
            for row in range(-(-total // LANES))
        ],
        axis=1,
    )
    inner_new = []
    for at, (which, layer) in enumerate(matrix_list()):
        outer_length = widths[which] * outer_count
        inner_new.append(
            decay_two * old_row(inner_refs, which, layer)
            + (1 - decay_two)
            * (square_scale * across_ref[at : at + 1, 0:rows] / outer_length + tiny_term)
        )
    stacked = jnp.concatenate(inner_new, axis=0)
    stacked = jnp.concatenate([stacked, jnp.ones((LANES - MATRICES, rows), jnp.float32)], axis=0)
    if rows < LANES:
        stacked = jnp.concatenate([stacked, jnp.ones((LANES, LANES - rows), jnp.float32)], axis=1)
    turned = lax.rsqrt(stacked).T
    outs[0][...] = pick(0)
    outs[1][...] = count_total
    outs[2][...] = norm_value
    first_out = {4: 3, 0: 7, 1: 11, 2: 15, 3: 19, 5: 23}
    for at, (which, layer) in enumerate(matrix_list()):
        column, width = plan[(which, layer)]
        outer_length, inner_length = width * outer_count, rows * inner_count
        row_length = inner_length if ROW_IS_INNER[which] else outer_length
        copies = outer_count if ROW_IS_INNER[which] else inner_count
        entries = outer_length * inner_length
        early = raw_early.shape[1]
        if column < early:
            raw = raw_early[:, column : column + width]
        else:
            raw = raw_late[:, column - early : column - early + width]
        outer_new = decay_two * old_row(outer_refs, which, layer) + (1 - decay_two) * (
            square_scale * outer_total[:, column : column + width] / inner_length + tiny_term
        )
        mean_rows = decay_two * (pick(2 + 2 * MATRICES + at) / (copies * row_length)) + (
            1 - decay_two
        ) * (square_scale * pick(2 + MATRICES + at) / entries + tiny_term)
        factor = step_rate * jnp.sqrt(pick(2 + at) / entries) * jnp.sqrt(mean_rows)
        grad = raw * scaling
        updated = master_of(masters, which, layer) - grad * (
            turned[0:rows, at : at + 1] * (factor * lax.rsqrt(outer_new))
        )
        first = first_out[which]
        row_new, column_new = (
            (inner_new[at], outer_new) if ROW_IS_INNER[which] else (outer_new, inner_new[at])
        )
        if which < 4:
            if which == 1:
                updated, grad = updated.T, grad.T
            outs[first][layer] = updated
            outs[first + 1][layer] = grad
            outs[first + 2][layer : layer + 1, :] = row_new
            outs[first + 3][layer : layer + 1, :] = column_new
        else:
            outs[first][...] = updated
            outs[first + 1][...] = grad
            outs[first + 2][...] = row_new
            outs[first + 3][...] = column_new
    gain_grad = gain_sum * scaling
    second_new = decay_two * second_ref[...] + (1 - decay_two) * (gain_grad * gain_grad + tiny_term)
    gains = gains_ref[...]
    spread = jnp.sqrt(jnp.mean(gains * gains, axis=-1, keepdims=True))
    outs[27][...] = gains - step_rate * spread * gain_grad * lax.rsqrt(second_new)
    outs[28][...] = gain_grad
    outs[29][...] = second_new


def run_update(widths, sizes, across, along, raw_early, raw_late, masters, inner, outer, gains, second):
    vmem = pl.BlockSpec(memory_space=pltpu.VMEM)
    operands = [across, along, raw_early, raw_late] + masters + inner + outer + [gains, second]
    shapes = [(1, 1)] * 3
    for which in [4, 0, 1, 2, 3, 5]:
        shapes = shapes + [masters[which].shape] * 2
        pair = [inner[which].shape, outer[which].shape]
        shapes = shapes + (pair if ROW_IS_INNER[which] else pair[::-1])
    shapes = shapes + [gains.shape] * 3
    return pl.pallas_call(
        functools.partial(update_kernel, widths, sizes),
        in_specs=[vmem] * len(operands),
        out_specs=[vmem] * len(shapes),
        out_shape=[jax.ShapeDtypeStruct(item, jnp.float32) for item in shapes],
        name="update",
    )(*operands)


def swap(value, axis, bit):
    pairs = [(place, place ^ bit) for place in range(lax.axis_size(axis))]
    return lax.ppermute(value, axis, pairs)


def tie(*values):
    return lax.optimization_barrier(values)


def exchange(blocks, axis):
    return lax.all_to_all(blocks, axis, split_axis=0, concat_axis=0, tiled=True)


def sum_over(value, axis):
    size = lax.axis_size(axis)
    return jnp.sum(exchange(jnp.broadcast_to(value, (size,) + value.shape), axis), axis=0)


class Gather:
    def __init__(self, piece, steps):
        self.held, self.steps, self.at = piece[None], steps, 0

    def send(self):
        if self.at == 0:
            size = lax.axis_size("dp")
            self.other = exchange(jnp.broadcast_to(self.held, (size,) + self.held.shape[1:]), "dp")
        else:
            self.other = swap(self.held, "fsdp", 1 << self.steps[self.at - 1])

    def join(self):
        if self.at == 0:
            self.held = self.other
        else:
            upper = (lax.axis_index("fsdp") >> self.steps[self.at - 1]) & 1 == 1
            self.held = jnp.where(
                upper,
                jnp.concatenate([self.other, self.held]),
                jnp.concatenate([self.held, self.other]),
            )
        self.at += 1

    def step(self, after=None):
        if after is not None:
            self.held, _ = tie(self.held, after.other)
        self.send()
        self.join()


class Scatter:
    def __init__(self, sent, kept, steps):
        self.sent, self.kept, self.steps, self.at = sent, kept, steps, 0

    def send(self):
        if self.at == len(self.steps):
            self.other = exchange(self.sent, "dp")
        else:
            self.other = swap(self.sent, "fsdp", 1 << self.steps[self.at])

    def join(self):
        self.at += 1
        if self.at > len(self.steps):
            self.kept = jnp.sum(self.other.astype(jnp.float32), axis=0)
            return
        summed = self.kept + self.other.astype(jnp.float32)
        if self.at == len(self.steps):
            self.sent = summed.astype(jnp.bfloat16)
            return
        side = (lax.axis_index("fsdp") >> self.steps[self.at]) & 1
        half = summed.shape[0] // 2
        parts = summed.reshape((2, half) + summed.shape[1:])
        self.sent = jnp.where(side == 1, parts[0], parts[1]).astype(jnp.bfloat16)
        self.kept = jnp.where(side == 1, parts[1], parts[0])


def shards(
    latents,
    targets,
    horizon,
    memory_valid,
    embed,
    qkv_weight,
    out_weight,
    up_weight,
    down_weight,
    head_weight,
    gains,
    embed_rows,
    embed_cols,
    qkv_rows,
    qkv_cols,
    out_rows,
    out_cols,
    up_rows,
    up_cols,
    down_rows,
    down_cols,
    head_rows,
    head_cols,
    gain_second,
):
    samples = latents.shape[0]
    sizes = (lax.axis_size("dp"), lax.axis_size("fsdp"))
    bits = (sizes[0].bit_length() - 1, sizes[1].bit_length() - 1)
    scatter_steps = list(range(bits[1]))
    gather_steps = scatter_steps[::-1]
    core = (lax.axis_index("fsdp") & 1).astype(jnp.int32).reshape(1)

    low = lambda item: item.astype(jnp.bfloat16)
    out_turned = jnp.swapaxes(out_weight, 1, 2)
    down_turned = jnp.swapaxes(down_weight, 1, 2)
    masters = [qkv_weight, out_turned, up_weight, down_turned, embed.T, head_weight]
    widths = [qkv_weight.shape[2], out_weight.shape[2], up_weight.shape[2], down_weight.shape[1]]
    widths = widths + [embed.shape[0], head_weight.shape[1]]
    att_parts = [[qkv_weight[at], out_weight[at]] for at in range(LAYERS)]
    ffn_parts = [[up_weight[at], down_turned[at]] for at in range(LAYERS)]
    pieces = [
        att_parts[0] + [embed.T],
        ffn_parts[0] + att_parts[1],
        ffn_parts[1] + att_parts[2] + ffn_parts[2] + [head_weight],
    ]
    att_widths, ffn_widths = widths[0:2], widths[2:4]
    first, second, third = [
        Gather(low(jnp.concatenate(piece, axis=1)), gather_steps) for piece in pieces
    ]
    chunk_widths = [
        att_widths + widths[4:5],
        ffn_widths + att_widths,
        ffn_widths + att_widths + ffn_widths + widths[5:6],
    ]

    latent_rows = low(latents).reshape(samples * CTX, CATS)
    target_rows = targets.transpose(2, 0, 1).reshape(CATS, samples * SEG)
    counted = jnp.arange(SEG, dtype=jnp.int32)[None, :] < horizon[:, None]
    counted = counted.astype(jnp.float32).reshape(1, samples * SEG)
    shared = (gains, memory_valid, core)

    count = len(gather_steps) + 1
    for at in range(count - 1):
        first.step()
        if at < count - 2:
            second.step(first)
        if at < count - 3:
            third.step(second)
    first.send()
    second.step(first)
    third.step(second)
    first.held, first.other, second.held, third.held = tie(
        first.held, first.other, second.held, third.held
    )
    second.send()
    third.send()
    kept = [run_forward(0, chunk_widths[0], bits, latent_rows, first.held, first.other, *shared)]
    middle, second.other, third.other = tie(kept[0][1], second.other, third.other)
    third.join()
    second.held, third.held = tie(second.held, third.held)
    third.send()
    kept.append(run_forward(1, chunk_widths[1], bits, middle, second.held, second.other, *shared))
    middle, third.other = tie(kept[1][1], third.other)
    kept.append(run_forward(2, chunk_widths[2], bits, middle, third.held, third.other, *shared))

    dmiddle, sent, held, gain_top, loss = run_top(
        ffn_widths + widths[5:6],
        bits,
        sum(ffn_widths + att_widths),
        kept[2][1],
        third.held,
        third.other,
        target_rows,
        counted,
        gains,
        core,
    )
    top = Scatter(sent, held, scatter_steps)
    top.send()
    like = first.held
    dmiddle, sent, held, gain_two = run_backward(
        2, chunk_widths[1], bits, like, kept[2], dmiddle, *shared, (kept[1][1], kept[2][6])
    )
    dmiddle, top.other = tie(dmiddle, top.other)
    top.join()
    two = Scatter(sent, held, scatter_steps)
    dmiddle, top.sent = tie(dmiddle, top.sent)
    top.send()
    two.send()
    dmiddle, sent, held, gain_one = run_backward(
        1, chunk_widths[1], bits, like, kept[1], dmiddle, *shared, (kept[0][1], kept[1][6])
    )
    dmiddle, top.other, two.other = tie(dmiddle, top.other, two.other)
    top.join()
    two.join()
    one = Scatter(sent, held, scatter_steps)
    dmiddle, top.sent, two.sent = tie(dmiddle, top.sent, two.sent)
    top.send()
    two.send()
    one.send()
    sent, held, gain_zero = run_backward(
        0, chunk_widths[0], bits, like, kept[0], dmiddle, *shared, latent_rows
    )
    sent, top.other, two.other, one.other = tie(sent, top.other, two.other, one.other)
    zero = Scatter(sent, held, scatter_steps)
    zero.send()
    chunks = [top, two, one, zero]
    top.join()
    two.join()
    two.send()
    one.join()
    one.send()
    while zero.at < count:
        for chunk in chunks[1:]:
            if chunk.at < count:
                chunk.join()
                if chunk.at < count:
                    chunk.send()
    while top.at < count:
        top.send()
        top.join()
    raw_early = jnp.concatenate([top.kept, two.kept, one.kept], axis=1)
    raw_late = zero.kept

    flat = lambda item: item if item.ndim == 2 else item.reshape(1, -1)
    inner = [flat(item) for item in (qkv_rows, out_rows, up_rows, down_cols, embed_cols, head_rows)]
    outer = [flat(item) for item in (qkv_cols, out_cols, up_cols, down_rows, embed_rows, head_cols)]
    row_stats = [inner[at] if ROW_IS_INNER[at] else outer[at] for at in range(6)]
    gain_parts = [gain_top, gain_two, gain_one, gain_zero]
    packet = run_stats(widths, raw_early, raw_late, masters, row_stats, gain_parts, loss, counted)
    edge = INNER_ROWS + COMMON_ROWS
    across = sum_over(packet[:edge], "dp")
    along = sum_over(jnp.concatenate([across[INNER_ROWS:], packet[edge:]]), "fsdp")
    results = run_update(
        widths, sizes, across, along, raw_early, raw_late, masters, inner, outer, gains, gain_second
    )
    results = list(results)
    for at in range(3):
        results[at] = results[at].reshape(())
    for at in (3, 4, 11, 12, 19, 20):
        results[at] = jnp.swapaxes(results[at], -1, -2)
    for at in (5, 6, 25, 26):
        results[at] = results[at].reshape(-1)
    return tuple(results)


def solution(mesh):
    return jax.shard_map(
        shards,
        mesh=mesh,
        in_specs=(
            P(("dp", "fsdp"), None, None),
            P(("dp", "fsdp"), None, None),
            P(("dp", "fsdp")),
            P(("dp", "fsdp")),
            P("dp", "fsdp"),
            P(None, "fsdp", "dp"),
            P(None, "fsdp", "dp"),
            P(None, "fsdp", "dp"),
            P(None, "dp", "fsdp"),
            P("fsdp", "dp"),
            P(),
            P("dp"),
            P("fsdp"),
            P(None, "fsdp"),
            P(None, "dp"),
            P(None, "fsdp"),
            P(None, "dp"),
            P(None, "fsdp"),
            P(None, "dp"),
            P(None, "dp"),
            P(None, "fsdp"),
            P("fsdp"),
            P("dp"),
            P(),
        ),
        out_specs=(
            P(),
            P(),
            P(),
            P("dp", "fsdp"),
            P("dp", "fsdp"),
            P("dp"),
            P("fsdp"),
            P(None, "fsdp", "dp"),
            P(None, "fsdp", "dp"),
            P(None, "fsdp"),
            P(None, "dp"),
            P(None, "fsdp", "dp"),
            P(None, "fsdp", "dp"),
            P(None, "fsdp"),
            P(None, "dp"),
            P(None, "fsdp", "dp"),
            P(None, "fsdp", "dp"),
            P(None, "fsdp"),
            P(None, "dp"),
            P(None, "dp", "fsdp"),
            P(None, "dp", "fsdp"),
            P(None, "dp"),
            P(None, "fsdp"),
            P("fsdp", "dp"),
            P("fsdp", "dp"),
            P("fsdp"),
            P("dp"),
            P(),
            P(),
            P(),
        ),
        check_vma=False,
    )
```

```python
import functools

import jax
import jax.numpy as jnp
from jax import lax
from jax.experimental import pallas as pl
from jax.experimental.pallas import tpu as pltpu
from jax.sharding import PartitionSpec as P

D = 256
HEADS = 8
HEAD = D // HEADS
FF = 1024
CATS = 32
CLASSES = 32
LAYERS = 3
SEG = 48
MEM = 48
CTX = 96
VOCAB = 1024
GROUP = 4
ROWS = GROUP * CTX
SPREAD = HEADS * CTX
LANES = 128
STRIP = 64
VMEM_BYTES = 56 * 1024 * 1024

decay_two = 0.9
step_rate = 0.3
clip_limit = 0.05
tiny_term = 1e-30
norm_eps = 1e-06
masked_score = -1e30
log2_e = 1.4426950408889634
score_scale = HEAD ** (-0.5)
gelu_one = 0.7978845608028654
gelu_two = 0.044715


def dot_nn(left, right):
    return lax.dot_general(
        left, right, (((1,), (0,)), ((), ())), preferred_element_type=jnp.float32
    )


def dot_nt(left, right):
    return lax.dot_general(
        left, right, (((1,), (1,)), ((), ())), preferred_element_type=jnp.float32
    )


def dot_tn(left, right):
    return lax.dot_general(
        left, right, (((0,), (0,)), ((), ())), preferred_element_type=jnp.float32
    )


def inverse_rms(values):
    return lax.rsqrt(jnp.mean(values * values, axis=-1, keepdims=True) + norm_eps)


def rms_back(values, inverse, gain_row, upstream):
    normed = values * inverse
    scaled = upstream * gain_row
    inner = jnp.mean(scaled * normed, axis=-1, keepdims=True)
    return (
        inverse * (scaled - normed * inner),
        jnp.sum(upstream * normed, axis=0, keepdims=True),
    )


def head_masks():
    lane = lax.broadcasted_iota(jnp.int32, (1, D // 2), 1) // HEAD
    return [lane == head for head in range(HEADS // 2)]


def expand_heads(rows, masks):
    half = D // 2
    nothing = jnp.zeros((rows.shape[0], half), rows.dtype)
    pieces = []
    for head in range(HEADS):
        side, at = divmod(head, HEADS // 2)
        kept = rows[:, side * half : (side + 1) * half] * masks[at].astype(rows.dtype)
        pair = [kept, nothing] if side == 0 else [nothing, kept]
        pieces.append(jnp.concatenate(pair, axis=1))
    return jnp.concatenate(pieces, axis=0)


def collapse_heads(spread, rows, masks):
    half, span = D // 2, spread.shape[1] // 2
    queries = span // (HEADS // 2)
    sides = []
    for side in range(2):
        product = dot_tn(
            spread[:, side * span : (side + 1) * span], rows[:, side * half : (side + 1) * half]
        )
        taken = product[(HEADS // 2 - 1) * queries :]
        for at in range(HEADS // 2 - 1):
            taken = jnp.where(masks[at], product[at * queries : (at + 1) * queries], taken)
        sides.append(taken)
    return jnp.concatenate(sides, axis=1)


def fill_bias(bias_ref):
    spread = bias_ref.shape[2]
    queries = spread // HEADS
    for start in range(0, spread, LANES):
        columns = slice(start, start + LANES)
        key_at = lax.broadcasted_iota(jnp.int32, (CTX, LANES), 0)
        query_at = (lax.broadcasted_iota(jnp.int32, (1, LANES), 1) + start) % queries
        query_at = query_at + (CTX - queries)
        later = key_at > query_at
        limit = jnp.where(query_at >= MEM, MEM, 0)
        bias_ref[0, :, columns] = jnp.where(later | (key_at < limit), masked_score, 0.0)
        bias_ref[1, :, columns] = jnp.where(later, masked_score, 0.0)


def block_place(outer_at, inner_high, steps):
    place = 0
    for at, (axis, bit) in enumerate(steps[:-1]):
        index = outer_at if axis == "dp" else 2 * inner_high
        place |= ((index >> bit) & 1) << at
    return place


def axis_bits(steps, axis):
    return sum(1 for name, _ in steps if name == axis)


def place_weights(targets, own_ref, other_ref, core, widths, steps, start=0):
    outer_bits, inner_bits = axis_bits(steps, "dp"), axis_bits(steps, "fsdp")
    rows = own_ref.shape[1]
    for high in range(1 << (inner_bits - 1)):
        for source, side in ((own_ref, core), (other_ref, 1 - core)):
            here = pl.ds(pl.multiple_of((2 * high + side) * rows, rows), rows)
            at = start
            for (target, column), width in zip(targets, widths):
                block = [
                    source[block_place(outer, high, steps), :, at : at + width]
                    for outer in range(1 << outer_bits)
                ]
                target[here, column : column + (width << outer_bits)] = jnp.concatenate(
                    block, axis=1
                )
                at += width


def write_blocks(send_ref, keep_ref, sum_ref, core, widths, steps):
    outer_bits, inner_bits = axis_bits(steps, "dp"), axis_bits(steps, "fsdp")
    rows = keep_ref.shape[1]
    for high in range(1 << (inner_bits - 1)):
        for target, side in ((keep_ref, core), (send_ref, 1 - core)):
            here = pl.ds(pl.multiple_of((2 * high + side) * rows, rows), rows)
            taken = sum_ref[here, :]
            for outer in range(1 << outer_bits):
                block, column = [], 0
                for width in widths:
                    block.append(taken[:, column + outer * width : column + (outer + 1) * width])
                    column += width << outer_bits
                target[block_place(outer, high, steps)] = jnp.concatenate(
                    block, axis=1
                ).astype(target.dtype)


def one_hot_rows(latent_rows, hot_ref, first):
    spot = lax.broadcasted_iota(jnp.int32, (CATS, VOCAB), 1) // CLASSES
    group = lax.broadcasted_iota(jnp.int32, (CATS, VOCAB), 0)
    spreader = jnp.where(spot == group, 1.0, 0.0).astype(jnp.bfloat16)
    classes = (lax.broadcasted_iota(jnp.int32, (1, LANES), 1) % CLASSES).astype(jnp.float32)
    rows = latent_rows.shape[0]
    for part in range(VOCAB // D):
        drawn = dot_nn(latent_rows, spreader[:, part * D : (part + 1) * D])
        for start in range(0, rows, STRIP):
            for side in range(D // LANES):
                piece = drawn[start : start + STRIP, side * LANES : (side + 1) * LANES]
                column = part * D + side * LANES
                hot_ref[pl.ds(first + start, STRIP), column : column + LANES] = jnp.where(
                    piece == classes, 1.0, 0.0
                ).astype(jnp.bfloat16)


def strips(count):
    return [slice(start, start + STRIP) for start in range(0, count, STRIP)]


def norm_rows(values, gain_row, target_ref, first=0):
    for strip in strips(values.shape[0]):
        piece = values[strip]
        target_ref[pl.ds(first + strip.start, STRIP), :] = (
            piece * inverse_rms(piece) * gain_row
        ).astype(jnp.bfloat16)


def norm_back(values, gain_row, upstream, carried, target_ref, first=0):
    total = jnp.zeros((1, D), jnp.float32)
    for strip in strips(values.shape[0]):
        piece = values[strip]
        through, gain_part = rms_back(piece, inverse_rms(piece), gain_row, upstream[strip])
        target_ref[pl.ds(first + strip.start, STRIP), :] = carried[strip] + through
        total = total + gain_part
    return total


def score_tiles(spread):
    return [(start, min(D, spread - start)) for start in range(0, spread, D)]


def softmax_columns(keys, spread, bias, lse_ref, sample):
    pieces = []
    for start, width in score_tiles(spread.shape[0]):
        scores = dot_nt(keys, spread[start : start + width])
        for side in range(0, width, LANES):
            columns = slice(start + side, start + side + LANES)
            piece = scores[:, side : side + LANES] + bias[:, columns]
            peak = jnp.max(piece, axis=0, keepdims=True)
            exponent = jnp.exp2((piece - peak) * (score_scale * log2_e))
            total = jnp.sum(exponent, axis=0, keepdims=True)
            pieces.append((exponent * (1.0 / total)).astype(jnp.bfloat16))
            lse_ref[sample, :, columns] = peak * (score_scale * log2_e) + jnp.log2(total)
    return jnp.concatenate(pieces, axis=1)


def softmax_back(keys, values, spread, slopes, bias, lse_ref, sample):
    chances, dscores = [], []
    for start, width in score_tiles(spread.shape[0]):
        scores = dot_nt(keys, spread[start : start + width])
        dchances = dot_nt(values, slopes[start : start + width])
        for side in range(0, width, LANES):
            columns = slice(start + side, start + side + LANES)
            piece = scores[:, side : side + LANES] + bias[:, columns]
            chance = jnp.exp2(piece * (score_scale * log2_e) - lse_ref[sample, :, columns])
            chances.append(chance.astype(jnp.bfloat16))
            dchance = dchances[:, side : side + LANES]
            inner = jnp.sum(chance * dchance, axis=0, keepdims=True)
            dscores.append((chance * (dchance - inner)).astype(jnp.bfloat16))
    return jnp.concatenate(chances, axis=1), jnp.concatenate(dscores, axis=1)


def tail_rows(values, queries):
    if queries == CTX:
        return values
    return jnp.concatenate(
        [
            values[(sample + 1) * CTX - queries : (sample + 1) * CTX]
            for sample in range(values.shape[0] // CTX)
        ],
        axis=0,
    )


def attend_forward(step, hidden_ref, gain_row, weight_ref, valid_ref, bias_ref, normed_ref, refs):
    middle_ref, qkv_ref, mix_ref, lse_ref = refs
    masks = head_masks()
    queries = lse_ref.shape[2] // HEADS
    norm_rows(hidden_ref[...], gain_row, normed_ref)
    qkv_ref[...] = dot_nn(normed_ref[...], weight_ref[:, 0 : 3 * D]).astype(jnp.bfloat16)
    for sample in range(GROUP):
        rows = slice(sample * CTX, (sample + 1) * CTX)
        spread = expand_heads(qkv_ref[(sample + 1) * CTX - queries : (sample + 1) * CTX, 0:D], masks)
        bias = bias_ref.at[valid_ref[step * GROUP + sample]]
        chance = softmax_columns(qkv_ref[rows, D : 2 * D], spread, bias, lse_ref, sample)
        mix_ref[sample * queries : (sample + 1) * queries, :] = collapse_heads(
            chance, qkv_ref[rows, 2 * D : 3 * D], masks
        ).astype(jnp.bfloat16)
    added = dot_nn(mix_ref[...], weight_ref[:, 3 * D : 4 * D])
    for sample in range(GROUP):
        rows = slice(sample * queries, (sample + 1) * queries)
        middle_ref[rows, :] = (
            hidden_ref[(sample + 1) * CTX - queries : (sample + 1) * CTX, :] + added[rows]
        )


def gelu_bend(value, square):
    return jnp.tanh(value * (gelu_one + (gelu_one * gelu_two) * square))


def gelu_slope(half_value, bend, square):
    return (0.5 + 0.5 * bend) + (half_value * (1.0 - bend * bend)) * (
        gelu_one + (3.0 * gelu_one * gelu_two) * square
    )


def feed_forward(middle_ref, gain_row, weight_ref, normed_ref, inner_ref, target_ref):
    norm_rows(middle_ref[...], gain_row, normed_ref)
    for part in range(FF // D):
        inner = dot_nn(normed_ref[...], weight_ref[:, part * D : (part + 1) * D])
        for strip in strips(ROWS):
            for side in range(0, D, LANES):
                value = inner[strip, side : side + LANES]
                bend = gelu_bend(value, value * value)
                column = part * D + side
                inner_ref[strip, column : column + LANES] = (
                    (0.5 * value) * (1.0 + bend)
                ).astype(jnp.bfloat16)
    added = dot_nt(inner_ref[...], weight_ref[:, FF : 2 * FF])
    for strip in strips(ROWS):
        target_ref[strip, :] = middle_ref[strip, :] + added[strip]


def feed_back(here, upstream_ref, middle_ref, gain_row, weight_ref, refs, target_ref):
    normed_ref, inner_ref, dinner_ref, dout_ref = refs
    dout_ref[here(0, ROWS), :] = upstream_ref[...].astype(jnp.bfloat16)
    norm_rows(middle_ref[...], gain_row, normed_ref, here.base(CTX))
    for part in range(FF // D):
        inner = dot_nn(normed_ref[here(0, ROWS), :], weight_ref[:, part * D : (part + 1) * D])
        dact = dot_nn(dout_ref[here(0, ROWS), :], weight_ref[:, FF + part * D : FF + (part + 1) * D])
        for strip in strips(ROWS):
            there = here(strip.start, STRIP)
            for side in range(0, D, LANES):
                columns = slice(part * D + side, part * D + side + LANES)
                value = inner[strip, side : side + LANES]
                square = value * value
                bend = gelu_bend(value, square)
                half_value = 0.5 * value
                inner_ref[there, columns] = (half_value * (1.0 + bend)).astype(jnp.bfloat16)
                dinner_ref[there, columns] = (
                    dact[strip, side : side + LANES] * gelu_slope(half_value, bend, square)
                ).astype(jnp.bfloat16)
    dnormed = dot_nt(dinner_ref[here(0, ROWS), :], weight_ref[:, 0:FF])
    return norm_back(middle_ref[...], gain_row, dnormed, upstream_ref[...], target_ref)


class Here:
    def __init__(self, step):
        self.step = step

    def base(self, unit):
        return pl.multiple_of(self.step * (GROUP * unit), 16)

    def __call__(self, start, length, unit=CTX):
        return pl.ds(pl.multiple_of(self.step * (GROUP * unit) + start, 16), length)


def attend_back(step, here, saved, dmiddle_in, gain_row, weight_ref, valid_ref, bias_ref, refs, target_ref):
    hidden_ref, qkv_ref, mix_ref, lse_ref = saved
    normed_ref, dmiddle_ref, dqkv_ref, mixes_ref = refs
    masks = head_masks()
    queries = lse_ref.shape[2] // HEADS
    short = here(0, GROUP * queries, queries)
    dmiddle_ref[short, :] = dmiddle_in[...].astype(jnp.bfloat16)
    mixes_ref[short, :] = mix_ref[...]
    dmix = dot_nt(dmiddle_ref[short, :], weight_ref[:, 3 * D : 4 * D]).astype(jnp.bfloat16)
    for sample in range(GROUP):
        rows = slice(sample * CTX, (sample + 1) * CTX)
        there = here(sample * CTX, CTX)
        spread = expand_heads(qkv_ref[(sample + 1) * CTX - queries : (sample + 1) * CTX, 0:D], masks)
        keys = qkv_ref[rows, D : 2 * D]
        slopes = expand_heads(dmix[sample * queries : (sample + 1) * queries], masks)
        bias = bias_ref.at[valid_ref[step * GROUP + sample]]
        chance, dscore = softmax_back(
            keys, qkv_ref[rows, 2 * D : 3 * D], spread, slopes, bias, lse_ref, sample
        )
        dqueries = (collapse_heads(dscore, keys, masks) * score_scale).astype(jnp.bfloat16)
        if queries < CTX:
            nothing = jnp.zeros((CTX - queries, D), jnp.bfloat16)
            dqueries = jnp.concatenate([nothing, dqueries], axis=0)
        dqkv_ref[there, 0:D] = dqueries
        dqkv_ref[there, D : 2 * D] = (dot_nn(dscore, spread) * score_scale).astype(jnp.bfloat16)
        dqkv_ref[there, 2 * D : 3 * D] = dot_nn(chance, slopes).astype(jnp.bfloat16)
    norm_rows(hidden_ref[...], gain_row, normed_ref, here.base(CTX))
    dnormed = dot_nt(dqkv_ref[here(0, ROWS), :], weight_ref[:, 0 : 3 * D])
    carried = dmiddle_in[...]
    if queries < CTX:
        nothing = jnp.zeros((CTX - queries, D), jnp.float32)
        pieces = []
        for sample in range(GROUP):
            pieces = pieces + [nothing, carried[sample * queries : (sample + 1) * queries]]
        carried = jnp.concatenate(pieces, axis=0)
    return norm_back(hidden_ref[...], gain_row, dnormed, carried, target_ref)


def row_spec(width, rows=ROWS):
    return pl.BlockSpec((rows, width), lambda step: (step, 0))


def lse_spec(queries):
    return pl.BlockSpec((GROUP, 1, HEADS * queries), lambda step: (step, 0, 0))


def whole_spec(shape):
    return pl.BlockSpec(shape, lambda step: (0,) * len(shape))


def smem_spec():
    return pl.BlockSpec(memory_space=pltpu.SMEM)


def forward_kernel(layer, widths, steps, source_ref, own_ref, other_ref, gains_ref, valid_ref, core_ref, *refs):
    entry_ref, att_ref, before_ref, bias_ref = refs[0], refs[5], refs[6], refs[7]
    normed_ref, inner_ref = refs[8:10]
    step = pl.program_id(0)

    @pl.when(step == 0)
    def _():
        fill_bias(bias_ref)
        att = [(att_ref, 0), (att_ref, 3 * D)]
        before = [(before_ref, 0)] if layer == 0 else [(before_ref, 0), (before_ref, FF)]
        targets = att + before if layer == 0 else before + att
        place_weights(targets, own_ref, other_ref, core_ref[0], widths[: len(targets)], steps)

    if layer == 0:
        one_hot_rows(source_ref[...], inner_ref, 0)
        entry_ref[...] = dot_nt(inner_ref[...], before_ref[...])
    else:
        gain_ffn = gains_ref[LAYERS + layer - 1 : LAYERS + layer, :]
        feed_forward(source_ref, gain_ffn, before_ref, normed_ref, inner_ref, entry_ref)
    attend_forward(
        step,
        entry_ref,
        gains_ref[layer : layer + 1, :],
        att_ref,
        valid_ref,
        bias_ref,
        normed_ref,
        refs[1:5],
    )


def run_forward(layer, widths, steps, source, own, other, gains, valid, core):
    tokens = source.shape[0]
    queries = SEG if layer == LAYERS - 1 else CTX
    f32, b16 = jnp.float32, jnp.bfloat16
    shape = jax.ShapeDtypeStruct
    short = tokens // CTX * queries
    outs = [
        (shape((tokens, D), f32), row_spec(D)),
        (shape((short, D), f32), row_spec(D, GROUP * queries)),
        (shape((tokens, 3 * D), b16), row_spec(3 * D)),
        (shape((short, D), b16), row_spec(D, GROUP * queries)),
        (shape((tokens // CTX, 1, HEADS * queries), f32), lse_spec(queries)),
        (shape((D, 4 * D), b16), whole_spec((D, 4 * D))),
    ]
    scratch = [
        pltpu.VMEM((2, CTX, HEADS * queries), f32),
        pltpu.VMEM((ROWS, D), b16),
        pltpu.VMEM((ROWS, FF), b16),
    ]
    if layer == 0:
        scratch = [pltpu.VMEM((D, VOCAB), b16)] + scratch
    else:
        outs.append((shape((D, 2 * FF), b16), whole_spec((D, 2 * FF))))
    return pl.pallas_call(
        functools.partial(forward_kernel, layer, widths, steps),
        grid=(tokens // ROWS,),
        in_specs=[
            row_spec(source.shape[1]),
            whole_spec(own.shape),
            whole_spec(other.shape),
            whole_spec(gains.shape),
            smem_spec(),
            smem_spec(),
        ],
        out_specs=[spec for _, spec in outs],
        out_shape=[item for item, _ in outs],
        scratch_shapes=scratch,
        compiler_params=pltpu.CompilerParams(vmem_limit_bytes=VMEM_BYTES),
        cost_estimate=pl.CostEstimate(
            flops=2 * tokens * D * 12 * D,
            bytes_accessed=tokens * D * 16 + D * 12 * D * 4,
            transcendentals=tokens * (FF + HEADS * CTX),
        ),
        name="forward_part",
    )(source, own, other, gains, valid, core)


def top_kernel(widths, gather_steps, scatter_steps, start, middle_ref, own_ref, other_ref, targets_ref, counted_ref, gains_ref, core_ref, *refs):
    dmiddle_ref, send_ref, keep_ref, gain_ref, loss_ref = refs[:5]
    weight_ref, head_ref, turned_ref, final_ref, dlogits_ref = refs[5:10]
    normed_ref, inner_ref, slope_ref, dinner_ref, dout_ref, last_ref, sum_ref = refs[10:]
    tokens = middle_ref.shape[0]
    gain_final = gains_ref[2 * LAYERS : 2 * LAYERS + 1, :]
    gain_ffn = gains_ref[2 * LAYERS - 1 : 2 * LAYERS, :]
    place_weights(
        [(weight_ref, 0), (weight_ref, FF), (head_ref, 0)],
        own_ref,
        other_ref,
        core_ref[0],
        widths,
        gather_steps,
        start,
    )
    turned_ref[...] = head_ref[...].T
    for block in range(tokens // ROWS):
        rows = slice(block * ROWS, (block + 1) * ROWS)
        norm_rows(middle_ref[rows, :], gain_ffn, normed_ref, block * ROWS)
        for part in range(FF // D):
            inner = dot_nn(normed_ref[rows, :], weight_ref[:, part * D : (part + 1) * D])
            for strip in strips(ROWS):
                there = slice(block * ROWS + strip.start, block * ROWS + strip.stop)
                for side in range(0, D, LANES):
                    columns = slice(part * D + side, part * D + side + LANES)
                    value = inner[strip, side : side + LANES]
                    square = value * value
                    bend = gelu_bend(value, square)
                    half_value = 0.5 * value
                    inner_ref[there, columns] = (half_value * (1.0 + bend)).astype(jnp.bfloat16)
                    slope_ref[there, columns] = gelu_slope(half_value, bend, square)
        added = dot_nt(inner_ref[rows, :], weight_ref[:, FF : 2 * FF])
        for strip in strips(ROWS):
            there = slice(block * ROWS + strip.start, block * ROWS + strip.stop)
            last = middle_ref[there, :] + added[strip]
            last_ref[there, :] = last
            final_ref[there, :] = (last * inverse_rms(last) * gain_final).astype(jnp.bfloat16)
    span = D
    loss = jnp.zeros((1, span), jnp.float32)
    spots = lax.broadcasted_iota(jnp.int32, (CLASSES, span), 0)
    for part in range(tokens // span):
        columns = slice(part * span, (part + 1) * span)
        counted = counted_ref[0:1, columns]
        final = final_ref[columns, :]
        for quarter in range(VOCAB // D):
            logits = dot_nt(turned_ref[quarter * D : (quarter + 1) * D, :], final)
            for inside in range(D // CLASSES):
                group = quarter * (D // CLASSES) + inside
                values = logits[inside * CLASSES : (inside + 1) * CLASSES]
                shifted = values - jnp.max(values, axis=0, keepdims=True)
                exponent = jnp.exp2(shifted * log2_e)
                total = jnp.sum(exponent, axis=0, keepdims=True)
                hot = spots == targets_ref[group : group + 1, columns]
                chosen = jnp.sum(jnp.where(hot, shifted, 0.0), axis=0, keepdims=True)
                loss = loss + counted * (jnp.log(total) - chosen)
                chance = exponent * (1.0 / total)
                slope = (chance - jnp.where(hot, 1.0, 0.0)) * counted
                dlogits_ref[group * CLASSES : (group + 1) * CLASSES, columns] = slope.astype(
                    jnp.bfloat16
                )
    loss_ref[...] = jnp.sum(loss, axis=1, keepdims=True)
    sum_ref[:, 2 * FF :] = dot_nt(final_ref[...].T, dlogits_ref[...])
    dfinal = dot_nn(head_ref[...], dlogits_ref[...]).T
    gain_sum = jnp.zeros((1, D), jnp.float32)
    for strip in strips(tokens):
        last = last_ref[strip, :]
        dlast, gain_part = rms_back(last, inverse_rms(last), gain_final, dfinal[strip])
        gain_sum = gain_sum + gain_part
        last_ref[strip, :] = dlast
        dout_ref[strip, :] = dlast.astype(jnp.bfloat16)
    gain_ref[1:2, :] = gain_sum
    gain_sum = jnp.zeros((1, D), jnp.float32)
    for block in range(tokens // ROWS):
        rows = slice(block * ROWS, (block + 1) * ROWS)
        for part in range(FF // D):
            dact = dot_nn(dout_ref[rows, :], weight_ref[:, FF + part * D : FF + (part + 1) * D])
            for strip in strips(ROWS):
                there = slice(block * ROWS + strip.start, block * ROWS + strip.stop)
                for side in range(0, D, LANES):
                    columns = slice(part * D + side, part * D + side + LANES)
                    dinner_ref[there, columns] = (
                        dact[strip, side : side + LANES] * slope_ref[there, columns]
                    ).astype(jnp.bfloat16)
        dnormed = dot_nt(dinner_ref[rows, :], weight_ref[:, 0:FF])
        gain_sum = gain_sum + norm_back(
            middle_ref[rows, :], gain_ffn, dnormed, last_ref[rows, :], dmiddle_ref, block * ROWS
        )
    gain_ref[0:1, :] = gain_sum
    sum_ref[:, 0:FF] = dot_nn(normed_ref[...].T, dinner_ref[...])
    sum_ref[:, FF : 2 * FF] = dot_nn(dout_ref[...].T, inner_ref[...])
    write_blocks(send_ref, keep_ref, sum_ref, core_ref[0], widths, scatter_steps)


def block_outs(own, widths):
    shape = jax.ShapeDtypeStruct
    blocks = own.shape[:2] + (sum(widths),)
    return [shape(blocks, jnp.bfloat16), shape(blocks, jnp.float32)]


def run_top(widths, gather_steps, scatter_steps, start, middle, own, other, targets, counted, gains, core):
    tokens = middle.shape[0]
    f32, b16 = jnp.float32, jnp.bfloat16
    shape = jax.ShapeDtypeStruct
    vmem = pl.BlockSpec(memory_space=pltpu.VMEM)
    return pl.pallas_call(
        functools.partial(top_kernel, widths, gather_steps, scatter_steps, start),
        in_specs=[vmem] * 6 + [smem_spec()],
        out_specs=[vmem] * 5,
        out_shape=[shape((tokens, D), f32)]
        + block_outs(own, widths)
        + [shape((2, D), f32), shape((1, 1), f32)],
        scratch_shapes=[
            pltpu.VMEM((D, 2 * FF), b16),
            pltpu.VMEM((D, VOCAB), b16),
            pltpu.VMEM((VOCAB, D), b16),
            pltpu.VMEM((tokens, D), b16),
            pltpu.VMEM((VOCAB, tokens), b16),
            pltpu.VMEM((tokens, D), b16),
            pltpu.VMEM((tokens, FF), b16),
            pltpu.VMEM((tokens, FF), f32),
            pltpu.VMEM((tokens, FF), b16),
            pltpu.VMEM((tokens, D), b16),
            pltpu.VMEM((tokens, D), f32),
            pltpu.VMEM((D, 2 * FF + VOCAB), f32),
        ],
        compiler_params=pltpu.CompilerParams(vmem_limit_bytes=VMEM_BYTES),
        cost_estimate=pl.CostEstimate(
            flops=6 * tokens * D * 3 * FF,
            bytes_accessed=tokens * D * 8 + D * 3 * FF * 10,
            transcendentals=tokens * (FF + VOCAB),
        ),
        name="loss_part",
    )(middle, own, other, targets, counted, gains, core)


def backward_kernel(layer, widths, steps, *refs):
    entry_ref, qkv_ref, mix_ref, lse_ref, dmiddle_ref, att_ref = refs[:6]
    gains_ref, valid_ref, core_ref = refs[6:9]
    if layer == 0:
        latent_ref, send_ref, keep_ref, gain_ref, bias_ref = refs[9:14]
        att_kept, before_kept, sum_ref, dentry_ref = refs[14:18], refs[18:20], refs[20], refs[21]
    else:
        before_ref, ffn_ref, out_ref, send_ref, keep_ref, gain_ref, bias_ref = refs[9:16]
        att_kept, before_kept, sum_ref, dentry_ref = refs[16:20], refs[20:24], refs[24], refs[25]
    step = pl.program_id(0)
    here = Here(step)

    @pl.when(step == 0)
    def _():
        fill_bias(bias_ref)
        gain_ref[...] = jnp.zeros_like(gain_ref)

    gain_ref[0:1, :] += attend_back(
        step,
        here,
        (entry_ref, qkv_ref, mix_ref, lse_ref),
        dmiddle_ref,
        gains_ref[layer : layer + 1, :],
        att_ref,
        valid_ref,
        bias_ref,
        att_kept,
        dentry_ref,
    )
    if layer == 0:
        before_kept[0][here(0, ROWS), :] = dentry_ref[...].astype(jnp.bfloat16)
        one_hot_rows(latent_ref[...], before_kept[1], here.base(CTX))
    else:
        gain_ref[1:2, :] += feed_back(
            here,
            dentry_ref,
            before_ref,
            gains_ref[LAYERS + layer - 1 : LAYERS + layer, :],
            ffn_ref,
            before_kept,
            out_ref,
        )

    @pl.when(step == pl.num_programs(0) - 1)
    def _():
        normed_ref, dattend_ref, dqkv_ref, mixes_ref = att_kept
        att = [(normed_ref, dqkv_ref), (mixes_ref, dattend_ref)]
        if layer == 0:
            pairs = att + [(before_kept[0], before_kept[1])]
        else:
            normed_two_ref, inner_ref, dinner_ref, dout_ref = before_kept
            pairs = [(normed_two_ref, dinner_ref), (dout_ref, inner_ref)] + att
        column = 0
        for left, right in pairs:
            wide = right.shape[1]
            sum_ref[:, column : column + wide] = dot_nn(left[...].T, right[...])
            column += wide
        write_blocks(send_ref, keep_ref, sum_ref, core_ref[0], widths, steps)


def run_backward(layer, widths, steps, blocks_like, saved, dmiddle, gains, valid, core, before):
    entry, _, qkv, mix, lse, weights = saved[:6]
    tokens = entry.shape[0]
    queries = lse.shape[2] // HEADS
    short = tokens // CTX * queries
    f32, b16 = jnp.float32, jnp.bfloat16
    shape = jax.ShapeDtypeStruct
    in_specs = [
        row_spec(D),
        row_spec(3 * D),
        row_spec(D, GROUP * queries),
        lse_spec(queries),
        row_spec(D, GROUP * queries),
        whole_spec(weights.shape),
        whole_spec(gains.shape),
        smem_spec(),
        smem_spec(),
    ]
    operands = [entry, qkv, mix, lse, dmiddle, weights, gains, valid, core]
    blocks = block_outs(blocks_like, widths)
    outs = [(item, whole_spec(item.shape)) for item in blocks]
    outs.append((shape((2, D), f32), whole_spec((2, D))))
    scratch = [
        pltpu.VMEM((2, CTX, HEADS * queries), f32),
        pltpu.VMEM((tokens, D), b16),
        pltpu.VMEM((short, D), b16),
        pltpu.VMEM((tokens, 3 * D), b16),
        pltpu.VMEM((short, D), b16),
    ]
    if layer == 0:
        in_specs.append(row_spec(CATS))
        operands.append(before)
        scratch = scratch + [pltpu.VMEM((tokens, D), b16), pltpu.VMEM((tokens, VOCAB), b16)]
        wide = 4 * D + VOCAB
    else:
        in_specs = in_specs + [row_spec(D), whole_spec(before[1].shape)]
        operands = operands + list(before)
        outs.insert(0, (shape((tokens, D), f32), row_spec(D)))
        scratch = scratch + [
            pltpu.VMEM((tokens, D), b16),
            pltpu.VMEM((tokens, FF), b16),
            pltpu.VMEM((tokens, FF), b16),
            pltpu.VMEM((tokens, D), b16),
        ]
        wide = 4 * D + 2 * FF
    return pl.pallas_call(
        functools.partial(backward_kernel, layer, widths, steps),
        grid=(tokens // ROWS,),
        in_specs=in_specs,
        out_specs=[spec for _, spec in outs],
        out_shape=[item for item, _ in outs],
        scratch_shapes=scratch + [pltpu.VMEM((D, wide), f32), pltpu.VMEM((ROWS, D), f32)],
        compiler_params=pltpu.CompilerParams(vmem_limit_bytes=VMEM_BYTES),
        cost_estimate=pl.CostEstimate(
            flops=6 * tokens * D * wide,
            bytes_accessed=tokens * D * 24 + D * wide * 6,
            transcendentals=tokens * (FF + HEADS * CTX),
        ),
        name="backward_part",
    )(*operands)


def matrix_plan(widths):
    order = [
        (2, 2), (3, 2), (5, 0), (2, 1), (3, 1), (0, 2), (1, 2),
        (2, 0), (3, 0), (0, 1), (1, 1), (0, 0), (1, 0), (4, 0),
    ]
    plan, column = {}, 0
    for which, layer in order:
        plan[(which, layer)] = (column, widths[which])
        column += widths[which]
    return plan, column


def matrix_list():
    return [(which, layer) for which in range(4) for layer in range(LAYERS)] + [(4, 0), (5, 0)]


MATRICES = 4 * LAYERS + 2
INNER_ROWS = 16
COMMON_ROWS = 16
ROW_IS_INNER = [True, True, True, False, False, True]


def master_of(masters, which, layer):
    if which == 1:
        return masters[1][layer].T
    return masters[which][layer] if which < 4 else masters[which][...]


def old_row(refs, which, layer):
    return refs[which][layer : layer + 1, :] if which < 4 else refs[which][...]


def stats_kernel(widths, *refs):
    raw_early, raw_late, masters, row_refs = refs[0], refs[1], refs[2:8], refs[8:14]
    gains_at, loss_ref, counted_ref, packet_ref = refs[14:18], refs[18], refs[19], refs[20]
    plan, total = matrix_plan(widths)
    square = jnp.concatenate([raw_early[...] * raw_early[...], raw_late[...] * raw_late[...]], axis=1)
    rows = square.shape[0]
    one = lambda value: jnp.sum(jnp.sum(value, axis=1, keepdims=True), axis=0, keepdims=True)
    inner, weights, entries, row_sums = [], [], [], []
    for which, layer in matrix_list():
        column, width = plan[(which, layer)]
        inner.append(jnp.sum(square[:, column : column + width], axis=1, keepdims=True))
        entries.append(jnp.sum(inner[-1], axis=0, keepdims=True))
        master = master_of(masters, which, layer)
        weights.append(one(master * master))
        row_sums.append(one(old_row(row_refs, which, layer)))
    packet_ref[...] = jnp.zeros_like(packet_ref)
    inner.append(jnp.zeros((rows, LANES - MATRICES), jnp.float32))
    packet_ref[0:INNER_ROWS, 0:rows] = jnp.concatenate(inner, axis=1).T[0:INNER_ROWS, :]
    top, two, one_at, zero = [ref[...] for ref in gains_at]
    gain = jnp.concatenate(
        [zero[0:1], one_at[0:1], two[0:1], one_at[1:2], two[1:2], top[0:1], top[1:2]], axis=0
    )
    scalars = [loss_ref[...], one(counted_ref[...])] + weights + entries + row_sums
    scalars.append(jnp.zeros((1, LANES - len(scalars)), jnp.float32))
    at = INNER_ROWS
    packet_ref[at : at + 7, :] = gain[:, 0:LANES]
    packet_ref[at + 7 : at + 8, :] = jnp.concatenate(scalars, axis=1)
    packet_ref[at + 8 : at + 15, :] = gain[:, LANES:]
    outer = jnp.sum(square, axis=0, keepdims=True)
    at = INNER_ROWS + COMMON_ROWS
    for row, start in enumerate(range(0, total, LANES)):
        stop = min(start + LANES, total)
        packet_ref[at + row : at + row + 1, 0 : stop - start] = outer[:, start:stop]


def outer_rows(widths):
    _, total = matrix_plan(widths)
    return -(-total // (8 * LANES)) * 8


def run_stats(widths, raw_early, raw_late, masters, rows, gain_parts, loss, counted):
    vmem = pl.BlockSpec(memory_space=pltpu.VMEM)
    operands = [raw_early, raw_late] + masters + rows + gain_parts + [loss, counted]
    packet = (INNER_ROWS + COMMON_ROWS + outer_rows(widths), LANES)
    return pl.pallas_call(
        functools.partial(stats_kernel, widths),
        in_specs=[vmem] * len(operands),
        out_specs=vmem,
        out_shape=jax.ShapeDtypeStruct(packet, jnp.float32),
        name="statistics",
    )(*operands)


def update_kernel(widths, sizes, *refs):
    across_ref, along_ref, raw_early, raw_late = refs[:4]
    masters, inner_refs, outer_refs = refs[4:10], refs[10:16], refs[16:22]
    gains_ref, second_ref = refs[22:24]
    outs = refs[24:]
    outer_count, inner_count = sizes
    plan, total = matrix_plan(widths)
    rows = raw_early.shape[0]
    scalars = along_ref[7:8, :]
    pick = lambda at: scalars[:, at : at + 1]
    gain_sum = jnp.concatenate([along_ref[0:7, :], along_ref[8:15, :]], axis=1)
    gain_square = jnp.sum(jnp.sum(gain_sum * gain_sum, axis=1, keepdims=True), axis=0, keepdims=True)
    square_total = gain_square
    for at in range(MATRICES):
        square_total = square_total + pick(2 + MATRICES + at)
    count_total = pick(1)
    norm_value = jnp.sqrt(square_total) / count_total
    scaling = jnp.minimum(1.0, clip_limit / norm_value) / count_total
    square_scale = scaling * scaling
    outer_total = jnp.concatenate(
        [
            along_ref[COMMON_ROWS + row : COMMON_ROWS + row + 1, 0 : min(LANES, total - row * LANES)]
            for row in range(-(-total // LANES))
        ],
        axis=1,
    )
    inner_new = []
    for at, (which, layer) in enumerate(matrix_list()):
        outer_length = widths[which] * outer_count
        inner_new.append(
            decay_two * old_row(inner_refs, which, layer)
            + (1 - decay_two)
            * (square_scale * across_ref[at : at + 1, 0:rows] / outer_length + tiny_term)
        )
    stacked = jnp.concatenate(inner_new, axis=0)
    stacked = jnp.concatenate([stacked, jnp.ones((LANES - MATRICES, rows), jnp.float32)], axis=0)
    if rows < LANES:
        stacked = jnp.concatenate([stacked, jnp.ones((LANES, LANES - rows), jnp.float32)], axis=1)
    turned = lax.rsqrt(stacked).T
    outs[0][...] = pick(0)
    outs[1][...] = count_total
    outs[2][...] = norm_value
    first_out = {4: 3, 0: 7, 1: 11, 2: 15, 3: 19, 5: 23}
    for at, (which, layer) in enumerate(matrix_list()):
        column, width = plan[(which, layer)]
        outer_length, inner_length = width * outer_count, rows * inner_count
        row_length = inner_length if ROW_IS_INNER[which] else outer_length
        copies = outer_count if ROW_IS_INNER[which] else inner_count
        entries = outer_length * inner_length
        early = raw_early.shape[1]
        if column < early:
            raw = raw_early[:, column : column + width]
        else:
            raw = raw_late[:, column - early : column - early + width]
        outer_new = decay_two * old_row(outer_refs, which, layer) + (1 - decay_two) * (
            square_scale * outer_total[:, column : column + width] / inner_length + tiny_term
        )
        mean_rows = decay_two * (pick(2 + 2 * MATRICES + at) / (copies * row_length)) + (
            1 - decay_two
        ) * (square_scale * pick(2 + MATRICES + at) / entries + tiny_term)
        factor = step_rate * jnp.sqrt(pick(2 + at) / entries) * jnp.sqrt(mean_rows)
        grad = raw * scaling
        updated = master_of(masters, which, layer) - grad * (
            turned[0:rows, at : at + 1] * (factor * lax.rsqrt(outer_new))
        )
        first = first_out[which]
        row_new, column_new = (
            (inner_new[at], outer_new) if ROW_IS_INNER[which] else (outer_new, inner_new[at])
        )
        if which < 4:
            if which == 1:
                updated, grad = updated.T, grad.T
            outs[first][layer] = updated
            outs[first + 1][layer] = grad
            outs[first + 2][layer : layer + 1, :] = row_new
            outs[first + 3][layer : layer + 1, :] = column_new
        else:
            outs[first][...] = updated
            outs[first + 1][...] = grad
            outs[first + 2][...] = row_new
            outs[first + 3][...] = column_new
    gain_grad = gain_sum * scaling
    second_new = decay_two * second_ref[...] + (1 - decay_two) * (gain_grad * gain_grad + tiny_term)
    gains = gains_ref[...]
    spread = jnp.sqrt(jnp.mean(gains * gains, axis=-1, keepdims=True))
    outs[27][...] = gains - step_rate * spread * gain_grad * lax.rsqrt(second_new)
    outs[28][...] = gain_grad
    outs[29][...] = second_new


def run_update(widths, sizes, across, along, raw_early, raw_late, masters, inner, outer, gains, second):
    vmem = pl.BlockSpec(memory_space=pltpu.VMEM)
    operands = [across, along, raw_early, raw_late] + masters + inner + outer + [gains, second]
    shapes = [(1, 1)] * 3
    for which in [4, 0, 1, 2, 3, 5]:
        shapes = shapes + [masters[which].shape] * 2
        pair = [inner[which].shape, outer[which].shape]
        shapes = shapes + (pair if ROW_IS_INNER[which] else pair[::-1])
    shapes = shapes + [gains.shape] * 3
    return pl.pallas_call(
        functools.partial(update_kernel, widths, sizes),
        in_specs=[vmem] * len(operands),
        out_specs=[vmem] * len(shapes),
        out_shape=[jax.ShapeDtypeStruct(item, jnp.float32) for item in shapes],
        name="update",
    )(*operands)


def swap(value, axis, bit):
    pairs = [(place, place ^ bit) for place in range(lax.axis_size(axis))]
    return lax.ppermute(value, axis, pairs)


def tie(*values):
    return lax.optimization_barrier(values)


class Gather:
    def __init__(self, piece, steps):
        self.held, self.steps, self.at = piece[None], steps, 0

    def send(self):
        axis, bit = self.steps[self.at]
        self.other = swap(self.held, axis, 1 << bit)

    def join(self):
        axis, bit = self.steps[self.at]
        upper = (lax.axis_index(axis) >> bit) & 1 == 1
        self.held = jnp.where(
            upper,
            jnp.concatenate([self.other, self.held]),
            jnp.concatenate([self.held, self.other]),
        )
        self.at += 1

    def step(self, after=None):
        if after is not None:
            self.held, _ = tie(self.held, after.other)
        self.send()
        self.join()


class Scatter:
    def __init__(self, sent, kept, steps):
        self.sent, self.kept, self.steps, self.at = sent, kept, steps, 0

    def send(self):
        axis, bit = self.steps[self.at]
        self.other = swap(self.sent, axis, 1 << bit)

    def join(self):
        self.at += 1
        summed = self.kept + self.other.astype(jnp.float32)
        if self.at == len(self.steps):
            self.kept = summed
            return
        axis, bit = self.steps[self.at]
        side = (lax.axis_index(axis) >> bit) & 1
        half = summed.shape[0] // 2
        parts = summed.reshape((2, half) + summed.shape[1:])
        self.sent = jnp.where(side == 1, parts[0], parts[1]).astype(jnp.bfloat16)
        self.kept = jnp.where(side == 1, parts[1], parts[0])


def merged(parts):
    whole = Scatter(
        jnp.concatenate([part.sent for part in parts], axis=2),
        jnp.concatenate([part.kept for part in parts], axis=2),
        parts[0].steps,
    )
    whole.at = parts[0].at
    return whole


def shards(
    latents,
    targets,
    horizon,
    memory_valid,
    embed,
    qkv_weight,
    out_weight,
    up_weight,
    down_weight,
    head_weight,
    gains,
    embed_rows,
    embed_cols,
    qkv_rows,
    qkv_cols,
    out_rows,
    out_cols,
    up_rows,
    up_cols,
    down_rows,
    down_cols,
    head_rows,
    head_cols,
    gain_second,
):
    samples = latents.shape[0]
    sizes = (lax.axis_size("dp"), lax.axis_size("fsdp"))
    bits = (sizes[0].bit_length() - 1, sizes[1].bit_length() - 1)
    outer_steps = [("dp", bit) for bit in reversed(range(bits[0]))]
    inner_steps = [("fsdp", bit) for bit in reversed(range(bits[1]))]
    gather_steps = outer_steps + inner_steps
    second_steps = outer_steps[:-1] + inner_steps[:-1] + outer_steps[-1:] + inner_steps[-1:]
    scatter_steps = gather_steps[::-1]
    core = (lax.axis_index("fsdp") & 1).astype(jnp.int32).reshape(1)

    low = lambda item: item.astype(jnp.bfloat16)
    out_turned = jnp.swapaxes(out_weight, 1, 2)
    down_turned = jnp.swapaxes(down_weight, 1, 2)
    masters = [qkv_weight, out_turned, up_weight, down_turned, embed.T, head_weight]
    widths = [qkv_weight.shape[2], out_weight.shape[2], up_weight.shape[2], down_weight.shape[1]]
    widths = widths + [embed.shape[0], head_weight.shape[1]]
    att_parts = [[qkv_weight[at], out_weight[at]] for at in range(LAYERS)]
    ffn_parts = [[up_weight[at], down_turned[at]] for at in range(LAYERS)]
    pieces = [
        att_parts[0] + [embed.T],
        ffn_parts[0] + att_parts[1],
        ffn_parts[1] + att_parts[2] + ffn_parts[2] + [head_weight],
    ]
    att_widths, ffn_widths = widths[0:2], widths[2:4]
    orders = [gather_steps, second_steps, gather_steps]
    first, second, third = [
        Gather(low(jnp.concatenate(piece, axis=1)), order) for piece, order in zip(pieces, orders)
    ]
    chunk_widths = [
        att_widths + widths[4:5],
        ffn_widths + att_widths,
        ffn_widths + att_widths + ffn_widths + widths[5:6],
    ]

    latent_rows = low(latents).reshape(samples * CTX, CATS)
    target_rows = targets.transpose(2, 0, 1).reshape(CATS, samples * SEG)
    counted = jnp.arange(SEG, dtype=jnp.int32)[None, :] < horizon[:, None]
    counted = counted.astype(jnp.float32).reshape(1, samples * SEG)
    shared = (gains, memory_valid, core)

    count = len(gather_steps)
    for at in range(count - 1):
        active = [first, second] + ([third] if at >= 2 else [])
        held = tie(*[chunk.held for chunk in active])
        for chunk, value in zip(active, held):
            chunk.held = value
            chunk.send()
        for chunk in active:
            chunk.join()
    while third.at < count - 3:
        third.step()
    first.held, second.held, third.held = tie(first.held, second.held, third.held)
    first.send()
    second.send()
    third.step()
    first.held, first.other, third.held = tie(first.held, first.other, third.held)
    third.send()
    kept = [
        run_forward(
            0, chunk_widths[0], gather_steps, latent_rows, first.held, first.other, *shared
        )
    ]
    middle, second.other, third.other = tie(kept[0][1], second.other, third.other)
    third.join()
    second.held, third.held = tie(second.held, third.held)
    third.send()
    kept.append(
        run_forward(1, chunk_widths[1], second_steps, middle, second.held, second.other, *shared)
    )
    middle, third.other = tie(kept[1][1], third.other)
    kept.append(
        run_forward(2, chunk_widths[2], gather_steps, middle, third.held, third.other, *shared)
    )

    dmiddle, sent, held, gain_top, loss = run_top(
        ffn_widths + widths[5:6],
        gather_steps,
        scatter_steps[::-1],
        sum(ffn_widths + att_widths),
        kept[2][1],
        third.held,
        third.other,
        target_rows,
        counted,
        gains,
        core,
    )
    top = Scatter(sent, held, scatter_steps)
    top.send()
    like = first.held
    dmiddle, sent, held, gain_two = run_backward(
        2, chunk_widths[1], gather_steps, like, kept[2], dmiddle, *shared, (kept[1][1], kept[2][6])
    )
    dmiddle, top.other = tie(dmiddle, top.other)
    top.join()
    two = Scatter(sent, held, scatter_steps)
    dmiddle, top.sent = tie(dmiddle, top.sent)
    top.send()
    two.send()
    dmiddle, sent, held, gain_one = run_backward(
        1, chunk_widths[1], gather_steps, like, kept[1], dmiddle, *shared, (kept[0][1], kept[1][6])
    )
    dmiddle, top.other, two.other = tie(dmiddle, top.other, two.other)
    top.join()
    two.join()
    one = Scatter(sent, held, scatter_steps)
    dmiddle, top.sent, two.sent = tie(dmiddle, top.sent, two.sent)
    top.send()
    two.send()
    one.send()
    sent, held, gain_zero = run_backward(
        0, chunk_widths[0], gather_steps, like, kept[0], dmiddle, *shared, latent_rows
    )
    sent, top.other, two.other, one.other = tie(sent, top.other, two.other, one.other)
    zero = Scatter(sent, held, scatter_steps)
    zero.send()
    top.join()
    two.join()
    one.join()
    two.send()
    one.send()
    zero.join()
    two.other, one.other, zero.sent = tie(two.other, one.other, zero.sent)
    zero.send()
    two.join()
    one.join()
    one.send()
    zero.other, one.sent = tie(zero.other, one.sent)
    zero.join()
    zero.send()
    one.other, zero.sent = tie(one.other, zero.sent)
    one.join()
    early = merged([top, two, one])
    early.send()
    while early.at < count:
        zero.other, early.sent = tie(zero.other, early.sent)
        zero.join()
        zero.send()
        early.other, zero.sent = tie(early.other, zero.sent)
        early.join()
        if early.at < count:
            early.send()
    while zero.at < count:
        zero.join()
        if zero.at < count:
            zero.send()
    raw_early, raw_late = early.kept[0], zero.kept[0]

    flat = lambda item: item if item.ndim == 2 else item.reshape(1, -1)
    inner = [flat(item) for item in (qkv_rows, out_rows, up_rows, down_cols, embed_cols, head_rows)]
    outer = [flat(item) for item in (qkv_cols, out_cols, up_cols, down_rows, embed_rows, head_cols)]
    row_stats = [inner[at] if ROW_IS_INNER[at] else outer[at] for at in range(6)]
    gain_parts = [gain_top, gain_two, gain_one, gain_zero]
    packet = run_stats(widths, raw_early, raw_late, masters, row_stats, gain_parts, loss, counted)
    edge = INNER_ROWS + COMMON_ROWS
    across = packet[:edge]
    for axis, bit in scatter_steps[bits[1] :]:
        across = across + swap(across, axis, 1 << bit)
    along = jnp.concatenate([across[INNER_ROWS:], packet[edge:]])
    for axis, bit in scatter_steps[: bits[1]][::-1]:
        along = along + swap(along, axis, 1 << bit)
    results = run_update(
        widths, sizes, across, along, raw_early, raw_late, masters, inner, outer, gains, gain_second
    )
    results = list(results)
    for at in range(3):
        results[at] = results[at].reshape(())
    for at in (3, 4, 11, 12, 19, 20):
        results[at] = jnp.swapaxes(results[at], -1, -2)
    for at in (5, 6, 25, 26):
        results[at] = results[at].reshape(-1)
    return tuple(results)


def solution(mesh):
    return jax.shard_map(
        shards,
        mesh=mesh,
        in_specs=(
            P(("dp", "fsdp"), None, None),
            P(("dp", "fsdp"), None, None),
            P(("dp", "fsdp")),
            P(("dp", "fsdp")),
            P("dp", "fsdp"),
            P(None, "fsdp", "dp"),
            P(None, "fsdp", "dp"),
            P(None, "fsdp", "dp"),
            P(None, "dp", "fsdp"),
            P("fsdp", "dp"),
            P(),
            P("dp"),
            P("fsdp"),
            P(None, "fsdp"),
            P(None, "dp"),
            P(None, "fsdp"),
            P(None, "dp"),
            P(None, "fsdp"),
            P(None, "dp"),
            P(None, "dp"),
            P(None, "fsdp"),
            P("fsdp"),
            P("dp"),
            P(),
        ),
        out_specs=(
            P(),
            P(),
            P(),
            P("dp", "fsdp"),
            P("dp", "fsdp"),
            P("dp"),
            P("fsdp"),
            P(None, "fsdp", "dp"),
            P(None, "fsdp", "dp"),
            P(None, "fsdp"),
            P(None, "dp"),
            P(None, "fsdp", "dp"),
            P(None, "fsdp", "dp"),
            P(None, "fsdp"),
            P(None, "dp"),
            P(None, "fsdp", "dp"),
            P(None, "fsdp", "dp"),
            P(None, "fsdp"),
            P(None, "dp"),
            P(None, "dp", "fsdp"),
            P(None, "dp", "fsdp"),
            P(None, "dp"),
            P(None, "fsdp"),
            P("fsdp", "dp"),
            P("fsdp", "dp"),
            P("fsdp"),
            P("dp"),
            P(),
            P(),
            P(),
        ),
        check_vma=False,
    )
```

```python
import functools

import jax
import jax.numpy as jnp
from jax import lax
from jax.experimental import pallas as pl
from jax.experimental.pallas import tpu as pltpu
from jax.sharding import PartitionSpec as P

D = 256
HEADS = 8
HEAD = D // HEADS
FF = 1024
CATS = 32
CLASSES = 32
LAYERS = 3
SEG = 48
MEM = 48
CTX = 96
VOCAB = 1024
GROUP = 4
ROWS = GROUP * CTX
SPREAD = HEADS * CTX
VMEM_BYTES = 56 * 1024 * 1024

decay_two = 0.9
step_rate = 0.3
clip_limit = 0.05
tiny_term = 1e-30
norm_eps = 1e-06
masked_score = -1e30
log2_e = 1.4426950408889634
score_scale = HEAD ** (-0.5)
gelu_one = 0.7978845608028654
gelu_two = 0.044715


def dot_nn(left, right):
    return lax.dot_general(
        left, right, (((1,), (0,)), ((), ())), preferred_element_type=jnp.float32
    )


def dot_nt(left, right):
    return lax.dot_general(
        left, right, (((1,), (1,)), ((), ())), preferred_element_type=jnp.float32
    )


def dot_tn(left, right):
    return lax.dot_general(
        left, right, (((0,), (0,)), ((), ())), preferred_element_type=jnp.float32
    )


def inverse_rms(values):
    return lax.rsqrt(jnp.mean(values * values, axis=-1, keepdims=True) + norm_eps)


def rms_back(values, inverse, gain_row, upstream):
    normed = values * inverse
    scaled = upstream * gain_row
    inner = jnp.mean(scaled * normed, axis=-1, keepdims=True)
    return (
        inverse * (scaled - normed * inner),
        jnp.sum(upstream * normed, axis=0, keepdims=True),
    )


def head_masks():
    lane = lax.broadcasted_iota(jnp.int32, (1, D // 2), 1) // HEAD
    return [lane == head for head in range(HEADS // 2)]


def expand_heads(rows, masks):
    half = D // 2
    nothing = jnp.zeros((rows.shape[0], half), rows.dtype)
    pieces = []
    for head in range(HEADS):
        side, at = divmod(head, HEADS // 2)
        kept = rows[:, side * half : (side + 1) * half] * masks[at].astype(rows.dtype)
        pair = [kept, nothing] if side == 0 else [nothing, kept]
        pieces.append(jnp.concatenate(pair, axis=1))
    return jnp.concatenate(pieces, axis=0)


def collapse_heads(spread, rows, masks):
    half, span = D // 2, spread.shape[1] // 2
    queries = span // (HEADS // 2)
    sides = []
    for side in range(2):
        product = dot_tn(
            spread[:, side * span : (side + 1) * span], rows[:, side * half : (side + 1) * half]
        )
        taken = product[(HEADS // 2 - 1) * queries :]
        for at in range(HEADS // 2 - 1):
            taken = jnp.where(masks[at], product[at * queries : (at + 1) * queries], taken)
        sides.append(taken)
    return jnp.concatenate(sides, axis=1)


def fill_bias(bias_ref):
    spread = bias_ref.shape[2]
    queries = spread // HEADS
    key_at = lax.broadcasted_iota(jnp.int32, (CTX, spread), 0)
    query_at = lax.broadcasted_iota(jnp.int32, (CTX, spread), 1) % queries + (CTX - queries)
    later = key_at > query_at
    crosses = (query_at >= MEM) & (key_at < MEM)
    bias_ref[0] = jnp.where(later | crosses, masked_score, 0.0)
    bias_ref[1] = jnp.where(later, masked_score, 0.0)


def block_place(device, steps):
    place, weight = 0, 1
    for step in steps[:-1]:
        digit = 0
        for bit in step:
            digit = 2 * digit + ((device >> bit) & 1)
        place += digit * weight
        weight <<= len(step)
    return place


def place_weights(targets, own_ref, other_ref, core, widths, mesh_plan, start=0):
    outer_count, inner_count, steps = mesh_plan
    rows = own_ref.shape[1]
    for high in range(inner_count // 2):
        for source, side in ((own_ref, core), (other_ref, 1 - core)):
            here = pl.ds(pl.multiple_of((2 * high + side) * rows, rows), rows)
            at = start
            for (target, column), width in zip(targets, widths):
                block = [
                    source[
                        block_place(outer * inner_count + 2 * high, steps), :, at : at + width
                    ]
                    for outer in range(outer_count)
                ]
                target[here, column : column + width * outer_count] = jnp.concatenate(
                    block, axis=1
                )
                at += width


def write_blocks(send_ref, keep_ref, sum_ref, core, widths, mesh_plan):
    outer_count, inner_count, steps = mesh_plan
    rows = keep_ref.shape[1]
    for high in range(inner_count // 2):
        for target, side in ((keep_ref, core), (send_ref, 1 - core)):
            here = pl.ds(pl.multiple_of((2 * high + side) * rows, rows), rows)
            taken = sum_ref[here, :]
            for outer in range(outer_count):
                block, column = [], 0
                for width in widths:
                    block.append(taken[:, column + outer * width : column + (outer + 1) * width])
                    column += width * outer_count
                target[block_place(outer * inner_count + 2 * high, steps)] = jnp.concatenate(
                    block, axis=1
                ).astype(target.dtype)


def one_hot_rows(latent_rows):
    spot = lax.broadcasted_iota(jnp.int32, (CATS, VOCAB), 1) // CLASSES
    group = lax.broadcasted_iota(jnp.int32, (CATS, VOCAB), 0)
    spreader = jnp.where(spot == group, 1.0, 0.0).astype(jnp.bfloat16)
    classes = (lax.broadcasted_iota(jnp.int32, (1, VOCAB), 1) % CLASSES).astype(jnp.float32)
    drawn = dot_nn(latent_rows, spreader)
    return jnp.where(drawn == classes, 1.0, 0.0).astype(jnp.bfloat16)


def tail_rows(values, queries):
    if queries == CTX:
        return values
    return jnp.concatenate(
        [
            values[(sample + 1) * CTX - queries : (sample + 1) * CTX]
            for sample in range(values.shape[0] // CTX)
        ],
        axis=0,
    )


def attend_forward(step, hidden, gain_row, weight_ref, valid_ref, bias_ref, masks, refs):
    middle_ref, qkv_ref, mix_ref, lse_ref = refs
    queries = lse_ref.shape[2] // HEADS
    normed = (hidden * inverse_rms(hidden) * gain_row).astype(jnp.bfloat16)
    qkv_ref[...] = dot_nn(normed, weight_ref[:, 0 : 3 * D]).astype(jnp.bfloat16)
    scores, chances = [], []
    for sample in range(GROUP):
        rows = slice(sample * CTX, (sample + 1) * CTX)
        spread = expand_heads(qkv_ref[(sample + 1) * CTX - queries : (sample + 1) * CTX, 0:D], masks)
        scores.append(dot_nt(qkv_ref[rows, D : 2 * D], spread))
    for sample in range(GROUP):
        score = scores[sample] + bias_ref[valid_ref[step * GROUP + sample]]
        peak = jnp.max(score, axis=0, keepdims=True)
        exponent = jnp.exp2((score - peak) * (score_scale * log2_e))
        total = jnp.sum(exponent, axis=0, keepdims=True)
        chances.append((exponent * (1.0 / total)).astype(jnp.bfloat16))
        lse_ref[sample] = peak * (score_scale * log2_e) + jnp.log2(total)
    for sample in range(GROUP):
        rows = slice(sample * CTX, (sample + 1) * CTX)
        mix_ref[sample * queries : (sample + 1) * queries, :] = collapse_heads(
            chances[sample], qkv_ref[rows, 2 * D : 3 * D], masks
        ).astype(jnp.bfloat16)
    middle_ref[...] = tail_rows(hidden, queries) + dot_nn(
        mix_ref[...], weight_ref[:, 3 * D : 4 * D]
    )


def gelu_bend(value, square):
    return jnp.tanh(value * (gelu_one + (gelu_one * gelu_two) * square))


def gelu_slope(half_value, bend, square):
    return (0.5 + 0.5 * bend) + (half_value * (1.0 - bend * bend)) * (
        gelu_one + (3.0 * gelu_one * gelu_two) * square
    )


def ahead(make, count, eager):
    if not eager:
        for at in range(count):
            yield make(at)
        return
    now = make(0)
    for at in range(count):
        later = make(at + 1) if at + 1 < count else None
        yield now
        now = later


def feed_forward(middle, gain_row, weight_ref, inner_ref, eager):
    normed = (middle * inverse_rms(middle) * gain_row).astype(jnp.bfloat16)
    products = ahead(
        lambda part: dot_nn(normed, weight_ref[:, part * D : (part + 1) * D]), FF // D, eager
    )
    for part, inner in enumerate(products):
        columns = slice(part * D, (part + 1) * D)
        for sample in range(GROUP):
            rows = slice(sample * CTX, (sample + 1) * CTX)
            value = inner[rows]
            bend = gelu_bend(value, value * value)
            inner_ref[rows, columns] = ((0.5 * value) * (1.0 + bend)).astype(jnp.bfloat16)
    return middle + dot_nt(inner_ref[...], weight_ref[:, FF : 2 * FF])


def feed_back(here, upstream, middle, gain_row, weight_ref, refs, eager):
    normed_ref, inner_ref, dinner_ref, dout_ref = refs
    dout = upstream.astype(jnp.bfloat16)
    dout_ref[here(0, ROWS), :] = dout
    inverse = inverse_rms(middle)
    normed = (middle * inverse * gain_row).astype(jnp.bfloat16)
    normed_ref[here(0, ROWS), :] = normed
    products = ahead(
        lambda part: (
            dot_nn(normed, weight_ref[:, part * D : (part + 1) * D]),
            dot_nn(dout, weight_ref[:, FF + part * D : FF + (part + 1) * D]),
        ),
        FF // D,
        eager,
    )
    for part, (inner, dact) in enumerate(products):
        columns = slice(part * D, (part + 1) * D)
        for sample in range(GROUP):
            rows = slice(sample * CTX, (sample + 1) * CTX)
            there = here(sample * CTX, CTX)
            value = inner[rows]
            square = value * value
            bend = gelu_bend(value, square)
            half_value = 0.5 * value
            inner_ref[there, columns] = (half_value * (1.0 + bend)).astype(jnp.bfloat16)
            dinner_ref[there, columns] = (
                dact[rows] * gelu_slope(half_value, bend, square)
            ).astype(jnp.bfloat16)
    dnormed = dot_nt(dinner_ref[here(0, ROWS), :], weight_ref[:, 0:FF])
    through, gain_part = rms_back(middle, inverse, gain_row, dnormed)
    return upstream + through, gain_part


def attend_back(step, here, saved, dmiddle, gain_row, weight_ref, valid_ref, bias_ref, masks, refs, abreast):
    hidden, qkv_ref, mix_ref, lse_ref = saved
    normed_ref, dmiddle_ref, dqkv_ref, mixes_ref = refs
    queries = lse_ref.shape[2] // HEADS
    short = here(0, GROUP * queries, queries)
    dattend = dmiddle.astype(jnp.bfloat16)
    dmiddle_ref[short, :] = dattend
    mixes_ref[short, :] = mix_ref[...]
    dmix = dot_nt(dattend, weight_ref[:, 3 * D : 4 * D]).astype(jnp.bfloat16)
    for first in range(0, GROUP, abreast):
        samples = range(first, first + abreast)
        spreads, slopes, scores, dchances, chances, dscores = [], [], [], [], [], []
        for sample in samples:
            rows = slice(sample * CTX, (sample + 1) * CTX)
            tail = slice((sample + 1) * CTX - queries, (sample + 1) * CTX)
            spreads.append(expand_heads(qkv_ref[tail, 0:D], masks))
            slopes.append(expand_heads(dmix[sample * queries : (sample + 1) * queries], masks))
            scores.append(dot_nt(qkv_ref[rows, D : 2 * D], spreads[-1]))
            dchances.append(dot_nt(qkv_ref[rows, 2 * D : 3 * D], slopes[-1]))
        for at, sample in enumerate(samples):
            score = scores[at] + bias_ref[valid_ref[step * GROUP + sample]]
            chance = jnp.exp2(score * (score_scale * log2_e) - lse_ref[sample])
            weighed = chance * dchances[at]
            dscores.append(
                (weighed - chance * jnp.sum(weighed, axis=0, keepdims=True)).astype(jnp.bfloat16)
            )
            chances.append(chance.astype(jnp.bfloat16))
        for at, sample in enumerate(samples):
            there = here(sample * CTX, CTX)
            keys = qkv_ref[sample * CTX : (sample + 1) * CTX, D : 2 * D]
            dvalues = dot_nn(chances[at], slopes[at])
            dkeys = dot_nn(dscores[at], spreads[at]) * score_scale
            dqueries = (collapse_heads(dscores[at], keys, masks) * score_scale).astype(jnp.bfloat16)
            if queries < CTX:
                nothing = jnp.zeros((CTX - queries, D), jnp.bfloat16)
                dqueries = jnp.concatenate([nothing, dqueries], axis=0)
            dqkv_ref[there, 0:D] = dqueries
            dqkv_ref[there, D : 2 * D] = dkeys.astype(jnp.bfloat16)
            dqkv_ref[there, 2 * D : 3 * D] = dvalues.astype(jnp.bfloat16)
    inverse = inverse_rms(hidden)
    normed_ref[here(0, ROWS), :] = (hidden * inverse * gain_row).astype(jnp.bfloat16)
    dnormed = dot_nt(dqkv_ref[here(0, ROWS), :], weight_ref[:, 0 : 3 * D])
    through, gain_part = rms_back(hidden, inverse, gain_row, dnormed)
    if queries < CTX:
        nothing = jnp.zeros((CTX - queries, D), jnp.float32)
        pieces = []
        for sample in range(GROUP):
            pieces = pieces + [nothing, dmiddle[sample * queries : (sample + 1) * queries]]
        dmiddle = jnp.concatenate(pieces, axis=0)
    return dmiddle + through, gain_part


def row_spec(width, rows=ROWS):
    return pl.BlockSpec((rows, width), lambda step: (step, 0))


def lse_spec(queries):
    return pl.BlockSpec((GROUP, 1, HEADS * queries), lambda step: (step, 0, 0))


def whole_spec(shape):
    return pl.BlockSpec(shape, lambda step: (0,) * len(shape))


def smem_spec():
    return pl.BlockSpec(memory_space=pltpu.SMEM)


def forward_kernel(layer, widths, mesh_plan, source_ref, own_ref, other_ref, gains_ref, valid_ref, core_ref, *refs):
    entry_ref, att_ref, before_ref, bias_ref = refs[0], refs[5], refs[6], refs[7]
    step = pl.program_id(0)

    @pl.when(step == 0)
    def _():
        fill_bias(bias_ref)
        att = [(att_ref, 0), (att_ref, 3 * D)]
        before = [(before_ref, 0)] if layer == 0 else [(before_ref, 0), (before_ref, FF)]
        targets = att + before if layer == 0 else before + att
        place_weights(targets, own_ref, other_ref, core_ref[0], widths[: len(targets)], mesh_plan)

    if layer == 0:
        hidden = dot_nt(one_hot_rows(source_ref[...]), before_ref[...])
    else:
        gain_ffn = gains_ref[LAYERS + layer - 1 : LAYERS + layer, :]
        hidden = feed_forward(source_ref[...], gain_ffn, before_ref, refs[8], layer == 1)
    entry_ref[...] = hidden
    attend_forward(
        step,
        hidden,
        gains_ref[layer : layer + 1, :],
        att_ref,
        valid_ref,
        bias_ref,
        head_masks(),
        refs[1:5],
    )


def run_forward(layer, widths, mesh_plan, source, own, other, gains, valid, core):
    tokens = source.shape[0]
    queries = SEG if layer == LAYERS - 1 else CTX
    f32, b16 = jnp.float32, jnp.bfloat16
    shape = jax.ShapeDtypeStruct
    short = tokens // CTX * queries
    outs = [
        (shape((tokens, D), f32), row_spec(D)),
        (shape((short, D), f32), row_spec(D, GROUP * queries)),
        (shape((tokens, 3 * D), b16), row_spec(3 * D)),
        (shape((short, D), b16), row_spec(D, GROUP * queries)),
        (shape((tokens // CTX, 1, HEADS * queries), f32), lse_spec(queries)),
        (shape((D, 4 * D), b16), whole_spec((D, 4 * D))),
    ]
    scratch = [pltpu.VMEM((2, CTX, HEADS * queries), f32)]
    if layer == 0:
        scratch = [pltpu.VMEM((D, VOCAB), b16)] + scratch
    else:
        outs.append((shape((D, 2 * FF), b16), whole_spec((D, 2 * FF))))
        scratch.append(pltpu.VMEM((ROWS, FF), b16))
    return pl.pallas_call(
        functools.partial(forward_kernel, layer, widths, mesh_plan),
        grid=(tokens // ROWS,),
        in_specs=[
            row_spec(source.shape[1]),
            whole_spec(own.shape),
            whole_spec(other.shape),
            whole_spec(gains.shape),
            smem_spec(),
            smem_spec(),
        ],
        out_specs=[spec for _, spec in outs],
        out_shape=[item for item, _ in outs],
        scratch_shapes=scratch,
        compiler_params=pltpu.CompilerParams(vmem_limit_bytes=VMEM_BYTES),
        cost_estimate=pl.CostEstimate(
            flops=2 * tokens * D * 12 * D,
            bytes_accessed=tokens * D * 16 + D * 12 * D * 4,
            transcendentals=tokens * (FF + HEADS * CTX),
        ),
        name="forward_part",
    )(source, own, other, gains, valid, core)


def top_kernel(widths, mesh_plan, start, middle_ref, own_ref, other_ref, targets_ref, counted_ref, gains_ref, core_ref, *refs):
    dmiddle_ref, send_ref, keep_ref, gain_ref, loss_ref = refs[:5]
    weight_ref, head_ref, turned_ref, final_ref, dlogits_ref = refs[5:10]
    normed_ref, inner_ref, slope_ref, dinner_ref, dout_ref, last_ref, sum_ref = refs[10:]
    tokens = middle_ref.shape[0]
    gain_final = gains_ref[2 * LAYERS : 2 * LAYERS + 1, :]
    gain_ffn = gains_ref[2 * LAYERS - 1 : 2 * LAYERS, :]
    place_weights(
        [(weight_ref, 0), (weight_ref, FF), (head_ref, 0)],
        own_ref,
        other_ref,
        core_ref[0],
        widths,
        mesh_plan,
        start,
    )
    turned_ref[...] = head_ref[...].T
    for block in range(tokens // ROWS):
        rows = slice(block * ROWS, (block + 1) * ROWS)
        middle = middle_ref[rows, :]
        normed = (middle * inverse_rms(middle) * gain_ffn).astype(jnp.bfloat16)
        normed_ref[rows, :] = normed
        for part in range(FF // D):
            columns = slice(part * D, (part + 1) * D)
            inner = dot_nn(normed, weight_ref[:, columns])
            for piece in range(GROUP):
                value = inner[piece * CTX : (piece + 1) * CTX]
                there = slice(block * ROWS + piece * CTX, block * ROWS + (piece + 1) * CTX)
                square = value * value
                bend = gelu_bend(value, square)
                half_value = 0.5 * value
                inner_ref[there, columns] = (half_value * (1.0 + bend)).astype(jnp.bfloat16)
                slope_ref[there, columns] = gelu_slope(half_value, bend, square)
        last = middle + dot_nt(inner_ref[rows, :], weight_ref[:, FF : 2 * FF])
        last_ref[rows, :] = last
        final_ref[rows, :] = (last * inverse_rms(last) * gain_final).astype(jnp.bfloat16)
    span = D
    loss = jnp.zeros((1, span), jnp.float32)
    spots = lax.broadcasted_iota(jnp.int32, (CLASSES, span), 0)
    for part in range(tokens // span):
        columns = slice(part * span, (part + 1) * span)
        counted = counted_ref[0:1, columns]
        final = final_ref[columns, :]
        for quarter in range(VOCAB // D):
            logits = dot_nt(turned_ref[quarter * D : (quarter + 1) * D, :], final)
            for inside in range(D // CLASSES):
                group = quarter * (D // CLASSES) + inside
                values = logits[inside * CLASSES : (inside + 1) * CLASSES]
                shifted = values - jnp.max(values, axis=0, keepdims=True)
                exponent = jnp.exp2(shifted * log2_e)
                total = jnp.sum(exponent, axis=0, keepdims=True)
                hot = spots == targets_ref[group : group + 1, columns]
                chosen = jnp.sum(jnp.where(hot, shifted, 0.0), axis=0, keepdims=True)
                loss = loss + counted * (jnp.log(total) - chosen)
                chance = exponent * (1.0 / total)
                slope = (chance - jnp.where(hot, 1.0, 0.0)) * counted
                dlogits_ref[group * CLASSES : (group + 1) * CLASSES, columns] = slope.astype(
                    jnp.bfloat16
                )
    loss_ref[...] = jnp.sum(loss, axis=1, keepdims=True)
    sum_ref[:, 2 * FF :] = dot_nt(final_ref[...].T, dlogits_ref[...])
    dfinal = dot_nn(head_ref[...], dlogits_ref[...]).T
    last = last_ref[...]
    dlast, gain_part = rms_back(last, inverse_rms(last), gain_final, dfinal)
    gain_ref[1:2, :] = gain_part
    last_ref[...] = dlast
    gain_sum = jnp.zeros((1, D), jnp.float32)
    for block in range(tokens // ROWS):
        rows = slice(block * ROWS, (block + 1) * ROWS)
        upstream = last_ref[rows, :]
        dout = upstream.astype(jnp.bfloat16)
        dout_ref[rows, :] = dout
        for part in range(FF // D):
            columns = slice(part * D, (part + 1) * D)
            dact = dot_nn(dout, weight_ref[:, FF + part * D : FF + (part + 1) * D])
            dinner_ref[rows, columns] = (dact * slope_ref[rows, columns]).astype(jnp.bfloat16)
        dnormed = dot_nt(dinner_ref[rows, :], weight_ref[:, 0:FF])
        middle = middle_ref[rows, :]
        through, gain_part = rms_back(middle, inverse_rms(middle), gain_ffn, dnormed)
        gain_sum = gain_sum + gain_part
        dmiddle_ref[rows, :] = upstream + through
    gain_ref[0:1, :] = gain_sum
    sum_ref[:, 0:FF] = dot_nn(normed_ref[...].T, dinner_ref[...])
    sum_ref[:, FF : 2 * FF] = dot_nn(dout_ref[...].T, inner_ref[...])
    write_blocks(send_ref, keep_ref, sum_ref, core_ref[0], widths, mesh_plan)


def block_outs(own, widths):
    shape = jax.ShapeDtypeStruct
    blocks = own.shape[:2] + (sum(widths),)
    return [shape(blocks, jnp.bfloat16), shape(blocks, jnp.float32)]


def run_top(widths, mesh_plan, start, middle, own, other, targets, counted, gains, core):
    tokens = middle.shape[0]
    f32, b16 = jnp.float32, jnp.bfloat16
    shape = jax.ShapeDtypeStruct
    vmem = pl.BlockSpec(memory_space=pltpu.VMEM)
    return pl.pallas_call(
        functools.partial(top_kernel, widths, mesh_plan, start),
        in_specs=[vmem] * 6 + [smem_spec()],
        out_specs=[vmem] * 5,
        out_shape=[shape((tokens, D), f32)]
        + block_outs(own, widths)
        + [shape((2, D), f32), shape((1, 1), f32)],
        scratch_shapes=[
            pltpu.VMEM((D, 2 * FF), b16),
            pltpu.VMEM((D, VOCAB), b16),
            pltpu.VMEM((VOCAB, D), b16),
            pltpu.VMEM((tokens, D), b16),
            pltpu.VMEM((VOCAB, tokens), b16),
            pltpu.VMEM((tokens, D), b16),
            pltpu.VMEM((tokens, FF), b16),
            pltpu.VMEM((tokens, FF), f32),
            pltpu.VMEM((tokens, FF), b16),
            pltpu.VMEM((tokens, D), b16),
            pltpu.VMEM((tokens, D), f32),
            pltpu.VMEM((D, 2 * FF + VOCAB), f32),
        ],
        compiler_params=pltpu.CompilerParams(vmem_limit_bytes=VMEM_BYTES),
        cost_estimate=pl.CostEstimate(
            flops=6 * tokens * D * 3 * FF,
            bytes_accessed=tokens * D * 8 + D * 3 * FF * 10,
            transcendentals=tokens * (FF + VOCAB),
        ),
        name="loss_part",
    )(middle, own, other, targets, counted, gains, core)


def backward_kernel(layer, widths, mesh_plan, *refs):
    entry_ref, qkv_ref, mix_ref, lse_ref, dmiddle_ref, att_ref = refs[:6]
    gains_ref, valid_ref, core_ref = refs[6:9]
    if layer == 0:
        latent_ref, send_ref, keep_ref, gain_ref, bias_ref = refs[9:14]
        att_kept, before_kept, sum_ref = refs[14:18], refs[18:20], refs[20]
    else:
        before_ref, ffn_ref, out_ref, send_ref, keep_ref, gain_ref, bias_ref = refs[9:16]
        att_kept, before_kept, sum_ref = refs[16:20], refs[20:24], refs[24]
    step = pl.program_id(0)

    def here(start, length, unit=CTX):
        base = step * (GROUP * unit)
        return pl.ds(pl.multiple_of(base + start, 16), length)

    @pl.when(step == 0)
    def _():
        fill_bias(bias_ref)
        gain_ref[...] = jnp.zeros_like(gain_ref)

    dentry, gain_part = attend_back(
        step,
        here,
        (entry_ref[...], qkv_ref, mix_ref, lse_ref),
        dmiddle_ref[...],
        gains_ref[layer : layer + 1, :],
        att_ref,
        valid_ref,
        bias_ref,
        head_masks(),
        att_kept,
        GROUP // 2 if layer == 1 else GROUP,
    )
    gain_ref[0:1, :] += gain_part
    if layer == 0:
        before_kept[0][here(0, ROWS), :] = dentry.astype(jnp.bfloat16)
        before_kept[1][here(0, ROWS), :] = one_hot_rows(latent_ref[...])
    else:
        dbefore, gain_part = feed_back(
            here,
            dentry,
            before_ref[...],
            gains_ref[LAYERS + layer - 1 : LAYERS + layer, :],
            ffn_ref,
            before_kept,
            layer == 1,
        )
        out_ref[...] = dbefore
        gain_ref[1:2, :] += gain_part

    @pl.when(step == pl.num_programs(0) - 1)
    def _():
        normed_ref, dattend_ref, dqkv_ref, mixes_ref = att_kept
        att = [(normed_ref, dqkv_ref), (mixes_ref, dattend_ref)]
        if layer == 0:
            pairs = att + [(before_kept[0], before_kept[1])]
        else:
            normed_two_ref, inner_ref, dinner_ref, dout_ref = before_kept
            pairs = [(normed_two_ref, dinner_ref), (dout_ref, inner_ref)] + att
        column = 0
        for left, right in pairs:
            wide = right.shape[1]
            sum_ref[:, column : column + wide] = dot_nn(left[...].T, right[...])
            column += wide
        write_blocks(send_ref, keep_ref, sum_ref, core_ref[0], widths, mesh_plan)


def run_backward(layer, widths, mesh_plan, blocks_like, saved, dmiddle, gains, valid, core, before):
    entry, _, qkv, mix, lse, weights = saved[:6]
    tokens = entry.shape[0]
    queries = lse.shape[2] // HEADS
    short = tokens // CTX * queries
    f32, b16 = jnp.float32, jnp.bfloat16
    shape = jax.ShapeDtypeStruct
    in_specs = [
        row_spec(D),
        row_spec(3 * D),
        row_spec(D, GROUP * queries),
        lse_spec(queries),
        row_spec(D, GROUP * queries),
        whole_spec(weights.shape),
        whole_spec(gains.shape),
        smem_spec(),
        smem_spec(),
    ]
    operands = [entry, qkv, mix, lse, dmiddle, weights, gains, valid, core]
    blocks = block_outs(blocks_like, widths)
    outs = [(item, whole_spec(item.shape)) for item in blocks]
    outs.append((shape((2, D), f32), whole_spec((2, D))))
    scratch = [
        pltpu.VMEM((2, CTX, HEADS * queries), f32),
        pltpu.VMEM((tokens, D), b16),
        pltpu.VMEM((short, D), b16),
        pltpu.VMEM((tokens, 3 * D), b16),
        pltpu.VMEM((short, D), b16),
    ]
    if layer == 0:
        in_specs.append(row_spec(CATS))
        operands.append(before)
        scratch = scratch + [pltpu.VMEM((tokens, D), b16), pltpu.VMEM((tokens, VOCAB), b16)]
        wide = 4 * D + VOCAB
    else:
        in_specs = in_specs + [row_spec(D), whole_spec(before[1].shape)]
        operands = operands + list(before)
        outs.insert(0, (shape((tokens, D), f32), row_spec(D)))
        scratch = scratch + [
            pltpu.VMEM((tokens, D), b16),
            pltpu.VMEM((tokens, FF), b16),
            pltpu.VMEM((tokens, FF), b16),
            pltpu.VMEM((tokens, D), b16),
        ]
        wide = 4 * D + 2 * FF
    return pl.pallas_call(
        functools.partial(backward_kernel, layer, widths, mesh_plan),
        grid=(tokens // ROWS,),
        in_specs=in_specs,
        out_specs=[spec for _, spec in outs],
        out_shape=[item for item, _ in outs],
        scratch_shapes=scratch + [pltpu.VMEM((D, wide), f32)],
        compiler_params=pltpu.CompilerParams(vmem_limit_bytes=VMEM_BYTES),
        cost_estimate=pl.CostEstimate(
            flops=6 * tokens * D * wide,
            bytes_accessed=tokens * D * 24 + D * wide * 6,
            transcendentals=tokens * (FF + HEADS * CTX),
        ),
        name="backward_part",
    )(*operands)


def matrix_plan(widths):
    order = [
        (2, 2), (3, 2), (5, 0), (2, 1), (3, 1), (0, 2), (1, 2),
        (2, 0), (3, 0), (0, 1), (1, 1), (0, 0), (1, 0), (4, 0),
    ]
    plan, column = {}, 0
    for which, layer in order:
        plan[(which, layer)] = (column, widths[which])
        column += widths[which]
    return plan, column


def matrix_list():
    return [(which, layer) for which in range(4) for layer in range(LAYERS)] + [(4, 0), (5, 0)]


MATRICES = 4 * LAYERS + 2
LANES = 128
INNER_ROWS = 16
COMMON_ROWS = 16
ROW_IS_INNER = [True, True, True, False, False, True]


def master_of(masters, which, layer):
    if which == 1:
        return masters[1][layer].T
    return masters[which][layer] if which < 4 else masters[which][...]


def old_row(refs, which, layer):
    return refs[which][layer : layer + 1, :] if which < 4 else refs[which][...]


def stats_kernel(widths, *refs):
    raw_early, raw_late, masters, row_refs = refs[0], refs[1], refs[2:8], refs[8:14]
    gains_at, loss_ref, counted_ref, packet_ref = refs[14:18], refs[18], refs[19], refs[20]
    plan, total = matrix_plan(widths)
    square = jnp.concatenate([raw_early[...] * raw_early[...], raw_late[...] * raw_late[...]], axis=1)
    rows = square.shape[0]
    one = lambda value: jnp.sum(jnp.sum(value, axis=1, keepdims=True), axis=0, keepdims=True)
    inner, weights, entries, row_sums = [], [], [], []
    for which, layer in matrix_list():
        column, width = plan[(which, layer)]
        inner.append(jnp.sum(square[:, column : column + width], axis=1, keepdims=True))
        entries.append(jnp.sum(inner[-1], axis=0, keepdims=True))
        master = master_of(masters, which, layer)
        weights.append(one(master * master))
        row_sums.append(one(old_row(row_refs, which, layer)))
    packet_ref[...] = jnp.zeros_like(packet_ref)
    inner.append(jnp.zeros((rows, LANES - MATRICES), jnp.float32))
    packet_ref[0:INNER_ROWS, 0:rows] = jnp.concatenate(inner, axis=1).T[0:INNER_ROWS, :]
    top, two, one_at, zero = [ref[...] for ref in gains_at]
    gain = jnp.concatenate(
        [zero[0:1], one_at[0:1], two[0:1], one_at[1:2], two[1:2], top[0:1], top[1:2]], axis=0
    )
    scalars = [loss_ref[...], one(counted_ref[...])] + weights + entries + row_sums
    scalars.append(jnp.zeros((1, LANES - len(scalars)), jnp.float32))
    at = INNER_ROWS
    packet_ref[at : at + 7, :] = gain[:, 0:LANES]
    packet_ref[at + 7 : at + 8, :] = jnp.concatenate(scalars, axis=1)
    packet_ref[at + 8 : at + 15, :] = gain[:, LANES:]
    outer = jnp.sum(square, axis=0, keepdims=True)
    at = INNER_ROWS + COMMON_ROWS
    for row, start in enumerate(range(0, total, LANES)):
        stop = min(start + LANES, total)
        packet_ref[at + row : at + row + 1, 0 : stop - start] = outer[:, start:stop]


def outer_rows(widths):
    _, total = matrix_plan(widths)
    return -(-total // (8 * LANES)) * 8


def run_stats(widths, raw_early, raw_late, masters, rows, gain_parts, loss, counted):
    vmem = pl.BlockSpec(memory_space=pltpu.VMEM)
    operands = [raw_early, raw_late] + masters + rows + gain_parts + [loss, counted]
    packet = (INNER_ROWS + COMMON_ROWS + outer_rows(widths), LANES)
    return pl.pallas_call(
        functools.partial(stats_kernel, widths),
        in_specs=[vmem] * len(operands),
        out_specs=vmem,
        out_shape=jax.ShapeDtypeStruct(packet, jnp.float32),
        name="statistics",
    )(*operands)


def update_kernel(widths, sizes, *refs):
    across_ref, along_ref, raw_early, raw_late = refs[:4]
    masters, inner_refs, outer_refs = refs[4:10], refs[10:16], refs[16:22]
    gains_ref, second_ref = refs[22:24]
    outs = refs[24:]
    outer_count, inner_count = sizes
    plan, total = matrix_plan(widths)
    rows = raw_early.shape[0]
    scalars = along_ref[7:8, :]
    pick = lambda at: scalars[:, at : at + 1]
    gain_sum = jnp.concatenate([along_ref[0:7, :], along_ref[8:15, :]], axis=1)
    gain_square = jnp.sum(jnp.sum(gain_sum * gain_sum, axis=1, keepdims=True), axis=0, keepdims=True)
    square_total = gain_square
    for at in range(MATRICES):
        square_total = square_total + pick(2 + MATRICES + at)
    count_total = pick(1)
    norm_value = jnp.sqrt(square_total) / count_total
    scaling = jnp.minimum(1.0, clip_limit / norm_value) / count_total
    square_scale = scaling * scaling
    outer_total = jnp.concatenate(
        [
            along_ref[COMMON_ROWS + row : COMMON_ROWS + row + 1, 0 : min(LANES, total - row * LANES)]
            for row in range(-(-total // LANES))
        ],
        axis=1,
    )
    inner_new = []
    for at, (which, layer) in enumerate(matrix_list()):
        outer_length = widths[which] * outer_count
        inner_new.append(
            decay_two * old_row(inner_refs, which, layer)
            + (1 - decay_two)
            * (square_scale * across_ref[at : at + 1, 0:rows] / outer_length + tiny_term)
        )
    stacked = jnp.concatenate(inner_new, axis=0)
    stacked = jnp.concatenate([stacked, jnp.ones((LANES - MATRICES, rows), jnp.float32)], axis=0)
    if rows < LANES:
        stacked = jnp.concatenate([stacked, jnp.ones((LANES, LANES - rows), jnp.float32)], axis=1)
    turned = lax.rsqrt(stacked).T
    outs[0][...] = pick(0)
    outs[1][...] = count_total
    outs[2][...] = norm_value
    first_out = {4: 3, 0: 7, 1: 11, 2: 15, 3: 19, 5: 23}
    for at, (which, layer) in enumerate(matrix_list()):
        column, width = plan[(which, layer)]
        outer_length, inner_length = width * outer_count, rows * inner_count
        row_length = inner_length if ROW_IS_INNER[which] else outer_length
        copies = outer_count if ROW_IS_INNER[which] else inner_count
        entries = outer_length * inner_length
        early = raw_early.shape[1]
        if column < early:
            raw = raw_early[:, column : column + width]
        else:
            raw = raw_late[:, column - early : column - early + width]
        outer_new = decay_two * old_row(outer_refs, which, layer) + (1 - decay_two) * (
            square_scale * outer_total[:, column : column + width] / inner_length + tiny_term
        )
        mean_rows = decay_two * (pick(2 + 2 * MATRICES + at) / (copies * row_length)) + (
            1 - decay_two
        ) * (square_scale * pick(2 + MATRICES + at) / entries + tiny_term)
        factor = step_rate * jnp.sqrt(pick(2 + at) / entries) * jnp.sqrt(mean_rows)
        grad = raw * scaling
        updated = master_of(masters, which, layer) - grad * (
            turned[0:rows, at : at + 1] * (factor * lax.rsqrt(outer_new))
        )
        first = first_out[which]
        row_new, column_new = (
            (inner_new[at], outer_new) if ROW_IS_INNER[which] else (outer_new, inner_new[at])
        )
        if which < 4:
            if which == 1:
                updated, grad = updated.T, grad.T
            outs[first][layer] = updated
            outs[first + 1][layer] = grad
            outs[first + 2][layer : layer + 1, :] = row_new
            outs[first + 3][layer : layer + 1, :] = column_new
        else:
            outs[first][...] = updated
            outs[first + 1][...] = grad
            outs[first + 2][...] = row_new
            outs[first + 3][...] = column_new
    gain_grad = gain_sum * scaling
    second_new = decay_two * second_ref[...] + (1 - decay_two) * (gain_grad * gain_grad + tiny_term)
    gains = gains_ref[...]
    spread = jnp.sqrt(jnp.mean(gains * gains, axis=-1, keepdims=True))
    outs[27][...] = gains - step_rate * spread * gain_grad * lax.rsqrt(second_new)
    outs[28][...] = gain_grad
    outs[29][...] = second_new


def run_update(widths, sizes, across, along, raw_early, raw_late, masters, inner, outer, gains, second):
    vmem = pl.BlockSpec(memory_space=pltpu.VMEM)
    operands = [across, along, raw_early, raw_late] + masters + inner + outer + [gains, second]
    shapes = [(1, 1)] * 3
    for which in [4, 0, 1, 2, 3, 5]:
        shapes = shapes + [masters[which].shape] * 2
        pair = [inner[which].shape, outer[which].shape]
        shapes = shapes + (pair if ROW_IS_INNER[which] else pair[::-1])
    shapes = shapes + [gains.shape] * 3
    return pl.pallas_call(
        functools.partial(update_kernel, widths, sizes),
        in_specs=[vmem] * len(operands),
        out_specs=[vmem] * len(shapes),
        out_shape=[jax.ShapeDtypeStruct(item, jnp.float32) for item in shapes],
        name="update",
    )(*operands)


def swap(value, mask):
    count = lax.axis_size("dp") * lax.axis_size("fsdp")
    return lax.ppermute(value, ("dp", "fsdp"), [(place, place ^ mask) for place in range(count)])


def device_index():
    return lax.axis_index("dp") * lax.axis_size("fsdp") + lax.axis_index("fsdp")


def step_masks(step):
    masks = []
    for digit in range(1, 1 << len(step)):
        masks.append(sum(1 << bit for at, bit in enumerate(step[::-1]) if (digit >> at) & 1))
    return masks


def tie(*values):
    return lax.optimization_barrier(values)


class Gather:
    def __init__(self, piece, steps):
        self.held, self.steps, self.at = piece[None], steps, 0

    def send(self):
        self.others = tuple(swap(self.held, mask) for mask in step_masks(self.steps[self.at]))

    def join(self):
        step = self.steps[self.at]
        pieces = [self.held] + list(self.others)
        for at, bit in enumerate(step[::-1]):
            upper = (device_index() >> bit) & 1 == 1
            pieces = [
                jnp.where(upper, pieces[place ^ (1 << at)], pieces[place])
                for place in range(len(pieces))
            ]
        self.held = jnp.concatenate(pieces)
        self.at += 1


class Scatter:
    def __init__(self, sent, kept, steps):
        self.sent, self.kept, self.steps, self.at = (sent,), kept, steps, 0

    def send(self):
        masks = step_masks(self.steps[self.at])
        self.others = tuple(swap(sent, mask) for sent, mask in zip(self.sent, masks))

    def join(self):
        self.at += 1
        summed = self.kept
        for other in self.others:
            summed = summed + other.astype(jnp.float32)
        if self.at == len(self.steps):
            self.kept = summed
            return
        step = self.steps[self.at]
        count = 1 << len(step)
        own = 0
        for bit in step:
            own = 2 * own + ((device_index() >> bit) & 1)
        parts = summed.reshape((count, summed.shape[0] // count) + summed.shape[1:])
        if count == 2:
            self.sent = (jnp.where(own == 1, parts[0], parts[1]).astype(jnp.bfloat16),)
            self.kept = jnp.where(own == 1, parts[1], parts[0])
            return
        pick = lambda digit: lax.dynamic_index_in_dim(parts, own ^ digit, 0, keepdims=False)
        self.sent = tuple(pick(digit).astype(jnp.bfloat16) for digit in range(1, count))
        self.kept = pick(0)


def merged(parts):
    whole = Scatter(None, jnp.concatenate([part.kept for part in parts], axis=2), parts[0].steps)
    whole.sent = tuple(
        jnp.concatenate(pieces, axis=2) for pieces in zip(*[part.sent for part in parts])
    )
    whole.at = parts[0].at
    return whole


def shards(
    latents,
    targets,
    horizon,
    memory_valid,
    embed,
    qkv_weight,
    out_weight,
    up_weight,
    down_weight,
    head_weight,
    gains,
    embed_rows,
    embed_cols,
    qkv_rows,
    qkv_cols,
    out_rows,
    out_cols,
    up_rows,
    up_cols,
    down_rows,
    down_cols,
    head_rows,
    head_cols,
    gain_second,
):
    samples = latents.shape[0]
    sizes = (lax.axis_size("dp"), lax.axis_size("fsdp"))
    highest = (sizes[0] * sizes[1]).bit_length() - 1
    gather_steps = [(bit,) for bit in reversed(range(3, highest))] + [(2, 1), (0,)]
    scatter_steps = gather_steps[::-1]
    mesh_plan = (sizes[0], sizes[1], gather_steps)
    core = (lax.axis_index("fsdp") & 1).astype(jnp.int32).reshape(1)

    low = lambda item: item.astype(jnp.bfloat16)
    out_turned = jnp.swapaxes(out_weight, 1, 2)
    down_turned = jnp.swapaxes(down_weight, 1, 2)
    masters = [qkv_weight, out_turned, up_weight, down_turned, embed.T, head_weight]
    widths = [qkv_weight.shape[2], out_weight.shape[2], up_weight.shape[2], down_weight.shape[1]]
    widths = widths + [embed.shape[0], head_weight.shape[1]]
    att_parts = [[qkv_weight[at], out_weight[at]] for at in range(LAYERS)]
    ffn_parts = [[up_weight[at], down_turned[at]] for at in range(LAYERS)]
    pieces = [
        att_parts[0] + [embed.T],
        ffn_parts[0] + att_parts[1],
        ffn_parts[1] + att_parts[2] + ffn_parts[2] + [head_weight],
    ]
    att_widths, ffn_widths = widths[0:2], widths[2:4]
    first, second, third = [
        Gather(low(jnp.concatenate(piece, axis=1)), gather_steps) for piece in pieces
    ]
    chunk_widths = [
        att_widths + widths[4:5],
        ffn_widths + att_widths,
        ffn_widths + att_widths + ffn_widths + widths[5:6],
    ]

    latent_rows = low(latents).reshape(samples * CTX, CATS)
    target_rows = targets.transpose(2, 0, 1).reshape(CATS, samples * SEG)
    counted = jnp.arange(SEG, dtype=jnp.int32)[None, :] < horizon[:, None]
    counted = counted.astype(jnp.float32).reshape(1, samples * SEG)
    shared = (gains, memory_valid, core)

    count = len(gather_steps)
    for at in range(count - 1):
        active = [first, second] + ([third] if at >= 1 else [])
        held = tie(*[chunk.held for chunk in active])
        for chunk, value in zip(active, held):
            chunk.held = value
            chunk.send()
        for chunk in active:
            chunk.join()
    first.send()
    (other,) = first.others
    first.held, other, second.held, third.held = tie(first.held, other, second.held, third.held)
    second.send()
    third.send()
    kept = [run_forward(0, chunk_widths[0], mesh_plan, latent_rows, first.held, other, *shared)]
    middle, (other,), third.others = tie(kept[0][1], second.others, third.others)
    third.join()
    second.held, third.held = tie(second.held, third.held)
    third.send()
    kept.append(
        run_forward(1, chunk_widths[1], mesh_plan, middle, second.held, other, *shared)
    )
    middle, (other,) = tie(kept[1][1], third.others)
    kept.append(run_forward(2, chunk_widths[2], mesh_plan, middle, third.held, other, *shared))

    dmiddle, sent, held, gain_top, loss = run_top(
        ffn_widths + widths[5:6],
        mesh_plan,
        sum(ffn_widths + att_widths),
        kept[2][1],
        third.held,
        other,
        target_rows,
        counted,
        gains,
        core,
    )
    top = Scatter(sent, held, scatter_steps)
    top.send()
    like = first.held
    dmiddle, sent, held, gain_two = run_backward(
        2, chunk_widths[1], mesh_plan, like, kept[2], dmiddle, *shared, (kept[1][1], kept[2][6])
    )
    dmiddle, top.others = tie(dmiddle, top.others)
    top.join()
    two = Scatter(sent, held, scatter_steps)
    dmiddle, top.sent = tie(dmiddle, top.sent)
    top.send()
    two.send()
    dmiddle, sent, held, gain_one = run_backward(
        1, chunk_widths[1], mesh_plan, like, kept[1], dmiddle, *shared, (kept[0][1], kept[1][6])
    )
    dmiddle, top.others, two.others = tie(dmiddle, top.others, two.others)
    top.join()
    two.join()
    one = Scatter(sent, held, scatter_steps)
    dmiddle, top.sent, two.sent = tie(dmiddle, top.sent, two.sent)
    two.send()
    one.send()
    sent, held, gain_zero = run_backward(
        0, chunk_widths[0], mesh_plan, like, kept[0], dmiddle, *shared, latent_rows
    )
    sent, two.others, one.others = tie(sent, two.others, one.others)
    zero = Scatter(sent, held, scatter_steps)
    zero.send()
    one.join()
    one.send()
    two.join()
    zero.join()
    one.others, zero.sent = tie(one.others, zero.sent)
    zero.send()
    one.join()
    early = merged([top, two, one])
    early.send()
    while early.at < count:
        zero.others, early.sent = tie(zero.others, early.sent)
        zero.join()
        zero.send()
        early.others, zero.sent = tie(early.others, zero.sent)
        early.join()
        if early.at < count:
            early.send()
    while zero.at < count:
        zero.join()
        if zero.at < count:
            zero.send()
    raw_early, raw_late = early.kept[0], zero.kept[0]

    flat = lambda item: item if item.ndim == 2 else item.reshape(1, -1)
    inner = [flat(item) for item in (qkv_rows, out_rows, up_rows, down_cols, embed_cols, head_rows)]
    outer = [flat(item) for item in (qkv_cols, out_cols, up_cols, down_rows, embed_rows, head_cols)]
    row_stats = [inner[at] if ROW_IS_INNER[at] else outer[at] for at in range(6)]
    gain_parts = [gain_top, gain_two, gain_one, gain_zero]
    packet = run_stats(widths, raw_early, raw_late, masters, row_stats, gain_parts, loss, counted)
    edge = INNER_ROWS + COMMON_ROWS
    across = packet[:edge]
    inner_bits = sizes[1].bit_length() - 1
    for bit in range(inner_bits, highest):
        across = across + swap(across, 1 << bit)
    along = jnp.concatenate([across[INNER_ROWS:], packet[edge:]])
    for bit in reversed(range(inner_bits)):
        along = along + swap(along, 1 << bit)
    results = run_update(
        widths, sizes, across, along, raw_early, raw_late, masters, inner, outer, gains, gain_second
    )
    results = list(results)
    for at in range(3):
        results[at] = results[at].reshape(())
    for at in (3, 4, 11, 12, 19, 20):
        results[at] = jnp.swapaxes(results[at], -1, -2)
    for at in (5, 6, 25, 26):
        results[at] = results[at].reshape(-1)
    return tuple(results)


def solution(mesh):
    return jax.shard_map(
        shards,
        mesh=mesh,
        in_specs=(
            P(("dp", "fsdp"), None, None),
            P(("dp", "fsdp"), None, None),
            P(("dp", "fsdp")),
            P(("dp", "fsdp")),
            P("dp", "fsdp"),
            P(None, "fsdp", "dp"),
            P(None, "fsdp", "dp"),
            P(None, "fsdp", "dp"),
            P(None, "dp", "fsdp"),
            P("fsdp", "dp"),
            P(),
            P("dp"),
            P("fsdp"),
            P(None, "fsdp"),
            P(None, "dp"),
            P(None, "fsdp"),
            P(None, "dp"),
            P(None, "fsdp"),
            P(None, "dp"),
            P(None, "dp"),
            P(None, "fsdp"),
            P("fsdp"),
            P("dp"),
            P(),
        ),
        out_specs=(
            P(),
            P(),
            P(),
            P("dp", "fsdp"),
            P("dp", "fsdp"),
            P("dp"),
            P("fsdp"),
            P(None, "fsdp", "dp"),
            P(None, "fsdp", "dp"),
            P(None, "fsdp"),
            P(None, "dp"),
            P(None, "fsdp", "dp"),
            P(None, "fsdp", "dp"),
            P(None, "fsdp"),
            P(None, "dp"),
            P(None, "fsdp", "dp"),
            P(None, "fsdp", "dp"),
            P(None, "fsdp"),
            P(None, "dp"),
            P(None, "dp", "fsdp"),
            P(None, "dp", "fsdp"),
            P(None, "dp"),
            P(None, "fsdp"),
            P("fsdp", "dp"),
            P("fsdp", "dp"),
            P("fsdp"),
            P("dp"),
            P(),
            P(),
            P(),
        ),
        check_vma=False,
    )
```

```python
import functools

import jax
import jax.numpy as jnp
from jax import lax
from jax.experimental import pallas as pl
from jax.experimental.pallas import tpu as pltpu
from jax.sharding import PartitionSpec as P

D = 256
HEADS = 8
HEAD = D // HEADS
FF = 1024
CATS = 32
CLASSES = 32
LAYERS = 3
SEG = 48
MEM = 48
CTX = 96
VOCAB = 1024
GROUP = 4
ROWS = GROUP * CTX
HALF = D // 2
VMEM_BYTES = 56 * 1024 * 1024

decay_two = 0.9
step_rate = 0.3
clip_limit = 0.05
tiny_term = 1e-30
norm_eps = 1e-06
masked_score = -1e30
log2_e = 1.4426950408889634
score_scale = HEAD ** (-0.5)
gelu_one = 0.7978845608028654
gelu_two = 0.044715


def dot_nn(left, right):
    return lax.dot_general(
        left, right, (((1,), (0,)), ((), ())), preferred_element_type=jnp.float32
    )


def dot_nt(left, right):
    return lax.dot_general(
        left, right, (((1,), (1,)), ((), ())), preferred_element_type=jnp.float32
    )


def dot_tn(left, right):
    return lax.dot_general(
        left, right, (((0,), (0,)), ((), ())), preferred_element_type=jnp.float32
    )


def inverse_rms(values):
    return lax.rsqrt(jnp.mean(values * values, axis=-1, keepdims=True) + norm_eps)


def rms_back(values, inverse, gain_row, upstream):
    normed = values * inverse
    scaled = upstream * gain_row
    inner = jnp.mean(scaled * normed, axis=-1, keepdims=True)
    return (
        inverse * (scaled - normed * inner),
        jnp.sum(upstream * normed, axis=0, keepdims=True),
    )


def head_masks():
    lane = lax.broadcasted_iota(jnp.int32, (1, D // 2), 1) // HEAD
    return [lane == head for head in range(HEADS // 2)]


def expand_heads(rows, masks):
    return jnp.concatenate([rows * mask.astype(rows.dtype) for mask in masks], axis=0)


def collapse_heads(spread, rows, masks):
    product = dot_tn(spread, rows)
    queries = product.shape[0] // len(masks)
    taken = product[(len(masks) - 1) * queries :]
    for at, mask in enumerate(masks[:-1]):
        taken = jnp.where(mask, product[at * queries : (at + 1) * queries], taken)
    return taken


def half_of(part, side):
    start = part * D + side * HALF
    return slice(start, start + HALF)


def fill_bias(bias_ref):
    spread = bias_ref.shape[2]
    queries = spread // (HEADS // 2)
    key_at = lax.broadcasted_iota(jnp.int32, (CTX, spread), 0)
    query_at = lax.broadcasted_iota(jnp.int32, (CTX, spread), 1) % queries + (CTX - queries)
    later = key_at > query_at
    crosses = (query_at >= MEM) & (key_at < MEM)
    bias_ref[0] = jnp.where(later | crosses, masked_score, 0.0)
    bias_ref[1] = jnp.where(later, masked_score, 0.0)


def block_place(device, steps):
    place, weight = 0, 1
    for step in steps[:-1]:
        digit = 0
        for bit in step:
            digit = 2 * digit + ((device >> bit) & 1)
        place += digit * weight
        weight <<= len(step)
    return place


def place_weights(targets, own_ref, other_ref, core, widths, mesh_plan, start=0):
    outer_count, inner_count, steps = mesh_plan
    rows = own_ref.shape[1]
    for high in range(inner_count // 2):
        for source, side in ((own_ref, core), (other_ref, 1 - core)):
            here = pl.ds(pl.multiple_of((2 * high + side) * rows, rows), rows)
            at = start
            for (target, column), width in zip(targets, widths):
                block = [
                    source[
                        block_place(outer * inner_count + 2 * high, steps), :, at : at + width
                    ]
                    for outer in range(outer_count)
                ]
                target[here, column : column + width * outer_count] = jnp.concatenate(
                    block, axis=1
                )
                at += width


def write_blocks(send_ref, keep_ref, sum_ref, core, widths, mesh_plan):
    outer_count, inner_count, steps = mesh_plan
    rows = keep_ref.shape[1]
    for high in range(inner_count // 2):
        for target, side in ((keep_ref, core), (send_ref, 1 - core)):
            here = pl.ds(pl.multiple_of((2 * high + side) * rows, rows), rows)
            taken = sum_ref[here, :]
            for outer in range(outer_count):
                block, column = [], 0
                for width in widths:
                    block.append(taken[:, column + outer * width : column + (outer + 1) * width])
                    column += width * outer_count
                target[block_place(outer * inner_count + 2 * high, steps)] = jnp.concatenate(
                    block, axis=1
                ).astype(target.dtype)


def one_hot_rows(latent_rows):
    spot = lax.broadcasted_iota(jnp.int32, (CATS, VOCAB), 1) // CLASSES
    group = lax.broadcasted_iota(jnp.int32, (CATS, VOCAB), 0)
    spreader = jnp.where(spot == group, 1.0, 0.0).astype(jnp.bfloat16)
    classes = (lax.broadcasted_iota(jnp.int32, (1, VOCAB), 1) % CLASSES).astype(jnp.float32)
    drawn = dot_nn(latent_rows, spreader)
    return jnp.where(drawn == classes, 1.0, 0.0).astype(jnp.bfloat16)


def tail_rows(values, queries):
    if queries == CTX:
        return values
    return jnp.concatenate(
        [
            values[(sample + 1) * CTX - queries : (sample + 1) * CTX]
            for sample in range(values.shape[0] // CTX)
        ],
        axis=0,
    )


def attend_forward(step, hidden, gain_row, weight_ref, valid_ref, bias_ref, masks, refs):
    middle_ref, qkv_ref, mix_ref, chance_ref = refs
    queries = chance_ref.shape[3] // (HEADS // 2)
    normed = (hidden * inverse_rms(hidden) * gain_row).astype(jnp.bfloat16)
    qkv_ref[...] = dot_nn(normed, weight_ref[:, 0 : 3 * D]).astype(jnp.bfloat16)
    units = [(sample, side) for sample in range(GROUP) for side in range(2)]
    scores = []
    for sample, side in units:
        rows = slice(sample * CTX, (sample + 1) * CTX)
        tail = slice((sample + 1) * CTX - queries, (sample + 1) * CTX)
        spread = expand_heads(qkv_ref[tail, half_of(0, side)], masks)
        scores.append(dot_nt(qkv_ref[rows, half_of(1, side)], spread))
    for (sample, side), score in zip(units, scores):
        score = score + bias_ref[valid_ref[step * GROUP + sample]]
        peak = jnp.max(score, axis=0, keepdims=True)
        exponent = jnp.exp2((score - peak) * (score_scale * log2_e))
        total = jnp.sum(exponent, axis=0, keepdims=True)
        chance_ref[sample, side] = (exponent * (1.0 / total)).astype(jnp.bfloat16)
    for sample, side in units:
        rows = slice(sample * CTX, (sample + 1) * CTX)
        mix_ref[sample * queries : (sample + 1) * queries, half_of(0, side)] = collapse_heads(
            chance_ref[sample, side], qkv_ref[rows, half_of(2, side)], masks
        ).astype(jnp.bfloat16)
    middle_ref[...] = tail_rows(hidden, queries) + dot_nn(
        mix_ref[...], weight_ref[:, 3 * D : 4 * D]
    )


def gelu_bend(value, square):
    return jnp.tanh(value * (gelu_one + (gelu_one * gelu_two) * square))


def gelu_slope(half_value, bend, square):
    return (0.5 + 0.5 * bend) + (half_value * (1.0 - bend * bend)) * (
        gelu_one + (3.0 * gelu_one * gelu_two) * square
    )


def feed_forward(middle, gain_row, weight_ref, inner_ref, slope_ref):
    normed = (middle * inverse_rms(middle) * gain_row).astype(jnp.bfloat16)
    for part in range(FF // D):
        columns = slice(part * D, (part + 1) * D)
        inner = dot_nn(normed, weight_ref[:, columns])
        for sample in range(GROUP):
            rows = slice(sample * CTX, (sample + 1) * CTX)
            value = inner[rows]
            square = value * value
            bend = gelu_bend(value, square)
            half_value = 0.5 * value
            inner_ref[rows, columns] = (half_value * (1.0 + bend)).astype(jnp.bfloat16)
            slope_ref[rows, columns] = gelu_slope(half_value, bend, square).astype(jnp.bfloat16)
    return middle + dot_nt(inner_ref[...], weight_ref[:, FF : 2 * FF])


def feed_back(here, upstream, middle, gain_row, weight_ref, slope_ref, refs):
    normed_ref, dinner_ref, dout_ref = refs
    dout = upstream.astype(jnp.bfloat16)
    dout_ref[here(0, ROWS), :] = dout
    inverse = inverse_rms(middle)
    normed_ref[here(0, ROWS), :] = (middle * inverse * gain_row).astype(jnp.bfloat16)
    for part in range(FF // D):
        columns = slice(part * D, (part + 1) * D)
        dact = dot_nn(dout, weight_ref[:, FF + part * D : FF + (part + 1) * D])
        dinner_ref[here(0, ROWS), columns] = (
            dact * slope_ref[:, columns].astype(jnp.float32)
        ).astype(jnp.bfloat16)
    dnormed = dot_nt(dinner_ref[here(0, ROWS), :], weight_ref[:, 0:FF])
    through, gain_part = rms_back(middle, inverse, gain_row, dnormed)
    return upstream + through, gain_part


def attend_back(step, here, saved, dmiddle, gain_row, weight_ref, masks, refs):
    hidden, qkv_ref, mix_ref, chance_ref = saved
    normed_ref, dmiddle_ref, dqkv_ref, mixes_ref = refs
    queries = chance_ref.shape[3] // (HEADS // 2)
    short = here(0, GROUP * queries, queries)
    dattend = dmiddle.astype(jnp.bfloat16)
    dmiddle_ref[short, :] = dattend
    mixes_ref[short, :] = mix_ref[...]
    dmix = dot_nt(dattend, weight_ref[:, 3 * D : 4 * D]).astype(jnp.bfloat16)
    units = [(sample, side) for sample in range(GROUP) for side in range(2)]
    slopes, dchances, dscores = [], [], []
    for sample, side in units:
        rows = slice(sample * CTX, (sample + 1) * CTX)
        slopes.append(
            expand_heads(
                dmix[sample * queries : (sample + 1) * queries, half_of(0, side)], masks
            )
        )
        dchances.append(dot_nt(qkv_ref[rows, half_of(2, side)], slopes[-1]))
    for (sample, side), dchance in zip(units, dchances):
        chance = chance_ref[sample, side].astype(jnp.float32)
        weighed = chance * dchance
        dscores.append(
            (weighed - chance * jnp.sum(weighed, axis=0, keepdims=True)).astype(jnp.bfloat16)
        )
    for at, (sample, side) in enumerate(units):
        rows = slice(sample * CTX, (sample + 1) * CTX)
        tail = slice((sample + 1) * CTX - queries, (sample + 1) * CTX)
        there = here(sample * CTX, CTX)
        spread = expand_heads(qkv_ref[tail, half_of(0, side)], masks)
        keys = qkv_ref[rows, half_of(1, side)]
        dvalues = dot_nn(chance_ref[sample, side], slopes[at])
        dkeys = dot_nn(dscores[at], spread) * score_scale
        dqueries = (collapse_heads(dscores[at], keys, masks) * score_scale).astype(jnp.bfloat16)
        if queries < CTX:
            nothing = jnp.zeros((CTX - queries, HALF), jnp.bfloat16)
            dqueries = jnp.concatenate([nothing, dqueries], axis=0)
        dqkv_ref[there, half_of(0, side)] = dqueries
        dqkv_ref[there, half_of(1, side)] = dkeys.astype(jnp.bfloat16)
        dqkv_ref[there, half_of(2, side)] = dvalues.astype(jnp.bfloat16)
    inverse = inverse_rms(hidden)
    normed_ref[here(0, ROWS), :] = (hidden * inverse * gain_row).astype(jnp.bfloat16)
    dnormed = dot_nt(dqkv_ref[here(0, ROWS), :], weight_ref[:, 0 : 3 * D])
    through, gain_part = rms_back(hidden, inverse, gain_row, dnormed)
    if queries < CTX:
        nothing = jnp.zeros((CTX - queries, D), jnp.float32)
        pieces = []
        for sample in range(GROUP):
            pieces = pieces + [nothing, dmiddle[sample * queries : (sample + 1) * queries]]
        dmiddle = jnp.concatenate(pieces, axis=0)
    return dmiddle + through, gain_part


def row_spec(width, rows=ROWS):
    return pl.BlockSpec((rows, width), lambda step: (step, 0))


def chance_spec(queries):
    return pl.BlockSpec((GROUP, 2, CTX, HEADS // 2 * queries), lambda step: (step, 0, 0, 0))


def whole_spec(shape):
    return pl.BlockSpec(shape, lambda step: (0,) * len(shape))


def smem_spec():
    return pl.BlockSpec(memory_space=pltpu.SMEM)


def forward_kernel(layer, widths, mesh_plan, source_ref, own_ref, other_ref, gains_ref, valid_ref, core_ref, *refs):
    entry_ref, att_ref, before_ref = refs[0], refs[5], refs[6]
    bias_ref = refs[7] if layer == 0 else refs[9]
    step = pl.program_id(0)

    @pl.when(step == 0)
    def _():
        fill_bias(bias_ref)
        att = [(att_ref, 0), (att_ref, 3 * D)]
        before = [(before_ref, 0)] if layer == 0 else [(before_ref, 0), (before_ref, FF)]
        targets = att + before if layer == 0 else before + att
        place_weights(targets, own_ref, other_ref, core_ref[0], widths[: len(targets)], mesh_plan)

    if layer == 0:
        hidden = dot_nt(one_hot_rows(source_ref[...]), before_ref[...])
    else:
        gain_ffn = gains_ref[LAYERS + layer - 1 : LAYERS + layer, :]
        hidden = feed_forward(source_ref[...], gain_ffn, before_ref, refs[7], refs[8])
    entry_ref[...] = hidden
    attend_forward(
        step,
        hidden,
        gains_ref[layer : layer + 1, :],
        att_ref,
        valid_ref,
        bias_ref,
        head_masks(),
        refs[1:5],
    )


def run_forward(layer, widths, mesh_plan, source, own, other, gains, valid, core):
    tokens = source.shape[0]
    queries = SEG if layer == LAYERS - 1 else CTX
    f32, b16 = jnp.float32, jnp.bfloat16
    shape = jax.ShapeDtypeStruct
    short = tokens // CTX * queries
    outs = [
        (shape((tokens, D), f32), row_spec(D)),
        (shape((short, D), f32), row_spec(D, GROUP * queries)),
        (shape((tokens, 3 * D), b16), row_spec(3 * D)),
        (shape((short, D), b16), row_spec(D, GROUP * queries)),
        (shape((tokens // CTX, 2, CTX, HEADS // 2 * queries), b16), chance_spec(queries)),
        (shape((D, 4 * D), b16), whole_spec((D, 4 * D))),
    ]
    scratch = [pltpu.VMEM((2, CTX, HEADS // 2 * queries), f32)]
    if layer == 0:
        scratch = [pltpu.VMEM((D, VOCAB), b16)] + scratch
    else:
        outs.append((shape((D, 2 * FF), b16), whole_spec((D, 2 * FF))))
        outs = outs + [(shape((tokens, FF), b16), row_spec(FF))] * 2
    return pl.pallas_call(
        functools.partial(forward_kernel, layer, widths, mesh_plan),
        grid=(tokens // ROWS,),
        in_specs=[
            row_spec(source.shape[1]),
            whole_spec(own.shape),
            whole_spec(other.shape),
            whole_spec(gains.shape),
            smem_spec(),
            smem_spec(),
        ],
        out_specs=[spec for _, spec in outs],
        out_shape=[item for item, _ in outs],
        scratch_shapes=scratch,
        compiler_params=pltpu.CompilerParams(vmem_limit_bytes=VMEM_BYTES),
        cost_estimate=pl.CostEstimate(
            flops=2 * tokens * D * 12 * D,
            bytes_accessed=tokens * D * 16 + D * 12 * D * 4,
            transcendentals=tokens * (FF + HEADS * CTX),
        ),
        name="forward_part",
    )(source, own, other, gains, valid, core)


def top_kernel(widths, mesh_plan, start, middle_ref, own_ref, other_ref, targets_ref, counted_ref, gains_ref, core_ref, *refs):
    dmiddle_ref, send_ref, keep_ref, gain_ref, loss_ref = refs[:5]
    weight_ref, head_ref, turned_ref, final_ref, dlogits_ref = refs[5:10]
    normed_ref, inner_ref, slope_ref, dinner_ref, dout_ref, last_ref, sum_ref = refs[10:]
    tokens = middle_ref.shape[0]
    gain_final = gains_ref[2 * LAYERS : 2 * LAYERS + 1, :]
    gain_ffn = gains_ref[2 * LAYERS - 1 : 2 * LAYERS, :]
    place_weights(
        [(weight_ref, 0), (weight_ref, FF), (head_ref, 0)],
        own_ref,
        other_ref,
        core_ref[0],
        widths,
        mesh_plan,
        start,
    )
    turned_ref[...] = head_ref[...].T
    for block in range(tokens // ROWS):
        rows = slice(block * ROWS, (block + 1) * ROWS)
        middle = middle_ref[rows, :]
        normed = (middle * inverse_rms(middle) * gain_ffn).astype(jnp.bfloat16)
        normed_ref[rows, :] = normed
        for part in range(FF // D):
            columns = slice(part * D, (part + 1) * D)
            inner = dot_nn(normed, weight_ref[:, columns])
            for piece in range(GROUP):
                value = inner[piece * CTX : (piece + 1) * CTX]
                there = slice(block * ROWS + piece * CTX, block * ROWS + (piece + 1) * CTX)
                square = value * value
                bend = gelu_bend(value, square)
                half_value = 0.5 * value
                inner_ref[there, columns] = (half_value * (1.0 + bend)).astype(jnp.bfloat16)
                slope_ref[there, columns] = gelu_slope(half_value, bend, square)
        last = middle + dot_nt(inner_ref[rows, :], weight_ref[:, FF : 2 * FF])
        last_ref[rows, :] = last
        final_ref[rows, :] = (last * inverse_rms(last) * gain_final).astype(jnp.bfloat16)
    span = D
    loss = jnp.zeros((1, span), jnp.float32)
    spots = lax.broadcasted_iota(jnp.int32, (CLASSES, span), 0)
    for part in range(tokens // span):
        columns = slice(part * span, (part + 1) * span)
        counted = counted_ref[0:1, columns]
        final = final_ref[columns, :]
        for quarter in range(VOCAB // D):
            logits = dot_nt(turned_ref[quarter * D : (quarter + 1) * D, :], final)
            for inside in range(D // CLASSES):
                group = quarter * (D // CLASSES) + inside
                values = logits[inside * CLASSES : (inside + 1) * CLASSES]
                shifted = values - jnp.max(values, axis=0, keepdims=True)
                exponent = jnp.exp2(shifted * log2_e)
                total = jnp.sum(exponent, axis=0, keepdims=True)
                hot = spots == targets_ref[group : group + 1, columns]
                chosen = jnp.sum(jnp.where(hot, shifted, 0.0), axis=0, keepdims=True)
                loss = loss + counted * (jnp.log(total) - chosen)
                chance = exponent * (1.0 / total)
                slope = (chance - jnp.where(hot, 1.0, 0.0)) * counted
                dlogits_ref[group * CLASSES : (group + 1) * CLASSES, columns] = slope.astype(
                    jnp.bfloat16
                )
    loss_ref[...] = jnp.sum(loss, axis=1, keepdims=True)
    sum_ref[:, 2 * FF :] = dot_nt(final_ref[...].T, dlogits_ref[...])
    dfinal = dot_nn(head_ref[...], dlogits_ref[...]).T
    last = last_ref[...]
    dlast, gain_part = rms_back(last, inverse_rms(last), gain_final, dfinal)
    gain_ref[1:2, :] = gain_part
    last_ref[...] = dlast
    gain_sum = jnp.zeros((1, D), jnp.float32)
    for block in range(tokens // ROWS):
        rows = slice(block * ROWS, (block + 1) * ROWS)
        upstream = last_ref[rows, :]
        dout = upstream.astype(jnp.bfloat16)
        dout_ref[rows, :] = dout
        for part in range(FF // D):
            columns = slice(part * D, (part + 1) * D)
            dact = dot_nn(dout, weight_ref[:, FF + part * D : FF + (part + 1) * D])
            dinner_ref[rows, columns] = (dact * slope_ref[rows, columns]).astype(jnp.bfloat16)
        dnormed = dot_nt(dinner_ref[rows, :], weight_ref[:, 0:FF])
        middle = middle_ref[rows, :]
        through, gain_part = rms_back(middle, inverse_rms(middle), gain_ffn, dnormed)
        gain_sum = gain_sum + gain_part
        dmiddle_ref[rows, :] = upstream + through
    gain_ref[0:1, :] = gain_sum
    sum_ref[:, 0:FF] = dot_nn(normed_ref[...].T, dinner_ref[...])
    sum_ref[:, FF : 2 * FF] = dot_nn(dout_ref[...].T, inner_ref[...])
    write_blocks(send_ref, keep_ref, sum_ref, core_ref[0], widths, mesh_plan)


def block_outs(own, widths):
    shape = jax.ShapeDtypeStruct
    blocks = own.shape[:2] + (sum(widths),)
    return [shape(blocks, jnp.bfloat16), shape(blocks, jnp.float32)]


def run_top(widths, mesh_plan, start, middle, own, other, targets, counted, gains, core):
    tokens = middle.shape[0]
    f32, b16 = jnp.float32, jnp.bfloat16
    shape = jax.ShapeDtypeStruct
    vmem = pl.BlockSpec(memory_space=pltpu.VMEM)
    return pl.pallas_call(
        functools.partial(top_kernel, widths, mesh_plan, start),
        in_specs=[vmem] * 6 + [smem_spec()],
        out_specs=[vmem] * 5,
        out_shape=[shape((tokens, D), f32)]
        + block_outs(own, widths)
        + [shape((2, D), f32), shape((1, 1), f32)],
        scratch_shapes=[
            pltpu.VMEM((D, 2 * FF), b16),
            pltpu.VMEM((D, VOCAB), b16),
            pltpu.VMEM((VOCAB, D), b16),
            pltpu.VMEM((tokens, D), b16),
            pltpu.VMEM((VOCAB, tokens), b16),
            pltpu.VMEM((tokens, D), b16),
            pltpu.VMEM((tokens, FF), b16),
            pltpu.VMEM((tokens, FF), f32),
            pltpu.VMEM((tokens, FF), b16),
            pltpu.VMEM((tokens, D), b16),
            pltpu.VMEM((tokens, D), f32),
            pltpu.VMEM((D, 2 * FF + VOCAB), f32),
        ],
        compiler_params=pltpu.CompilerParams(vmem_limit_bytes=VMEM_BYTES),
        cost_estimate=pl.CostEstimate(
            flops=6 * tokens * D * 3 * FF,
            bytes_accessed=tokens * D * 8 + D * 3 * FF * 10,
            transcendentals=tokens * (FF + VOCAB),
        ),
        name="loss_part",
    )(middle, own, other, targets, counted, gains, core)


def backward_kernel(layer, widths, mesh_plan, *refs):
    entry_ref, qkv_ref, mix_ref, chance_ref, dmiddle_ref, att_ref, gains_ref, core_ref = refs[:8]
    if layer == 0:
        latent_ref, send_ref, keep_ref, gain_ref = refs[8:12]
        att_kept, before_kept, sum_ref = refs[12:16], refs[16:18], refs[18]
    else:
        before_ref, ffn_ref, slope_ref, inner_hbm, out_ref, send_ref, keep_ref, gain_ref = refs[8:16]
        att_kept, before_kept, sum_ref = refs[16:20], refs[20:23], refs[23]
        inner_ref, inner_sem = refs[24:26]
        copy = pltpu.make_async_copy(inner_hbm, inner_ref, inner_sem)
    step = pl.program_id(0)

    def here(start, length, unit=CTX):
        base = step * (GROUP * unit)
        return pl.ds(pl.multiple_of(base + start, 16), length)

    @pl.when(step == 0)
    def _():
        gain_ref[...] = jnp.zeros_like(gain_ref)
        if layer > 0:
            copy.start()

    dentry, gain_part = attend_back(
        step,
        here,
        (entry_ref[...], qkv_ref, mix_ref, chance_ref),
        dmiddle_ref[...],
        gains_ref[layer : layer + 1, :],
        att_ref,
        head_masks(),
        att_kept,
    )
    gain_ref[0:1, :] += gain_part
    if layer == 0:
        before_kept[0][here(0, ROWS), :] = dentry.astype(jnp.bfloat16)
        before_kept[1][here(0, ROWS), :] = one_hot_rows(latent_ref[...])
    else:
        dbefore, gain_part = feed_back(
            here,
            dentry,
            before_ref[...],
            gains_ref[LAYERS + layer - 1 : LAYERS + layer, :],
            ffn_ref,
            slope_ref,
            before_kept,
        )
        out_ref[...] = dbefore
        gain_ref[1:2, :] += gain_part

    @pl.when(step == pl.num_programs(0) - 1)
    def _():
        normed_ref, dattend_ref, dqkv_ref, mixes_ref = att_kept
        att = [(normed_ref, dqkv_ref), (mixes_ref, dattend_ref)]
        if layer == 0:
            pairs = att + [(before_kept[0], before_kept[1])]
        else:
            copy.wait()
            normed_two_ref, dinner_ref, dout_ref = before_kept
            pairs = [(normed_two_ref, dinner_ref), (dout_ref, inner_ref)] + att
        column = 0
        for left, right in pairs:
            wide = right.shape[1]
            sum_ref[:, column : column + wide] = dot_nn(left[...].T, right[...])
            column += wide
        write_blocks(send_ref, keep_ref, sum_ref, core_ref[0], widths, mesh_plan)


def run_backward(layer, widths, mesh_plan, blocks_like, saved, dmiddle, gains, core, before):
    entry, _, qkv, mix, chance, weights = saved[:6]
    tokens = entry.shape[0]
    queries = chance.shape[3] // (HEADS // 2)
    short = tokens // CTX * queries
    f32, b16 = jnp.float32, jnp.bfloat16
    shape = jax.ShapeDtypeStruct
    in_specs = [
        row_spec(D),
        row_spec(3 * D),
        row_spec(D, GROUP * queries),
        chance_spec(queries),
        row_spec(D, GROUP * queries),
        whole_spec(weights.shape),
        whole_spec(gains.shape),
        smem_spec(),
    ]
    operands = [entry, qkv, mix, chance, dmiddle, weights, gains, core]
    blocks = block_outs(blocks_like, widths)
    outs = [(item, whole_spec(item.shape)) for item in blocks]
    outs.append((shape((2, D), f32), whole_spec((2, D))))
    scratch = [
        pltpu.VMEM((tokens, D), b16),
        pltpu.VMEM((short, D), b16),
        pltpu.VMEM((tokens, 3 * D), b16),
        pltpu.VMEM((short, D), b16),
    ]
    if layer == 0:
        in_specs.append(row_spec(CATS))
        operands.append(before)
        scratch = scratch + [pltpu.VMEM((tokens, D), b16), pltpu.VMEM((tokens, VOCAB), b16)]
        wide = 4 * D + VOCAB
    else:
        in_specs = in_specs + [row_spec(D), whole_spec(before[1].shape), row_spec(FF)]
        in_specs.append(pl.BlockSpec(memory_space=pl.ANY))
        operands = operands + list(before)
        outs.insert(0, (shape((tokens, D), f32), row_spec(D)))
        scratch = scratch + [
            pltpu.VMEM((tokens, D), b16),
            pltpu.VMEM((tokens, FF), b16),
            pltpu.VMEM((tokens, D), b16),
        ]
        wide = 4 * D + 2 * FF
    scratch.append(pltpu.VMEM((D, wide), f32))
    if layer > 0:
        scratch = scratch + [pltpu.VMEM((tokens, FF), b16), pltpu.SemaphoreType.DMA]
    return pl.pallas_call(
        functools.partial(backward_kernel, layer, widths, mesh_plan),
        grid=(tokens // ROWS,),
        in_specs=in_specs,
        out_specs=[spec for _, spec in outs],
        out_shape=[item for item, _ in outs],
        scratch_shapes=scratch,
        compiler_params=pltpu.CompilerParams(vmem_limit_bytes=VMEM_BYTES),
        cost_estimate=pl.CostEstimate(
            flops=6 * tokens * D * wide,
            bytes_accessed=tokens * D * 24 + D * wide * 6,
            transcendentals=tokens * FF,
        ),
        name="backward_part",
    )(*operands)


def pack_kernel(*refs):
    qkv_ref, out_ref, up_ref, down_ref, embed_ref, head_ref = refs[:6]
    low = lambda value: value.astype(jnp.bfloat16)
    att = [[low(qkv_ref[at]), low(out_ref[at].T)] for at in range(LAYERS)]
    ffn = [[low(up_ref[at]), low(down_ref[at])] for at in range(LAYERS)]
    pieces = [
        att[0] + [low(embed_ref[...])],
        ffn[0] + att[1],
        ffn[1] + att[2] + ffn[2] + [low(head_ref[...])],
    ]
    for target, piece in zip(refs[6:], pieces):
        target[...] = jnp.concatenate(piece, axis=1)


def run_pack(masters, chunk_widths):
    vmem = pl.BlockSpec(memory_space=pltpu.VMEM)
    rows = masters[0].shape[1]
    return pl.pallas_call(
        pack_kernel,
        in_specs=[vmem] * 6,
        out_specs=[vmem] * 3,
        out_shape=[
            jax.ShapeDtypeStruct((rows, sum(widths)), jnp.bfloat16) for widths in chunk_widths
        ],
        name="pack",
    )(*masters)


def matrix_plan(widths):
    order = [
        (2, 2), (3, 2), (5, 0), (2, 1), (3, 1), (0, 2), (1, 2),
        (2, 0), (3, 0), (0, 1), (1, 1), (0, 0), (1, 0), (4, 0),
    ]
    plan, column = {}, 0
    for which, layer in order:
        plan[(which, layer)] = (column, widths[which])
        column += widths[which]
    return plan, column


def matrix_list():
    return [(which, layer) for which in range(4) for layer in range(LAYERS)] + [(4, 0), (5, 0)]


MATRICES = 4 * LAYERS + 2
LANES = 128
INNER_ROWS = 16
COMMON_ROWS = 16
ROW_IS_INNER = [True, True, True, False, False, True]


def master_of(masters, which, layer):
    if which == 1:
        return masters[1][layer].T
    return masters[which][layer] if which < 4 else masters[which][...]


def old_row(refs, which, layer):
    return refs[which][layer : layer + 1, :] if which < 4 else refs[which][...]


LATE = [(0, 0), (1, 0), (4, 0)]
EDGE = INNER_ROWS + COMMON_ROWS


def whole_sum(value):
    return jnp.sum(jnp.sum(value, axis=1, keepdims=True), axis=0, keepdims=True)


def square_sums(raw, chosen, plan, first):
    square = raw * raw
    rows = square.shape[0]
    inner, entries = [], []
    for item in matrix_list():
        if item in chosen:
            column, width = plan[item]
            part = square[:, column - first : column - first + width]
            inner.append(jnp.sum(part, axis=1, keepdims=True))
        else:
            inner.append(jnp.zeros((rows, 1), jnp.float32))
        entries.append(jnp.sum(inner[-1], axis=0, keepdims=True))
    inner.append(jnp.zeros((rows, LANES - MATRICES), jnp.float32))
    return jnp.concatenate(inner, axis=1).T, entries, jnp.sum(square, axis=0, keepdims=True)


def store_row(target_ref, row, values):
    total = values.shape[1]
    for at, start in enumerate(range(0, total, LANES)):
        stop = min(start + LANES, total)
        target_ref[row + at : row + at + 1, 0 : stop - start] = values[:, start:stop]


def load_row(source_ref, row, total):
    return jnp.concatenate(
        [
            source_ref[row + at : row + at + 1, 0 : min(LANES, total - start)]
            for at, start in enumerate(range(0, total, LANES))
        ],
        axis=1,
    )


def late_row(widths):
    _, total = matrix_plan(widths)
    late = sum(widths[which] for which, _ in LATE)
    return EDGE + -(-(total - late) // LANES)


def packet_rows(widths):
    late = sum(widths[which] for which, _ in LATE)
    return -(-(late_row(widths) + -(-late // LANES)) // 8) * 8


def early_kernel(widths, *refs):
    raw_ref, masters, row_refs = refs[0], refs[1:7], refs[7:13]
    gains_at, loss_ref, counted_ref, packet_ref = refs[13:16], refs[16], refs[17], refs[18]
    plan, _ = matrix_plan(widths)
    chosen = [item for item in matrix_list() if item not in LATE]
    inner, entries, outer = square_sums(raw_ref[...], chosen, plan, 0)
    weights, row_sums = [], []
    for which, layer in matrix_list():
        master = masters[which][layer] if which < 4 else masters[which][...]
        weights.append(whole_sum(master * master))
        row_sums.append(whole_sum(old_row(row_refs, which, layer)))
    packet_ref[...] = jnp.zeros_like(packet_ref)
    packet_ref[0:INNER_ROWS, 0 : inner.shape[1]] = inner[0:INNER_ROWS, :]
    top, two, one = [ref[...] for ref in gains_at]
    gain = jnp.concatenate(
        [jnp.zeros((1, D), jnp.float32), one[0:1], two[0:1], one[1:2], two[1:2], top], axis=0
    )
    scalars = [loss_ref[...], whole_sum(counted_ref[...])] + weights + entries + row_sums
    scalars.append(jnp.zeros((1, LANES - len(scalars)), jnp.float32))
    at = INNER_ROWS
    packet_ref[at : at + 7, :] = gain[:, 0:LANES]
    packet_ref[at + 7 : at + 8, :] = jnp.concatenate(scalars, axis=1)
    packet_ref[at + 8 : at + 15, :] = gain[:, LANES:]
    store_row(packet_ref, EDGE, outer)


def late_kernel(widths, early_ref, raw_ref, gain_ref, packet_ref):
    plan, total = matrix_plan(widths)
    inner, entries, outer = square_sums(raw_ref[...], LATE, plan, total - raw_ref.shape[1])
    packet_ref[...] = early_ref[...]
    packet_ref[0:INNER_ROWS, 0 : inner.shape[1]] += inner[0:INNER_ROWS, :]
    at = INNER_ROWS
    packet_ref[at : at + 1, :] = gain_ref[0:1, 0:LANES]
    packet_ref[at + 8 : at + 9, :] = gain_ref[0:1, LANES:]
    before = jnp.zeros((1, 2 + MATRICES), jnp.float32)
    behind = jnp.zeros((1, LANES - 2 - 2 * MATRICES), jnp.float32)
    packet_ref[at + 7 : at + 8, :] += jnp.concatenate([before] + entries + [behind], axis=1)
    store_row(packet_ref, late_row(widths), outer)


def run_early(widths, raw, masters, rows, gain_parts, loss, counted):
    vmem = pl.BlockSpec(memory_space=pltpu.VMEM)
    operands = [raw] + masters + rows + gain_parts + [loss, counted]
    return pl.pallas_call(
        functools.partial(early_kernel, widths),
        in_specs=[vmem] * len(operands),
        out_specs=vmem,
        out_shape=jax.ShapeDtypeStruct((packet_rows(widths), LANES), jnp.float32),
        name="early_statistics",
    )(*operands)


def run_late(widths, packet, raw, gain_part):
    vmem = pl.BlockSpec(memory_space=pltpu.VMEM)
    return pl.pallas_call(
        functools.partial(late_kernel, widths),
        in_specs=[vmem] * 3,
        out_specs=vmem,
        out_shape=jax.ShapeDtypeStruct(packet.shape, jnp.float32),
        name="late_statistics",
    )(packet, raw, gain_part)


def update_kernel(widths, sizes, *refs):
    packet_ref, raw_early, raw_late = refs[:3]
    masters, inner_refs, outer_refs = refs[3:9], refs[9:15], refs[15:21]
    gains_ref, second_ref = refs[21:23]
    outs = refs[23:]
    outer_count, inner_count = sizes
    plan, total = matrix_plan(widths)
    rows = raw_early.shape[0]
    at = INNER_ROWS
    scalars = packet_ref[at + 7 : at + 8, :]
    pick = lambda at: scalars[:, at : at + 1]
    gain_sum = jnp.concatenate(
        [packet_ref[at : at + 7, :], packet_ref[at + 8 : at + 15, :]], axis=1
    )
    gain_square = jnp.sum(jnp.sum(gain_sum * gain_sum, axis=1, keepdims=True), axis=0, keepdims=True)
    square_total = gain_square
    for at in range(MATRICES):
        square_total = square_total + pick(2 + MATRICES + at)
    count_total = pick(1)
    norm_value = jnp.sqrt(square_total) / count_total
    scaling = jnp.minimum(1.0, clip_limit / norm_value) / count_total
    square_scale = scaling * scaling
    early = raw_early.shape[1]
    outer_early = load_row(packet_ref, EDGE, early)
    outer_late = load_row(packet_ref, late_row(widths), total - early)
    inner_new = []
    for at, (which, layer) in enumerate(matrix_list()):
        outer_length = widths[which] * outer_count
        inner_new.append(
            decay_two * old_row(inner_refs, which, layer)
            + (1 - decay_two)
            * (square_scale * packet_ref[at : at + 1, 0:rows] / outer_length + tiny_term)
        )
    stacked = jnp.concatenate(inner_new, axis=0)
    stacked = jnp.concatenate([stacked, jnp.ones((LANES - MATRICES, rows), jnp.float32)], axis=0)
    if rows < LANES:
        stacked = jnp.concatenate([stacked, jnp.ones((LANES, LANES - rows), jnp.float32)], axis=1)
    turned = lax.rsqrt(stacked).T
    outs[0][...] = pick(0)
    outs[1][...] = count_total
    outs[2][...] = norm_value
    first_out = {4: 3, 0: 7, 1: 11, 2: 15, 3: 19, 5: 23}
    for at, (which, layer) in enumerate(matrix_list()):
        column, width = plan[(which, layer)]
        outer_length, inner_length = width * outer_count, rows * inner_count
        row_length = inner_length if ROW_IS_INNER[which] else outer_length
        copies = outer_count if ROW_IS_INNER[which] else inner_count
        entries = outer_length * inner_length
        if column < early:
            raw = raw_early[:, column : column + width]
            outer_total = outer_early[:, column : column + width]
        else:
            raw = raw_late[:, column - early : column - early + width]
            outer_total = outer_late[:, column - early : column - early + width]
        outer_new = decay_two * old_row(outer_refs, which, layer) + (1 - decay_two) * (
            square_scale * outer_total / inner_length + tiny_term
        )
        mean_rows = decay_two * (pick(2 + 2 * MATRICES + at) / (copies * row_length)) + (
            1 - decay_two
        ) * (square_scale * pick(2 + MATRICES + at) / entries + tiny_term)
        factor = step_rate * jnp.sqrt(pick(2 + at) / entries) * jnp.sqrt(mean_rows)
        grad = raw * scaling
        updated = master_of(masters, which, layer) - grad * (
            turned[0:rows, at : at + 1] * (factor * lax.rsqrt(outer_new))
        )
        first = first_out[which]
        row_new, column_new = (
            (inner_new[at], outer_new) if ROW_IS_INNER[which] else (outer_new, inner_new[at])
        )
        if which < 4:
            if which == 1:
                updated, grad = updated.T, grad.T
            outs[first][layer] = updated
            outs[first + 1][layer] = grad
            outs[first + 2][layer : layer + 1, :] = row_new
            outs[first + 3][layer : layer + 1, :] = column_new
        else:
            outs[first][...] = updated
            outs[first + 1][...] = grad
            outs[first + 2][...] = row_new
            outs[first + 3][...] = column_new
    gain_grad = gain_sum * scaling
    second_new = decay_two * second_ref[...] + (1 - decay_two) * (gain_grad * gain_grad + tiny_term)
    gains = gains_ref[...]
    spread = jnp.sqrt(jnp.mean(gains * gains, axis=-1, keepdims=True))
    outs[27][...] = gains - step_rate * spread * gain_grad * lax.rsqrt(second_new)
    outs[28][...] = gain_grad
    outs[29][...] = second_new


def run_update(widths, sizes, packet, raw_early, raw_late, masters, inner, outer, gains, second):
    vmem = pl.BlockSpec(memory_space=pltpu.VMEM)
    operands = [packet, raw_early, raw_late] + masters + inner + outer + [gains, second]
    shapes = [(1, 1)] * 3
    for which in [4, 0, 1, 2, 3, 5]:
        shapes = shapes + [masters[which].shape] * 2
        pair = [inner[which].shape, outer[which].shape]
        shapes = shapes + (pair if ROW_IS_INNER[which] else pair[::-1])
    shapes = shapes + [gains.shape] * 3
    return pl.pallas_call(
        functools.partial(update_kernel, widths, sizes),
        in_specs=[vmem] * len(operands),
        out_specs=[vmem] * len(shapes),
        out_shape=[jax.ShapeDtypeStruct(item, jnp.float32) for item in shapes],
        name="update",
    )(*operands)


def swap(value, mask):
    count = lax.axis_size("dp") * lax.axis_size("fsdp")
    return lax.ppermute(value, ("dp", "fsdp"), [(place, place ^ mask) for place in range(count)])


def device_index():
    return lax.axis_index("dp") * lax.axis_size("fsdp") + lax.axis_index("fsdp")


def step_masks(step):
    masks = []
    for digit in range(1, 1 << len(step)):
        masks.append(sum(1 << bit for at, bit in enumerate(step[::-1]) if (digit >> at) & 1))
    return masks


def tie(*values):
    return lax.optimization_barrier(values)


class Gather:
    def __init__(self, piece, steps):
        self.held, self.steps, self.at = piece[None], steps, 0

    def send(self):
        self.others = tuple(swap(self.held, mask) for mask in step_masks(self.steps[self.at]))

    def join(self):
        step = self.steps[self.at]
        pieces = [self.held] + list(self.others)
        for at, bit in enumerate(step[::-1]):
            upper = (device_index() >> bit) & 1 == 1
            pieces = [
                jnp.where(upper, pieces[place ^ (1 << at)], pieces[place])
                for place in range(len(pieces))
            ]
        self.held = jnp.concatenate(pieces)
        self.at += 1


class Scatter:
    def __init__(self, sent, kept, steps):
        self.sent, self.kept, self.steps, self.at = (sent,), kept, steps, 0

    def send(self):
        masks = step_masks(self.steps[self.at])
        self.others = tuple(swap(sent, mask) for sent, mask in zip(self.sent, masks))

    def join(self):
        self.at += 1
        summed = self.kept
        for other in self.others:
            summed = summed + other.astype(jnp.float32)
        if self.at == len(self.steps):
            self.kept = summed
            return
        step = self.steps[self.at]
        count = 1 << len(step)
        own = 0
        for bit in step:
            own = 2 * own + ((device_index() >> bit) & 1)
        parts = summed.reshape((count, summed.shape[0] // count) + summed.shape[1:])
        if count == 2:
            self.sent = (jnp.where(own == 1, parts[0], parts[1]).astype(jnp.bfloat16),)
            self.kept = jnp.where(own == 1, parts[1], parts[0])
            return
        pick = lambda digit: lax.dynamic_index_in_dim(parts, own ^ digit, 0, keepdims=False)
        self.sent = tuple(pick(digit).astype(jnp.bfloat16) for digit in range(1, count))
        self.kept = pick(0)


def sum_packets(packet, group, inner_bits):
    masks = step_masks(group)
    others = [swap(packet, mask) for mask in masks]
    inner, outer = packet[:INNER_ROWS], packet[EDGE:]
    common = [packet[INNER_ROWS:EDGE]]
    inner, outer = [inner], [outer]
    for mask, other in zip(masks, others):
        common.append(other[INNER_ROWS:EDGE])
        if mask >> inner_bits << inner_bits == mask:
            inner.append(other[:INNER_ROWS])
        if mask >> inner_bits == 0:
            outer.append(other[EDGE:])
    tree = lambda items: (
        items[0] if len(items) == 1 else tree(
            [items[at] + items[at + 1] for at in range(0, len(items), 2)]
        )
    )
    return jnp.concatenate([tree(inner), tree(common), tree(outer)])


def merged(parts):
    whole = Scatter(None, jnp.concatenate([part.kept for part in parts], axis=2), parts[0].steps)
    whole.sent = tuple(
        jnp.concatenate(pieces, axis=2) for pieces in zip(*[part.sent for part in parts])
    )
    whole.at = parts[0].at
    return whole


def shards(
    latents,
    targets,
    horizon,
    memory_valid,
    embed,
    qkv_weight,
    out_weight,
    up_weight,
    down_weight,
    head_weight,
    gains,
    embed_rows,
    embed_cols,
    qkv_rows,
    qkv_cols,
    out_rows,
    out_cols,
    up_rows,
    up_cols,
    down_rows,
    down_cols,
    head_rows,
    head_cols,
    gain_second,
):
    samples = latents.shape[0]
    sizes = (lax.axis_size("dp"), lax.axis_size("fsdp"))
    highest = (sizes[0] * sizes[1]).bit_length() - 1
    gather_steps = [(bit,) for bit in reversed(range(3, highest))] + [(2, 1), (0,)]
    scatter_steps = gather_steps[::-1]
    mesh_plan = (sizes[0], sizes[1], gather_steps)
    core = (lax.axis_index("fsdp") & 1).astype(jnp.int32).reshape(1)

    out_turned = jnp.swapaxes(out_weight, 1, 2)
    down_turned = jnp.swapaxes(down_weight, 1, 2)
    masters = [qkv_weight, out_turned, up_weight, down_turned, embed.T, head_weight]
    widths = [qkv_weight.shape[2], out_weight.shape[2], up_weight.shape[2], down_weight.shape[1]]
    widths = widths + [embed.shape[0], head_weight.shape[1]]
    att_widths, ffn_widths = widths[0:2], widths[2:4]
    chunk_widths = [
        att_widths + widths[4:5],
        ffn_widths + att_widths,
        ffn_widths + att_widths + ffn_widths + widths[5:6],
    ]
    chunks = [Gather(piece, gather_steps) for piece in run_pack(masters, chunk_widths)]
    first, second, third = chunks

    latent_rows = latents.astype(jnp.bfloat16).reshape(samples * CTX, CATS)
    target_rows = targets.transpose(2, 0, 1).reshape(CATS, samples * SEG)
    counted = jnp.arange(SEG, dtype=jnp.int32)[None, :] < horizon[:, None]
    counted = counted.astype(jnp.float32).reshape(1, samples * SEG)
    shared = (gains, memory_valid, core)
    back_shared = (gains, core)

    count = len(gather_steps)
    for at in range(count - 1):
        for chunk in chunks:
            chunk.send()
        if at == 0:
            first.held, latent_rows, target_rows, counted = tie(
                first.held, latent_rows, target_rows, counted
            )
        for chunk in chunks[: 2 if at == count - 2 else 3]:
            chunk.join()
            if at == count - 3 and chunk is first:
                first.held, third.held = tie(first.held, third.held)
    first.send()
    (other,) = first.others
    first.held, other, second.held = tie(first.held, other, second.held)
    second.send()
    kept = [run_forward(0, chunk_widths[0], mesh_plan, latent_rows, first.held, other, *shared)]
    middle, (other,), third.others = tie(kept[0][1], second.others, third.others)
    third.join()
    second.held, third.held = tie(second.held, third.held)
    third.send()
    kept.append(
        run_forward(1, chunk_widths[1], mesh_plan, middle, second.held, other, *shared)
    )
    middle, (other,) = tie(kept[1][1], third.others)
    kept.append(run_forward(2, chunk_widths[2], mesh_plan, middle, third.held, other, *shared))

    dmiddle, sent, held, gain_top, loss = run_top(
        ffn_widths + widths[5:6],
        mesh_plan,
        sum(ffn_widths + att_widths),
        kept[2][1],
        third.held,
        other,
        target_rows,
        counted,
        gains,
        core,
    )
    top = Scatter(sent, held, scatter_steps)
    top.send()
    like = first.held
    before = [(kept[at][1], kept[at + 1][6], kept[at + 1][8], kept[at + 1][7]) for at in range(2)]
    dmiddle, sent, held, gain_two = run_backward(
        2, chunk_widths[1], mesh_plan, like, kept[2], dmiddle, *back_shared, before[1]
    )
    dmiddle, top.others = tie(dmiddle, top.others)
    top.join()
    two = Scatter(sent, held, scatter_steps)
    dmiddle, top.sent = tie(dmiddle, top.sent)
    top.send()
    two.send()
    dmiddle, sent, held, gain_one = run_backward(
        1, chunk_widths[1], mesh_plan, like, kept[1], dmiddle, *back_shared, before[0]
    )
    dmiddle, top.others, two.others = tie(dmiddle, top.others, two.others)
    one = Scatter(sent, held, scatter_steps)
    one.send()
    top.join()
    two.join()
    one.join()
    pair = merged([two, one])
    dmiddle, pair.sent = tie(dmiddle, pair.sent)
    pair.send()
    sent, held, gain_zero = run_backward(
        0, chunk_widths[0], mesh_plan, like, kept[0], dmiddle, *back_shared, latent_rows
    )
    sent, pair.others = tie(sent, pair.others)
    zero = Scatter(sent, held, scatter_steps)
    zero.send()
    pair.join()
    early = merged([top, pair])
    early.send()
    zero.join()
    while early.at < count:
        early.others, zero.sent = tie(early.others, zero.sent)
        zero.send()
        early.join()
        if early.at < count:
            early.send()
            zero.others, early.sent = tie(zero.others, early.sent)
        else:
            zero.others, early.kept = tie(zero.others, early.kept)
        zero.join()
    raw_early = early.kept[0]
    zero.send()

    flat = lambda item: item if item.ndim == 2 else item.reshape(1, -1)
    inner = [flat(item) for item in (qkv_rows, out_rows, up_rows, down_cols, embed_cols, head_rows)]
    outer = [flat(item) for item in (qkv_cols, out_cols, up_cols, down_rows, embed_rows, head_cols)]
    row_stats = [inner[at] if ROW_IS_INNER[at] else outer[at] for at in range(6)]
    packet = run_early(
        widths, raw_early, masters, row_stats, [gain_top, gain_two, gain_one], loss, counted
    )
    packet, zero.others = tie(packet, zero.others)
    zero.join()
    while zero.at < count:
        zero.send()
        zero.join()
    raw_late = zero.kept[0]
    packet = run_late(widths, packet, raw_late, gain_zero)
    inner_bits = sizes[1].bit_length() - 1
    rest = list(range(3, highest))
    groups = [(0,), (2, 1)] + [tuple(rest[at : at + 2][::-1]) for at in range(0, len(rest), 2)]
    for group in groups:
        packet = sum_packets(packet, group, inner_bits)
    results = run_update(
        widths, sizes, packet, raw_early, raw_late, masters, inner, outer, gains, gain_second
    )
    results = list(results)
    for at in range(3):
        results[at] = results[at].reshape(())
    for at in (3, 4, 11, 12, 19, 20):
        results[at] = jnp.swapaxes(results[at], -1, -2)
    for at in (5, 6, 25, 26):
        results[at] = results[at].reshape(-1)
    return tuple(results)


def solution(mesh):
    return jax.shard_map(
        shards,
        mesh=mesh,
        in_specs=(
            P(("dp", "fsdp"), None, None),
            P(("dp", "fsdp"), None, None),
            P(("dp", "fsdp")),
            P(("dp", "fsdp")),
            P("dp", "fsdp"),
            P(None, "fsdp", "dp"),
            P(None, "fsdp", "dp"),
            P(None, "fsdp", "dp"),
            P(None, "dp", "fsdp"),
            P("fsdp", "dp"),
            P(),
            P("dp"),
            P("fsdp"),
            P(None, "fsdp"),
            P(None, "dp"),
            P(None, "fsdp"),
            P(None, "dp"),
            P(None, "fsdp"),
            P(None, "dp"),
            P(None, "dp"),
            P(None, "fsdp"),
            P("fsdp"),
            P("dp"),
            P(),
        ),
        out_specs=(
            P(),
            P(),
            P(),
            P("dp", "fsdp"),
            P("dp", "fsdp"),
            P("dp"),
            P("fsdp"),
            P(None, "fsdp", "dp"),
            P(None, "fsdp", "dp"),
            P(None, "fsdp"),
            P(None, "dp"),
            P(None, "fsdp", "dp"),
            P(None, "fsdp", "dp"),
            P(None, "fsdp"),
            P(None, "dp"),
            P(None, "fsdp", "dp"),
            P(None, "fsdp", "dp"),
            P(None, "fsdp"),
            P(None, "dp"),
            P(None, "dp", "fsdp"),
            P(None, "dp", "fsdp"),
            P(None, "dp"),
            P(None, "fsdp"),
            P("fsdp", "dp"),
            P("fsdp", "dp"),
            P("fsdp"),
            P("dp"),
            P(),
            P(),
            P(),
        ),
        check_vma=False,
    )
```

```python
import functools

import jax
import jax.numpy as jnp
from jax import lax
from jax.experimental import pallas as pl
from jax.experimental.pallas import tpu as pltpu
from jax.sharding import PartitionSpec as P

D = 256
HEADS = 8
HEAD = D // HEADS
FF = 1024
CATS = 32
CLASSES = 32
LAYERS = 3
SEG = 48
MEM = 48
CTX = 96
VOCAB = 1024
GROUP = 4
ROWS = GROUP * CTX
HALF = D // 2
VMEM_BYTES = 24 * 1024 * 1024

decay_two = 0.9
step_rate = 0.3
clip_limit = 0.05
tiny_term = 1e-30
norm_eps = 1e-06
masked_score = -1e30
log2_e = 1.4426950408889634
score_scale = HEAD ** (-0.5)
gelu_one = 0.7978845608028654
gelu_two = 0.044715


def dot_nn(left, right):
    return lax.dot_general(
        left, right, (((1,), (0,)), ((), ())), preferred_element_type=jnp.float32
    )


def dot_nt(left, right):
    return lax.dot_general(
        left, right, (((1,), (1,)), ((), ())), preferred_element_type=jnp.float32
    )


def dot_tn(left, right):
    return lax.dot_general(
        left, right, (((0,), (0,)), ((), ())), preferred_element_type=jnp.float32
    )


def inverse_rms(values):
    return lax.rsqrt(jnp.mean(values * values, axis=-1, keepdims=True) + norm_eps)


def rms_back(values, inverse, gain_row, upstream):
    normed = values * inverse
    scaled = upstream * gain_row
    inner = jnp.mean(scaled * normed, axis=-1, keepdims=True)
    return (
        inverse * (scaled - normed * inner),
        jnp.sum(upstream * normed, axis=0, keepdims=True),
    )


def head_masks():
    lane = lax.broadcasted_iota(jnp.int32, (1, D // 2), 1) // HEAD
    return [lane == head for head in range(HEADS // 2)]


def expand_heads(rows, masks):
    return jnp.concatenate([rows * mask.astype(rows.dtype) for mask in masks], axis=0)


def collapse_heads(spread, rows, masks):
    product = dot_tn(spread, rows)
    queries = product.shape[0] // len(masks)
    taken = product[(len(masks) - 1) * queries :]
    for at, mask in enumerate(masks[:-1]):
        taken = jnp.where(mask, product[at * queries : (at + 1) * queries], taken)
    return taken


def half_of(part, side):
    start = part * D + side * HALF
    return slice(start, start + HALF)


def fill_bias(bias_ref):
    spread = bias_ref.shape[2]
    queries = spread // (HEADS // 2)
    key_at = lax.broadcasted_iota(jnp.int32, (CTX, spread), 0)
    query_at = lax.broadcasted_iota(jnp.int32, (CTX, spread), 1) % queries + (CTX - queries)
    later = key_at > query_at
    crosses = (query_at >= MEM) & (key_at < MEM)
    bias_ref[0] = jnp.where(later | crosses, masked_score, 0.0)
    bias_ref[1] = jnp.where(later, masked_score, 0.0)


def block_place(device, steps):
    place, weight = 0, 1
    for step in steps[:-1]:
        digit = 0
        for bit in step:
            digit = 2 * digit + ((device >> bit) & 1)
        place += digit * weight
        weight <<= len(step)
    return place


def place_weights(targets, own_ref, other_ref, core, widths, mesh_plan, start=0):
    outer_count, inner_count, steps = mesh_plan
    rows = own_ref.shape[1]
    for high in range(inner_count // 2):
        for source, side in ((own_ref, core), (other_ref, 1 - core)):
            here = pl.ds(pl.multiple_of((2 * high + side) * rows, rows), rows)
            at = start
            for (target, column), width in zip(targets, widths):
                block = [
                    source[
                        block_place(outer * inner_count + 2 * high, steps), :, at : at + width
                    ]
                    for outer in range(outer_count)
                ]
                target[here, column : column + width * outer_count] = jnp.concatenate(
                    block, axis=1
                )
                at += width


def write_blocks(send_ref, keep_ref, sum_ref, core, widths, mesh_plan):
    outer_count, inner_count, steps = mesh_plan
    rows = keep_ref.shape[1]
    for high in range(inner_count // 2):
        for target, side in ((keep_ref, core), (send_ref, 1 - core)):
            here = pl.ds(pl.multiple_of((2 * high + side) * rows, rows), rows)
            taken = sum_ref[here, :]
            for outer in range(outer_count):
                block, column = [], 0
                for width in widths:
                    block.append(taken[:, column + outer * width : column + (outer + 1) * width])
                    column += width * outer_count
                target[block_place(outer * inner_count + 2 * high, steps)] = jnp.concatenate(
                    block, axis=1
                ).astype(target.dtype)


def one_hot_rows(latent_ref, hot_ref, first):
    spot = lax.broadcasted_iota(jnp.int32, (CATS, VOCAB), 1) // CLASSES
    group = lax.broadcasted_iota(jnp.int32, (CATS, VOCAB), 0)
    spreader = jnp.where(spot == group, 1.0, 0.0).astype(jnp.bfloat16)
    classes = (lax.broadcasted_iota(jnp.int32, (1, VOCAB), 1) % CLASSES).astype(jnp.float32)
    for sample in range(GROUP):
        drawn = dot_tn(latent_ref[sample].astype(jnp.float32).astype(jnp.bfloat16), spreader)
        hot_ref[pl.ds(first + sample * CTX, CTX), :] = jnp.where(
            drawn == classes, 1.0, 0.0
        ).astype(jnp.bfloat16)


def tail_rows(values, queries):
    if queries == CTX:
        return values
    return jnp.concatenate(
        [
            values[(sample + 1) * CTX - queries : (sample + 1) * CTX]
            for sample in range(values.shape[0] // CTX)
        ],
        axis=0,
    )


def attend_forward(step, hidden, gain_row, weight_ref, valid_ref, bias_ref, masks, refs):
    middle_ref, qkv_ref, mix_ref, chance_ref = refs
    queries = chance_ref.shape[3] // (HEADS // 2)
    normed = (hidden * inverse_rms(hidden) * gain_row).astype(jnp.bfloat16)
    qkv_ref[...] = dot_nn(normed, weight_ref[:, 0 : 3 * D]).astype(jnp.bfloat16)
    units = [(sample, side) for sample in range(GROUP) for side in range(2)]
    scores = []
    for sample, side in units:
        rows = slice(sample * CTX, (sample + 1) * CTX)
        tail = slice((sample + 1) * CTX - queries, (sample + 1) * CTX)
        spread = expand_heads(qkv_ref[tail, half_of(0, side)], masks)
        scores.append(dot_nt(qkv_ref[rows, half_of(1, side)], spread))
    for (sample, side), score in zip(units, scores):
        score = score + bias_ref[valid_ref[step * GROUP + sample]]
        peak = jnp.max(score, axis=0, keepdims=True)
        exponent = jnp.exp2((score - peak) * (score_scale * log2_e))
        total = jnp.sum(exponent, axis=0, keepdims=True)
        chance_ref[sample, side] = (exponent * (1.0 / total)).astype(jnp.bfloat16)
    for sample, side in units:
        rows = slice(sample * CTX, (sample + 1) * CTX)
        mix_ref[sample * queries : (sample + 1) * queries, half_of(0, side)] = collapse_heads(
            chance_ref[sample, side], qkv_ref[rows, half_of(2, side)], masks
        ).astype(jnp.bfloat16)
    middle_ref[...] = tail_rows(hidden, queries) + dot_nn(
        mix_ref[...], weight_ref[:, 3 * D : 4 * D]
    )


def gelu_parts(value):
    square = value * value
    share = 0.5 + 0.5 * jnp.tanh(value * (gelu_one + (gelu_one * gelu_two) * square))
    active = value * share
    bent = active * (1.0 - share)
    return active, share + bent * (2.0 * gelu_one + (6.0 * gelu_one * gelu_two) * square)


def feed_forward(middle, gain_row, weight_ref, inner_ref, slope_ref):
    normed = (middle * inverse_rms(middle) * gain_row).astype(jnp.bfloat16)
    for part in range(FF // D):
        columns = slice(part * D, (part + 1) * D)
        inner = dot_nn(normed, weight_ref[:, columns])
        for sample in range(GROUP):
            rows = slice(sample * CTX, (sample + 1) * CTX)
            active, slope = gelu_parts(inner[rows])
            inner_ref[rows, columns] = active.astype(jnp.bfloat16)
            slope_ref[rows, columns] = slope.astype(jnp.bfloat16)
    return middle + dot_nt(inner_ref[...], weight_ref[:, FF : 2 * FF])


def feed_back(here, upstream, middle, gain_row, weight_ref, slope_ref, refs):
    normed_ref, dinner_ref, dout_ref = refs
    dout = upstream.astype(jnp.bfloat16)
    dout_ref[here(0, ROWS), :] = dout
    inverse = inverse_rms(middle)
    normed_ref[here(0, ROWS), :] = (middle * inverse * gain_row).astype(jnp.bfloat16)
    for part in range(FF // D):
        columns = slice(part * D, (part + 1) * D)
        dact = dot_nn(dout, weight_ref[:, FF + part * D : FF + (part + 1) * D])
        dinner_ref[here(0, ROWS), columns] = (
            dact * slope_ref[:, columns].astype(jnp.float32)
        ).astype(jnp.bfloat16)
    dnormed = dot_nt(dinner_ref[here(0, ROWS), :], weight_ref[:, 0:FF])
    through, gain_part = rms_back(middle, inverse, gain_row, dnormed)
    return upstream + through, gain_part


def attend_back(step, here, saved, dmiddle, gain_row, weight_ref, masks, refs):
    hidden, qkv_ref, mix_ref, chance_ref = saved
    normed_ref, dmiddle_ref, dqkv_ref, mixes_ref = refs
    queries = chance_ref.shape[3] // (HEADS // 2)
    short = here(0, GROUP * queries, queries)
    dattend = dmiddle.astype(jnp.bfloat16)
    dmiddle_ref[short, :] = dattend
    mixes_ref[short, :] = mix_ref[...]
    dmix = dot_nt(dattend, weight_ref[:, 3 * D : 4 * D]).astype(jnp.bfloat16)
    units = [(sample, side) for sample in range(GROUP) for side in range(2)]
    slopes, dchances, dscores = [], [], []
    for sample, side in units:
        rows = slice(sample * CTX, (sample + 1) * CTX)
        slopes.append(
            expand_heads(
                dmix[sample * queries : (sample + 1) * queries, half_of(0, side)], masks
            )
        )
        dchances.append(dot_nt(qkv_ref[rows, half_of(2, side)], slopes[-1]))
    for (sample, side), dchance in zip(units, dchances):
        chance = chance_ref[sample, side].astype(jnp.float32)
        weighed = chance * dchance
        dscores.append(
            (weighed - chance * jnp.sum(weighed, axis=0, keepdims=True)).astype(jnp.bfloat16)
        )
    for at, (sample, side) in enumerate(units):
        rows = slice(sample * CTX, (sample + 1) * CTX)
        tail = slice((sample + 1) * CTX - queries, (sample + 1) * CTX)
        there = here(sample * CTX, CTX)
        spread = expand_heads(qkv_ref[tail, half_of(0, side)], masks)
        keys = qkv_ref[rows, half_of(1, side)]
        dvalues = dot_nn(chance_ref[sample, side], slopes[at])
        dkeys = dot_nn(dscores[at], spread) * score_scale
        dqueries = (collapse_heads(dscores[at], keys, masks) * score_scale).astype(jnp.bfloat16)
        if queries < CTX:
            nothing = jnp.zeros((CTX - queries, HALF), jnp.bfloat16)
            dqueries = jnp.concatenate([nothing, dqueries], axis=0)
        dqkv_ref[there, half_of(0, side)] = dqueries
        dqkv_ref[there, half_of(1, side)] = dkeys.astype(jnp.bfloat16)
        dqkv_ref[there, half_of(2, side)] = dvalues.astype(jnp.bfloat16)
    inverse = inverse_rms(hidden)
    normed_ref[here(0, ROWS), :] = (hidden * inverse * gain_row).astype(jnp.bfloat16)
    dnormed = dot_nt(dqkv_ref[here(0, ROWS), :], weight_ref[:, 0 : 3 * D])
    through, gain_part = rms_back(hidden, inverse, gain_row, dnormed)
    if queries < CTX:
        nothing = jnp.zeros((CTX - queries, D), jnp.float32)
        pieces = []
        for sample in range(GROUP):
            pieces = pieces + [nothing, dmiddle[sample * queries : (sample + 1) * queries]]
        dmiddle = jnp.concatenate(pieces, axis=0)
    return dmiddle + through, gain_part


def row_spec(width, rows=ROWS):
    return pl.BlockSpec((rows, width), lambda step: (step, 0))


def chance_spec(queries):
    return pl.BlockSpec((GROUP, 2, CTX, HEADS // 2 * queries), lambda step: (step, 0, 0, 0))


def latent_spec():
    return pl.BlockSpec((GROUP, CATS, CTX), lambda step: (step, 0, 0))


def whole_spec(shape):
    return pl.BlockSpec(shape, lambda step: (0,) * len(shape))


def smem_spec():
    return pl.BlockSpec(memory_space=pltpu.SMEM)


def forward_kernel(layer, widths, mesh_plan, source_ref, own_ref, other_ref, gains_ref, valid_ref, core_ref, *refs):
    entry_ref, att_ref, before_ref = refs[0], refs[5], refs[6]
    bias_ref = refs[7] if layer == 0 else refs[9]
    step = pl.program_id(0)

    @pl.when(step == 0)
    def _():
        fill_bias(bias_ref)
        att = [(att_ref, 0), (att_ref, 3 * D)]
        before = [(before_ref, 0)] if layer == 0 else [(before_ref, 0), (before_ref, FF)]
        targets = att + before if layer == 0 else before + att
        place_weights(targets, own_ref, other_ref, core_ref[0], widths[: len(targets)], mesh_plan)

    if layer == 0:
        one_hot_rows(source_ref, refs[8], 0)
        hidden = dot_nt(refs[8][...], before_ref[...])
    else:
        gain_ffn = gains_ref[LAYERS + layer - 1 : LAYERS + layer, :]
        hidden = feed_forward(source_ref[...], gain_ffn, before_ref, refs[7], refs[8])
    entry_ref[...] = hidden
    attend_forward(
        step,
        hidden,
        gains_ref[layer : layer + 1, :],
        att_ref,
        valid_ref,
        bias_ref,
        head_masks(),
        refs[1:5],
    )


def run_forward(layer, widths, mesh_plan, source, own, other, gains, valid, core):
    tokens = valid.shape[0] * CTX
    queries = SEG if layer == LAYERS - 1 else CTX
    f32, b16 = jnp.float32, jnp.bfloat16
    shape = jax.ShapeDtypeStruct
    short = tokens // CTX * queries
    outs = [
        (shape((tokens, D), f32), row_spec(D)),
        (shape((short, D), f32), row_spec(D, GROUP * queries)),
        (shape((tokens, 3 * D), b16), row_spec(3 * D)),
        (shape((short, D), b16), row_spec(D, GROUP * queries)),
        (shape((tokens // CTX, 2, CTX, HEADS // 2 * queries), b16), chance_spec(queries)),
        (shape((D, 4 * D), b16), whole_spec((D, 4 * D))),
    ]
    scratch = [pltpu.VMEM((2, CTX, HEADS // 2 * queries), f32)]
    if layer == 0:
        scratch = [pltpu.VMEM((D, VOCAB), b16)] + scratch + [pltpu.VMEM((ROWS, VOCAB), b16)]
        source_spec = latent_spec()
    else:
        source_spec = row_spec(D)
        outs.append((shape((D, 2 * FF), b16), whole_spec((D, 2 * FF))))
        outs = outs + [(shape((tokens, FF), b16), row_spec(FF))] * 2
    return pl.pallas_call(
        functools.partial(forward_kernel, layer, widths, mesh_plan),
        grid=(tokens // ROWS,),
        in_specs=[
            source_spec,
            whole_spec(own.shape),
            whole_spec(other.shape),
            whole_spec(gains.shape),
            smem_spec(),
            smem_spec(),
        ],
        out_specs=[spec for _, spec in outs],
        out_shape=[item for item, _ in outs],
        scratch_shapes=scratch,
        compiler_params=pltpu.CompilerParams(vmem_limit_bytes=VMEM_BYTES),
        cost_estimate=pl.CostEstimate(
            flops=2 * tokens * D * 12 * D,
            bytes_accessed=tokens * D * 16 + D * 12 * D * 4,
            transcendentals=tokens * (FF + HEADS * CTX),
        ),
        name="forward_part",
    )(source, own, other, gains, valid, core)


def top_kernel(widths, gather_plan, mesh_plan, start, middle_ref, own_ref, other_ref, drawn_ref, gains_ref, horizon_ref, core_ref, *refs):
    dmiddle_ref, send_ref, keep_ref, gain_ref, loss_ref, count_ref = refs[:6]
    weight_ref, head_ref, turned_ref, final_ref, dlogits_ref = refs[6:11]
    normed_ref, inner_ref, slope_ref, dinner_ref, dout_ref, last_ref, sum_ref = refs[11:18]
    targets_ref, counted_ref = refs[18:]
    tokens = middle_ref.shape[0]
    gain_final = gains_ref[2 * LAYERS : 2 * LAYERS + 1, :]
    gain_ffn = gains_ref[2 * LAYERS - 1 : 2 * LAYERS, :]
    place_weights(
        [(weight_ref, 0), (weight_ref, FF), (head_ref, 0)],
        own_ref,
        other_ref,
        core_ref[0],
        widths,
        gather_plan,
        start,
    )
    turned_ref[...] = head_ref[...].T
    samples = tokens // SEG
    targets_ref[...] = jnp.concatenate([drawn_ref[at] for at in range(samples)], axis=1)
    position = lax.broadcasted_iota(jnp.int32, (1, SEG), 1)
    counted_ref[...] = jnp.concatenate(
        [jnp.where(position < horizon_ref[at], 1.0, 0.0) for at in range(samples)], axis=1
    )
    count_ref[...] = jnp.sum(counted_ref[...], axis=1, keepdims=True)
    for block in range(tokens // ROWS):
        rows = slice(block * ROWS, (block + 1) * ROWS)
        middle = middle_ref[rows, :]
        normed = (middle * inverse_rms(middle) * gain_ffn).astype(jnp.bfloat16)
        normed_ref[rows, :] = normed
        for part in range(FF // D):
            columns = slice(part * D, (part + 1) * D)
            inner = dot_nn(normed, weight_ref[:, columns])
            for piece in range(GROUP):
                there = slice(block * ROWS + piece * CTX, block * ROWS + (piece + 1) * CTX)
                active, slope = gelu_parts(inner[piece * CTX : (piece + 1) * CTX])
                inner_ref[there, columns] = active.astype(jnp.bfloat16)
                slope_ref[there, columns] = slope
        last = middle + dot_nt(inner_ref[rows, :], weight_ref[:, FF : 2 * FF])
        last_ref[rows, :] = last
        final_ref[rows, :] = (last * inverse_rms(last) * gain_final).astype(jnp.bfloat16)
    span = D
    loss = jnp.zeros((1, span), jnp.float32)
    spots = lax.broadcasted_iota(jnp.int32, (CLASSES, span), 0)
    for part in range(tokens // span):
        columns = slice(part * span, (part + 1) * span)
        counted = counted_ref[0:1, columns]
        final = final_ref[columns, :]
        for quarter in range(VOCAB // D):
            logits = dot_nt(turned_ref[quarter * D : (quarter + 1) * D, :], final)
            for inside in range(D // CLASSES):
                group = quarter * (D // CLASSES) + inside
                values = logits[inside * CLASSES : (inside + 1) * CLASSES]
                shifted = values - jnp.max(values, axis=0, keepdims=True)
                exponent = jnp.exp2(shifted * log2_e)
                total = jnp.sum(exponent, axis=0, keepdims=True)
                hot = spots == targets_ref[group : group + 1, columns]
                chosen = jnp.sum(jnp.where(hot, shifted, 0.0), axis=0, keepdims=True)
                loss = loss + counted * (jnp.log(total) - chosen)
                chance = exponent * (1.0 / total)
                slope = (chance - jnp.where(hot, 1.0, 0.0)) * counted
                dlogits_ref[group * CLASSES : (group + 1) * CLASSES, columns] = slope.astype(
                    jnp.bfloat16
                )
    loss_ref[...] = jnp.sum(loss, axis=1, keepdims=True)
    sum_ref[:, 2 * FF :] = dot_nt(final_ref[...].T, dlogits_ref[...])
    dfinal = dot_nn(head_ref[...], dlogits_ref[...]).T
    last = last_ref[...]
    dlast, gain_part = rms_back(last, inverse_rms(last), gain_final, dfinal)
    gain_ref[1:2, :] = gain_part
    last_ref[...] = dlast
    gain_sum = jnp.zeros((1, D), jnp.float32)
    for block in range(tokens // ROWS):
        rows = slice(block * ROWS, (block + 1) * ROWS)
        upstream = last_ref[rows, :]
        dout = upstream.astype(jnp.bfloat16)
        dout_ref[rows, :] = dout
        for part in range(FF // D):
            columns = slice(part * D, (part + 1) * D)
            dact = dot_nn(dout, weight_ref[:, FF + part * D : FF + (part + 1) * D])
            dinner_ref[rows, columns] = (dact * slope_ref[rows, columns]).astype(jnp.bfloat16)
        dnormed = dot_nt(dinner_ref[rows, :], weight_ref[:, 0:FF])
        middle = middle_ref[rows, :]
        through, gain_part = rms_back(middle, inverse_rms(middle), gain_ffn, dnormed)
        gain_sum = gain_sum + gain_part
        dmiddle_ref[rows, :] = upstream + through
    gain_ref[0:1, :] = gain_sum
    sum_ref[:, 0:FF] = dot_nn(normed_ref[...].T, dinner_ref[...])
    sum_ref[:, FF : 2 * FF] = dot_nn(dout_ref[...].T, inner_ref[...])
    write_blocks(send_ref, keep_ref, sum_ref, core_ref[0], widths, mesh_plan)


def block_outs(own, widths):
    shape = jax.ShapeDtypeStruct
    blocks = own.shape[:2] + (sum(widths),)
    return [shape(blocks, jnp.bfloat16), shape(blocks, jnp.float32)]


def run_top(widths, gather_plan, mesh_plan, start, middle, own, other, targets, gains, horizon, core):
    tokens = middle.shape[0]
    f32, b16 = jnp.float32, jnp.bfloat16
    shape = jax.ShapeDtypeStruct
    vmem = pl.BlockSpec(memory_space=pltpu.VMEM)
    return pl.pallas_call(
        functools.partial(top_kernel, widths, gather_plan, mesh_plan, start),
        in_specs=[vmem] * 5 + [smem_spec()] * 2,
        out_specs=[vmem] * 6,
        out_shape=[shape((tokens, D), f32)]
        + block_outs(own, widths)
        + [shape((2, D), f32), shape((1, 1), f32), shape((1, 1), f32)],
        scratch_shapes=[
            pltpu.VMEM((D, 2 * FF), b16),
            pltpu.VMEM((D, VOCAB), b16),
            pltpu.VMEM((VOCAB, D), b16),
            pltpu.VMEM((tokens, D), b16),
            pltpu.VMEM((VOCAB, tokens), b16),
            pltpu.VMEM((tokens, D), b16),
            pltpu.VMEM((tokens, FF), b16),
            pltpu.VMEM((tokens, FF), f32),
            pltpu.VMEM((tokens, FF), b16),
            pltpu.VMEM((tokens, D), b16),
            pltpu.VMEM((tokens, D), f32),
            pltpu.VMEM((D, 2 * FF + VOCAB), f32),
            pltpu.VMEM((CATS, tokens), jnp.int32),
            pltpu.VMEM((1, tokens), f32),
        ],
        compiler_params=pltpu.CompilerParams(vmem_limit_bytes=VMEM_BYTES),
        cost_estimate=pl.CostEstimate(
            flops=6 * tokens * D * 3 * FF,
            bytes_accessed=tokens * D * 8 + D * 3 * FF * 10,
            transcendentals=tokens * (FF + VOCAB),
        ),
        name="loss_part",
    )(middle, own, other, targets, gains, horizon, core)


def backward_kernel(layer, widths, mesh_plan, *refs):
    entry_ref, qkv_ref, mix_ref, chance_ref, dmiddle_ref, att_ref, gains_ref, core_ref = refs[:8]
    if layer == 0:
        latent_ref, send_ref, keep_ref, gain_ref = refs[8:12]
        att_kept, before_kept, sum_ref = refs[12:16], refs[16:18], refs[18]
    else:
        before_ref, ffn_ref, slope_ref, inner_hbm, out_ref, send_ref, keep_ref, gain_ref = refs[8:16]
        att_kept, before_kept, sum_ref = refs[16:20], refs[20:23], refs[23]
        inner_ref, inner_sem = refs[24:26]
        copy = pltpu.make_async_copy(inner_hbm, inner_ref, inner_sem)
    step = pl.program_id(0)

    def here(start, length, unit=CTX):
        base = step * (GROUP * unit)
        return pl.ds(pl.multiple_of(base + start, 16), length)

    @pl.when(step == 0)
    def _():
        gain_ref[...] = jnp.zeros_like(gain_ref)
        if layer > 0:
            copy.start()

    dentry, gain_part = attend_back(
        step,
        here,
        (entry_ref[...], qkv_ref, mix_ref, chance_ref),
        dmiddle_ref[...],
        gains_ref[layer : layer + 1, :],
        att_ref,
        head_masks(),
        att_kept,
    )
    gain_ref[0:1, :] += gain_part
    if layer == 0:
        before_kept[0][here(0, ROWS), :] = dentry.astype(jnp.bfloat16)
        one_hot_rows(latent_ref, before_kept[1], pl.multiple_of(step * ROWS, ROWS))
    else:
        dbefore, gain_part = feed_back(
            here,
            dentry,
            before_ref[...],
            gains_ref[LAYERS + layer - 1 : LAYERS + layer, :],
            ffn_ref,
            slope_ref,
            before_kept,
        )
        out_ref[...] = dbefore
        gain_ref[1:2, :] += gain_part

    @pl.when(step == pl.num_programs(0) - 1)
    def _():
        normed_ref, dattend_ref, dqkv_ref, mixes_ref = att_kept
        att = [(normed_ref, dqkv_ref), (mixes_ref, dattend_ref)]
        if layer == 0:
            pairs = att + [(before_kept[0], before_kept[1])]
        else:
            copy.wait()
            normed_two_ref, dinner_ref, dout_ref = before_kept
            pairs = [(normed_two_ref, dinner_ref), (dout_ref, inner_ref)] + att
        column = 0
        for left, right in pairs:
            wide = right.shape[1]
            sum_ref[:, column : column + wide] = dot_nn(left[...].T, right[...])
            column += wide
        write_blocks(send_ref, keep_ref, sum_ref, core_ref[0], widths, mesh_plan)


def run_backward(layer, widths, mesh_plan, blocks_like, saved, dmiddle, gains, core, before):
    entry, _, qkv, mix, chance, weights = saved[:6]
    tokens = entry.shape[0]
    queries = chance.shape[3] // (HEADS // 2)
    short = tokens // CTX * queries
    f32, b16 = jnp.float32, jnp.bfloat16
    shape = jax.ShapeDtypeStruct
    in_specs = [
        row_spec(D),
        row_spec(3 * D),
        row_spec(D, GROUP * queries),
        chance_spec(queries),
        row_spec(D, GROUP * queries),
        whole_spec(weights.shape),
        whole_spec(gains.shape),
        smem_spec(),
    ]
    operands = [entry, qkv, mix, chance, dmiddle, weights, gains, core]
    blocks = block_outs(blocks_like, widths)
    outs = [(item, whole_spec(item.shape)) for item in blocks]
    outs.append((shape((2, D), f32), whole_spec((2, D))))
    scratch = [
        pltpu.VMEM((tokens, D), b16),
        pltpu.VMEM((short, D), b16),
        pltpu.VMEM((tokens, 3 * D), b16),
        pltpu.VMEM((short, D), b16),
    ]
    if layer == 0:
        in_specs.append(latent_spec())
        operands.append(before)
        scratch = scratch + [pltpu.VMEM((tokens, D), b16), pltpu.VMEM((tokens, VOCAB), b16)]
        wide = 4 * D + VOCAB
    else:
        in_specs = in_specs + [row_spec(D), whole_spec(before[1].shape), row_spec(FF)]
        in_specs.append(pl.BlockSpec(memory_space=pl.ANY))
        operands = operands + list(before)
        outs.insert(0, (shape((tokens, D), f32), row_spec(D)))
        scratch = scratch + [
            pltpu.VMEM((tokens, D), b16),
            pltpu.VMEM((tokens, FF), b16),
            pltpu.VMEM((tokens, D), b16),
        ]
        wide = 4 * D + 2 * FF
    scratch.append(pltpu.VMEM((D, wide), f32))
    if layer > 0:
        scratch = scratch + [pltpu.VMEM((tokens, FF), b16), pltpu.SemaphoreType.DMA]
    return pl.pallas_call(
        functools.partial(backward_kernel, layer, widths, mesh_plan),
        grid=(tokens // ROWS,),
        in_specs=in_specs,
        out_specs=[spec for _, spec in outs],
        out_shape=[item for item, _ in outs],
        scratch_shapes=scratch,
        compiler_params=pltpu.CompilerParams(vmem_limit_bytes=VMEM_BYTES),
        cost_estimate=pl.CostEstimate(
            flops=6 * tokens * D * wide,
            bytes_accessed=tokens * D * 24 + D * wide * 6,
            transcendentals=tokens * FF,
        ),
        name="backward_part",
    )(*operands)


def pack_kernel(*refs):
    qkv_ref, out_ref, up_ref, down_ref, embed_ref, head_ref = refs[:6]
    low = lambda value: value.astype(jnp.bfloat16)
    att = [[low(qkv_ref[at]), low(out_ref[at].T)] for at in range(LAYERS)]
    ffn = [[low(up_ref[at]), low(down_ref[at])] for at in range(LAYERS)]
    pieces = [
        att[0] + [low(embed_ref[...])],
        ffn[0] + att[1],
        ffn[1] + att[2] + ffn[2] + [low(head_ref[...])],
    ]
    for target, piece in zip(refs[6:], pieces):
        target[...] = jnp.concatenate(piece, axis=1)


def run_pack(masters, chunk_widths):
    vmem = pl.BlockSpec(memory_space=pltpu.VMEM)
    rows = masters[0].shape[1]
    return pl.pallas_call(
        pack_kernel,
        in_specs=[vmem] * 6,
        out_specs=[vmem] * 3,
        out_shape=[
            jax.ShapeDtypeStruct((rows, sum(widths)), jnp.bfloat16) for widths in chunk_widths
        ],
        name="pack",
    )(*masters)


def matrix_plan(widths):
    order = [
        (2, 2), (3, 2), (5, 0), (2, 1), (3, 1), (0, 2), (1, 2),
        (2, 0), (3, 0), (0, 1), (1, 1), (0, 0), (1, 0), (4, 0),
    ]
    plan, column = {}, 0
    for which, layer in order:
        plan[(which, layer)] = (column, widths[which])
        column += widths[which]
    return plan, column


def matrix_list():
    return [(which, layer) for which in range(4) for layer in range(LAYERS)] + [(4, 0), (5, 0)]


MATRICES = 4 * LAYERS + 2
LANES = 128
INNER_ROWS = 16
COMMON_ROWS = 16
ROW_IS_INNER = [True, True, True, False, False, True]


def master_of(masters, which, layer):
    if which == 1:
        return masters[1][layer].T
    return masters[which][layer] if which < 4 else masters[which][...]


def old_row(refs, which, layer):
    return refs[which][layer : layer + 1, :] if which < 4 else refs[which][...]


LATE = [(0, 0), (1, 0), (4, 0)]
EDGE = INNER_ROWS + COMMON_ROWS


def whole_sum(value):
    return jnp.sum(jnp.sum(value, axis=1, keepdims=True), axis=0, keepdims=True)


def square_sums(raw, chosen, plan, first):
    square = raw * raw
    rows = square.shape[0]
    inner, entries = [], []
    for item in matrix_list():
        if item in chosen:
            column, width = plan[item]
            part = square[:, column - first : column - first + width]
            inner.append(jnp.sum(part, axis=1, keepdims=True))
        else:
            inner.append(jnp.zeros((rows, 1), jnp.float32))
        entries.append(jnp.sum(inner[-1], axis=0, keepdims=True))
    inner.append(jnp.zeros((rows, LANES - MATRICES), jnp.float32))
    return jnp.concatenate(inner, axis=1).T, entries, jnp.sum(square, axis=0, keepdims=True)


def store_row(target_ref, row, values):
    total = values.shape[1]
    for at, start in enumerate(range(0, total, LANES)):
        stop = min(start + LANES, total)
        target_ref[row + at : row + at + 1, 0 : stop - start] = values[:, start:stop]


def load_row(source_ref, row, total):
    return jnp.concatenate(
        [
            source_ref[row + at : row + at + 1, 0 : min(LANES, total - start)]
            for at, start in enumerate(range(0, total, LANES))
        ],
        axis=1,
    )


def late_row(widths):
    _, total = matrix_plan(widths)
    late = sum(widths[which] for which, _ in LATE)
    return EDGE + -(-(total - late) // LANES)


def packet_rows(widths):
    late = sum(widths[which] for which, _ in LATE)
    return -(-(late_row(widths) + -(-late // LANES)) // 8) * 8


def early_kernel(widths, *refs):
    raw_ref, masters, row_refs = refs[0], refs[1:7], refs[7:13]
    gains_at, loss_ref, count_ref, packet_ref = refs[13:16], refs[16], refs[17], refs[18]
    plan, _ = matrix_plan(widths)
    chosen = [item for item in matrix_list() if item not in LATE]
    inner, entries, outer = square_sums(raw_ref[...], chosen, plan, 0)
    weights, row_sums = [], []
    for which, layer in matrix_list():
        master = masters[which][layer] if which < 4 else masters[which][...]
        weights.append(whole_sum(master * master))
        row_sums.append(whole_sum(old_row(row_refs, which, layer)))
    packet_ref[...] = jnp.zeros_like(packet_ref)
    packet_ref[0:INNER_ROWS, 0 : inner.shape[1]] = inner[0:INNER_ROWS, :]
    top, two, one = [ref[...] for ref in gains_at]
    gain = jnp.concatenate(
        [jnp.zeros((1, D), jnp.float32), one[0:1], two[0:1], one[1:2], two[1:2], top], axis=0
    )
    scalars = [loss_ref[...], count_ref[...]] + weights + entries + row_sums
    scalars.append(jnp.zeros((1, LANES - len(scalars)), jnp.float32))
    at = INNER_ROWS
    packet_ref[at : at + 7, :] = gain[:, 0:LANES]
    packet_ref[at + 7 : at + 8, :] = jnp.concatenate(scalars, axis=1)
    packet_ref[at + 8 : at + 15, :] = gain[:, LANES:]
    store_row(packet_ref, EDGE, outer)


def late_kernel(widths, early_ref, raw_ref, gain_ref, packet_ref):
    plan, total = matrix_plan(widths)
    inner, entries, outer = square_sums(raw_ref[...], LATE, plan, total - raw_ref.shape[1])
    packet_ref[...] = early_ref[...]
    packet_ref[0:INNER_ROWS, 0 : inner.shape[1]] += inner[0:INNER_ROWS, :]
    at = INNER_ROWS
    packet_ref[at : at + 1, :] = gain_ref[0:1, 0:LANES]
    packet_ref[at + 8 : at + 9, :] = gain_ref[0:1, LANES:]
    before = jnp.zeros((1, 2 + MATRICES), jnp.float32)
    behind = jnp.zeros((1, LANES - 2 - 2 * MATRICES), jnp.float32)
    packet_ref[at + 7 : at + 8, :] += jnp.concatenate([before] + entries + [behind], axis=1)
    store_row(packet_ref, late_row(widths), outer)


def run_early(widths, raw, masters, rows, gain_parts, loss, count):
    vmem = pl.BlockSpec(memory_space=pltpu.VMEM)
    operands = [raw] + masters + rows + gain_parts + [loss, count]
    return pl.pallas_call(
        functools.partial(early_kernel, widths),
        in_specs=[vmem] * len(operands),
        out_specs=vmem,
        out_shape=jax.ShapeDtypeStruct((packet_rows(widths), LANES), jnp.float32),
        name="early_statistics",
    )(*operands)


def run_late(widths, packet, raw, gain_part):
    vmem = pl.BlockSpec(memory_space=pltpu.VMEM)
    return pl.pallas_call(
        functools.partial(late_kernel, widths),
        in_specs=[vmem] * 3,
        out_specs=vmem,
        out_shape=jax.ShapeDtypeStruct(packet.shape, jnp.float32),
        name="late_statistics",
    )(packet, raw, gain_part)


def update_kernel(widths, sizes, *refs):
    packet_ref, raw_early, raw_late = refs[:3]
    masters, inner_refs, outer_refs = refs[3:9], refs[9:15], refs[15:21]
    gains_ref, second_ref = refs[21:23]
    outs = refs[23:]
    outer_count, inner_count = sizes
    plan, total = matrix_plan(widths)
    rows = raw_early.shape[0]
    at = INNER_ROWS
    scalars = packet_ref[at + 7 : at + 8, :]
    pick = lambda at: scalars[:, at : at + 1]
    gain_sum = jnp.concatenate(
        [packet_ref[at : at + 7, :], packet_ref[at + 8 : at + 15, :]], axis=1
    )
    gain_square = jnp.sum(jnp.sum(gain_sum * gain_sum, axis=1, keepdims=True), axis=0, keepdims=True)
    square_total = gain_square
    for at in range(MATRICES):
        square_total = square_total + pick(2 + MATRICES + at)
    count_total = pick(1)
    norm_value = jnp.sqrt(square_total) / count_total
    scaling = jnp.minimum(1.0, clip_limit / norm_value) / count_total
    square_scale = scaling * scaling
    early = raw_early.shape[1]
    outer_early = load_row(packet_ref, EDGE, early)
    outer_late = load_row(packet_ref, late_row(widths), total - early)
    inner_new = []
    for at, (which, layer) in enumerate(matrix_list()):
        outer_length = widths[which] * outer_count
        inner_new.append(
            decay_two * old_row(inner_refs, which, layer)
            + (1 - decay_two)
            * (square_scale * packet_ref[at : at + 1, 0:rows] / outer_length + tiny_term)
        )
    stacked = jnp.concatenate(inner_new, axis=0)
    stacked = jnp.concatenate([stacked, jnp.ones((LANES - MATRICES, rows), jnp.float32)], axis=0)
    if rows < LANES:
        stacked = jnp.concatenate([stacked, jnp.ones((LANES, LANES - rows), jnp.float32)], axis=1)
    turned = lax.rsqrt(stacked).T
    outs[0][...] = pick(0)
    outs[1][...] = count_total
    outs[2][...] = norm_value
    first_out = {4: 3, 0: 7, 1: 11, 2: 15, 3: 19, 5: 23}
    for at, (which, layer) in enumerate(matrix_list()):
        column, width = plan[(which, layer)]
        outer_length, inner_length = width * outer_count, rows * inner_count
        row_length = inner_length if ROW_IS_INNER[which] else outer_length
        copies = outer_count if ROW_IS_INNER[which] else inner_count
        entries = outer_length * inner_length
        if column < early:
            raw = raw_early[:, column : column + width]
            outer_total = outer_early[:, column : column + width]
        else:
            raw = raw_late[:, column - early : column - early + width]
            outer_total = outer_late[:, column - early : column - early + width]
        outer_new = decay_two * old_row(outer_refs, which, layer) + (1 - decay_two) * (
            square_scale * outer_total / inner_length + tiny_term
        )
        mean_rows = decay_two * (pick(2 + 2 * MATRICES + at) / (copies * row_length)) + (
            1 - decay_two
        ) * (square_scale * pick(2 + MATRICES + at) / entries + tiny_term)
        factor = step_rate * jnp.sqrt(pick(2 + at) / entries) * jnp.sqrt(mean_rows)
        grad = raw * scaling
        updated = master_of(masters, which, layer) - grad * (
            turned[0:rows, at : at + 1] * (factor * lax.rsqrt(outer_new))
        )
        first = first_out[which]
        row_new, column_new = (
            (inner_new[at], outer_new) if ROW_IS_INNER[which] else (outer_new, inner_new[at])
        )
        if which < 4:
            if which == 1:
                updated, grad = updated.T, grad.T
            outs[first][layer] = updated
            outs[first + 1][layer] = grad
            outs[first + 2][layer : layer + 1, :] = row_new
            outs[first + 3][layer : layer + 1, :] = column_new
        else:
            outs[first][...] = updated
            outs[first + 1][...] = grad
            outs[first + 2][...] = row_new
            outs[first + 3][...] = column_new
    gain_grad = gain_sum * scaling
    second_new = decay_two * second_ref[...] + (1 - decay_two) * (gain_grad * gain_grad + tiny_term)
    gains = gains_ref[...]
    spread = jnp.sqrt(jnp.mean(gains * gains, axis=-1, keepdims=True))
    outs[27][...] = gains - step_rate * spread * gain_grad * lax.rsqrt(second_new)
    outs[28][...] = gain_grad
    outs[29][...] = second_new


def run_update(widths, sizes, packet, raw_early, raw_late, masters, inner, outer, gains, second):
    vmem = pl.BlockSpec(memory_space=pltpu.VMEM)
    operands = [packet, raw_early, raw_late] + masters + inner + outer + [gains, second]
    shapes = [(1, 1)] * 3
    for which in [4, 0, 1, 2, 3, 5]:
        shapes = shapes + [masters[which].shape] * 2
        pair = [inner[which].shape, outer[which].shape]
        shapes = shapes + (pair if ROW_IS_INNER[which] else pair[::-1])
    shapes = shapes + [gains.shape] * 3
    return pl.pallas_call(
        functools.partial(update_kernel, widths, sizes),
        in_specs=[vmem] * len(operands),
        out_specs=[vmem] * len(shapes),
        out_shape=[jax.ShapeDtypeStruct(item, jnp.float32) for item in shapes],
        name="update",
    )(*operands)


def swap(value, mask):
    count = lax.axis_size("dp") * lax.axis_size("fsdp")
    return lax.ppermute(value, ("dp", "fsdp"), [(place, place ^ mask) for place in range(count)])


def device_index():
    return lax.axis_index("dp") * lax.axis_size("fsdp") + lax.axis_index("fsdp")


def step_masks(step):
    masks = []
    for digit in range(1, 1 << len(step)):
        masks.append(sum(1 << bit for at, bit in enumerate(step[::-1]) if (digit >> at) & 1))
    return masks


def tie(*values):
    return lax.optimization_barrier(values)


def behind(value, *ahead):
    return lax.optimization_barrier((value,) + ahead)[0]


class Gather:
    def __init__(self, piece, steps):
        self.held, self.steps, self.at = piece[None], steps, 0

    def send(self):
        self.others = tuple(swap(self.held, mask) for mask in step_masks(self.steps[self.at]))

    def join(self):
        step = self.steps[self.at]
        pieces = [self.held] + list(self.others)
        for at, bit in enumerate(step[::-1]):
            upper = (device_index() >> bit) & 1 == 1
            pieces = [
                jnp.where(upper, pieces[place ^ (1 << at)], pieces[place])
                for place in range(len(pieces))
            ]
        self.held = jnp.concatenate(pieces)
        self.at += 1


class Scatter:
    def __init__(self, sent, kept, steps):
        self.sent, self.kept, self.steps, self.at = (sent,), kept, steps, 0

    def send(self):
        masks = step_masks(self.steps[self.at])
        self.others = tuple(swap(sent, mask) for sent, mask in zip(self.sent, masks))

    def join(self):
        self.at += 1
        summed = self.kept
        for other in self.others:
            summed = summed + other.astype(jnp.float32)
        if self.at == len(self.steps):
            self.kept = summed
            return
        step = self.steps[self.at]
        count = 1 << len(step)
        own = 0
        for bit in step:
            own = 2 * own + ((device_index() >> bit) & 1)
        parts = summed.reshape((count, summed.shape[0] // count) + summed.shape[1:])
        if count == 2:
            self.sent = (jnp.where(own == 1, parts[0], parts[1]).astype(jnp.bfloat16),)
            self.kept = jnp.where(own == 1, parts[1], parts[0])
            return
        pick = lambda digit: lax.dynamic_index_in_dim(parts, own ^ digit, 0, keepdims=False)
        self.sent = tuple(pick(digit).astype(jnp.bfloat16) for digit in range(1, count))
        self.kept = pick(0)


def sum_packets(packet, group, inner_bits):
    masks = step_masks(group)
    others = [swap(packet, mask) for mask in masks]
    inner, outer = packet[:INNER_ROWS], packet[EDGE:]
    common = [packet[INNER_ROWS:EDGE]]
    inner, outer = [inner], [outer]
    for mask, other in zip(masks, others):
        common.append(other[INNER_ROWS:EDGE])
        if mask >> inner_bits << inner_bits == mask:
            inner.append(other[:INNER_ROWS])
        if mask >> inner_bits == 0:
            outer.append(other[EDGE:])
    tree = lambda items: (
        items[0] if len(items) == 1 else tree(
            [items[at] + items[at + 1] for at in range(0, len(items), 2)]
        )
    )
    return jnp.concatenate([tree(inner), tree(common), tree(outer)])


def merged(parts):
    whole = Scatter(None, jnp.concatenate([part.kept for part in parts], axis=2), parts[0].steps)
    whole.sent = tuple(
        jnp.concatenate(pieces, axis=2) for pieces in zip(*[part.sent for part in parts])
    )
    whole.at = parts[0].at
    return whole


def shards(
    latents,
    targets,
    horizon,
    memory_valid,
    embed,
    qkv_weight,
    out_weight,
    up_weight,
    down_weight,
    head_weight,
    gains,
    embed_rows,
    embed_cols,
    qkv_rows,
    qkv_cols,
    out_rows,
    out_cols,
    up_rows,
    up_cols,
    down_rows,
    down_cols,
    head_rows,
    head_cols,
    gain_second,
):
    samples = latents.shape[0]
    sizes = (lax.axis_size("dp"), lax.axis_size("fsdp"))
    highest = (sizes[0] * sizes[1]).bit_length() - 1
    gather_steps = [(bit,) for bit in reversed(range(3, highest))] + [(2, 1), (0,)]
    third_steps = [(4, 3)] + [(bit,) for bit in range(5, highest)] + [(2, 1), (0,)]
    scatter_steps = gather_steps[::-1]
    mesh_plan = (sizes[0], sizes[1], gather_steps)
    third_plan = (sizes[0], sizes[1], third_steps)
    core = (lax.axis_index("fsdp") & 1).astype(jnp.int32).reshape(1)

    out_turned = jnp.swapaxes(out_weight, 1, 2)
    down_turned = jnp.swapaxes(down_weight, 1, 2)
    masters = [qkv_weight, out_turned, up_weight, down_turned, embed.T, head_weight]
    widths = [qkv_weight.shape[2], out_weight.shape[2], up_weight.shape[2], down_weight.shape[1]]
    widths = widths + [embed.shape[0], head_weight.shape[1]]
    att_widths, ffn_widths = widths[0:2], widths[2:4]
    chunk_widths = [
        att_widths + widths[4:5],
        ffn_widths + att_widths,
        ffn_widths + att_widths + ffn_widths + widths[5:6],
    ]
    first, second, third = [
        Gather(piece, steps)
        for piece, steps in zip(
            run_pack(masters, chunk_widths), [gather_steps, gather_steps, third_steps]
        )
    ]
    latent_rows = latents.transpose(0, 2, 1)
    target_rows = targets.transpose(0, 2, 1)
    shared = (gains, memory_valid, core)
    back_shared = (gains, core)

    count = len(gather_steps)
    while first.at < count - 1:
        first.send()
        second.send()
        first.join()
        second.join()
    while third.at < len(third_steps) - 2:
        third.send()
        third.join()
    third.send()
    first.send()
    (other,) = first.others
    held, other, second.held = tie(first.held, other, second.held)
    second.send()
    kept = [run_forward(0, chunk_widths[0], mesh_plan, latent_rows, held, other, *shared)]
    middle, (other,), third.others = tie(kept[0][1], second.others, third.others)
    third.join()
    middle, third.held = tie(middle, third.held)
    third.send()
    kept.append(
        run_forward(1, chunk_widths[1], mesh_plan, middle, second.held, other, *shared)
    )
    middle, (other,) = tie(kept[1][1], third.others)
    kept.append(run_forward(2, chunk_widths[2], third_plan, middle, third.held, other, *shared))

    dmiddle, sent, held, gain_top, loss, counted = run_top(
        ffn_widths + widths[5:6],
        third_plan,
        mesh_plan,
        sum(ffn_widths + att_widths),
        kept[2][1],
        third.held,
        other,
        target_rows,
        gains,
        horizon,
        core,
    )
    top = Scatter(sent, held, scatter_steps)
    top.send()
    like = first.held
    before = [(kept[at][1], kept[at + 1][6], kept[at + 1][8], kept[at + 1][7]) for at in range(2)]
    dmiddle, sent, held, gain_two = run_backward(
        2, chunk_widths[1], mesh_plan, like, kept[2], dmiddle, *back_shared, before[1]
    )
    dmiddle, sent, held, top.others = tie(dmiddle, sent, held, top.others)
    two = Scatter(sent, held, scatter_steps)
    two.send()
    top.join()
    two.join()
    pair = merged([top, two])
    dmiddle, pair.sent = tie(dmiddle, pair.sent)
    pair.send()
    dmiddle, sent, held, gain_one = run_backward(
        1, chunk_widths[1], mesh_plan, like, kept[1], dmiddle, *back_shared, before[0]
    )
    dmiddle, sent, held, pair.others = tie(dmiddle, sent, held, pair.others)
    one = Scatter(sent, held, scatter_steps)
    one.send()
    pair.join()
    one.join()
    dmiddle, pair.sent, one.sent = tie(dmiddle, pair.sent, one.sent)
    one.send()
    pair.send()
    sent, held, gain_zero = run_backward(
        0, chunk_widths[0], mesh_plan, like, kept[0], dmiddle, *back_shared, latent_rows
    )
    sent, held, pair.others, one.others = tie(sent, held, pair.others, one.others)
    zero = Scatter(sent, held, scatter_steps)
    zero.send()
    one.join()
    one.send()
    pair.join()
    zero.join()
    one.others = behind(one.others, zero.sent)
    zero.send()
    one.join()
    early = merged([pair, one])
    while early.at < count:
        early.send()
        zero.others = behind(zero.others, early.sent)
        early.join()
    raw_early = early.kept[0]

    flat = lambda item: item if item.ndim == 2 else item.reshape(1, -1)
    inner = [flat(item) for item in (qkv_rows, out_rows, up_rows, down_cols, embed_cols, head_rows)]
    outer = [flat(item) for item in (qkv_cols, out_cols, up_cols, down_rows, embed_rows, head_cols)]
    row_stats = [inner[at] if ROW_IS_INNER[at] else outer[at] for at in range(6)]
    packet = run_early(
        widths, raw_early, masters, row_stats, [gain_top, gain_two, gain_one], loss, counted
    )
    while zero.at < count:
        zero.join()
        if zero.at < count:
            zero.send()
    raw_late = zero.kept[0]
    packet = run_late(widths, packet, raw_late, gain_zero)
    inner_bits = sizes[1].bit_length() - 1
    rest = list(range(3, highest))
    groups = [(0,), (2, 1)] + [tuple(rest[at : at + 2][::-1]) for at in range(0, len(rest), 2)]
    for group in groups:
        packet = sum_packets(packet, group, inner_bits)
    results = run_update(
        widths, sizes, packet, raw_early, raw_late, masters, inner, outer, gains, gain_second
    )
    results = list(results)
    for at in range(3):
        results[at] = results[at].reshape(())
    for at in (3, 4, 11, 12, 19, 20):
        results[at] = jnp.swapaxes(results[at], -1, -2)
    for at in (5, 6, 25, 26):
        results[at] = results[at].reshape(-1)
    return tuple(results)


def solution(mesh):
    return jax.shard_map(
        shards,
        mesh=mesh,
        in_specs=(
            P(("dp", "fsdp"), None, None),
            P(("dp", "fsdp"), None, None),
            P(("dp", "fsdp")),
            P(("dp", "fsdp")),
            P("dp", "fsdp"),
            P(None, "fsdp", "dp"),
            P(None, "fsdp", "dp"),
            P(None, "fsdp", "dp"),
            P(None, "dp", "fsdp"),
            P("fsdp", "dp"),
            P(),
            P("dp"),
            P("fsdp"),
            P(None, "fsdp"),
            P(None, "dp"),
            P(None, "fsdp"),
            P(None, "dp"),
            P(None, "fsdp"),
            P(None, "dp"),
            P(None, "dp"),
            P(None, "fsdp"),
            P("fsdp"),
            P("dp"),
            P(),
        ),
        out_specs=(
            P(),
            P(),
            P(),
            P("dp", "fsdp"),
            P("dp", "fsdp"),
            P("dp"),
            P("fsdp"),
            P(None, "fsdp", "dp"),
            P(None, "fsdp", "dp"),
            P(None, "fsdp"),
            P(None, "dp"),
            P(None, "fsdp", "dp"),
            P(None, "fsdp", "dp"),
            P(None, "fsdp"),
            P(None, "dp"),
            P(None, "fsdp", "dp"),
            P(None, "fsdp", "dp"),
            P(None, "fsdp"),
            P(None, "dp"),
            P(None, "dp", "fsdp"),
            P(None, "dp", "fsdp"),
            P(None, "dp"),
            P(None, "fsdp"),
            P("fsdp", "dp"),
            P("fsdp", "dp"),
            P("fsdp"),
            P("dp"),
            P(),
            P(),
            P(),
        ),
        check_vma=False,
    )
```

```python
import functools

import jax
import jax.numpy as jnp
from jax import lax
from jax.experimental import pallas as pl
from jax.experimental.pallas import tpu as pltpu
from jax.sharding import PartitionSpec as P

D = 256
HEADS = 8
HEAD = D // HEADS
FF = 1024
CATS = 32
CLASSES = 32
LAYERS = 3
SEG = 48
MEM = 48
CTX = 96
VOCAB = 1024
GROUP = 4
ROWS = GROUP * CTX
HALF = D // 2
VMEM_BYTES = 24 * 1024 * 1024

decay_two = 0.9
step_rate = 0.3
clip_limit = 0.05
tiny_term = 1e-30
norm_eps = 1e-06
masked_score = -1e30
log2_e = 1.4426950408889634
score_scale = HEAD ** (-0.5)
gelu_one = 0.7978845608028654
gelu_two = 0.044715


def dot_nn(left, right):
    return lax.dot_general(
        left, right, (((1,), (0,)), ((), ())), preferred_element_type=jnp.float32
    )


def dot_nt(left, right):
    return lax.dot_general(
        left, right, (((1,), (1,)), ((), ())), preferred_element_type=jnp.float32
    )


def dot_tn(left, right):
    return lax.dot_general(
        left, right, (((0,), (0,)), ((), ())), preferred_element_type=jnp.float32
    )


def inverse_rms(values):
    return lax.rsqrt(jnp.mean(values * values, axis=-1, keepdims=True) + norm_eps)


def rms_back(values, inverse, gain_row, upstream):
    normed = values * inverse
    scaled = upstream * gain_row
    inner = jnp.mean(scaled * normed, axis=-1, keepdims=True)
    return (
        inverse * (scaled - normed * inner),
        jnp.sum(upstream * normed, axis=0, keepdims=True),
    )


def head_masks():
    lane = lax.broadcasted_iota(jnp.int32, (1, D // 2), 1) // HEAD
    return [lane == head for head in range(HEADS // 2)]


def expand_heads(rows, masks):
    return jnp.concatenate([rows * mask.astype(rows.dtype) for mask in masks], axis=0)


def collapse_heads(spread, rows, masks):
    product = dot_tn(spread, rows)
    queries = product.shape[0] // len(masks)
    taken = product[(len(masks) - 1) * queries :]
    for at, mask in enumerate(masks[:-1]):
        taken = jnp.where(mask, product[at * queries : (at + 1) * queries], taken)
    return taken


def half_of(part, side):
    start = part * D + side * HALF
    return slice(start, start + HALF)


def fill_bias(bias_ref):
    spread = bias_ref.shape[2]
    queries = spread // (HEADS // 2)
    key_at = lax.broadcasted_iota(jnp.int32, (CTX, spread), 0)
    query_at = lax.broadcasted_iota(jnp.int32, (CTX, spread), 1) % queries + (CTX - queries)
    later = key_at > query_at
    crosses = (query_at >= MEM) & (key_at < MEM)
    bias_ref[0] = jnp.where(later | crosses, masked_score, 0.0)
    bias_ref[1] = jnp.where(later, masked_score, 0.0)


def block_place(device, steps):
    place, weight = 0, 1
    for step in steps[:-1]:
        digit = 0
        for bit in step:
            digit = 2 * digit + ((device >> bit) & 1)
        place += digit * weight
        weight <<= len(step)
    return place


def place_weights(targets, own_ref, other_ref, core, widths, mesh_plan, start=0):
    outer_count, inner_count, steps = mesh_plan
    rows = own_ref.shape[1]
    for high in range(inner_count // 2):
        for source, side in ((own_ref, core), (other_ref, 1 - core)):
            here = pl.ds(pl.multiple_of((2 * high + side) * rows, rows), rows)
            at = start
            for (target, column), width in zip(targets, widths):
                block = [
                    source[
                        block_place(outer * inner_count + 2 * high, steps), :, at : at + width
                    ]
                    for outer in range(outer_count)
                ]
                target[here, column : column + width * outer_count] = jnp.concatenate(
                    block, axis=1
                )
                at += width


def write_blocks(send_ref, keep_ref, sum_ref, core, widths, mesh_plan):
    outer_count, inner_count, steps = mesh_plan
    rows = keep_ref.shape[1]
    for high in range(inner_count // 2):
        for target, side in ((keep_ref, core), (send_ref, 1 - core)):
            here = pl.ds(pl.multiple_of((2 * high + side) * rows, rows), rows)
            taken = sum_ref[here, :]
            for outer in range(outer_count):
                block, column = [], 0
                for width in widths:
                    block.append(taken[:, column + outer * width : column + (outer + 1) * width])
                    column += width * outer_count
                target[block_place(outer * inner_count + 2 * high, steps)] = jnp.concatenate(
                    block, axis=1
                ).astype(target.dtype)


def one_hot_rows(latent_ref, hot_ref, first):
    spot = lax.broadcasted_iota(jnp.int32, (CATS, VOCAB), 1) // CLASSES
    group = lax.broadcasted_iota(jnp.int32, (CATS, VOCAB), 0)
    spreader = jnp.where(spot == group, 1.0, 0.0).astype(jnp.bfloat16)
    classes = (lax.broadcasted_iota(jnp.int32, (1, VOCAB), 1) % CLASSES).astype(jnp.float32)
    for sample in range(GROUP):
        drawn = dot_tn(latent_ref[sample].astype(jnp.float32).astype(jnp.bfloat16), spreader)
        hot_ref[pl.ds(first + sample * CTX, CTX), :] = jnp.where(
            drawn == classes, 1.0, 0.0
        ).astype(jnp.bfloat16)


def tail_rows(values, queries):
    if queries == CTX:
        return values
    return jnp.concatenate(
        [
            values[(sample + 1) * CTX - queries : (sample + 1) * CTX]
            for sample in range(values.shape[0] // CTX)
        ],
        axis=0,
    )


def attend_forward(step, hidden, gain_row, weight_ref, valid_ref, bias_ref, masks, refs):
    middle_ref, qkv_ref, mix_ref, chance_ref = refs
    queries = chance_ref.shape[3] // (HEADS // 2)
    normed = (hidden * inverse_rms(hidden) * gain_row).astype(jnp.bfloat16)
    qkv_ref[...] = dot_nn(normed, weight_ref[:, 0 : 3 * D]).astype(jnp.bfloat16)
    units = [(sample, side) for sample in range(GROUP) for side in range(2)]
    scores = []
    for sample, side in units:
        rows = slice(sample * CTX, (sample + 1) * CTX)
        tail = slice((sample + 1) * CTX - queries, (sample + 1) * CTX)
        spread = expand_heads(qkv_ref[tail, half_of(0, side)], masks)
        scores.append(dot_nt(qkv_ref[rows, half_of(1, side)], spread))
    for (sample, side), score in zip(units, scores):
        score = score + bias_ref[valid_ref[step * GROUP + sample]]
        peak = jnp.max(score, axis=0, keepdims=True)
        exponent = jnp.exp2((score - peak) * (score_scale * log2_e))
        total = jnp.sum(exponent, axis=0, keepdims=True)
        chance_ref[sample, side] = (exponent * (1.0 / total)).astype(jnp.bfloat16)
    for sample, side in units:
        rows = slice(sample * CTX, (sample + 1) * CTX)
        mix_ref[sample * queries : (sample + 1) * queries, half_of(0, side)] = collapse_heads(
            chance_ref[sample, side], qkv_ref[rows, half_of(2, side)], masks
        ).astype(jnp.bfloat16)
    middle_ref[...] = tail_rows(hidden, queries) + dot_nn(
        mix_ref[...], weight_ref[:, 3 * D : 4 * D]
    )


def gelu_parts(value):
    square = value * value
    share = 0.5 + 0.5 * jnp.tanh(value * (gelu_one + (gelu_one * gelu_two) * square))
    active = value * share
    bent = active * (1.0 - share)
    return active, share + bent * (2.0 * gelu_one + (6.0 * gelu_one * gelu_two) * square)


def feed_forward(middle, gain_row, weight_ref, inner_ref, slope_ref):
    normed = (middle * inverse_rms(middle) * gain_row).astype(jnp.bfloat16)
    for part in range(FF // D):
        columns = slice(part * D, (part + 1) * D)
        inner = dot_nn(normed, weight_ref[:, columns])
        for sample in range(GROUP):
            rows = slice(sample * CTX, (sample + 1) * CTX)
            active, slope = gelu_parts(inner[rows])
            inner_ref[rows, columns] = active.astype(jnp.bfloat16)
            slope_ref[rows, columns] = slope.astype(jnp.bfloat16)
    return middle + dot_nt(inner_ref[...], weight_ref[:, FF : 2 * FF])


def feed_back(here, upstream, middle, gain_row, weight_ref, slope_ref, refs):
    normed_ref, dinner_ref, dout_ref = refs
    dout = upstream.astype(jnp.bfloat16)
    dout_ref[here(0, ROWS), :] = dout
    inverse = inverse_rms(middle)
    normed_ref[here(0, ROWS), :] = (middle * inverse * gain_row).astype(jnp.bfloat16)
    for part in range(FF // D):
        columns = slice(part * D, (part + 1) * D)
        dact = dot_nn(dout, weight_ref[:, FF + part * D : FF + (part + 1) * D])
        dinner_ref[here(0, ROWS), columns] = (
            dact * slope_ref[:, columns].astype(jnp.float32)
        ).astype(jnp.bfloat16)
    dnormed = dot_nt(dinner_ref[here(0, ROWS), :], weight_ref[:, 0:FF])
    through, gain_part = rms_back(middle, inverse, gain_row, dnormed)
    return upstream + through, gain_part


def attend_back(step, here, saved, dmiddle, gain_row, weight_ref, masks, refs):
    hidden, qkv_ref, mix_ref, chance_ref = saved
    normed_ref, dmiddle_ref, dqkv_ref, mixes_ref = refs
    queries = chance_ref.shape[3] // (HEADS // 2)
    short = here(0, GROUP * queries, queries)
    dattend = dmiddle.astype(jnp.bfloat16)
    dmiddle_ref[short, :] = dattend
    mixes_ref[short, :] = mix_ref[...]
    dmix = dot_nt(dattend, weight_ref[:, 3 * D : 4 * D]).astype(jnp.bfloat16)
    units = [(sample, side) for sample in range(GROUP) for side in range(2)]
    slopes, dchances, dscores = [], [], []
    for sample, side in units:
        rows = slice(sample * CTX, (sample + 1) * CTX)
        slopes.append(
            expand_heads(
                dmix[sample * queries : (sample + 1) * queries, half_of(0, side)], masks
            )
        )
        dchances.append(dot_nt(qkv_ref[rows, half_of(2, side)], slopes[-1]))
    for (sample, side), dchance in zip(units, dchances):
        chance = chance_ref[sample, side].astype(jnp.float32)
        weighed = chance * dchance
        dscores.append(
            (weighed - chance * jnp.sum(weighed, axis=0, keepdims=True)).astype(jnp.bfloat16)
        )
    for at, (sample, side) in enumerate(units):
        rows = slice(sample * CTX, (sample + 1) * CTX)
        tail = slice((sample + 1) * CTX - queries, (sample + 1) * CTX)
        there = here(sample * CTX, CTX)
        spread = expand_heads(qkv_ref[tail, half_of(0, side)], masks)
        keys = qkv_ref[rows, half_of(1, side)]
        dvalues = dot_nn(chance_ref[sample, side], slopes[at])
        dkeys = dot_nn(dscores[at], spread) * score_scale
        dqueries = (collapse_heads(dscores[at], keys, masks) * score_scale).astype(jnp.bfloat16)
        if queries < CTX:
            nothing = jnp.zeros((CTX - queries, HALF), jnp.bfloat16)
            dqueries = jnp.concatenate([nothing, dqueries], axis=0)
        dqkv_ref[there, half_of(0, side)] = dqueries
        dqkv_ref[there, half_of(1, side)] = dkeys.astype(jnp.bfloat16)
        dqkv_ref[there, half_of(2, side)] = dvalues.astype(jnp.bfloat16)
    inverse = inverse_rms(hidden)
    normed_ref[here(0, ROWS), :] = (hidden * inverse * gain_row).astype(jnp.bfloat16)
    dnormed = dot_nt(dqkv_ref[here(0, ROWS), :], weight_ref[:, 0 : 3 * D])
    through, gain_part = rms_back(hidden, inverse, gain_row, dnormed)
    if queries < CTX:
        nothing = jnp.zeros((CTX - queries, D), jnp.float32)
        pieces = []
        for sample in range(GROUP):
            pieces = pieces + [nothing, dmiddle[sample * queries : (sample + 1) * queries]]
        dmiddle = jnp.concatenate(pieces, axis=0)
    return dmiddle + through, gain_part


def vmem_bytes(blocks, share=1.0):
    return int(VMEM_BYTES * share) if blocks.shape[1] >= 64 else 2 * VMEM_BYTES


def row_spec(width, rows=ROWS):
    return pl.BlockSpec((rows, width), lambda step: (step, 0))


def chance_spec(queries):
    return pl.BlockSpec((GROUP, 2, CTX, HEADS // 2 * queries), lambda step: (step, 0, 0, 0))


def latent_spec():
    return pl.BlockSpec((GROUP, CATS, CTX), lambda step: (step, 0, 0))


def whole_spec(shape):
    return pl.BlockSpec(shape, lambda step: (0,) * len(shape))


def smem_spec():
    return pl.BlockSpec(memory_space=pltpu.SMEM)


def forward_kernel(layer, widths, mesh_plan, source_ref, own_ref, other_ref, gains_ref, valid_ref, core_ref, *refs):
    entry_ref, att_ref, before_ref = refs[0], refs[5], refs[6]
    bias_ref = refs[7] if layer == 0 else refs[9]
    step = pl.program_id(0)

    @pl.when(step == 0)
    def _():
        fill_bias(bias_ref)
        att = [(att_ref, 0), (att_ref, 3 * D)]
        before = [(before_ref, 0)] if layer == 0 else [(before_ref, 0), (before_ref, FF)]
        targets = att + before if layer == 0 else before + att
        place_weights(targets, own_ref, other_ref, core_ref[0] & 1, widths[: len(targets)], mesh_plan)

    if layer == 0:
        one_hot_rows(source_ref, refs[8], 0)
        hidden = dot_nt(refs[8][...], before_ref[...])
    else:
        gain_ffn = gains_ref[LAYERS + layer - 1 : LAYERS + layer, :]
        hidden = feed_forward(source_ref[...], gain_ffn, before_ref, refs[7], refs[8])
    entry_ref[...] = hidden
    attend_forward(
        step,
        hidden,
        gains_ref[layer : layer + 1, :],
        att_ref,
        valid_ref,
        bias_ref,
        head_masks(),
        refs[1:5],
    )


def run_forward(layer, widths, mesh_plan, source, own, other, gains, valid, core):
    tokens = valid.shape[0] * CTX
    queries = SEG if layer == LAYERS - 1 else CTX
    f32, b16 = jnp.float32, jnp.bfloat16
    shape = jax.ShapeDtypeStruct
    short = tokens // CTX * queries
    outs = [
        (shape((tokens, D), f32), row_spec(D)),
        (shape((short, D), f32), row_spec(D, GROUP * queries)),
        (shape((tokens, 3 * D), b16), row_spec(3 * D)),
        (shape((short, D), b16), row_spec(D, GROUP * queries)),
        (
            (shape if layer == LAYERS - 1 else pltpu.HBM)(
                (tokens // CTX, 2, CTX, HEADS // 2 * queries), b16
            ),
            chance_spec(queries),
        ),
        (shape((D, 4 * D), b16), whole_spec((D, 4 * D))),
    ]
    scratch = [pltpu.VMEM((2, CTX, HEADS // 2 * queries), f32)]
    if layer == 0:
        scratch = [pltpu.VMEM((D, VOCAB), b16)] + scratch + [pltpu.VMEM((ROWS, VOCAB), b16)]
        source_spec = latent_spec()
    else:
        source_spec = row_spec(D)
        outs.append((shape((D, 2 * FF), b16), whole_spec((D, 2 * FF))))
        outs = outs + [(pltpu.HBM((tokens, FF), b16), row_spec(FF))] * 2
    return pl.pallas_call(
        functools.partial(forward_kernel, layer, widths, mesh_plan),
        grid=(tokens // ROWS,),
        in_specs=[
            source_spec,
            whole_spec(own.shape),
            whole_spec(other.shape),
            whole_spec(gains.shape),
            smem_spec(),
            smem_spec(),
        ],
        out_specs=[spec for _, spec in outs],
        out_shape=[item for item, _ in outs],
        scratch_shapes=scratch,
        compiler_params=pltpu.CompilerParams(vmem_limit_bytes=vmem_bytes(own, 0.6)),
        cost_estimate=pl.CostEstimate(
            flops=2 * tokens * D * 12 * D,
            bytes_accessed=tokens * D * 16 + D * 12 * D * 4,
            transcendentals=tokens * (FF + HEADS * CTX),
        ),
        name="forward_part",
    )(source, own, other, gains, valid, core)


def top_kernel(widths, gather_plan, mesh_plan, start, middle_ref, own_ref, other_ref, drawn_ref, gains_ref, horizon_ref, core_ref, *refs):
    dmiddle_ref, send_ref, keep_ref, gain_ref, loss_ref, count_ref = refs[:6]
    weight_ref, head_ref, turned_ref, final_ref, dlogits_ref = refs[6:11]
    normed_ref, inner_ref, slope_ref, dinner_ref, dout_ref, last_ref, sum_ref = refs[11:18]
    targets_ref, counted_ref = refs[18:]
    tokens = middle_ref.shape[0]
    gain_final = gains_ref[2 * LAYERS : 2 * LAYERS + 1, :]
    gain_ffn = gains_ref[2 * LAYERS - 1 : 2 * LAYERS, :]
    place_weights(
        [(weight_ref, 0), (weight_ref, FF), (head_ref, 0)],
        own_ref,
        other_ref,
        core_ref[0] & 1,
        widths,
        gather_plan,
        start,
    )
    turned_ref[...] = head_ref[...].T
    samples = tokens // SEG
    targets_ref[...] = jnp.concatenate([drawn_ref[at] for at in range(samples)], axis=1)
    position = lax.broadcasted_iota(jnp.int32, (1, SEG), 1)
    counted_ref[...] = jnp.concatenate(
        [jnp.where(position < horizon_ref[at], 1.0, 0.0) for at in range(samples)], axis=1
    )
    count_ref[...] = jnp.sum(counted_ref[...], axis=1, keepdims=True)
    for block in range(tokens // ROWS):
        rows = slice(block * ROWS, (block + 1) * ROWS)
        middle = middle_ref[rows, :]
        normed = (middle * inverse_rms(middle) * gain_ffn).astype(jnp.bfloat16)
        normed_ref[rows, :] = normed
        for part in range(FF // D):
            columns = slice(part * D, (part + 1) * D)
            inner = dot_nn(normed, weight_ref[:, columns])
            for piece in range(GROUP):
                there = slice(block * ROWS + piece * CTX, block * ROWS + (piece + 1) * CTX)
                active, slope = gelu_parts(inner[piece * CTX : (piece + 1) * CTX])
                inner_ref[there, columns] = active.astype(jnp.bfloat16)
                slope_ref[there, columns] = slope
        last = middle + dot_nt(inner_ref[rows, :], weight_ref[:, FF : 2 * FF])
        last_ref[rows, :] = last
        final_ref[rows, :] = (last * inverse_rms(last) * gain_final).astype(jnp.bfloat16)
    span = D
    loss = jnp.zeros((1, span), jnp.float32)
    spots = lax.broadcasted_iota(jnp.int32, (CLASSES, span), 0)
    for part in range(tokens // span):
        columns = slice(part * span, (part + 1) * span)
        counted = counted_ref[0:1, columns]
        final = final_ref[columns, :]
        for quarter in range(VOCAB // D):
            logits = dot_nt(turned_ref[quarter * D : (quarter + 1) * D, :], final)
            for inside in range(D // CLASSES):
                group = quarter * (D // CLASSES) + inside
                values = logits[inside * CLASSES : (inside + 1) * CLASSES]
                shifted = values - jnp.max(values, axis=0, keepdims=True)
                exponent = jnp.exp2(shifted * log2_e)
                total = jnp.sum(exponent, axis=0, keepdims=True)
                hot = spots == targets_ref[group : group + 1, columns]
                chosen = jnp.sum(jnp.where(hot, shifted, 0.0), axis=0, keepdims=True)
                loss = loss + counted * (jnp.log(total) - chosen)
                chance = exponent * (1.0 / total)
                slope = (chance - jnp.where(hot, 1.0, 0.0)) * counted
                dlogits_ref[group * CLASSES : (group + 1) * CLASSES, columns] = slope.astype(
                    jnp.bfloat16
                )
    loss_ref[...] = jnp.sum(loss, axis=1, keepdims=True)
    sum_ref[:, 2 * FF :] = dot_nt(final_ref[...].T, dlogits_ref[...])
    dfinal = dot_nn(head_ref[...], dlogits_ref[...]).T
    last = last_ref[...]
    dlast, gain_part = rms_back(last, inverse_rms(last), gain_final, dfinal)
    gain_ref[1:2, :] = gain_part
    last_ref[...] = dlast
    gain_sum = jnp.zeros((1, D), jnp.float32)
    for block in range(tokens // ROWS):
        rows = slice(block * ROWS, (block + 1) * ROWS)
        upstream = last_ref[rows, :]
        dout = upstream.astype(jnp.bfloat16)
        dout_ref[rows, :] = dout
        for part in range(FF // D):
            columns = slice(part * D, (part + 1) * D)
            dact = dot_nn(dout, weight_ref[:, FF + part * D : FF + (part + 1) * D])
            dinner_ref[rows, columns] = (dact * slope_ref[rows, columns]).astype(jnp.bfloat16)
        dnormed = dot_nt(dinner_ref[rows, :], weight_ref[:, 0:FF])
        middle = middle_ref[rows, :]
        through, gain_part = rms_back(middle, inverse_rms(middle), gain_ffn, dnormed)
        gain_sum = gain_sum + gain_part
        dmiddle_ref[rows, :] = upstream + through
    gain_ref[0:1, :] = gain_sum
    sum_ref[:, 0:FF] = dot_nn(normed_ref[...].T, dinner_ref[...])
    sum_ref[:, FF : 2 * FF] = dot_nn(dout_ref[...].T, inner_ref[...])
    write_blocks(send_ref, keep_ref, sum_ref, core_ref[0] & 1, widths, mesh_plan)


def block_outs(own, widths):
    shape = jax.ShapeDtypeStruct
    blocks = own.shape[:2] + (sum(widths),)
    return [shape(blocks, jnp.bfloat16), shape(blocks, jnp.float32)]


def run_top(widths, gather_plan, mesh_plan, start, middle, own, other, targets, gains, horizon, core):
    tokens = middle.shape[0]
    f32, b16 = jnp.float32, jnp.bfloat16
    shape = jax.ShapeDtypeStruct
    vmem = pl.BlockSpec(memory_space=pltpu.VMEM)
    return pl.pallas_call(
        functools.partial(top_kernel, widths, gather_plan, mesh_plan, start),
        in_specs=[vmem] * 5 + [smem_spec()] * 2,
        out_specs=[vmem] * 6,
        out_shape=[shape((tokens, D), f32)]
        + block_outs(own, widths)
        + [shape((2, D), f32), shape((1, 1), f32), shape((1, 1), f32)],
        scratch_shapes=[
            pltpu.VMEM((D, 2 * FF), b16),
            pltpu.VMEM((D, VOCAB), b16),
            pltpu.VMEM((VOCAB, D), b16),
            pltpu.VMEM((tokens, D), b16),
            pltpu.VMEM((VOCAB, tokens), b16),
            pltpu.VMEM((tokens, D), b16),
            pltpu.VMEM((tokens, FF), b16),
            pltpu.VMEM((tokens, FF), f32),
            pltpu.VMEM((tokens, FF), b16),
            pltpu.VMEM((tokens, D), b16),
            pltpu.VMEM((tokens, D), f32),
            pltpu.VMEM((D, 2 * FF + VOCAB), f32),
            pltpu.VMEM((CATS, tokens), jnp.int32),
            pltpu.VMEM((1, tokens), f32),
        ],
        compiler_params=pltpu.CompilerParams(vmem_limit_bytes=vmem_bytes(own)),
        cost_estimate=pl.CostEstimate(
            flops=6 * tokens * D * 3 * FF,
            bytes_accessed=tokens * D * 8 + D * 3 * FF * 10,
            transcendentals=tokens * (FF + VOCAB),
        ),
        name="loss_part",
    )(middle, own, other, targets, gains, horizon, core)


def backward_kernel(layer, widths, mesh_plan, *refs):
    entry_ref, qkv_ref, mix_ref, chance_ref, dmiddle_ref, att_ref, gains_ref, core_ref = refs[:8]
    if layer == 0:
        latent_ref, send_ref, keep_ref, gain_ref = refs[8:12]
        att_kept, before_kept, sum_ref = refs[12:16], refs[16:18], refs[18]
    else:
        before_ref, ffn_ref, slope_ref, inner_hbm, out_ref, send_ref, keep_ref, gain_ref = refs[8:16]
        att_kept, before_kept, sum_ref = refs[16:20], refs[20:23], refs[23]
        inner_ref, inner_sem = refs[24:26]
        copy = pltpu.make_async_copy(inner_hbm, inner_ref, inner_sem)
    step = pl.program_id(0)

    def here(start, length, unit=CTX):
        base = step * (GROUP * unit)
        return pl.ds(pl.multiple_of(base + start, 16), length)

    @pl.when(step == 0)
    def _():
        gain_ref[...] = jnp.zeros_like(gain_ref)
        if layer > 0:
            copy.start()

    dentry, gain_part = attend_back(
        step,
        here,
        (entry_ref[...], qkv_ref, mix_ref, chance_ref),
        dmiddle_ref[...],
        gains_ref[layer : layer + 1, :],
        att_ref,
        head_masks(),
        att_kept,
    )
    gain_ref[0:1, :] += gain_part
    if layer == 0:
        before_kept[0][here(0, ROWS), :] = dentry.astype(jnp.bfloat16)
        one_hot_rows(latent_ref, before_kept[1], pl.multiple_of(step * ROWS, ROWS))
    else:
        dbefore, gain_part = feed_back(
            here,
            dentry,
            before_ref[...],
            gains_ref[LAYERS + layer - 1 : LAYERS + layer, :],
            ffn_ref,
            slope_ref,
            before_kept,
        )
        out_ref[...] = dbefore
        gain_ref[1:2, :] += gain_part

    @pl.when(step == pl.num_programs(0) - 1)
    def _():
        normed_ref, dattend_ref, dqkv_ref, mixes_ref = att_kept
        att = [(normed_ref, dqkv_ref), (mixes_ref, dattend_ref)]
        if layer == 0:
            pairs = att + [(before_kept[0], before_kept[1])]
        else:
            copy.wait()
            normed_two_ref, dinner_ref, dout_ref = before_kept
            pairs = [(normed_two_ref, dinner_ref), (dout_ref, inner_ref)] + att
        column = 0
        for left, right in pairs:
            wide = right.shape[1]
            sum_ref[:, column : column + wide] = dot_nn(left[...].T, right[...])
            column += wide
        write_blocks(send_ref, keep_ref, sum_ref, core_ref[0] & 1, widths, mesh_plan)


def run_backward(layer, widths, mesh_plan, blocks_like, saved, dmiddle, gains, core, before):
    entry, _, qkv, mix, chance, weights = saved[:6]
    tokens = entry.shape[0]
    queries = chance.shape[3] // (HEADS // 2)
    short = tokens // CTX * queries
    f32, b16 = jnp.float32, jnp.bfloat16
    shape = jax.ShapeDtypeStruct
    in_hbm = lambda item: pltpu.with_memory_space_constraint(item, pltpu.HBM)
    if layer < LAYERS - 1:
        chance = in_hbm(chance)
    if layer > 0:
        before = before[:2] + (in_hbm(before[2]), in_hbm(before[3]))
    in_specs = [
        row_spec(D),
        row_spec(3 * D),
        row_spec(D, GROUP * queries),
        chance_spec(queries),
        row_spec(D, GROUP * queries),
        whole_spec(weights.shape),
        whole_spec(gains.shape),
        smem_spec(),
    ]
    operands = [entry, qkv, mix, chance, dmiddle, weights, gains, core]
    blocks = block_outs(blocks_like, widths)
    outs = [(item, whole_spec(item.shape)) for item in blocks]
    outs.append((shape((2, D), f32), whole_spec((2, D))))
    scratch = [
        pltpu.VMEM((tokens, D), b16),
        pltpu.VMEM((short, D), b16),
        pltpu.VMEM((tokens, 3 * D), b16),
        pltpu.VMEM((short, D), b16),
    ]
    if layer == 0:
        in_specs.append(latent_spec())
        operands.append(before)
        scratch = scratch + [pltpu.VMEM((tokens, D), b16), pltpu.VMEM((tokens, VOCAB), b16)]
        wide = 4 * D + VOCAB
    else:
        in_specs = in_specs + [row_spec(D), whole_spec(before[1].shape), row_spec(FF)]
        in_specs.append(pl.BlockSpec(memory_space=pl.ANY))
        operands = operands + list(before)
        outs.insert(0, (shape((tokens, D), f32), row_spec(D)))
        scratch = scratch + [
            pltpu.VMEM((tokens, D), b16),
            pltpu.VMEM((tokens, FF), b16),
            pltpu.VMEM((tokens, D), b16),
        ]
        wide = 4 * D + 2 * FF
    scratch.append(pltpu.VMEM((D, wide), f32))
    if layer > 0:
        scratch = scratch + [pltpu.VMEM((tokens, FF), b16), pltpu.SemaphoreType.DMA]
    return pl.pallas_call(
        functools.partial(backward_kernel, layer, widths, mesh_plan),
        grid=(tokens // ROWS,),
        in_specs=in_specs,
        out_specs=[spec for _, spec in outs],
        out_shape=[item for item, _ in outs],
        scratch_shapes=scratch,
        compiler_params=pltpu.CompilerParams(vmem_limit_bytes=vmem_bytes(blocks_like)),
        cost_estimate=pl.CostEstimate(
            flops=6 * tokens * D * wide,
            bytes_accessed=tokens * D * 24 + D * wide * 6,
            transcendentals=tokens * FF,
        ),
        name="backward_part",
    )(*operands)


def pack_kernel(*refs):
    qkv_ref, out_ref, up_ref, down_ref, embed_ref, head_ref = refs[:6]
    low = lambda value: value.astype(jnp.bfloat16)
    att = [[low(qkv_ref[at]), low(out_ref[at].T)] for at in range(LAYERS)]
    ffn = [[low(up_ref[at]), low(down_ref[at])] for at in range(LAYERS)]
    pieces = [
        att[0] + [low(embed_ref[...])],
        ffn[0] + att[1],
        ffn[1] + att[2] + ffn[2] + [low(head_ref[...])],
    ]
    for target, piece in zip(refs[6:], pieces):
        target[...] = jnp.concatenate(piece, axis=1)


def run_pack(masters, chunk_widths):
    vmem = pl.BlockSpec(memory_space=pltpu.VMEM)
    rows = masters[0].shape[1]
    return pl.pallas_call(
        pack_kernel,
        in_specs=[vmem] * 6,
        out_specs=[vmem] * 3,
        out_shape=[
            jax.ShapeDtypeStruct((rows, sum(widths)), jnp.bfloat16) for widths in chunk_widths
        ],
        name="pack",
    )(*masters)


def matrix_plan(widths):
    order = [
        (2, 2), (3, 2), (5, 0), (2, 1), (3, 1), (0, 2), (1, 2),
        (2, 0), (3, 0), (0, 1), (1, 1), (0, 0), (1, 0), (4, 0),
    ]
    plan, column = {}, 0
    for which, layer in order:
        plan[(which, layer)] = (column, widths[which])
        column += widths[which]
    return plan, column


def matrix_list():
    return [(which, layer) for which in range(4) for layer in range(LAYERS)] + [(4, 0), (5, 0)]


MATRICES = 4 * LAYERS + 2
LANES = 128
INNER_ROWS = 16
COMMON_ROWS = 16
ROW_IS_INNER = [True, True, True, False, False, True]


def master_of(masters, which, layer):
    if which == 1:
        return masters[1][layer].T
    return masters[which][layer] if which < 4 else masters[which][...]


def old_row(refs, which, layer):
    return refs[which][layer : layer + 1, :] if which < 4 else refs[which][...]


LATE = [(0, 0), (1, 0), (4, 0)]
EDGE = INNER_ROWS + COMMON_ROWS


def whole_sum(value):
    return jnp.sum(jnp.sum(value, axis=1, keepdims=True), axis=0, keepdims=True)


def square_sums(raw, chosen, plan, first):
    square = raw * raw
    rows = square.shape[0]
    inner, entries = [], []
    for item in matrix_list():
        if item in chosen:
            column, width = plan[item]
            part = square[:, column - first : column - first + width]
            inner.append(jnp.sum(part, axis=1, keepdims=True))
        else:
            inner.append(jnp.zeros((rows, 1), jnp.float32))
        entries.append(jnp.sum(inner[-1], axis=0, keepdims=True))
    inner.append(jnp.zeros((rows, LANES - MATRICES), jnp.float32))
    return jnp.concatenate(inner, axis=1).T, entries, jnp.sum(square, axis=0, keepdims=True)


def store_row(target_ref, row, values):
    total = values.shape[1]
    for at, start in enumerate(range(0, total, LANES)):
        stop = min(start + LANES, total)
        target_ref[row + at : row + at + 1, 0 : stop - start] = values[:, start:stop]


def load_row(source_ref, row, total):
    return jnp.concatenate(
        [
            source_ref[row + at : row + at + 1, 0 : min(LANES, total - start)]
            for at, start in enumerate(range(0, total, LANES))
        ],
        axis=1,
    )


def late_row(widths):
    _, total = matrix_plan(widths)
    late = sum(widths[which] for which, _ in LATE)
    return EDGE + -(-(total - late) // LANES)


def packet_rows(widths):
    late = sum(widths[which] for which, _ in LATE)
    return -(-(late_row(widths) + -(-late // LANES)) // 8) * 8


def early_kernel(widths, *refs):
    raw_ref, masters, row_refs = refs[0], refs[1:7], refs[7:13]
    gains_at, loss_ref, count_ref, packet_ref = refs[13:16], refs[16], refs[17], refs[18]
    plan, _ = matrix_plan(widths)
    chosen = [item for item in matrix_list() if item not in LATE]
    inner, entries, outer = square_sums(raw_ref[...], chosen, plan, 0)
    weights, row_sums = [], []
    for which, layer in matrix_list():
        master = masters[which][layer] if which < 4 else masters[which][...]
        weights.append(whole_sum(master * master))
        row_sums.append(whole_sum(old_row(row_refs, which, layer)))
    packet_ref[...] = jnp.zeros_like(packet_ref)
    packet_ref[0:INNER_ROWS, 0 : inner.shape[1]] = inner[0:INNER_ROWS, :]
    top, two, one = [ref[...] for ref in gains_at]
    gain = jnp.concatenate(
        [jnp.zeros((1, D), jnp.float32), one[0:1], two[0:1], one[1:2], two[1:2], top], axis=0
    )
    scalars = [loss_ref[...], count_ref[...]] + weights + entries + row_sums
    scalars.append(jnp.zeros((1, LANES - len(scalars)), jnp.float32))
    at = INNER_ROWS
    packet_ref[at : at + 7, :] = gain[:, 0:LANES]
    packet_ref[at + 7 : at + 8, :] = jnp.concatenate(scalars, axis=1)
    packet_ref[at + 8 : at + 15, :] = gain[:, LANES:]
    store_row(packet_ref, EDGE, outer)


def late_kernel(widths, early_ref, raw_ref, gain_ref, packet_ref):
    plan, total = matrix_plan(widths)
    inner, entries, outer = square_sums(raw_ref[...], LATE, plan, total - raw_ref.shape[1])
    packet_ref[...] = early_ref[...]
    packet_ref[0:INNER_ROWS, 0 : inner.shape[1]] += inner[0:INNER_ROWS, :]
    at = INNER_ROWS
    packet_ref[at : at + 1, :] = gain_ref[0:1, 0:LANES]
    packet_ref[at + 8 : at + 9, :] = gain_ref[0:1, LANES:]
    before = jnp.zeros((1, 2 + MATRICES), jnp.float32)
    behind = jnp.zeros((1, LANES - 2 - 2 * MATRICES), jnp.float32)
    packet_ref[at + 7 : at + 8, :] += jnp.concatenate([before] + entries + [behind], axis=1)
    store_row(packet_ref, late_row(widths), outer)


def run_early(widths, raw, masters, rows, gain_parts, loss, count):
    vmem = pl.BlockSpec(memory_space=pltpu.VMEM)
    operands = [raw] + masters + rows + gain_parts + [loss, count]
    return pl.pallas_call(
        functools.partial(early_kernel, widths),
        in_specs=[vmem] * len(operands),
        out_specs=vmem,
        out_shape=jax.ShapeDtypeStruct((packet_rows(widths), LANES), jnp.float32),
        name="early_statistics",
    )(*operands)


def run_late(widths, packet, raw, gain_part):
    vmem = pl.BlockSpec(memory_space=pltpu.VMEM)
    return pl.pallas_call(
        functools.partial(late_kernel, widths),
        in_specs=[vmem] * 3,
        out_specs=vmem,
        out_shape=jax.ShapeDtypeStruct(packet.shape, jnp.float32),
        name="late_statistics",
    )(packet, raw, gain_part)


def update_kernel(widths, sizes, *refs):
    packet_ref, raw_early, raw_late = refs[:3]
    masters, inner_refs, outer_refs = refs[3:9], refs[9:15], refs[15:21]
    gains_ref, second_ref = refs[21:23]
    outs = refs[23:]
    outer_count, inner_count = sizes
    plan, total = matrix_plan(widths)
    rows = raw_early.shape[0]
    at = INNER_ROWS
    scalars = packet_ref[at + 7 : at + 8, :]
    pick = lambda at: scalars[:, at : at + 1]
    gain_sum = jnp.concatenate(
        [packet_ref[at : at + 7, :], packet_ref[at + 8 : at + 15, :]], axis=1
    )
    gain_square = jnp.sum(jnp.sum(gain_sum * gain_sum, axis=1, keepdims=True), axis=0, keepdims=True)
    square_total = gain_square
    for at in range(MATRICES):
        square_total = square_total + pick(2 + MATRICES + at)
    count_total = pick(1)
    norm_value = jnp.sqrt(square_total) / count_total
    scaling = jnp.minimum(1.0, clip_limit / norm_value) / count_total
    square_scale = scaling * scaling
    early = raw_early.shape[1]
    outer_early = load_row(packet_ref, EDGE, early)
    outer_late = load_row(packet_ref, late_row(widths), total - early)
    inner_new = []
    for at, (which, layer) in enumerate(matrix_list()):
        outer_length = widths[which] * outer_count
        inner_new.append(
            decay_two * old_row(inner_refs, which, layer)
            + (1 - decay_two)
            * (square_scale * packet_ref[at : at + 1, 0:rows] / outer_length + tiny_term)
        )
    stacked = jnp.concatenate(inner_new, axis=0)
    stacked = jnp.concatenate([stacked, jnp.ones((LANES - MATRICES, rows), jnp.float32)], axis=0)
    if rows < LANES:
        stacked = jnp.concatenate([stacked, jnp.ones((LANES, LANES - rows), jnp.float32)], axis=1)
    turned = lax.rsqrt(stacked).T
    outs[0][...] = pick(0)
    outs[1][...] = count_total
    outs[2][...] = norm_value
    first_out = {4: 3, 0: 7, 1: 11, 2: 15, 3: 19, 5: 23}
    for at, (which, layer) in enumerate(matrix_list()):
        column, width = plan[(which, layer)]
        outer_length, inner_length = width * outer_count, rows * inner_count
        row_length = inner_length if ROW_IS_INNER[which] else outer_length
        copies = outer_count if ROW_IS_INNER[which] else inner_count
        entries = outer_length * inner_length
        if column < early:
            raw = raw_early[:, column : column + width]
            outer_total = outer_early[:, column : column + width]
        else:
            raw = raw_late[:, column - early : column - early + width]
            outer_total = outer_late[:, column - early : column - early + width]
        outer_new = decay_two * old_row(outer_refs, which, layer) + (1 - decay_two) * (
            square_scale * outer_total / inner_length + tiny_term
        )
        mean_rows = decay_two * (pick(2 + 2 * MATRICES + at) / (copies * row_length)) + (
            1 - decay_two
        ) * (square_scale * pick(2 + MATRICES + at) / entries + tiny_term)
        factor = step_rate * jnp.sqrt(pick(2 + at) / entries) * jnp.sqrt(mean_rows)
        grad = raw * scaling
        updated = master_of(masters, which, layer) - grad * (
            turned[0:rows, at : at + 1] * (factor * lax.rsqrt(outer_new))
        )
        first = first_out[which]
        row_new, column_new = (
            (inner_new[at], outer_new) if ROW_IS_INNER[which] else (outer_new, inner_new[at])
        )
        if which < 4:
            if which == 1:
                updated, grad = updated.T, grad.T
            outs[first][layer] = updated
            outs[first + 1][layer] = grad
            outs[first + 2][layer : layer + 1, :] = row_new
            outs[first + 3][layer : layer + 1, :] = column_new
        else:
            outs[first][...] = updated
            outs[first + 1][...] = grad
            outs[first + 2][...] = row_new
            outs[first + 3][...] = column_new
    gain_grad = gain_sum * scaling
    second_new = decay_two * second_ref[...] + (1 - decay_two) * (gain_grad * gain_grad + tiny_term)
    gains = gains_ref[...]
    spread = jnp.sqrt(jnp.mean(gains * gains, axis=-1, keepdims=True))
    outs[27][...] = gains - step_rate * spread * gain_grad * lax.rsqrt(second_new)
    outs[28][...] = gain_grad
    outs[29][...] = second_new


def run_update(widths, sizes, packet, raw_early, raw_late, masters, inner, outer, gains, second):
    vmem = pl.BlockSpec(memory_space=pltpu.VMEM)
    operands = [packet, raw_early, raw_late] + masters + inner + outer + [gains, second]
    shapes = [(1, 1)] * 3
    for which in [4, 0, 1, 2, 3, 5]:
        shapes = shapes + [masters[which].shape] * 2
        pair = [inner[which].shape, outer[which].shape]
        shapes = shapes + (pair if ROW_IS_INNER[which] else pair[::-1])
    shapes = shapes + [gains.shape] * 3
    return pl.pallas_call(
        functools.partial(update_kernel, widths, sizes),
        in_specs=[vmem] * len(operands),
        out_specs=[vmem] * len(shapes),
        out_shape=[jax.ShapeDtypeStruct(item, jnp.float32) for item in shapes],
        name="update",
    )(*operands)


def swap(value, mask):
    count = lax.axis_size("dp") * lax.axis_size("fsdp")
    return lax.ppermute(value, ("dp", "fsdp"), [(place, place ^ mask) for place in range(count)])


def device_index():
    return lax.axis_index("dp") * lax.axis_size("fsdp") + lax.axis_index("fsdp")


def step_masks(step):
    masks = []
    for digit in range(1, 1 << len(step)):
        masks.append(sum(1 << bit for at, bit in enumerate(step[::-1]) if (digit >> at) & 1))
    return masks


def tie(*values):
    return lax.optimization_barrier(values)


def behind(value, *ahead):
    return lax.optimization_barrier((value,) + ahead)[0]


def own_digit(device_ref, step):
    digit = 0
    for bit in step:
        digit = 2 * digit + ((device_ref[0] >> bit) & 1)
    return digit


def gather_kernel(step, device_ref, *refs):
    count = 1 << len(step)
    own = own_digit(device_ref, step)
    blocks = refs[0].shape[0]
    for digit in range(count):
        base = (own ^ digit) * blocks
        for block in range(blocks):
            refs[count][base + block] = refs[digit][block]


def run_gather_join(step, pieces, device):
    vmem = pl.BlockSpec(memory_space=pltpu.VMEM)
    blocks, rows, width = pieces[0].shape
    return pl.pallas_call(
        functools.partial(gather_kernel, step),
        in_specs=[smem_spec()] + [vmem] * len(pieces),
        out_specs=vmem,
        out_shape=jax.ShapeDtypeStruct((blocks * len(pieces), rows, width), jnp.bfloat16),
        name="gather_join",
    )(device, *pieces)


def scatter_kernel(step, counts, device_ref, *refs):
    parts, at = [], 0
    for count in counts:
        parts.append(refs[at : at + 1 + count])
        at += 1 + count
    targets = refs[at:]
    own = own_digit(device_ref, step)
    blocks = targets[0].shape[0]
    for digit, target in enumerate(targets):
        base = (own ^ digit) * blocks
        for block in range(blocks):
            columns = []
            for part in parts:
                total = part[0][base + block]
                for other in part[1:]:
                    total = total + other[base + block].astype(jnp.float32)
                columns.append(total)
            target[block] = jnp.concatenate(columns, axis=1).astype(target.dtype)


def run_scatter_join(step, chunks, device):
    vmem = pl.BlockSpec(memory_space=pltpu.VMEM)
    count = 1 << len(step)
    blocks, rows, _ = chunks[0].kept.shape
    shape = (blocks // count, rows, sum(chunk.kept.shape[2] for chunk in chunks))
    operands = []
    for chunk in chunks:
        operands = operands + [chunk.kept] + list(chunk.others)
    return pl.pallas_call(
        functools.partial(scatter_kernel, step, [len(chunk.others) for chunk in chunks]),
        in_specs=[smem_spec()] + [vmem] * len(operands),
        out_specs=[vmem] * count,
        out_shape=[
            jax.ShapeDtypeStruct(shape, jnp.bfloat16 if digit else jnp.float32)
            for digit in range(count)
        ],
        name="scatter_join",
    )(device, *operands)


class Gather:
    def __init__(self, held, steps, device, at=0):
        self.held, self.steps, self.device, self.at = held, steps, device, at

    def send(self):
        self.others = tuple(swap(self.held, mask) for mask in step_masks(self.steps[self.at]))

    def join(self):
        pieces = [self.held] + list(self.others)
        self.held = run_gather_join(self.steps[self.at], pieces, self.device)
        self.at += 1


class Scatter:
    def __init__(self, sent, kept, steps, device, at=0):
        self.sent, self.kept, self.steps, self.device, self.at = sent, kept, steps, device, at

    def send(self):
        masks = step_masks(self.steps[self.at])
        self.others = tuple(swap(sent, mask) for sent, mask in zip(self.sent, masks))

    def join(self):
        joined = join_all([self])
        self.sent, self.kept, self.at = joined.sent, joined.kept, joined.at


def join_all(chunks):
    steps, at, device = chunks[0].steps, chunks[0].at + 1, chunks[0].device
    step = steps[at] if at < len(steps) else ()
    kept, *sent = run_scatter_join(step, chunks, device)
    return Scatter(tuple(sent), kept, steps, device, at)


def sum_packets(packet, group, inner_bits):
    masks = step_masks(group)
    others = [swap(packet, mask) for mask in masks]
    inner, outer = packet[:INNER_ROWS], packet[EDGE:]
    common = [packet[INNER_ROWS:EDGE]]
    inner, outer = [inner], [outer]
    for mask, other in zip(masks, others):
        common.append(other[INNER_ROWS:EDGE])
        if mask >> inner_bits << inner_bits == mask:
            inner.append(other[:INNER_ROWS])
        if mask >> inner_bits == 0:
            outer.append(other[EDGE:])
    tree = lambda items: (
        items[0] if len(items) == 1 else tree(
            [items[at] + items[at + 1] for at in range(0, len(items), 2)]
        )
    )
    return jnp.concatenate([tree(inner), tree(common), tree(outer)])


def merged(parts):
    whole = Scatter(None, jnp.concatenate([part.kept for part in parts], axis=2), parts[0].steps)
    whole.sent = tuple(
        jnp.concatenate(pieces, axis=2) for pieces in zip(*[part.sent for part in parts])
    )
    whole.at = parts[0].at
    return whole


def shards(
    latents,
    targets,
    horizon,
    memory_valid,
    embed,
    qkv_weight,
    out_weight,
    up_weight,
    down_weight,
    head_weight,
    gains,
    embed_rows,
    embed_cols,
    qkv_rows,
    qkv_cols,
    out_rows,
    out_cols,
    up_rows,
    up_cols,
    down_rows,
    down_cols,
    head_rows,
    head_cols,
    gain_second,
):
    samples = latents.shape[0]
    sizes = (lax.axis_size("dp"), lax.axis_size("fsdp"))
    highest = (sizes[0] * sizes[1]).bit_length() - 1
    gather_steps = [(bit,) for bit in reversed(range(3, highest))] + [(2, 1), (0,)]
    scatter_steps = gather_steps[::-1]
    mesh_plan = (sizes[0], sizes[1], gather_steps)
    device = device_index().astype(jnp.int32).reshape(1)
    out_turned = jnp.swapaxes(out_weight, 1, 2)
    down_turned = jnp.swapaxes(down_weight, 1, 2)
    masters = [qkv_weight, out_turned, up_weight, down_turned, embed.T, head_weight]
    widths = [qkv_weight.shape[2], out_weight.shape[2], up_weight.shape[2], down_weight.shape[1]]
    widths = widths + [embed.shape[0], head_weight.shape[1]]
    att_widths, ffn_widths = widths[0:2], widths[2:4]
    chunk_widths = [
        att_widths + widths[4:5],
        ffn_widths + att_widths,
        ffn_widths + att_widths + ffn_widths + widths[5:6],
    ]
    chunks = [
        Gather(piece[None], gather_steps, device) for piece in run_pack(masters, chunk_widths)
    ]
    first, second, third = chunks
    latent_rows = latents.transpose(0, 2, 1)
    target_rows = targets.transpose(0, 2, 1)
    shared = (gains, memory_valid, device)
    back_shared = (gains, device)

    count = len(gather_steps)
    for at in range(count - 2):
        first.send()
        second.send()
        if at == 0:
            third.send()
            first.others, second.others = tie(first.others, second.others)
        else:
            first.others, second.others, third.others = tie(
                first.others, second.others, third.others
            )
            third.join()
        first.join()
        second.join()
        if at > 0:
            first.held, second.held, third.held = tie(first.held, second.held, third.held)
            third.send()
    first.send()
    second.send()
    first.others, second.others, third.others = tie(first.others, second.others, third.others)
    first.join()
    first.send()
    second.join()
    third.join()
    third.send()
    (other,) = first.others
    held, other, second.held = tie(first.held, other, second.held)
    second.send()
    kept = [run_forward(0, chunk_widths[0], mesh_plan, latent_rows, held, other, *shared)]
    middle, (other,), third.others = tie(kept[0][1], second.others, third.others)
    third.join()
    middle, third.held = tie(middle, third.held)
    third.send()
    kept.append(
        run_forward(1, chunk_widths[1], mesh_plan, middle, second.held, other, *shared)
    )
    middle, (other,) = tie(kept[1][1], third.others)
    kept.append(run_forward(2, chunk_widths[2], mesh_plan, middle, third.held, other, *shared))

    dmiddle, sent, held, gain_top, loss, counted = run_top(
        ffn_widths + widths[5:6],
        mesh_plan,
        mesh_plan,
        sum(ffn_widths + att_widths),
        kept[2][1],
        third.held,
        other,
        target_rows,
        gains,
        horizon,
        device,
    )
    top = Scatter((sent,), held, scatter_steps, device)
    top.send()
    like = first.held
    before = [(kept[at][1], kept[at + 1][6], kept[at + 1][8], kept[at + 1][7]) for at in range(2)]
    dmiddle, sent, held, gain_two = run_backward(
        2, chunk_widths[1], mesh_plan, like, kept[2], dmiddle, *back_shared, before[1]
    )
    dmiddle, sent, held, top.others = tie(dmiddle, sent, held, top.others)
    two = Scatter((sent,), held, scatter_steps, device)
    two.send()
    pair = join_all([top, two])
    dmiddle, pair.sent = tie(dmiddle, pair.sent)
    pair.send()
    dmiddle, sent, held, gain_one = run_backward(
        1, chunk_widths[1], mesh_plan, like, kept[1], dmiddle, *back_shared, before[0]
    )
    dmiddle, sent, held, pair.others = tie(dmiddle, sent, held, pair.others)
    one = Scatter((sent,), held, scatter_steps, device)
    one.send()
    pair.join()
    one.join()
    dmiddle, pair.sent, one.sent = tie(dmiddle, pair.sent, one.sent)
    one.send()
    pair.send()
    sent, held, gain_zero = run_backward(
        0, chunk_widths[0], mesh_plan, like, kept[0], dmiddle, *back_shared, latent_rows
    )
    sent, held, pair.others, one.others = tie(sent, held, pair.others, one.others)
    zero = Scatter((sent,), held, scatter_steps, device)
    zero.send()
    one.join()
    one.send()
    while pair.at < one.at:
        pair.join()
        pair.send()
    zero.join()
    one.others = behind(one.others, zero.sent)
    zero.send()
    early = join_all([pair, one])
    while early.at < count:
        early.send()
        zero.others = behind(zero.others, early.sent)
        early.join()
    raw_early = early.kept[0]

    flat = lambda item: item if item.ndim == 2 else item.reshape(1, -1)
    inner = [flat(item) for item in (qkv_rows, out_rows, up_rows, down_cols, embed_cols, head_rows)]
    outer = [flat(item) for item in (qkv_cols, out_cols, up_cols, down_rows, embed_rows, head_cols)]
    row_stats = [inner[at] if ROW_IS_INNER[at] else outer[at] for at in range(6)]
    packet = run_early(
        widths, raw_early, masters, row_stats, [gain_top, gain_two, gain_one], loss, counted
    )
    while zero.at < count:
        zero.join()
        if zero.at < count:
            zero.send()
    raw_late = zero.kept[0]
    packet = run_late(widths, packet, raw_late, gain_zero)
    inner_bits = sizes[1].bit_length() - 1
    rest = list(range(3, highest))
    groups = [(0,), (2, 1)] + [tuple(rest[at : at + 2][::-1]) for at in range(0, len(rest), 2)]
    for group in groups:
        packet = sum_packets(packet, group, inner_bits)
    results = run_update(
        widths, sizes, packet, raw_early, raw_late, masters, inner, outer, gains, gain_second
    )
    results = list(results)
    for at in range(3):
        results[at] = results[at].reshape(())
    for at in (3, 4, 11, 12, 19, 20):
        results[at] = jnp.swapaxes(results[at], -1, -2)
    for at in (5, 6, 25, 26):
        results[at] = results[at].reshape(-1)
    return tuple(results)


def solution(mesh):
    return jax.shard_map(
        shards,
        mesh=mesh,
        in_specs=(
            P(("dp", "fsdp"), None, None),
            P(("dp", "fsdp"), None, None),
            P(("dp", "fsdp")),
            P(("dp", "fsdp")),
            P("dp", "fsdp"),
            P(None, "fsdp", "dp"),
            P(None, "fsdp", "dp"),
            P(None, "fsdp", "dp"),
            P(None, "dp", "fsdp"),
            P("fsdp", "dp"),
            P(),
            P("dp"),
            P("fsdp"),
            P(None, "fsdp"),
            P(None, "dp"),
            P(None, "fsdp"),
            P(None, "dp"),
            P(None, "fsdp"),
            P(None, "dp"),
            P(None, "dp"),
            P(None, "fsdp"),
            P("fsdp"),
            P("dp"),
            P(),
        ),
        out_specs=(
            P(),
            P(),
            P(),
            P("dp", "fsdp"),
            P("dp", "fsdp"),
            P("dp"),
            P("fsdp"),
            P(None, "fsdp", "dp"),
            P(None, "fsdp", "dp"),
            P(None, "fsdp"),
            P(None, "dp"),
            P(None, "fsdp", "dp"),
            P(None, "fsdp", "dp"),
            P(None, "fsdp"),
            P(None, "dp"),
            P(None, "fsdp", "dp"),
            P(None, "fsdp", "dp"),
            P(None, "fsdp"),
            P(None, "dp"),
            P(None, "dp", "fsdp"),
            P(None, "dp", "fsdp"),
            P(None, "dp"),
            P(None, "fsdp"),
            P("fsdp", "dp"),
            P("fsdp", "dp"),
            P("fsdp"),
            P("dp"),
            P(),
            P(),
            P(),
        ),
        check_vma=False,
    )
```

```python
import functools

import jax
import jax.numpy as jnp
from jax import lax
from jax.experimental import pallas as pl
from jax.experimental.pallas import tpu as pltpu
from jax.sharding import PartitionSpec as P

D = 256
HEADS = 8
HEAD = D // HEADS
FF = 1024
CATS = 32
CLASSES = 32
LAYERS = 3
SEG = 48
MEM = 48
CTX = 96
VOCAB = 1024
GROUP = 4
ROWS = GROUP * CTX
HALF = D // 2
VMEM_BYTES = 24 * 1024 * 1024
MIDDLE_BYTES = 46 * 1024 * 1024

decay_two = 0.9
step_rate = 0.3
clip_limit = 0.05
tiny_term = 1e-30
norm_eps = 1e-06
masked_score = -1e30
log2_e = 1.4426950408889634
score_scale = HEAD ** (-0.5)
gelu_one = 0.7978845608028654
gelu_two = 0.044715


def dot_nn(left, right):
    return lax.dot_general(
        left, right, (((1,), (0,)), ((), ())), preferred_element_type=jnp.float32
    )


def dot_nt(left, right):
    return lax.dot_general(
        left, right, (((1,), (1,)), ((), ())), preferred_element_type=jnp.float32
    )


def dot_tn(left, right):
    return lax.dot_general(
        left, right, (((0,), (0,)), ((), ())), preferred_element_type=jnp.float32
    )


def inverse_rms(values):
    return lax.rsqrt(jnp.mean(values * values, axis=-1, keepdims=True) + norm_eps)


def rms_back(values, inverse, gain_row, upstream):
    normed = values * inverse
    scaled = upstream * gain_row
    inner = jnp.mean(scaled * normed, axis=-1, keepdims=True)
    return (
        inverse * (scaled - normed * inner),
        jnp.sum(upstream * normed, axis=0, keepdims=True),
    )


def head_masks():
    lane = lax.broadcasted_iota(jnp.int32, (1, D // 2), 1) // HEAD
    return [lane == head for head in range(HEADS // 2)]


def expand_heads(rows, masks):
    return jnp.concatenate([rows * mask.astype(rows.dtype) for mask in masks], axis=0)


def collapse_heads(spread, rows, masks):
    product = dot_tn(spread, rows)
    queries = product.shape[0] // len(masks)
    taken = product[(len(masks) - 1) * queries :]
    for at, mask in enumerate(masks[:-1]):
        taken = jnp.where(mask, product[at * queries : (at + 1) * queries], taken)
    return taken


def half_of(part, side):
    start = part * D + side * HALF
    return slice(start, start + HALF)


def fill_bias(bias_ref):
    spread = bias_ref.shape[2]
    queries = spread // (HEADS // 2)
    key_at = lax.broadcasted_iota(jnp.int32, (CTX, spread), 0)
    query_at = lax.broadcasted_iota(jnp.int32, (CTX, spread), 1) % queries + (CTX - queries)
    later = key_at > query_at
    crosses = (query_at >= MEM) & (key_at < MEM)
    bias_ref[0] = jnp.where(later | crosses, masked_score, 0.0)
    bias_ref[1] = jnp.where(later, masked_score, 0.0)


def block_place(device, steps):
    place, weight = 0, 1
    for step in steps[:-1]:
        digit = 0
        for bit in step:
            digit = 2 * digit + ((device >> bit) & 1)
        place += digit * weight
        weight <<= len(step)
    return place


def place_weights(targets, own_ref, other_ref, core, widths, mesh_plan, start=0):
    outer_count, inner_count, steps = mesh_plan
    rows = own_ref.shape[1]
    for high in range(inner_count // 2):
        for source, side in ((own_ref, core), (other_ref, 1 - core)):
            here = pl.ds(pl.multiple_of((2 * high + side) * rows, rows), rows)
            at = start
            for (target, column), width in zip(targets, widths):
                block = [
                    source[
                        block_place(outer * inner_count + 2 * high, steps), :, at : at + width
                    ]
                    for outer in range(outer_count)
                ]
                target[here, column : column + width * outer_count] = jnp.concatenate(
                    block, axis=1
                )
                at += width


def write_blocks(send_ref, keep_ref, sum_ref, core, widths, mesh_plan, start=0):
    outer_count, inner_count, steps = mesh_plan
    rows = keep_ref.shape[1]
    for high in range(inner_count // 2):
        for target, side in ((keep_ref, core), (send_ref, 1 - core)):
            here = pl.ds(pl.multiple_of((2 * high + side) * rows, rows), rows)
            taken = sum_ref[here, :]
            for outer in range(outer_count):
                block, column = [], 0
                for width in widths:
                    block.append(taken[:, column + outer * width : column + (outer + 1) * width])
                    column += width * outer_count
                place = block_place(outer * inner_count + 2 * high, steps)
                target[place, :, start : start + sum(widths)] = jnp.concatenate(
                    block, axis=1
                ).astype(target.dtype)


def one_hot_rows(latent_ref, hot_ref, first):
    spot = lax.broadcasted_iota(jnp.int32, (CATS, VOCAB), 1) // CLASSES
    group = lax.broadcasted_iota(jnp.int32, (CATS, VOCAB), 0)
    spreader = jnp.where(spot == group, 1.0, 0.0).astype(jnp.bfloat16)
    classes = (lax.broadcasted_iota(jnp.int32, (1, VOCAB), 1) % CLASSES).astype(jnp.float32)
    for sample in range(GROUP):
        drawn = dot_tn(latent_ref[sample].astype(jnp.float32).astype(jnp.bfloat16), spreader)
        hot_ref[pl.ds(first + sample * CTX, CTX), :] = jnp.where(
            drawn == classes, 1.0, 0.0
        ).astype(jnp.bfloat16)


def tail_rows(values, queries):
    if queries == CTX:
        return values
    return jnp.concatenate(
        [
            values[(sample + 1) * CTX - queries : (sample + 1) * CTX]
            for sample in range(values.shape[0] // CTX)
        ],
        axis=0,
    )


def attend_forward(step, hidden, gain_row, weight_ref, valid_ref, bias_ref, masks, refs):
    middle_ref, qkv_ref, mix_ref, chance_ref = refs
    queries = chance_ref.shape[3] // (HEADS // 2)
    normed = (hidden * inverse_rms(hidden) * gain_row).astype(jnp.bfloat16)
    qkv_ref[...] = dot_nn(normed, weight_ref[:, 0 : 3 * D]).astype(jnp.bfloat16)
    units = [(sample, side) for sample in range(GROUP) for side in range(2)]
    scores = []
    for sample, side in units:
        rows = slice(sample * CTX, (sample + 1) * CTX)
        tail = slice((sample + 1) * CTX - queries, (sample + 1) * CTX)
        spread = expand_heads(qkv_ref[tail, half_of(0, side)], masks)
        scores.append(dot_nt(qkv_ref[rows, half_of(1, side)], spread))
    for (sample, side), score in zip(units, scores):
        score = score + bias_ref[valid_ref[step * GROUP + sample]]
        peak = jnp.max(score, axis=0, keepdims=True)
        exponent = jnp.exp2((score - peak) * (score_scale * log2_e))
        total = jnp.sum(exponent, axis=0, keepdims=True)
        chance_ref[sample, side] = (exponent * (1.0 / total)).astype(jnp.bfloat16)
    for sample, side in units:
        rows = slice(sample * CTX, (sample + 1) * CTX)
        mix_ref[sample * queries : (sample + 1) * queries, half_of(0, side)] = collapse_heads(
            chance_ref[sample, side], qkv_ref[rows, half_of(2, side)], masks
        ).astype(jnp.bfloat16)
    middle_ref[...] = tail_rows(hidden, queries) + dot_nn(
        mix_ref[...], weight_ref[:, 3 * D : 4 * D]
    )


def gelu_parts(value):
    square = value * value
    share = 0.5 + 0.5 * jnp.tanh(value * (gelu_one + (gelu_one * gelu_two) * square))
    active = value * share
    bent = active * (1.0 - share)
    return active, share + bent * (2.0 * gelu_one + (6.0 * gelu_one * gelu_two) * square)


def feed_forward(middle, gain_row, weight_ref, inner_ref, slope_ref):
    normed = (middle * inverse_rms(middle) * gain_row).astype(jnp.bfloat16)
    for part in range(FF // D):
        columns = slice(part * D, (part + 1) * D)
        inner = dot_nn(normed, weight_ref[:, columns])
        for sample in range(GROUP):
            rows = slice(sample * CTX, (sample + 1) * CTX)
            active, slope = gelu_parts(inner[rows])
            inner_ref[rows, columns] = active.astype(jnp.bfloat16)
            slope_ref[rows, columns] = slope.astype(jnp.bfloat16)
    return middle + dot_nt(inner_ref[...], weight_ref[:, FF : 2 * FF])


def feed_back(here, upstream, middle, gain_row, weight_ref, slope_ref, refs):
    normed_ref, dinner_ref, dout_ref = refs
    dout = upstream.astype(jnp.bfloat16)
    dout_ref[here(0, ROWS), :] = dout
    inverse = inverse_rms(middle)
    normed_ref[here(0, ROWS), :] = (middle * inverse * gain_row).astype(jnp.bfloat16)
    for part in range(FF // D):
        columns = slice(part * D, (part + 1) * D)
        dact = dot_nn(dout, weight_ref[:, FF + part * D : FF + (part + 1) * D])
        dinner_ref[here(0, ROWS), columns] = (
            dact * slope_ref[:, columns].astype(jnp.float32)
        ).astype(jnp.bfloat16)
    dnormed = dot_nt(dinner_ref[here(0, ROWS), :], weight_ref[:, 0:FF])
    through, gain_part = rms_back(middle, inverse, gain_row, dnormed)
    return upstream + through, gain_part


def attend_back(step, here, saved, dmiddle, gain_row, weight_ref, masks, refs):
    hidden, qkv_ref, mix_ref, chance_ref = saved
    normed_ref, dmiddle_ref, dqkv_ref, mixes_ref = refs
    queries = chance_ref.shape[3] // (HEADS // 2)
    short = here(0, GROUP * queries, queries)
    dattend = dmiddle.astype(jnp.bfloat16)
    dmiddle_ref[short, :] = dattend
    mixes_ref[short, :] = mix_ref[...]
    dmix = dot_nt(dattend, weight_ref[:, 3 * D : 4 * D]).astype(jnp.bfloat16)
    units = [(sample, side) for sample in range(GROUP) for side in range(2)]
    slopes, dchances, dscores = [], [], []
    for sample, side in units:
        rows = slice(sample * CTX, (sample + 1) * CTX)
        slopes.append(
            expand_heads(
                dmix[sample * queries : (sample + 1) * queries, half_of(0, side)], masks
            )
        )
        dchances.append(dot_nt(qkv_ref[rows, half_of(2, side)], slopes[-1]))
    for (sample, side), dchance in zip(units, dchances):
        chance = chance_ref[sample, side].astype(jnp.float32)
        weighed = chance * dchance
        dscores.append(
            (weighed - chance * jnp.sum(weighed, axis=0, keepdims=True)).astype(jnp.bfloat16)
        )
    for at, (sample, side) in enumerate(units):
        rows = slice(sample * CTX, (sample + 1) * CTX)
        tail = slice((sample + 1) * CTX - queries, (sample + 1) * CTX)
        there = here(sample * CTX, CTX)
        spread = expand_heads(qkv_ref[tail, half_of(0, side)], masks)
        keys = qkv_ref[rows, half_of(1, side)]
        dvalues = dot_nn(chance_ref[sample, side], slopes[at])
        dkeys = dot_nn(dscores[at], spread) * score_scale
        dqueries = (collapse_heads(dscores[at], keys, masks) * score_scale).astype(jnp.bfloat16)
        if queries < CTX:
            nothing = jnp.zeros((CTX - queries, HALF), jnp.bfloat16)
            dqueries = jnp.concatenate([nothing, dqueries], axis=0)
        dqkv_ref[there, half_of(0, side)] = dqueries
        dqkv_ref[there, half_of(1, side)] = dkeys.astype(jnp.bfloat16)
        dqkv_ref[there, half_of(2, side)] = dvalues.astype(jnp.bfloat16)
    inverse = inverse_rms(hidden)
    normed_ref[here(0, ROWS), :] = (hidden * inverse * gain_row).astype(jnp.bfloat16)
    dnormed = dot_nt(dqkv_ref[here(0, ROWS), :], weight_ref[:, 0 : 3 * D])
    through, gain_part = rms_back(hidden, inverse, gain_row, dnormed)
    if queries < CTX:
        nothing = jnp.zeros((CTX - queries, D), jnp.float32)
        pieces = []
        for sample in range(GROUP):
            pieces = pieces + [nothing, dmiddle[sample * queries : (sample + 1) * queries]]
        dmiddle = jnp.concatenate(pieces, axis=0)
    return dmiddle + through, gain_part


def row_spec(width, rows=ROWS):
    return pl.BlockSpec((rows, width), lambda step: (step, 0))


def chance_spec(queries):
    return pl.BlockSpec((GROUP, 2, CTX, HEADS // 2 * queries), lambda step: (step, 0, 0, 0))


def latent_spec():
    return pl.BlockSpec((GROUP, CATS, CTX), lambda step: (step, 0, 0))


def whole_spec(shape):
    return pl.BlockSpec(shape, lambda step: (0,) * len(shape))


def in_hbm(item):
    return pltpu.with_memory_space_constraint(item, pltpu.HBM)


def smem_spec():
    return pl.BlockSpec(memory_space=pltpu.SMEM)


def forward_kernel(layer, widths, mesh_plan, source_ref, own_ref, other_ref, gains_ref, valid_ref, core_ref, *refs):
    entry_ref, att_ref, before_ref = refs[0], refs[5], refs[6]
    bias_ref = refs[7] if layer == 0 else refs[9]
    step = pl.program_id(0)

    @pl.when(step == 0)
    def _():
        fill_bias(bias_ref)
        att = [(att_ref, 0), (att_ref, 3 * D)]
        before = [(before_ref, 0)] if layer == 0 else [(before_ref, 0), (before_ref, FF)]
        targets = att + before if layer == 0 else before + att
        place_weights(targets, own_ref, other_ref, core_ref[0], widths[: len(targets)], mesh_plan)

    if layer == 0:
        one_hot_rows(source_ref, refs[8], 0)
        hidden = dot_nt(refs[8][...], before_ref[...])
    else:
        gain_ffn = gains_ref[LAYERS + layer - 1 : LAYERS + layer, :]
        hidden = feed_forward(source_ref[...], gain_ffn, before_ref, refs[7], refs[8])
    entry_ref[...] = hidden
    attend_forward(
        step,
        hidden,
        gains_ref[layer : layer + 1, :],
        att_ref,
        valid_ref,
        bias_ref,
        head_masks(),
        refs[1:5],
    )


def run_forward(layer, widths, mesh_plan, source, own, other, gains, valid, core):
    tokens = valid.shape[0] * CTX
    f32, b16 = jnp.float32, jnp.bfloat16
    chances = HEADS // 2 * CTX
    outs = [
        (pltpu.HBM((tokens, D), f32), row_spec(D)),
        (pltpu.HBM((tokens, D), f32), row_spec(D)),
        (pltpu.HBM((tokens, 3 * D), b16), row_spec(3 * D)),
        (pltpu.HBM((tokens, D), b16), row_spec(D)),
        (pltpu.HBM((tokens // CTX, 2, CTX, chances), b16), chance_spec(CTX)),
        (pltpu.HBM((D, 4 * D), b16), whole_spec((D, 4 * D))),
    ]
    scratch = [pltpu.VMEM((2, CTX, chances), f32)]
    if layer == 0:
        scratch = [pltpu.VMEM((D, VOCAB), b16)] + scratch + [pltpu.VMEM((ROWS, VOCAB), b16)]
        source_spec = latent_spec()
    else:
        source_spec = row_spec(D)
        outs.append((pltpu.HBM((D, 2 * FF), b16), whole_spec((D, 2 * FF))))
        outs = outs + [(pltpu.HBM((tokens, FF), b16), row_spec(FF))] * 2
        source = in_hbm(source)
    return pl.pallas_call(
        functools.partial(forward_kernel, layer, widths, mesh_plan),
        grid=(tokens // ROWS,),
        in_specs=[
            source_spec,
            whole_spec(own.shape),
            whole_spec(other.shape),
            whole_spec(gains.shape),
            smem_spec(),
            smem_spec(),
        ],
        out_specs=[spec for _, spec in outs],
        out_shape=[item for item, _ in outs],
        scratch_shapes=scratch,
        compiler_params=pltpu.CompilerParams(vmem_limit_bytes=VMEM_BYTES),
        cost_estimate=pl.CostEstimate(
            flops=2 * tokens * D * 12 * D,
            bytes_accessed=tokens * D * 16 + D * 12 * D * 4,
            transcendentals=tokens * (FF + HEADS * CTX),
        ),
        name="forward_part",
    )(source, own, other, gains, valid, core)


def middle_kernel(widths, mesh_plan, *refs):
    source_ref, own_ref, other_ref, drawn_ref, gains_ref, valid_ref, horizon_ref, core_ref = refs[:8]
    out_ref, send_ref, keep_ref, gain_ref, loss_ref, count_ref = refs[8:14]
    bias_ref, weight_one_ref, att_ref, weight_two_ref, head_ref, turned_ref = refs[14:20]
    entry_ref, qkv_ref, mix_ref, chance_ref, middle_two_ref, inner_one_ref, slope_one_ref = refs[20:27]
    inner_ref, slope_ref, last_ref, dmiddle_ref, sum_ref, targets_ref, counted_ref = refs[27:34]
    normed_long, dattend_ref, dqkv_long, mixes_ref, normed_two_long, dinner_long, dout_long = refs[34:]
    tokens = middle_two_ref.shape[0]
    final_ref = normed_long.at[0:tokens]
    dlogits_ref = dqkv_long.at[0:VOCAB]
    normed_ref = normed_two_long.at[0:tokens]
    dinner_ref = dinner_long.at[0:tokens]
    dout_ref = dout_long.at[0:tokens]
    groups = source_ref.shape[0] // ROWS
    masks = head_masks()
    gain_att = gains_ref[LAYERS - 1 : LAYERS, :]
    gain_before = gains_ref[2 * LAYERS - 2 : 2 * LAYERS - 1, :]
    gain_ffn = gains_ref[2 * LAYERS - 1 : 2 * LAYERS, :]
    gain_final = gains_ref[2 * LAYERS : 2 * LAYERS + 1, :]
    fill_bias(bias_ref)
    place_weights(
        [
            (weight_one_ref, 0),
            (weight_one_ref, FF),
            (att_ref, 0),
            (att_ref, 3 * D),
            (weight_two_ref, 0),
            (weight_two_ref, FF),
            (head_ref, 0),
        ],
        own_ref,
        other_ref,
        core_ref[0],
        widths,
        mesh_plan,
    )

    def rows_of(group, unit=CTX):
        return pl.ds(pl.multiple_of(group * (GROUP * unit), GROUP * unit), GROUP * unit)

    def forward(group, carry):
        rows, short = rows_of(group), rows_of(group, SEG)
        hidden = feed_forward(
            source_ref[rows, :],
            gain_before,
            weight_one_ref,
            inner_one_ref.at[rows],
            slope_one_ref.at[rows],
        )
        entry_ref[rows, :] = hidden
        attend_forward(
            group,
            hidden,
            gain_att,
            att_ref,
            valid_ref,
            bias_ref,
            masks,
            (
                middle_two_ref.at[short],
                qkv_ref.at[rows],
                mix_ref.at[short],
                chance_ref.at[pl.ds(group * GROUP, GROUP)],
            ),
        )
        return carry

    lax.fori_loop(0, groups, forward, 0)
    turned_ref[...] = head_ref[...].T
    samples = tokens // SEG
    targets_ref[...] = jnp.concatenate([drawn_ref[at] for at in range(samples)], axis=1)
    position = lax.broadcasted_iota(jnp.int32, (1, SEG), 1)
    counted_ref[...] = jnp.concatenate(
        [jnp.where(position < horizon_ref[at], 1.0, 0.0) for at in range(samples)], axis=1
    )
    count_ref[...] = jnp.sum(counted_ref[...], axis=1, keepdims=True)
    for block in range(tokens // ROWS):
        rows = slice(block * ROWS, (block + 1) * ROWS)
        middle = middle_two_ref[rows, :]
        normed = (middle * inverse_rms(middle) * gain_ffn).astype(jnp.bfloat16)
        normed_ref[rows, :] = normed
        for part in range(FF // D):
            columns = slice(part * D, (part + 1) * D)
            inner = dot_nn(normed, weight_two_ref[:, columns])
            for piece in range(GROUP):
                there = slice(block * ROWS + piece * CTX, block * ROWS + (piece + 1) * CTX)
                active, slope = gelu_parts(inner[piece * CTX : (piece + 1) * CTX])
                inner_ref[there, columns] = active.astype(jnp.bfloat16)
                slope_ref[there, columns] = slope.astype(jnp.bfloat16)
        last = middle + dot_nt(inner_ref[rows, :], weight_two_ref[:, FF : 2 * FF])
        last_ref[rows, :] = last
        final_ref[rows, :] = (last * inverse_rms(last) * gain_final).astype(jnp.bfloat16)
    span = D
    loss = jnp.zeros((1, span), jnp.float32)
    spots = lax.broadcasted_iota(jnp.int32, (CLASSES, span), 0)
    for part in range(tokens // span):
        columns = slice(part * span, (part + 1) * span)
        counted = counted_ref[0:1, columns]
        final = final_ref[columns, :]
        for quarter in range(VOCAB // D):
            logits = dot_nt(turned_ref[quarter * D : (quarter + 1) * D, :], final)
            for inside in range(D // CLASSES):
                group = quarter * (D // CLASSES) + inside
                values = logits[inside * CLASSES : (inside + 1) * CLASSES]
                shifted = values - jnp.max(values, axis=0, keepdims=True)
                exponent = jnp.exp2(shifted * log2_e)
                total = jnp.sum(exponent, axis=0, keepdims=True)
                hot = spots == targets_ref[group : group + 1, columns]
                chosen = jnp.sum(jnp.where(hot, shifted, 0.0), axis=0, keepdims=True)
                loss = loss + counted * (jnp.log(total) - chosen)
                chance = exponent * (1.0 / total)
                slope = (chance - jnp.where(hot, 1.0, 0.0)) * counted
                dlogits_ref[group * CLASSES : (group + 1) * CLASSES, columns] = slope.astype(
                    jnp.bfloat16
                )
    loss_ref[...] = jnp.sum(loss, axis=1, keepdims=True)
    sum_ref[:, 2 * FF : 2 * FF + VOCAB] = dot_nt(final_ref[...].T, dlogits_ref[...])
    dfinal = dot_nn(head_ref[...], dlogits_ref[...]).T
    last = last_ref[...]
    dlast, gain_part = rms_back(last, inverse_rms(last), gain_final, dfinal)
    gain_ref[1:2, :] = gain_part
    last_ref[...] = dlast
    gain_sum = jnp.zeros((1, D), jnp.float32)
    for block in range(tokens // ROWS):
        rows = slice(block * ROWS, (block + 1) * ROWS)
        upstream = last_ref[rows, :]
        dout = upstream.astype(jnp.bfloat16)
        dout_ref[rows, :] = dout
        for part in range(FF // D):
            columns = slice(part * D, (part + 1) * D)
            dact = dot_nn(dout, weight_two_ref[:, FF + part * D : FF + (part + 1) * D])
            dinner_ref[rows, columns] = (dact * slope_ref[rows, columns].astype(jnp.float32)).astype(jnp.bfloat16)
        dnormed = dot_nt(dinner_ref[rows, :], weight_two_ref[:, 0:FF])
        middle = middle_two_ref[rows, :]
        through, gain_part = rms_back(middle, inverse_rms(middle), gain_ffn, dnormed)
        gain_sum = gain_sum + gain_part
        dmiddle_ref[rows, :] = upstream + through
    gain_ref[0:1, :] = gain_sum
    sum_ref[:, 0:FF] = dot_nn(normed_ref[...].T, dinner_ref[...])
    sum_ref[:, FF : 2 * FF] = dot_nn(dout_ref[...].T, inner_ref[...])
    write_blocks(send_ref, keep_ref, sum_ref, core_ref[0], widths[4:], mesh_plan)
    gain_ref[2:4, :] = jnp.zeros((2, D), jnp.float32)

    def backward(group, carry):
        rows, short = rows_of(group), rows_of(group, SEG)

        def here(start, length, unit=CTX):
            return pl.ds(pl.multiple_of(group * (GROUP * unit) + start, 16), length)

        dentry, gain_part = attend_back(
            group,
            here,
            (
                entry_ref[rows, :],
                qkv_ref.at[rows],
                mix_ref.at[short],
                chance_ref.at[pl.ds(group * GROUP, GROUP)],
            ),
            dmiddle_ref[short, :],
            gain_att,
            att_ref,
            masks,
            (normed_long, dattend_ref, dqkv_long, mixes_ref),
        )
        gain_ref[2:3, :] += gain_part
        dbefore, gain_part = feed_back(
            here,
            dentry,
            source_ref[rows, :],
            gain_before,
            weight_one_ref,
            slope_one_ref.at[rows],
            (normed_two_long, dinner_long, dout_long),
        )
        out_ref[rows, :] = dbefore
        gain_ref[3:4, :] += gain_part
        return carry

    lax.fori_loop(0, groups, backward, 0)
    column = 0
    for left, right in [
        (normed_two_long, dinner_long),
        (dout_long, inner_one_ref),
        (normed_long, dqkv_long),
        (mixes_ref, dattend_ref),
    ]:
        wide = right.shape[1]
        sum_ref[:, column : column + wide] = dot_nn(left[...].T, right[...])
        column += wide
    write_blocks(
        send_ref, keep_ref, sum_ref, core_ref[0], widths[:4], mesh_plan, sum(widths[4:])
    )


def block_outs(own, widths):
    shape = jax.ShapeDtypeStruct
    blocks = own.shape[:2] + (sum(widths),)
    return [shape(blocks, jnp.bfloat16), shape(blocks, jnp.float32)]


def run_middle(widths, mesh_plan, source, own, other, targets, gains, valid, horizon, core):
    tokens = source.shape[0]
    short = tokens // CTX * SEG
    samples = tokens // CTX
    chances = HEADS // 2 * SEG
    f32, b16 = jnp.float32, jnp.bfloat16
    shape = jax.ShapeDtypeStruct
    vmem = pl.BlockSpec(memory_space=pltpu.VMEM)
    return pl.pallas_call(
        functools.partial(middle_kernel, widths, mesh_plan),
        in_specs=[vmem] * 5 + [smem_spec()] * 3,
        out_specs=[vmem] * 6,
        out_shape=[shape((tokens, D), f32)]
        + block_outs(own, widths)
        + [shape((4, D), f32), shape((1, 1), f32), shape((1, 1), f32)],
        scratch_shapes=[
            pltpu.VMEM((2, CTX, chances), f32),
            pltpu.VMEM((D, 2 * FF), b16),
            pltpu.VMEM((D, 4 * D), b16),
            pltpu.VMEM((D, 2 * FF), b16),
            pltpu.VMEM((D, VOCAB), b16),
            pltpu.VMEM((VOCAB, D), b16),
            pltpu.VMEM((tokens, D), f32),
            pltpu.VMEM((tokens, 3 * D), b16),
            pltpu.VMEM((short, D), b16),
            pltpu.VMEM((samples, 2, CTX, chances), b16),
            pltpu.VMEM((short, D), f32),
            pltpu.VMEM((tokens, FF), b16),
            pltpu.VMEM((tokens, FF), b16),
            pltpu.VMEM((short, FF), b16),
            pltpu.VMEM((short, FF), b16),
            pltpu.VMEM((short, D), f32),
            pltpu.VMEM((short, D), f32),
            pltpu.VMEM((D, 2 * FF + max(4 * D, VOCAB)), f32),
            pltpu.VMEM((CATS, short), jnp.int32),
            pltpu.VMEM((1, short), f32),
            pltpu.VMEM((tokens, D), b16),
            pltpu.VMEM((short, D), b16),
            pltpu.VMEM((tokens, 3 * D), b16),
            pltpu.VMEM((short, D), b16),
            pltpu.VMEM((tokens, D), b16),
            pltpu.VMEM((tokens, FF), b16),
            pltpu.VMEM((tokens, D), b16),
        ],
        compiler_params=pltpu.CompilerParams(vmem_limit_bytes=MIDDLE_BYTES + (0 if own.shape[1] >= 64 else VMEM_BYTES // 2)),
        cost_estimate=pl.CostEstimate(
            flops=6 * tokens * D * 8 * FF,
            bytes_accessed=tokens * D * 8 + D * 6 * FF * 10,
            transcendentals=2 * tokens * (FF + VOCAB),
        ),
        name="middle_part",
    )(source, own, other, targets, gains, valid, horizon, core)


def backward_kernel(layer, widths, mesh_plan, *refs):
    entry_ref, qkv_ref, mix_ref, chance_ref, dmiddle_ref, att_ref, gains_ref, core_ref = refs[:8]
    if layer == 0:
        latent_ref, send_ref, keep_ref, gain_ref = refs[8:12]
        att_kept, before_kept, sum_ref = refs[12:16], refs[16:18], refs[18]
    else:
        before_ref, ffn_ref, slope_ref, inner_hbm, out_ref, send_ref, keep_ref, gain_ref = refs[8:16]
        att_kept, before_kept, sum_ref = refs[16:20], refs[20:23], refs[23]
        inner_ref, inner_sem = refs[24:26]
        copy = pltpu.make_async_copy(inner_hbm, inner_ref, inner_sem)
    step = pl.program_id(0)

    def here(start, length, unit=CTX):
        base = step * (GROUP * unit)
        return pl.ds(pl.multiple_of(base + start, 16), length)

    @pl.when(step == 0)
    def _():
        gain_ref[...] = jnp.zeros_like(gain_ref)
        if layer > 0:
            copy.start()

    dentry, gain_part = attend_back(
        step,
        here,
        (entry_ref[...], qkv_ref, mix_ref, chance_ref),
        dmiddle_ref[...],
        gains_ref[layer : layer + 1, :],
        att_ref,
        head_masks(),
        att_kept,
    )
    gain_ref[0:1, :] += gain_part
    if layer == 0:
        before_kept[0][here(0, ROWS), :] = dentry.astype(jnp.bfloat16)
        one_hot_rows(latent_ref, before_kept[1], pl.multiple_of(step * ROWS, ROWS))
    else:
        dbefore, gain_part = feed_back(
            here,
            dentry,
            before_ref[...],
            gains_ref[LAYERS + layer - 1 : LAYERS + layer, :],
            ffn_ref,
            slope_ref,
            before_kept,
        )
        out_ref[...] = dbefore
        gain_ref[1:2, :] += gain_part

    @pl.when(step == pl.num_programs(0) - 1)
    def _():
        normed_ref, dattend_ref, dqkv_ref, mixes_ref = att_kept
        att = [(normed_ref, dqkv_ref), (mixes_ref, dattend_ref)]
        if layer == 0:
            pairs = att + [(before_kept[0], before_kept[1])]
        else:
            copy.wait()
            normed_two_ref, dinner_ref, dout_ref = before_kept
            pairs = [(normed_two_ref, dinner_ref), (dout_ref, inner_ref)] + att
        column = 0
        for left, right in pairs:
            wide = right.shape[1]
            sum_ref[:, column : column + wide] = dot_nn(left[...].T, right[...])
            column += wide
        write_blocks(send_ref, keep_ref, sum_ref, core_ref[0], widths, mesh_plan)


def run_backward(layer, widths, mesh_plan, blocks_like, saved, dmiddle, gains, core, before):
    entry, _, qkv, mix, chance, weights = [in_hbm(item) for item in saved[:6]]
    if layer > 0:
        before = [in_hbm(item) for item in before]
    tokens = entry.shape[0]
    queries = chance.shape[3] // (HEADS // 2)
    short = tokens // CTX * queries
    f32, b16 = jnp.float32, jnp.bfloat16
    shape = jax.ShapeDtypeStruct
    in_specs = [
        row_spec(D),
        row_spec(3 * D),
        row_spec(D, GROUP * queries),
        chance_spec(queries),
        row_spec(D, GROUP * queries),
        whole_spec(weights.shape),
        whole_spec(gains.shape),
        smem_spec(),
    ]
    operands = [entry, qkv, mix, chance, dmiddle, weights, gains, core]
    blocks = block_outs(blocks_like, widths)
    outs = [(item, whole_spec(item.shape)) for item in blocks]
    outs.append((shape((2, D), f32), whole_spec((2, D))))
    scratch = [
        pltpu.VMEM((tokens, D), b16),
        pltpu.VMEM((short, D), b16),
        pltpu.VMEM((tokens, 3 * D), b16),
        pltpu.VMEM((short, D), b16),
    ]
    if layer == 0:
        in_specs.append(latent_spec())
        operands.append(before)
        scratch = scratch + [pltpu.VMEM((tokens, D), b16), pltpu.VMEM((tokens, VOCAB), b16)]
        wide = 4 * D + VOCAB
    else:
        in_specs = in_specs + [row_spec(D), whole_spec(before[1].shape), row_spec(FF)]
        in_specs.append(pl.BlockSpec(memory_space=pl.ANY))
        operands = operands + list(before)
        outs.insert(0, (shape((tokens, D), f32), row_spec(D)))
        scratch = scratch + [
            pltpu.VMEM((tokens, D), b16),
            pltpu.VMEM((tokens, FF), b16),
            pltpu.VMEM((tokens, D), b16),
        ]
        wide = 4 * D + 2 * FF
    scratch.append(pltpu.VMEM((D, wide), f32))
    if layer > 0:
        scratch = scratch + [pltpu.VMEM((tokens, FF), b16), pltpu.SemaphoreType.DMA]
    return pl.pallas_call(
        functools.partial(backward_kernel, layer, widths, mesh_plan),
        grid=(tokens // ROWS,),
        in_specs=in_specs,
        out_specs=[spec for _, spec in outs],
        out_shape=[item for item, _ in outs],
        scratch_shapes=scratch,
        compiler_params=pltpu.CompilerParams(vmem_limit_bytes=VMEM_BYTES * 3 // 2),
        cost_estimate=pl.CostEstimate(
            flops=6 * tokens * D * wide,
            bytes_accessed=tokens * D * 24 + D * wide * 6,
            transcendentals=tokens * FF,
        ),
        name="backward_part",
    )(*operands)


def pack_kernel(*refs):
    qkv_ref, out_ref, up_ref, down_ref, embed_ref, head_ref = refs[:6]
    low = lambda value: value.astype(jnp.bfloat16)
    att = [[low(qkv_ref[at]), low(out_ref[at].T)] for at in range(LAYERS)]
    ffn = [[low(up_ref[at]), low(down_ref[at])] for at in range(LAYERS)]
    pieces = [
        att[0] + [low(embed_ref[...])],
        ffn[0] + att[1],
        ffn[1] + att[2] + ffn[2] + [low(head_ref[...])],
    ]
    for target, piece in zip(refs[6:], pieces):
        target[...] = jnp.concatenate(piece, axis=1)


def run_pack(masters, chunk_widths):
    vmem = pl.BlockSpec(memory_space=pltpu.VMEM)
    rows = masters[0].shape[1]
    return pl.pallas_call(
        pack_kernel,
        in_specs=[vmem] * 6,
        out_specs=[vmem] * 3,
        out_shape=[
            jax.ShapeDtypeStruct((rows, sum(widths)), jnp.bfloat16) for widths in chunk_widths
        ],
        name="pack",
    )(*masters)


def matrix_plan(widths):
    order = [
        (2, 2), (3, 2), (5, 0), (2, 1), (3, 1), (0, 2), (1, 2),
        (2, 0), (3, 0), (0, 1), (1, 1), (0, 0), (1, 0), (4, 0),
    ]
    plan, column = {}, 0
    for which, layer in order:
        plan[(which, layer)] = (column, widths[which])
        column += widths[which]
    return plan, column


def matrix_list():
    return [(which, layer) for which in range(4) for layer in range(LAYERS)] + [(4, 0), (5, 0)]


MATRICES = 4 * LAYERS + 2
LANES = 128
INNER_ROWS = 16
COMMON_ROWS = 16
ROW_IS_INNER = [True, True, True, False, False, True]


def master_of(masters, which, layer):
    if which == 1:
        return masters[1][layer].T
    return masters[which][layer] if which < 4 else masters[which][...]


def old_row(refs, which, layer):
    return refs[which][layer : layer + 1, :] if which < 4 else refs[which][...]


LATE = [(0, 0), (1, 0), (4, 0)]
EDGE = INNER_ROWS + COMMON_ROWS


def whole_sum(value):
    return jnp.sum(jnp.sum(value, axis=1, keepdims=True), axis=0, keepdims=True)


def square_sums(raw, chosen, plan, first):
    square = raw * raw
    rows = square.shape[0]
    inner, entries = [], []
    for item in matrix_list():
        if item in chosen:
            column, width = plan[item]
            part = square[:, column - first : column - first + width]
            inner.append(jnp.sum(part, axis=1, keepdims=True))
        else:
            inner.append(jnp.zeros((rows, 1), jnp.float32))
        entries.append(jnp.sum(inner[-1], axis=0, keepdims=True))
    inner.append(jnp.zeros((rows, LANES - MATRICES), jnp.float32))
    return jnp.concatenate(inner, axis=1).T, entries, jnp.sum(square, axis=0, keepdims=True)


def store_row(target_ref, row, values):
    total = values.shape[1]
    for at, start in enumerate(range(0, total, LANES)):
        stop = min(start + LANES, total)
        target_ref[row + at : row + at + 1, 0 : stop - start] = values[:, start:stop]


def load_row(source_ref, row, total):
    return jnp.concatenate(
        [
            source_ref[row + at : row + at + 1, 0 : min(LANES, total - start)]
            for at, start in enumerate(range(0, total, LANES))
        ],
        axis=1,
    )


def late_row(widths):
    _, total = matrix_plan(widths)
    late = sum(widths[which] for which, _ in LATE)
    return EDGE + -(-(total - late) // LANES)


def packet_rows(widths):
    late = sum(widths[which] for which, _ in LATE)
    return -(-(late_row(widths) + -(-late // LANES)) // 8) * 8


def early_kernel(widths, *refs):
    raw_ref, masters, row_refs = refs[0], refs[1:7], refs[7:13]
    gains_at, loss_ref, count_ref, packet_ref = refs[13:15], refs[15], refs[16], refs[17]
    plan, _ = matrix_plan(widths)
    chosen = [item for item in matrix_list() if item not in LATE]
    inner, entries, outer = square_sums(raw_ref[...], chosen, plan, 0)
    weights, row_sums = [], []
    for which, layer in matrix_list():
        master = masters[which][layer] if which < 4 else masters[which][...]
        weights.append(whole_sum(master * master))
        row_sums.append(whole_sum(old_row(row_refs, which, layer)))
    packet_ref[...] = jnp.zeros_like(packet_ref)
    packet_ref[0:INNER_ROWS, 0 : inner.shape[1]] = inner[0:INNER_ROWS, :]
    last, one = [ref[...] for ref in gains_at]
    gain = jnp.concatenate(
        [jnp.zeros((1, D), jnp.float32), one[0:1], last[2:3], one[1:2], last[3:4], last[0:2]],
        axis=0,
    )
    scalars = [loss_ref[...], count_ref[...]] + weights + entries + row_sums
    scalars.append(jnp.zeros((1, LANES - len(scalars)), jnp.float32))
    at = INNER_ROWS
    packet_ref[at : at + 7, :] = gain[:, 0:LANES]
    packet_ref[at + 7 : at + 8, :] = jnp.concatenate(scalars, axis=1)
    packet_ref[at + 8 : at + 15, :] = gain[:, LANES:]
    store_row(packet_ref, EDGE, outer)


def late_kernel(widths, early_ref, raw_ref, gain_ref, packet_ref):
    plan, total = matrix_plan(widths)
    inner, entries, outer = square_sums(raw_ref[...], LATE, plan, total - raw_ref.shape[1])
    packet_ref[...] = early_ref[...]
    packet_ref[0:INNER_ROWS, 0 : inner.shape[1]] += inner[0:INNER_ROWS, :]
    at = INNER_ROWS
    packet_ref[at : at + 1, :] = gain_ref[0:1, 0:LANES]
    packet_ref[at + 8 : at + 9, :] = gain_ref[0:1, LANES:]
    before = jnp.zeros((1, 2 + MATRICES), jnp.float32)
    behind = jnp.zeros((1, LANES - 2 - 2 * MATRICES), jnp.float32)
    packet_ref[at + 7 : at + 8, :] += jnp.concatenate([before] + entries + [behind], axis=1)
    store_row(packet_ref, late_row(widths), outer)


def run_early(widths, raw, masters, rows, gain_parts, loss, count):
    vmem = pl.BlockSpec(memory_space=pltpu.VMEM)
    operands = [raw] + masters + rows + gain_parts + [loss, count]
    return pl.pallas_call(
        functools.partial(early_kernel, widths),
        in_specs=[vmem] * len(operands),
        out_specs=vmem,
        out_shape=jax.ShapeDtypeStruct((packet_rows(widths), LANES), jnp.float32),
        name="early_statistics",
    )(*operands)


def run_late(widths, packet, raw, gain_part):
    vmem = pl.BlockSpec(memory_space=pltpu.VMEM)
    return pl.pallas_call(
        functools.partial(late_kernel, widths),
        in_specs=[vmem] * 3,
        out_specs=vmem,
        out_shape=jax.ShapeDtypeStruct(packet.shape, jnp.float32),
        name="late_statistics",
    )(packet, raw, gain_part)


def update_kernel(widths, sizes, *refs):
    packet_ref, raw_early, raw_late = refs[:3]
    masters, inner_refs, outer_refs = refs[3:9], refs[9:15], refs[15:21]
    gains_ref, second_ref = refs[21:23]
    outs = refs[23:]
    outer_count, inner_count = sizes
    plan, total = matrix_plan(widths)
    rows = raw_early.shape[0]
    at = INNER_ROWS
    scalars = packet_ref[at + 7 : at + 8, :]
    pick = lambda at: scalars[:, at : at + 1]
    gain_sum = jnp.concatenate(
        [packet_ref[at : at + 7, :], packet_ref[at + 8 : at + 15, :]], axis=1
    )
    gain_square = jnp.sum(jnp.sum(gain_sum * gain_sum, axis=1, keepdims=True), axis=0, keepdims=True)
    square_total = gain_square
    for at in range(MATRICES):
        square_total = square_total + pick(2 + MATRICES + at)
    count_total = pick(1)
    norm_value = jnp.sqrt(square_total) / count_total
    scaling = jnp.minimum(1.0, clip_limit / norm_value) / count_total
    square_scale = scaling * scaling
    early = raw_early.shape[1]
    outer_early = load_row(packet_ref, EDGE, early)
    outer_late = load_row(packet_ref, late_row(widths), total - early)
    inner_new = []
    for at, (which, layer) in enumerate(matrix_list()):
        outer_length = widths[which] * outer_count
        inner_new.append(
            decay_two * old_row(inner_refs, which, layer)
            + (1 - decay_two)
            * (square_scale * packet_ref[at : at + 1, 0:rows] / outer_length + tiny_term)
        )
    stacked = jnp.concatenate(inner_new, axis=0)
    stacked = jnp.concatenate([stacked, jnp.ones((LANES - MATRICES, rows), jnp.float32)], axis=0)
    if rows < LANES:
        stacked = jnp.concatenate([stacked, jnp.ones((LANES, LANES - rows), jnp.float32)], axis=1)
    turned = lax.rsqrt(stacked).T
    outs[0][...] = pick(0)
    outs[1][...] = count_total
    outs[2][...] = norm_value
    first_out = {4: 3, 0: 7, 1: 11, 2: 15, 3: 19, 5: 23}
    for at, (which, layer) in enumerate(matrix_list()):
        column, width = plan[(which, layer)]
        outer_length, inner_length = width * outer_count, rows * inner_count
        row_length = inner_length if ROW_IS_INNER[which] else outer_length
        copies = outer_count if ROW_IS_INNER[which] else inner_count
        entries = outer_length * inner_length
        if column < early:
            raw = raw_early[:, column : column + width]
            outer_total = outer_early[:, column : column + width]
        else:
            raw = raw_late[:, column - early : column - early + width]
            outer_total = outer_late[:, column - early : column - early + width]
        outer_new = decay_two * old_row(outer_refs, which, layer) + (1 - decay_two) * (
            square_scale * outer_total / inner_length + tiny_term
        )
        mean_rows = decay_two * (pick(2 + 2 * MATRICES + at) / (copies * row_length)) + (
            1 - decay_two
        ) * (square_scale * pick(2 + MATRICES + at) / entries + tiny_term)
        factor = step_rate * jnp.sqrt(pick(2 + at) / entries) * jnp.sqrt(mean_rows)
        grad = raw * scaling
        updated = master_of(masters, which, layer) - grad * (
            turned[0:rows, at : at + 1] * (factor * lax.rsqrt(outer_new))
        )
        first = first_out[which]
        row_new, column_new = (
            (inner_new[at], outer_new) if ROW_IS_INNER[which] else (outer_new, inner_new[at])
        )
        if which < 4:
            if which == 1:
                updated, grad = updated.T, grad.T
            outs[first][layer] = updated
            outs[first + 1][layer] = grad
            outs[first + 2][layer : layer + 1, :] = row_new
            outs[first + 3][layer : layer + 1, :] = column_new
        else:
            outs[first][...] = updated
            outs[first + 1][...] = grad
            outs[first + 2][...] = row_new
            outs[first + 3][...] = column_new
    gain_grad = gain_sum * scaling
    second_new = decay_two * second_ref[...] + (1 - decay_two) * (gain_grad * gain_grad + tiny_term)
    gains = gains_ref[...]
    spread = jnp.sqrt(jnp.mean(gains * gains, axis=-1, keepdims=True))
    outs[27][...] = gains - step_rate * spread * gain_grad * lax.rsqrt(second_new)
    outs[28][...] = gain_grad
    outs[29][...] = second_new


def run_update(widths, sizes, packet, raw_early, raw_late, masters, inner, outer, gains, second):
    vmem = pl.BlockSpec(memory_space=pltpu.VMEM)
    operands = [packet, raw_early, raw_late] + masters + inner + outer + [gains, second]
    shapes = [(1, 1)] * 3
    for which in [4, 0, 1, 2, 3, 5]:
        shapes = shapes + [masters[which].shape] * 2
        pair = [inner[which].shape, outer[which].shape]
        shapes = shapes + (pair if ROW_IS_INNER[which] else pair[::-1])
    shapes = shapes + [gains.shape] * 3
    return pl.pallas_call(
        functools.partial(update_kernel, widths, sizes),
        in_specs=[vmem] * len(operands),
        out_specs=[vmem] * len(shapes),
        out_shape=[jax.ShapeDtypeStruct(item, jnp.float32) for item in shapes],
        name="update",
    )(*operands)


def swap(value, mask):
    count = lax.axis_size("dp") * lax.axis_size("fsdp")
    return lax.ppermute(value, ("dp", "fsdp"), [(place, place ^ mask) for place in range(count)])


def device_index():
    return lax.axis_index("dp") * lax.axis_size("fsdp") + lax.axis_index("fsdp")


def step_masks(step):
    masks = []
    for digit in range(1, 1 << len(step)):
        masks.append(sum(1 << bit for at, bit in enumerate(step[::-1]) if (digit >> at) & 1))
    return masks


def tie(*values):
    return lax.optimization_barrier(values)


def behind(value, *ahead):
    return lax.optimization_barrier((value,) + ahead)[0]


class Gather:
    def __init__(self, piece, steps):
        self.held, self.steps, self.at = piece[None], steps, 0

    def send(self):
        self.others = tuple(swap(self.held, mask) for mask in step_masks(self.steps[self.at]))

    def join(self):
        step = self.steps[self.at]
        pieces = [self.held] + list(self.others)
        for at, bit in enumerate(step[::-1]):
            upper = (device_index() >> bit) & 1 == 1
            pieces = [
                jnp.where(upper, pieces[place ^ (1 << at)], pieces[place])
                for place in range(len(pieces))
            ]
        self.held = jnp.concatenate(pieces)
        self.at += 1


class Scatter:
    def __init__(self, sent, kept, steps):
        self.sent, self.kept, self.steps, self.at = (sent,), kept, steps, 0

    def send(self):
        masks = step_masks(self.steps[self.at])
        self.others = tuple(swap(sent, mask) for sent, mask in zip(self.sent, masks))

    def join(self):
        self.at += 1
        step = self.steps[self.at] if self.at < len(self.steps) else ()
        count = 1 << len(step)
        own = 0
        for bit in step:
            own = 2 * own + ((device_index() >> bit) & 1)
        shape = (count, self.kept.shape[0] // count) + self.kept.shape[1:]
        terms = [item.reshape(shape) for item in (self.kept,) + self.others]

        def pick(digit):
            total = None
            for term in terms:
                part = lax.dynamic_index_in_dim(term, own ^ digit, 0, keepdims=False)
                part = part.astype(jnp.float32)
                total = part if total is None else total + part
            return total

        self.sent = tuple(pick(digit).astype(jnp.bfloat16) for digit in range(1, count))
        self.kept = pick(0)


def sum_packets(packet, group, inner_bits):
    masks = step_masks(group)
    others = [swap(packet, mask) for mask in masks]
    inner, outer = packet[:INNER_ROWS], packet[EDGE:]
    common = [packet[INNER_ROWS:EDGE]]
    inner, outer = [inner], [outer]
    for mask, other in zip(masks, others):
        common.append(other[INNER_ROWS:EDGE])
        if mask >> inner_bits << inner_bits == mask:
            inner.append(other[:INNER_ROWS])
        if mask >> inner_bits == 0:
            outer.append(other[EDGE:])
    tree = lambda items: (
        items[0] if len(items) == 1 else tree(
            [items[at] + items[at + 1] for at in range(0, len(items), 2)]
        )
    )
    return jnp.concatenate([tree(inner), tree(common), tree(outer)])


def merged(parts):
    whole = Scatter(None, jnp.concatenate([part.kept for part in parts], axis=2), parts[0].steps)
    whole.sent = tuple(
        jnp.concatenate(pieces, axis=2) for pieces in zip(*[part.sent for part in parts])
    )
    whole.at = parts[0].at
    return whole


def shards(
    latents,
    targets,
    horizon,
    memory_valid,
    embed,
    qkv_weight,
    out_weight,
    up_weight,
    down_weight,
    head_weight,
    gains,
    embed_rows,
    embed_cols,
    qkv_rows,
    qkv_cols,
    out_rows,
    out_cols,
    up_rows,
    up_cols,
    down_rows,
    down_cols,
    head_rows,
    head_cols,
    gain_second,
):
    samples = latents.shape[0]
    sizes = (lax.axis_size("dp"), lax.axis_size("fsdp"))
    highest = (sizes[0] * sizes[1]).bit_length() - 1
    gather_steps = [(bit,) for bit in reversed(range(3, highest))] + [(2, 1), (0,)]
    scatter_steps = gather_steps[::-1]
    mesh_plan = (sizes[0], sizes[1], gather_steps)
    core = (lax.axis_index("fsdp") & 1).astype(jnp.int32).reshape(1)

    out_turned = jnp.swapaxes(out_weight, 1, 2)
    down_turned = jnp.swapaxes(down_weight, 1, 2)
    masters = [qkv_weight, out_turned, up_weight, down_turned, embed.T, head_weight]
    widths = [qkv_weight.shape[2], out_weight.shape[2], up_weight.shape[2], down_weight.shape[1]]
    widths = widths + [embed.shape[0], head_weight.shape[1]]
    att_widths, ffn_widths = widths[0:2], widths[2:4]
    chunk_widths = [
        att_widths + widths[4:5],
        ffn_widths + att_widths,
        ffn_widths + att_widths + ffn_widths + widths[5:6],
    ]
    chunks = [Gather(piece, gather_steps) for piece in run_pack(masters, chunk_widths)]
    first, second, third = chunks
    latent_rows = latents.transpose(0, 2, 1)
    target_rows = targets.transpose(0, 2, 1)
    shared = (gains, memory_valid, core)
    back_shared = (gains, core)

    count = len(gather_steps)
    for at in range(count - 1):
        for chunk in chunks:
            chunk.send()
        for chunk in chunks[: 2 if at == count - 2 else 3]:
            chunk.join()
            if at == count - 3 and chunk is first:
                first.held, third.held = tie(first.held, third.held)
    first.send()
    (other,) = first.others
    held, other, second.held = tie(first.held, other, second.held)
    second.send()
    kept = [run_forward(0, chunk_widths[0], mesh_plan, latent_rows, held, other, *shared)]
    middle, (other,), third.others = tie(kept[0][1], second.others, third.others)
    third.join()
    middle, third.held = tie(middle, third.held)
    third.send()
    kept.append(
        run_forward(1, chunk_widths[1], mesh_plan, middle, second.held, other, *shared)
    )
    middle, (other,) = tie(kept[1][1], third.others)
    dmiddle, sent, held, gain_middle, loss, counted = run_middle(
        chunk_widths[2],
        mesh_plan,
        middle,
        third.held,
        other,
        target_rows,
        gains,
        memory_valid,
        horizon,
        core,
    )
    pair = Scatter(sent, held, scatter_steps)
    pair.send()
    pair.join()
    like = first.held
    before = (kept[0][1], kept[1][6], kept[1][8], kept[1][7])
    dmiddle, pair.sent = tie(dmiddle, pair.sent)
    pair.send()
    dmiddle, sent, held, gain_one = run_backward(
        1, chunk_widths[1], mesh_plan, like, kept[1], dmiddle, *back_shared, before
    )
    dmiddle, sent, held, pair.others = tie(dmiddle, sent, held, pair.others)
    one = Scatter(sent, held, scatter_steps)
    one.send()
    pair.join()
    one.join()
    dmiddle, pair.sent, one.sent = tie(dmiddle, pair.sent, one.sent)
    one.send()
    pair.send()
    sent, held, gain_zero = run_backward(
        0, chunk_widths[0], mesh_plan, like, kept[0], dmiddle, *back_shared, latent_rows
    )
    sent, held, pair.others, one.others = tie(sent, held, pair.others, one.others)
    zero = Scatter(sent, held, scatter_steps)
    zero.send()
    one.join()
    one.send()
    pair.join()
    zero.join()
    one.others = behind(one.others, zero.sent)
    zero.send()
    one.join()
    early = merged([pair, one])
    while early.at < count:
        early.send()
        zero.others = behind(zero.others, early.sent)
        early.join()
    raw_early = early.kept[0]

    flat = lambda item: item if item.ndim == 2 else item.reshape(1, -1)
    inner = [flat(item) for item in (qkv_rows, out_rows, up_rows, down_cols, embed_cols, head_rows)]
    outer = [flat(item) for item in (qkv_cols, out_cols, up_cols, down_rows, embed_rows, head_cols)]
    row_stats = [inner[at] if ROW_IS_INNER[at] else outer[at] for at in range(6)]
    packet = run_early(
        widths, raw_early, masters, row_stats, [gain_middle, gain_one], loss, counted
    )
    while zero.at < count:
        zero.join()
        if zero.at < count:
            zero.send()
    raw_late = zero.kept[0]
    packet = run_late(widths, packet, raw_late, gain_zero)
    inner_bits = sizes[1].bit_length() - 1
    rest = list(range(3, highest))
    groups = [(0,), (2, 1)] + [tuple(rest[at : at + 2][::-1]) for at in range(0, len(rest), 2)]
    for group in groups:
        packet = sum_packets(packet, group, inner_bits)
    results = run_update(
        widths, sizes, packet, raw_early, raw_late, masters, inner, outer, gains, gain_second
    )
    results = list(results)
    for at in range(3):
        results[at] = results[at].reshape(())
    for at in (3, 4, 11, 12, 19, 20):
        results[at] = jnp.swapaxes(results[at], -1, -2)
    for at in (5, 6, 25, 26):
        results[at] = results[at].reshape(-1)
    return tuple(results)


def solution(mesh):
    return jax.shard_map(
        shards,
        mesh=mesh,
        in_specs=(
            P(("dp", "fsdp"), None, None),
            P(("dp", "fsdp"), None, None),
            P(("dp", "fsdp")),
            P(("dp", "fsdp")),
            P("dp", "fsdp"),
            P(None, "fsdp", "dp"),
            P(None, "fsdp", "dp"),
            P(None, "fsdp", "dp"),
            P(None, "dp", "fsdp"),
            P("fsdp", "dp"),
            P(),
            P("dp"),
            P("fsdp"),
            P(None, "fsdp"),
            P(None, "dp"),
            P(None, "fsdp"),
            P(None, "dp"),
            P(None, "fsdp"),
            P(None, "dp"),
            P(None, "dp"),
            P(None, "fsdp"),
            P("fsdp"),
            P("dp"),
            P(),
        ),
        out_specs=(
            P(),
            P(),
            P(),
            P("dp", "fsdp"),
            P("dp", "fsdp"),
            P("dp"),
            P("fsdp"),
            P(None, "fsdp", "dp"),
            P(None, "fsdp", "dp"),
            P(None, "fsdp"),
            P(None, "dp"),
            P(None, "fsdp", "dp"),
            P(None, "fsdp", "dp"),
            P(None, "fsdp"),
            P(None, "dp"),
            P(None, "fsdp", "dp"),
            P(None, "fsdp", "dp"),
            P(None, "fsdp"),
            P(None, "dp"),
            P(None, "dp", "fsdp"),
            P(None, "dp", "fsdp"),
            P(None, "dp"),
            P(None, "fsdp"),
            P("fsdp", "dp"),
            P("fsdp", "dp"),
            P("fsdp"),
            P("dp"),
            P(),
            P(),
            P(),
        ),
        check_vma=False,
    )
```

```python
import functools

import jax
import jax.numpy as jnp
from jax import lax
from jax.experimental import pallas as pl
from jax.experimental.pallas import tpu as pltpu
from jax.sharding import PartitionSpec as P

D = 256
HEADS = 8
HEAD = D // HEADS
FF = 1024
CATS = 32
CLASSES = 32
LAYERS = 3
SEG = 48
MEM = 48
CTX = 96
VOCAB = 1024
GROUP = 4
WIDE_GROUP = 8
ROWS = GROUP * CTX
HALF = D // 2
VMEM_BYTES = 24 * 1024 * 1024
MIDDLE_BYTES = 46 * 1024 * 1024

decay_two = 0.9
step_rate = 0.3
clip_limit = 0.05
tiny_term = 1e-30
norm_eps = 1e-06
masked_score = -1e30
log2_e = 1.4426950408889634
score_scale = HEAD ** (-0.5)
gelu_one = 0.7978845608028654
gelu_two = 0.044715


def dot_nn(left, right):
    return lax.dot_general(
        left, right, (((1,), (0,)), ((), ())), preferred_element_type=jnp.float32
    )


def dot_nt(left, right):
    return lax.dot_general(
        left, right, (((1,), (1,)), ((), ())), preferred_element_type=jnp.float32
    )


def dot_tn(left, right):
    return lax.dot_general(
        left, right, (((0,), (0,)), ((), ())), preferred_element_type=jnp.float32
    )


def inverse_rms(values):
    return lax.rsqrt(jnp.mean(values * values, axis=-1, keepdims=True) + norm_eps)


def rms_back(values, inverse, gain_row, upstream):
    normed = values * inverse
    scaled = upstream * gain_row
    inner = jnp.mean(scaled * normed, axis=-1, keepdims=True)
    return (
        inverse * (scaled - normed * inner),
        jnp.sum(upstream * normed, axis=0, keepdims=True),
    )


def head_masks():
    lane = lax.broadcasted_iota(jnp.int32, (1, D // 2), 1) // HEAD
    return [lane == head for head in range(HEADS // 2)]


def expand_heads(rows, masks):
    return jnp.concatenate([rows * mask.astype(rows.dtype) for mask in masks], axis=0)


def collapse_heads(spread, rows, masks):
    product = dot_tn(spread, rows)
    queries = product.shape[0] // len(masks)
    taken = product[(len(masks) - 1) * queries :]
    for at, mask in enumerate(masks[:-1]):
        taken = jnp.where(mask, product[at * queries : (at + 1) * queries], taken)
    return taken


def half_of(part, side):
    start = part * D + side * HALF
    return slice(start, start + HALF)


def fill_bias(bias_ref):
    spread = bias_ref.shape[2]
    queries = spread // (HEADS // 2)
    key_at = lax.broadcasted_iota(jnp.int32, (CTX, spread), 0)
    query_at = lax.broadcasted_iota(jnp.int32, (CTX, spread), 1) % queries + (CTX - queries)
    later = key_at > query_at
    crosses = (query_at >= MEM) & (key_at < MEM)
    bias_ref[0] = jnp.where(later | crosses, masked_score, 0.0)
    bias_ref[1] = jnp.where(later, masked_score, 0.0)


def block_place(device, steps):
    place, weight = 0, 1
    for step in steps[:-1]:
        digit = 0
        for bit in step:
            digit = 2 * digit + ((device >> bit) & 1)
        place += digit * weight
        weight <<= len(step)
    return place


def place_weights(targets, own_ref, other_ref, core, widths, mesh_plan, start=0):
    outer_count, inner_count, steps = mesh_plan
    rows = own_ref.shape[1]
    for high in range(inner_count // 2):
        for source, side in ((own_ref, core), (other_ref, 1 - core)):
            here = pl.ds(pl.multiple_of((2 * high + side) * rows, rows), rows)
            at = start
            for (target, column), width in zip(targets, widths):
                block = [
                    source[
                        block_place(outer * inner_count + 2 * high, steps), :, at : at + width
                    ]
                    for outer in range(outer_count)
                ]
                target[here, column : column + width * outer_count] = jnp.concatenate(
                    block, axis=1
                )
                at += width


def write_blocks(send_ref, keep_ref, sum_ref, core, widths, mesh_plan, start=0):
    outer_count, inner_count, steps = mesh_plan
    rows = keep_ref.shape[1]
    for high in range(inner_count // 2):
        for target, side in ((keep_ref, core), (send_ref, 1 - core)):
            here = pl.ds(pl.multiple_of((2 * high + side) * rows, rows), rows)
            taken = sum_ref[here, :]
            for outer in range(outer_count):
                block, column = [], 0
                for width in widths:
                    block.append(taken[:, column + outer * width : column + (outer + 1) * width])
                    column += width * outer_count
                place = block_place(outer * inner_count + 2 * high, steps)
                target[place, :, start : start + sum(widths)] = jnp.concatenate(
                    block, axis=1
                ).astype(target.dtype)


def one_hot_rows(latent_ref, hot_ref, first):
    spot = lax.broadcasted_iota(jnp.int32, (CATS, VOCAB), 1) // CLASSES
    group = lax.broadcasted_iota(jnp.int32, (CATS, VOCAB), 0)
    spreader = jnp.where(spot == group, 1.0, 0.0).astype(jnp.bfloat16)
    classes = (lax.broadcasted_iota(jnp.int32, (1, VOCAB), 1) % CLASSES).astype(jnp.float32)
    for sample in range(GROUP):
        drawn = dot_tn(latent_ref[sample].astype(jnp.float32).astype(jnp.bfloat16), spreader)
        hot_ref[pl.ds(first + sample * CTX, CTX), :] = jnp.where(
            drawn == classes, 1.0, 0.0
        ).astype(jnp.bfloat16)


def tail_rows(values, queries):
    if queries == CTX:
        return values
    return jnp.concatenate(
        [
            values[(sample + 1) * CTX - queries : (sample + 1) * CTX]
            for sample in range(values.shape[0] // CTX)
        ],
        axis=0,
    )


def attend_forward(step, hidden, gain_row, weight_ref, valid_ref, bias_ref, masks, refs):
    middle_ref, qkv_ref, mix_ref, chance_ref = refs
    queries = chance_ref.shape[3] // (HEADS // 2)
    group = hidden.shape[0] // CTX
    normed = (hidden * inverse_rms(hidden) * gain_row).astype(jnp.bfloat16)
    qkv_ref[...] = dot_nn(normed, weight_ref[:, 0 : 3 * D]).astype(jnp.bfloat16)
    units = [(sample, side) for sample in range(group) for side in range(2)]
    scores = []
    for sample, side in units:
        rows = slice(sample * CTX, (sample + 1) * CTX)
        tail = slice((sample + 1) * CTX - queries, (sample + 1) * CTX)
        spread = expand_heads(qkv_ref[tail, half_of(0, side)], masks)
        scores.append(dot_nt(qkv_ref[rows, half_of(1, side)], spread))
    for (sample, side), score in zip(units, scores):
        score = score + bias_ref[valid_ref[step * group + sample]]
        peak = jnp.max(score, axis=0, keepdims=True)
        exponent = jnp.exp2((score - peak) * (score_scale * log2_e))
        total = jnp.sum(exponent, axis=0, keepdims=True)
        chance_ref[sample, side] = (exponent * (1.0 / total)).astype(jnp.bfloat16)
    for sample, side in units:
        rows = slice(sample * CTX, (sample + 1) * CTX)
        mix_ref[sample * queries : (sample + 1) * queries, half_of(0, side)] = collapse_heads(
            chance_ref[sample, side], qkv_ref[rows, half_of(2, side)], masks
        ).astype(jnp.bfloat16)
    middle_ref[...] = tail_rows(hidden, queries) + dot_nn(
        mix_ref[...], weight_ref[:, 3 * D : 4 * D]
    )


def gelu_parts(value):
    square = value * value
    share = 0.5 + 0.5 * jnp.tanh(value * (gelu_one + (gelu_one * gelu_two) * square))
    active = value * share
    bent = active * (1.0 - share)
    return active, share + bent * (2.0 * gelu_one + (6.0 * gelu_one * gelu_two) * square)


def feed_forward(middle, gain_row, weight_ref, inner_ref, slope_ref):
    normed = (middle * inverse_rms(middle) * gain_row).astype(jnp.bfloat16)
    for part in range(FF // D):
        columns = slice(part * D, (part + 1) * D)
        inner = dot_nn(normed, weight_ref[:, columns])
        for sample in range(middle.shape[0] // CTX):
            rows = slice(sample * CTX, (sample + 1) * CTX)
            active, slope = gelu_parts(inner[rows])
            inner_ref[rows, columns] = active.astype(jnp.bfloat16)
            slope_ref[rows, columns] = slope.astype(jnp.bfloat16)
    return middle + dot_nt(inner_ref[...], weight_ref[:, FF : 2 * FF])


def feed_back(here, upstream, middle, gain_row, weight_ref, slope_ref, refs):
    normed_ref, dinner_ref, dout_ref = refs
    dout = upstream.astype(jnp.bfloat16)
    dout_ref[here(0, middle.shape[0]), :] = dout
    inverse = inverse_rms(middle)
    normed_ref[here(0, middle.shape[0]), :] = (middle * inverse * gain_row).astype(jnp.bfloat16)
    for part in range(FF // D):
        columns = slice(part * D, (part + 1) * D)
        dact = dot_nn(dout, weight_ref[:, FF + part * D : FF + (part + 1) * D])
        dinner_ref[here(0, middle.shape[0]), columns] = (
            dact * slope_ref[:, columns].astype(jnp.float32)
        ).astype(jnp.bfloat16)
    dnormed = dot_nt(dinner_ref[here(0, middle.shape[0]), :], weight_ref[:, 0:FF])
    through, gain_part = rms_back(middle, inverse, gain_row, dnormed)
    return upstream + through, gain_part


def attend_back(step, here, saved, dmiddle, gain_row, weight_ref, masks, refs):
    hidden, qkv_ref, mix_ref, chance_ref = saved
    normed_ref, dmiddle_ref, dqkv_ref, mixes_ref = refs
    group = hidden.shape[0] // CTX
    queries = chance_ref.shape[3] // (HEADS // 2)
    short = here(0, group * queries, queries)
    dattend = dmiddle.astype(jnp.bfloat16)
    dmiddle_ref[short, :] = dattend
    mixes_ref[short, :] = mix_ref[...]
    dmix = dot_nt(dattend, weight_ref[:, 3 * D : 4 * D]).astype(jnp.bfloat16)
    units = [(sample, side) for sample in range(group) for side in range(2)]
    slopes, dchances, dscores = [], [], []
    for sample, side in units:
        rows = slice(sample * CTX, (sample + 1) * CTX)
        slopes.append(
            expand_heads(
                dmix[sample * queries : (sample + 1) * queries, half_of(0, side)], masks
            )
        )
        dchances.append(dot_nt(qkv_ref[rows, half_of(2, side)], slopes[-1]))
    for (sample, side), dchance in zip(units, dchances):
        chance = chance_ref[sample, side].astype(jnp.float32)
        weighed = chance * dchance
        dscores.append(
            (weighed - chance * jnp.sum(weighed, axis=0, keepdims=True)).astype(jnp.bfloat16)
        )
    for at, (sample, side) in enumerate(units):
        rows = slice(sample * CTX, (sample + 1) * CTX)
        tail = slice((sample + 1) * CTX - queries, (sample + 1) * CTX)
        there = here(sample * CTX, CTX)
        spread = expand_heads(qkv_ref[tail, half_of(0, side)], masks)
        keys = qkv_ref[rows, half_of(1, side)]
        dvalues = dot_nn(chance_ref[sample, side], slopes[at])
        dkeys = dot_nn(dscores[at], spread) * score_scale
        dqueries = (collapse_heads(dscores[at], keys, masks) * score_scale).astype(jnp.bfloat16)
        if queries < CTX:
            nothing = jnp.zeros((CTX - queries, HALF), jnp.bfloat16)
            dqueries = jnp.concatenate([nothing, dqueries], axis=0)
        dqkv_ref[there, half_of(0, side)] = dqueries
        dqkv_ref[there, half_of(1, side)] = dkeys.astype(jnp.bfloat16)
        dqkv_ref[there, half_of(2, side)] = dvalues.astype(jnp.bfloat16)
    inverse = inverse_rms(hidden)
    normed_ref[here(0, hidden.shape[0]), :] = (hidden * inverse * gain_row).astype(jnp.bfloat16)
    dnormed = dot_nt(dqkv_ref[here(0, hidden.shape[0]), :], weight_ref[:, 0 : 3 * D])
    through, gain_part = rms_back(hidden, inverse, gain_row, dnormed)
    if queries < CTX:
        nothing = jnp.zeros((CTX - queries, D), jnp.float32)
        pieces = []
        for sample in range(group):
            pieces = pieces + [nothing, dmiddle[sample * queries : (sample + 1) * queries]]
        dmiddle = jnp.concatenate(pieces, axis=0)
    return dmiddle + through, gain_part


def row_spec(width, rows=ROWS):
    return pl.BlockSpec((rows, width), lambda step: (step, 0))


def chance_spec(queries):
    return pl.BlockSpec((GROUP, 2, CTX, HEADS // 2 * queries), lambda step: (step, 0, 0, 0))


def latent_spec():
    return pl.BlockSpec((GROUP, CATS, CTX), lambda step: (step, 0, 0))


def whole_spec(shape):
    return pl.BlockSpec(shape, lambda step: (0,) * len(shape))


def in_hbm(item):
    return pltpu.with_memory_space_constraint(item, pltpu.HBM)


def smem_spec():
    return pl.BlockSpec(memory_space=pltpu.SMEM)


def forward_kernel(layer, widths, mesh_plan, source_ref, own_ref, other_ref, gains_ref, valid_ref, core_ref, *refs):
    entry_ref, att_ref, before_ref = refs[0], refs[5], refs[6]
    bias_ref = refs[7] if layer == 0 else refs[9]
    step = pl.program_id(0)

    @pl.when(step == 0)
    def _():
        fill_bias(bias_ref)
        att = [(att_ref, 0), (att_ref, 3 * D)]
        before = [(before_ref, 0)] if layer == 0 else [(before_ref, 0), (before_ref, FF)]
        targets = att + before if layer == 0 else before + att
        place_weights(targets, own_ref, other_ref, core_ref[0], widths[: len(targets)], mesh_plan)

    if layer == 0:
        one_hot_rows(source_ref, refs[8], 0)
        hidden = dot_nt(refs[8][...], before_ref[...])
    else:
        gain_ffn = gains_ref[LAYERS + layer - 1 : LAYERS + layer, :]
        hidden = feed_forward(source_ref[...], gain_ffn, before_ref, refs[7], refs[8])
    entry_ref[...] = hidden
    attend_forward(
        step,
        hidden,
        gains_ref[layer : layer + 1, :],
        att_ref,
        valid_ref,
        bias_ref,
        head_masks(),
        refs[1:5],
    )


def run_forward(layer, widths, mesh_plan, source, own, other, gains, valid, core):
    tokens = valid.shape[0] * CTX
    f32, b16 = jnp.float32, jnp.bfloat16
    chances = HEADS // 2 * CTX
    outs = [
        (pltpu.HBM((tokens, D), f32), row_spec(D)),
        (pltpu.HBM((tokens, D), f32), row_spec(D)),
        (pltpu.HBM((tokens, 3 * D), b16), row_spec(3 * D)),
        (pltpu.HBM((tokens, D), b16), row_spec(D)),
        (pltpu.HBM((tokens // CTX, 2, CTX, chances), b16), chance_spec(CTX)),
        (pltpu.HBM((D, 4 * D), b16), whole_spec((D, 4 * D))),
    ]
    scratch = [pltpu.VMEM((2, CTX, chances), f32)]
    if layer == 0:
        scratch = [pltpu.VMEM((D, VOCAB), b16)] + scratch + [pltpu.VMEM((ROWS, VOCAB), b16)]
        source_spec = latent_spec()
    else:
        source_spec = row_spec(D)
        outs.append((pltpu.HBM((D, 2 * FF), b16), whole_spec((D, 2 * FF))))
        outs = outs + [(pltpu.HBM((tokens, FF), b16), row_spec(FF))] * 2
        source = in_hbm(source)
    return pl.pallas_call(
        functools.partial(forward_kernel, layer, widths, mesh_plan),
        grid=(tokens // ROWS,),
        in_specs=[
            source_spec,
            whole_spec(own.shape),
            whole_spec(other.shape),
            whole_spec(gains.shape),
            smem_spec(),
            smem_spec(),
        ],
        out_specs=[spec for _, spec in outs],
        out_shape=[item for item, _ in outs],
        scratch_shapes=scratch,
        compiler_params=pltpu.CompilerParams(vmem_limit_bytes=VMEM_BYTES),
        cost_estimate=pl.CostEstimate(
            flops=2 * tokens * D * 12 * D,
            bytes_accessed=tokens * D * 16 + D * 12 * D * 4,
            transcendentals=tokens * (FF + HEADS * CTX),
        ),
        name="forward_part",
    )(source, own, other, gains, valid, core)


def middle_kernel(widths, mesh_plan, *refs):
    source_ref, own_ref, other_ref, drawn_ref, gains_ref, valid_ref, horizon_ref, core_ref = refs[:8]
    out_ref, send_ref, keep_ref, gain_ref, loss_ref, count_ref = refs[8:14]
    bias_ref, weight_one_ref, att_ref, weight_two_ref, head_ref, turned_ref = refs[14:20]
    entry_ref, qkv_ref, mix_ref, chance_ref, middle_two_ref, inner_one_ref, slope_one_ref = refs[20:27]
    inner_ref, slope_ref, last_ref, dmiddle_ref, sum_ref, targets_ref, counted_ref = refs[27:34]
    normed_long, dattend_ref, dqkv_long, mixes_ref, normed_two_long, dinner_long, dout_long = refs[34:]
    tokens = middle_two_ref.shape[0]
    final_ref = normed_long.at[0:tokens]
    dlogits_ref = dqkv_long.at[0:VOCAB]
    normed_ref = normed_two_long.at[0:tokens]
    dinner_ref = dinner_long.at[0:tokens]
    dout_ref = dout_long.at[0:tokens]
    groups = source_ref.shape[0] // (WIDE_GROUP * CTX)
    masks = head_masks()
    gain_att = gains_ref[LAYERS - 1 : LAYERS, :]
    gain_before = gains_ref[2 * LAYERS - 2 : 2 * LAYERS - 1, :]
    gain_ffn = gains_ref[2 * LAYERS - 1 : 2 * LAYERS, :]
    gain_final = gains_ref[2 * LAYERS : 2 * LAYERS + 1, :]
    fill_bias(bias_ref)
    place_weights(
        [
            (weight_one_ref, 0),
            (weight_one_ref, FF),
            (att_ref, 0),
            (att_ref, 3 * D),
            (weight_two_ref, 0),
            (weight_two_ref, FF),
            (head_ref, 0),
        ],
        own_ref,
        other_ref,
        core_ref[0],
        widths,
        mesh_plan,
    )

    def rows_of(group, unit=CTX):
        return pl.ds(pl.multiple_of(group * (WIDE_GROUP * unit), WIDE_GROUP * unit), WIDE_GROUP * unit)

    def forward(group, carry):
        rows, short = rows_of(group), rows_of(group, SEG)
        hidden = feed_forward(
            source_ref[rows, :],
            gain_before,
            weight_one_ref,
            inner_one_ref.at[rows],
            slope_one_ref.at[rows],
        )
        entry_ref[rows, :] = hidden
        attend_forward(
            group,
            hidden,
            gain_att,
            att_ref,
            valid_ref,
            bias_ref,
            masks,
            (
                middle_two_ref.at[short],
                qkv_ref.at[rows],
                mix_ref.at[short],
                chance_ref.at[pl.ds(group * WIDE_GROUP, WIDE_GROUP)],
            ),
        )
        return carry

    lax.fori_loop(0, groups, forward, 0)
    turned_ref[...] = head_ref[...].T
    samples = tokens // SEG
    targets_ref[...] = jnp.concatenate([drawn_ref[at] for at in range(samples)], axis=1)
    position = lax.broadcasted_iota(jnp.int32, (1, SEG), 1)
    counted_ref[...] = jnp.concatenate(
        [jnp.where(position < horizon_ref[at], 1.0, 0.0) for at in range(samples)], axis=1
    )
    count_ref[...] = jnp.sum(counted_ref[...], axis=1, keepdims=True)
    for block in range(tokens // ROWS):
        rows = slice(block * ROWS, (block + 1) * ROWS)
        middle = middle_two_ref[rows, :]
        normed = (middle * inverse_rms(middle) * gain_ffn).astype(jnp.bfloat16)
        normed_ref[rows, :] = normed
        for part in range(FF // D):
            columns = slice(part * D, (part + 1) * D)
            inner = dot_nn(normed, weight_two_ref[:, columns])
            for piece in range(GROUP):
                there = slice(block * ROWS + piece * CTX, block * ROWS + (piece + 1) * CTX)
                active, slope = gelu_parts(inner[piece * CTX : (piece + 1) * CTX])
                inner_ref[there, columns] = active.astype(jnp.bfloat16)
                slope_ref[there, columns] = slope.astype(jnp.bfloat16)
        last = middle + dot_nt(inner_ref[rows, :], weight_two_ref[:, FF : 2 * FF])
        last_ref[rows, :] = last
        final_ref[rows, :] = (last * inverse_rms(last) * gain_final).astype(jnp.bfloat16)
    span = D
    loss = jnp.zeros((1, span), jnp.float32)
    spots = lax.broadcasted_iota(jnp.int32, (CLASSES, span), 0)
    for part in range(tokens // span):
        columns = slice(part * span, (part + 1) * span)
        counted = counted_ref[0:1, columns]
        final = final_ref[columns, :]
        for quarter in range(VOCAB // D):
            logits = dot_nt(turned_ref[quarter * D : (quarter + 1) * D, :], final)
            for inside in range(D // CLASSES):
                group = quarter * (D // CLASSES) + inside
                values = logits[inside * CLASSES : (inside + 1) * CLASSES]
                shifted = values - jnp.max(values, axis=0, keepdims=True)
                exponent = jnp.exp2(shifted * log2_e)
                total = jnp.sum(exponent, axis=0, keepdims=True)
                hot = spots == targets_ref[group : group + 1, columns]
                chosen = jnp.sum(jnp.where(hot, shifted, 0.0), axis=0, keepdims=True)
                loss = loss + counted * (jnp.log(total) - chosen)
                chance = exponent * (1.0 / total)
                slope = (chance - jnp.where(hot, 1.0, 0.0)) * counted
                dlogits_ref[group * CLASSES : (group + 1) * CLASSES, columns] = slope.astype(
                    jnp.bfloat16
                )
    loss_ref[...] = jnp.sum(loss, axis=1, keepdims=True)
    sum_ref[:, 2 * FF : 2 * FF + VOCAB] = dot_nt(final_ref[...].T, dlogits_ref[...])
    dfinal = dot_nn(head_ref[...], dlogits_ref[...]).T
    last = last_ref[...]
    dlast, gain_part = rms_back(last, inverse_rms(last), gain_final, dfinal)
    gain_ref[1:2, :] = gain_part
    last_ref[...] = dlast
    gain_sum = jnp.zeros((1, D), jnp.float32)
    for block in range(tokens // ROWS):
        rows = slice(block * ROWS, (block + 1) * ROWS)
        upstream = last_ref[rows, :]
        dout = upstream.astype(jnp.bfloat16)
        dout_ref[rows, :] = dout
        for part in range(FF // D):
            columns = slice(part * D, (part + 1) * D)
            dact = dot_nn(dout, weight_two_ref[:, FF + part * D : FF + (part + 1) * D])
            dinner_ref[rows, columns] = (dact * slope_ref[rows, columns].astype(jnp.float32)).astype(jnp.bfloat16)
        dnormed = dot_nt(dinner_ref[rows, :], weight_two_ref[:, 0:FF])
        middle = middle_two_ref[rows, :]
        through, gain_part = rms_back(middle, inverse_rms(middle), gain_ffn, dnormed)
        gain_sum = gain_sum + gain_part
        dmiddle_ref[rows, :] = upstream + through
    gain_ref[0:1, :] = gain_sum
    sum_ref[:, 0:FF] = dot_nn(normed_ref[...].T, dinner_ref[...])
    sum_ref[:, FF : 2 * FF] = dot_nn(dout_ref[...].T, inner_ref[...])
    write_blocks(send_ref, keep_ref, sum_ref, core_ref[0], widths[4:], mesh_plan)
    gain_ref[2:4, :] = jnp.zeros((2, D), jnp.float32)

    def backward(group, carry):
        rows, short = rows_of(group), rows_of(group, SEG)

        def here(start, length, unit=CTX):
            return pl.ds(pl.multiple_of(group * (WIDE_GROUP * unit) + start, 16), length)

        dentry, gain_part = attend_back(
            group,
            here,
            (
                entry_ref[rows, :],
                qkv_ref.at[rows],
                mix_ref.at[short],
                chance_ref.at[pl.ds(group * WIDE_GROUP, WIDE_GROUP)],
            ),
            dmiddle_ref[short, :],
            gain_att,
            att_ref,
            masks,
            (normed_long, dattend_ref, dqkv_long, mixes_ref),
        )
        gain_ref[2:3, :] += gain_part
        dbefore, gain_part = feed_back(
            here,
            dentry,
            source_ref[rows, :],
            gain_before,
            weight_one_ref,
            slope_one_ref.at[rows],
            (normed_two_long, dinner_long, dout_long),
        )
        out_ref[rows, :] = dbefore
        gain_ref[3:4, :] += gain_part
        return carry

    lax.fori_loop(0, groups, backward, 0)
    column = 0
    for left, right in [
        (normed_two_long, dinner_long),
        (dout_long, inner_one_ref),
        (normed_long, dqkv_long),
        (mixes_ref, dattend_ref),
    ]:
        wide = right.shape[1]
        sum_ref[:, column : column + wide] = dot_nn(left[...].T, right[...])
        column += wide
    write_blocks(
        send_ref, keep_ref, sum_ref, core_ref[0], widths[:4], mesh_plan, sum(widths[4:])
    )


def block_outs(own, widths):
    shape = jax.ShapeDtypeStruct
    blocks = own.shape[:2] + (sum(widths),)
    return [shape(blocks, jnp.bfloat16)] * 2


def run_middle(widths, mesh_plan, source, own, other, targets, gains, valid, horizon, core):
    tokens = source.shape[0]
    short = tokens // CTX * SEG
    samples = tokens // CTX
    chances = HEADS // 2 * SEG
    f32, b16 = jnp.float32, jnp.bfloat16
    shape = jax.ShapeDtypeStruct
    vmem = pl.BlockSpec(memory_space=pltpu.VMEM)
    return pl.pallas_call(
        functools.partial(middle_kernel, widths, mesh_plan),
        in_specs=[vmem] * 5 + [smem_spec()] * 3,
        out_specs=[vmem] * 6,
        out_shape=[shape((tokens, D), f32)]
        + block_outs(own, widths)
        + [shape((4, D), f32), shape((1, 1), f32), shape((1, 1), f32)],
        scratch_shapes=[
            pltpu.VMEM((2, CTX, chances), f32),
            pltpu.VMEM((D, 2 * FF), b16),
            pltpu.VMEM((D, 4 * D), b16),
            pltpu.VMEM((D, 2 * FF), b16),
            pltpu.VMEM((D, VOCAB), b16),
            pltpu.VMEM((VOCAB, D), b16),
            pltpu.VMEM((tokens, D), f32),
            pltpu.VMEM((tokens, 3 * D), b16),
            pltpu.VMEM((short, D), b16),
            pltpu.VMEM((samples, 2, CTX, chances), b16),
            pltpu.VMEM((short, D), f32),
            pltpu.VMEM((tokens, FF), b16),
            pltpu.VMEM((tokens, FF), b16),
            pltpu.VMEM((short, FF), b16),
            pltpu.VMEM((short, FF), b16),
            pltpu.VMEM((short, D), f32),
            pltpu.VMEM((short, D), f32),
            pltpu.VMEM((D, 2 * FF + max(4 * D, VOCAB)), f32),
            pltpu.VMEM((CATS, short), jnp.int32),
            pltpu.VMEM((1, short), f32),
            pltpu.VMEM((tokens, D), b16),
            pltpu.VMEM((short, D), b16),
            pltpu.VMEM((tokens, 3 * D), b16),
            pltpu.VMEM((short, D), b16),
            pltpu.VMEM((tokens, D), b16),
            pltpu.VMEM((tokens, FF), b16),
            pltpu.VMEM((tokens, D), b16),
        ],
        compiler_params=pltpu.CompilerParams(vmem_limit_bytes=MIDDLE_BYTES + (0 if own.shape[1] >= 64 else VMEM_BYTES // 2)),
        cost_estimate=pl.CostEstimate(
            flops=6 * tokens * D * 8 * FF,
            bytes_accessed=tokens * D * 8 + D * 6 * FF * 10,
            transcendentals=2 * tokens * (FF + VOCAB),
        ),
        name="middle_part",
    )(source, own, other, targets, gains, valid, horizon, core)


def backward_kernel(layer, widths, mesh_plan, *refs):
    entry_ref, qkv_ref, mix_ref, chance_ref, dmiddle_ref, att_ref, gains_ref, core_ref = refs[:8]
    if layer == 0:
        latent_ref, send_ref, keep_ref, gain_ref = refs[8:12]
        att_kept, before_kept, sum_ref = refs[12:16], refs[16:18], refs[18]
    else:
        before_ref, ffn_ref, slope_ref, inner_hbm, out_ref, send_ref, keep_ref, gain_ref = refs[8:16]
        att_kept, before_kept, sum_ref = refs[16:20], refs[20:23], refs[23]
        inner_ref, inner_sem = refs[24:26]
        copy = pltpu.make_async_copy(inner_hbm, inner_ref, inner_sem)
    step = pl.program_id(0)

    def here(start, length, unit=CTX):
        base = step * (GROUP * unit)
        return pl.ds(pl.multiple_of(base + start, 16), length)

    @pl.when(step == 0)
    def _():
        gain_ref[...] = jnp.zeros_like(gain_ref)
        if layer > 0:
            copy.start()

    dentry, gain_part = attend_back(
        step,
        here,
        (entry_ref[...], qkv_ref, mix_ref, chance_ref),
        dmiddle_ref[...],
        gains_ref[layer : layer + 1, :],
        att_ref,
        head_masks(),
        att_kept,
    )
    gain_ref[0:1, :] += gain_part
    if layer == 0:
        before_kept[0][here(0, ROWS), :] = dentry.astype(jnp.bfloat16)
        one_hot_rows(latent_ref, before_kept[1], pl.multiple_of(step * ROWS, ROWS))
    else:
        dbefore, gain_part = feed_back(
            here,
            dentry,
            before_ref[...],
            gains_ref[LAYERS + layer - 1 : LAYERS + layer, :],
            ffn_ref,
            slope_ref,
            before_kept,
        )
        out_ref[...] = dbefore
        gain_ref[1:2, :] += gain_part

    @pl.when(step == pl.num_programs(0) - 1)
    def _():
        normed_ref, dattend_ref, dqkv_ref, mixes_ref = att_kept
        att = [(normed_ref, dqkv_ref), (mixes_ref, dattend_ref)]
        if layer == 0:
            pairs = att + [(before_kept[0], before_kept[1])]
        else:
            copy.wait()
            normed_two_ref, dinner_ref, dout_ref = before_kept
            pairs = [(normed_two_ref, dinner_ref), (dout_ref, inner_ref)] + att
        column = 0
        for left, right in pairs:
            wide = right.shape[1]
            sum_ref[:, column : column + wide] = dot_nn(left[...].T, right[...])
            column += wide
        write_blocks(send_ref, keep_ref, sum_ref, core_ref[0], widths, mesh_plan)


def run_backward(layer, widths, mesh_plan, blocks_like, saved, dmiddle, gains, core, before):
    entry, _, qkv, mix, chance, weights = [in_hbm(item) for item in saved[:6]]
    if layer > 0:
        before = [in_hbm(item) for item in before]
    tokens = entry.shape[0]
    queries = chance.shape[3] // (HEADS // 2)
    short = tokens // CTX * queries
    f32, b16 = jnp.float32, jnp.bfloat16
    shape = jax.ShapeDtypeStruct
    in_specs = [
        row_spec(D),
        row_spec(3 * D),
        row_spec(D, GROUP * queries),
        chance_spec(queries),
        row_spec(D, GROUP * queries),
        whole_spec(weights.shape),
        whole_spec(gains.shape),
        smem_spec(),
    ]
    operands = [entry, qkv, mix, chance, dmiddle, weights, gains, core]
    blocks = block_outs(blocks_like, widths)
    outs = [(item, whole_spec(item.shape)) for item in blocks]
    outs.append((shape((2, D), f32), whole_spec((2, D))))
    scratch = [
        pltpu.VMEM((tokens, D), b16),
        pltpu.VMEM((short, D), b16),
        pltpu.VMEM((tokens, 3 * D), b16),
        pltpu.VMEM((short, D), b16),
    ]
    if layer == 0:
        in_specs.append(latent_spec())
        operands.append(before)
        scratch = scratch + [pltpu.VMEM((tokens, D), b16), pltpu.VMEM((tokens, VOCAB), b16)]
        wide = 4 * D + VOCAB
    else:
        in_specs = in_specs + [row_spec(D), whole_spec(before[1].shape), row_spec(FF)]
        in_specs.append(pl.BlockSpec(memory_space=pl.ANY))
        operands = operands + list(before)
        outs.insert(0, (shape((tokens, D), f32), row_spec(D)))
        scratch = scratch + [
            pltpu.VMEM((tokens, D), b16),
            pltpu.VMEM((tokens, FF), b16),
            pltpu.VMEM((tokens, D), b16),
        ]
        wide = 4 * D + 2 * FF
    scratch.append(pltpu.VMEM((D, wide), f32))
    if layer > 0:
        scratch = scratch + [pltpu.VMEM((tokens, FF), b16), pltpu.SemaphoreType.DMA]
    return pl.pallas_call(
        functools.partial(backward_kernel, layer, widths, mesh_plan),
        grid=(tokens // ROWS,),
        in_specs=in_specs,
        out_specs=[spec for _, spec in outs],
        out_shape=[item for item, _ in outs],
        scratch_shapes=scratch,
        compiler_params=pltpu.CompilerParams(vmem_limit_bytes=VMEM_BYTES * 3 // 2),
        cost_estimate=pl.CostEstimate(
            flops=6 * tokens * D * wide,
            bytes_accessed=tokens * D * 24 + D * wide * 6,
            transcendentals=tokens * FF,
        ),
        name="backward_part",
    )(*operands)


def pack_kernel(*refs):
    qkv_ref, out_ref, up_ref, down_ref, embed_ref, head_ref = refs[:6]
    low = lambda value: value.astype(jnp.bfloat16)
    att = [[low(qkv_ref[at]), low(out_ref[at].T)] for at in range(LAYERS)]
    ffn = [[low(up_ref[at]), low(down_ref[at])] for at in range(LAYERS)]
    pieces = [
        att[0] + [low(embed_ref[...])],
        ffn[0] + att[1],
        ffn[1] + att[2] + ffn[2] + [low(head_ref[...])],
    ]
    for target, piece in zip(refs[6:], pieces):
        target[...] = jnp.concatenate(piece, axis=1)


def run_pack(masters, chunk_widths):
    vmem = pl.BlockSpec(memory_space=pltpu.VMEM)
    rows = masters[0].shape[1]
    return pl.pallas_call(
        pack_kernel,
        in_specs=[vmem] * 6,
        out_specs=[vmem] * 3,
        out_shape=[
            jax.ShapeDtypeStruct((rows, sum(widths)), jnp.bfloat16) for widths in chunk_widths
        ],
        name="pack",
    )(*masters)


def matrix_plan(widths):
    order = [
        (2, 2), (3, 2), (5, 0), (2, 1), (3, 1), (0, 2), (1, 2),
        (2, 0), (3, 0), (0, 1), (1, 1), (0, 0), (1, 0), (4, 0),
    ]
    plan, column = {}, 0
    for which, layer in order:
        plan[(which, layer)] = (column, widths[which])
        column += widths[which]
    return plan, column


def matrix_list():
    return [(which, layer) for which in range(4) for layer in range(LAYERS)] + [(4, 0), (5, 0)]


MATRICES = 4 * LAYERS + 2
LANES = 128
INNER_ROWS = 16
COMMON_ROWS = 16
ROW_IS_INNER = [True, True, True, False, False, True]


def master_of(masters, which, layer):
    if which == 1:
        return masters[1][layer].T
    return masters[which][layer] if which < 4 else masters[which][...]


def old_row(refs, which, layer):
    return refs[which][layer : layer + 1, :] if which < 4 else refs[which][...]


LATE = [(0, 0), (1, 0), (4, 0)]
EDGE = INNER_ROWS + COMMON_ROWS


def whole_sum(value):
    return jnp.sum(jnp.sum(value, axis=1, keepdims=True), axis=0, keepdims=True)


def square_sums(raw, chosen, plan, first):
    square = raw * raw
    rows = square.shape[0]
    inner, entries = [], []
    for item in matrix_list():
        if item in chosen:
            column, width = plan[item]
            part = square[:, column - first : column - first + width]
            inner.append(jnp.sum(part, axis=1, keepdims=True))
        else:
            inner.append(jnp.zeros((rows, 1), jnp.float32))
        entries.append(jnp.sum(inner[-1], axis=0, keepdims=True))
    inner.append(jnp.zeros((rows, LANES - MATRICES), jnp.float32))
    return jnp.concatenate(inner, axis=1).T, entries, jnp.sum(square, axis=0, keepdims=True)


def store_row(target_ref, row, values):
    total = values.shape[1]
    for at, start in enumerate(range(0, total, LANES)):
        stop = min(start + LANES, total)
        target_ref[row + at : row + at + 1, 0 : stop - start] = values[:, start:stop]


def load_row(source_ref, row, total):
    return jnp.concatenate(
        [
            source_ref[row + at : row + at + 1, 0 : min(LANES, total - start)]
            for at, start in enumerate(range(0, total, LANES))
        ],
        axis=1,
    )


def late_row(widths):
    _, total = matrix_plan(widths)
    late = sum(widths[which] for which, _ in LATE)
    return EDGE + -(-(total - late) // LANES)


def packet_rows(widths):
    late = sum(widths[which] for which, _ in LATE)
    return -(-(late_row(widths) + -(-late // LANES)) // 8) * 8


def first_kernel(*refs):
    masters, row_refs, row_ref = refs[0:6], refs[6:12], refs[12]
    weights, row_sums = [], []
    for which, layer in matrix_list():
        master = masters[which][layer] if which < 4 else masters[which][...]
        weights.append(whole_sum(master * master))
        row_sums.append(whole_sum(old_row(row_refs, which, layer)))
    nothing = lambda count: [jnp.zeros((1, count), jnp.float32)]
    pieces = nothing(2) + weights + nothing(MATRICES) + row_sums
    row_ref[...] = jnp.concatenate(pieces + nothing(LANES - 2 - 3 * MATRICES), axis=1)


def run_first(masters, rows):
    vmem = pl.BlockSpec(memory_space=pltpu.VMEM)
    return pl.pallas_call(
        first_kernel,
        in_specs=[vmem] * 12,
        out_specs=vmem,
        out_shape=jax.ShapeDtypeStruct((1, LANES), jnp.float32),
        name="first_statistics",
    )(*masters, *rows)


def early_kernel(widths, *refs):
    raw_ref, row_ref, gains_at, loss_ref, count_ref, packet_ref = (
        refs[0],
        refs[1],
        refs[2:4],
        refs[4],
        refs[5],
        refs[6],
    )
    plan, _ = matrix_plan(widths)
    chosen = [item for item in matrix_list() if item not in LATE]
    inner, entries, outer = square_sums(raw_ref[...], chosen, plan, 0)
    packet_ref[...] = jnp.zeros_like(packet_ref)
    packet_ref[0:INNER_ROWS, 0 : inner.shape[1]] = inner[0:INNER_ROWS, :]
    last, one = [ref[...] for ref in gains_at]
    gain = jnp.concatenate(
        [jnp.zeros((1, D), jnp.float32), one[0:1], last[2:3], one[1:2], last[3:4], last[0:2]],
        axis=0,
    )
    nothing = lambda count: [jnp.zeros((1, count), jnp.float32)]
    scalars = [loss_ref[...], count_ref[...]] + nothing(MATRICES) + entries
    scalars = scalars + nothing(LANES - 2 - 2 * MATRICES)
    at = INNER_ROWS
    packet_ref[at : at + 7, :] = gain[:, 0:LANES]
    packet_ref[at + 7 : at + 8, :] = row_ref[...] + jnp.concatenate(scalars, axis=1)
    packet_ref[at + 8 : at + 15, :] = gain[:, LANES:]
    store_row(packet_ref, EDGE, outer)


def late_kernel(widths, early_ref, raw_ref, gain_ref, packet_ref):
    plan, total = matrix_plan(widths)
    inner, entries, outer = square_sums(raw_ref[...], LATE, plan, total - raw_ref.shape[1])
    packet_ref[...] = early_ref[...]
    packet_ref[0:INNER_ROWS, 0 : inner.shape[1]] += inner[0:INNER_ROWS, :]
    at = INNER_ROWS
    packet_ref[at : at + 1, :] = gain_ref[0:1, 0:LANES]
    packet_ref[at + 8 : at + 9, :] = gain_ref[0:1, LANES:]
    before = jnp.zeros((1, 2 + MATRICES), jnp.float32)
    behind = jnp.zeros((1, LANES - 2 - 2 * MATRICES), jnp.float32)
    packet_ref[at + 7 : at + 8, :] += jnp.concatenate([before] + entries + [behind], axis=1)
    store_row(packet_ref, late_row(widths), outer)


def run_early(widths, raw, row, gain_parts, loss, count):
    vmem = pl.BlockSpec(memory_space=pltpu.VMEM)
    operands = [raw, row] + gain_parts + [loss, count]
    return pl.pallas_call(
        functools.partial(early_kernel, widths),
        in_specs=[vmem] * len(operands),
        out_specs=vmem,
        out_shape=jax.ShapeDtypeStruct((packet_rows(widths), LANES), jnp.float32),
        name="early_statistics",
    )(*operands)


def run_late(widths, packet, raw, gain_part):
    vmem = pl.BlockSpec(memory_space=pltpu.VMEM)
    return pl.pallas_call(
        functools.partial(late_kernel, widths),
        in_specs=[vmem] * 3,
        out_specs=vmem,
        out_shape=jax.ShapeDtypeStruct(packet.shape, jnp.float32),
        name="late_statistics",
    )(packet, raw, gain_part)


def update_kernel(widths, sizes, *refs):
    packet_ref, raw_early, raw_late = refs[:3]
    masters, inner_refs, outer_refs = refs[3:9], refs[9:15], refs[15:21]
    gains_ref, second_ref = refs[21:23]
    outs = refs[23:]
    outer_count, inner_count = sizes
    plan, total = matrix_plan(widths)
    rows = raw_early.shape[0]
    at = INNER_ROWS
    scalars = packet_ref[at + 7 : at + 8, :]
    pick = lambda at: scalars[:, at : at + 1]
    gain_sum = jnp.concatenate(
        [packet_ref[at : at + 7, :], packet_ref[at + 8 : at + 15, :]], axis=1
    )
    gain_square = jnp.sum(jnp.sum(gain_sum * gain_sum, axis=1, keepdims=True), axis=0, keepdims=True)
    square_total = gain_square
    for at in range(MATRICES):
        square_total = square_total + pick(2 + MATRICES + at)
    count_total = pick(1)
    norm_value = jnp.sqrt(square_total) / count_total
    scaling = jnp.minimum(1.0, clip_limit / norm_value) / count_total
    square_scale = scaling * scaling
    early = raw_early.shape[1]
    outer_early = load_row(packet_ref, EDGE, early)
    outer_late = load_row(packet_ref, late_row(widths), total - early)
    inner_new = []
    for at, (which, layer) in enumerate(matrix_list()):
        outer_length = widths[which] * outer_count
        inner_new.append(
            decay_two * old_row(inner_refs, which, layer)
            + (1 - decay_two)
            * (square_scale * packet_ref[at : at + 1, 0:rows] / outer_length + tiny_term)
        )
    stacked = jnp.concatenate(inner_new, axis=0)
    stacked = jnp.concatenate([stacked, jnp.ones((LANES - MATRICES, rows), jnp.float32)], axis=0)
    if rows < LANES:
        stacked = jnp.concatenate([stacked, jnp.ones((LANES, LANES - rows), jnp.float32)], axis=1)
    turned = lax.rsqrt(stacked).T
    outs[0][...] = pick(0)
    outs[1][...] = count_total
    outs[2][...] = norm_value
    first_out = {4: 3, 0: 7, 1: 11, 2: 15, 3: 19, 5: 23}
    for at, (which, layer) in enumerate(matrix_list()):
        column, width = plan[(which, layer)]
        outer_length, inner_length = width * outer_count, rows * inner_count
        row_length = inner_length if ROW_IS_INNER[which] else outer_length
        copies = outer_count if ROW_IS_INNER[which] else inner_count
        entries = outer_length * inner_length
        if column < early:
            raw = raw_early[:, column : column + width]
            outer_total = outer_early[:, column : column + width]
        else:
            raw = raw_late[:, column - early : column - early + width]
            outer_total = outer_late[:, column - early : column - early + width]
        outer_new = decay_two * old_row(outer_refs, which, layer) + (1 - decay_two) * (
            square_scale * outer_total / inner_length + tiny_term
        )
        mean_rows = decay_two * (pick(2 + 2 * MATRICES + at) / (copies * row_length)) + (
            1 - decay_two
        ) * (square_scale * pick(2 + MATRICES + at) / entries + tiny_term)
        factor = step_rate * jnp.sqrt(pick(2 + at) / entries) * jnp.sqrt(mean_rows)
        grad = raw * scaling
        updated = master_of(masters, which, layer) - grad * (
            turned[0:rows, at : at + 1] * (factor * lax.rsqrt(outer_new))
        )
        first = first_out[which]
        row_new, column_new = (
            (inner_new[at], outer_new) if ROW_IS_INNER[which] else (outer_new, inner_new[at])
        )
        if which < 4:
            if which == 1:
                updated, grad = updated.T, grad.T
            outs[first][layer] = updated
            outs[first + 1][layer] = grad
            outs[first + 2][layer : layer + 1, :] = row_new
            outs[first + 3][layer : layer + 1, :] = column_new
        else:
            outs[first][...] = updated
            outs[first + 1][...] = grad
            outs[first + 2][...] = row_new
            outs[first + 3][...] = column_new
    gain_grad = gain_sum * scaling
    second_new = decay_two * second_ref[...] + (1 - decay_two) * (gain_grad * gain_grad + tiny_term)
    gains = gains_ref[...]
    spread = jnp.sqrt(jnp.mean(gains * gains, axis=-1, keepdims=True))
    outs[27][...] = gains - step_rate * spread * gain_grad * lax.rsqrt(second_new)
    outs[28][...] = gain_grad
    outs[29][...] = second_new


def run_update(widths, sizes, packet, raw_early, raw_late, masters, inner, outer, gains, second):
    vmem = pl.BlockSpec(memory_space=pltpu.VMEM)
    operands = [packet, raw_early, raw_late] + masters + inner + outer + [gains, second]
    shapes = [(1, 1)] * 3
    for which in [4, 0, 1, 2, 3, 5]:
        shapes = shapes + [masters[which].shape] * 2
        pair = [inner[which].shape, outer[which].shape]
        shapes = shapes + (pair if ROW_IS_INNER[which] else pair[::-1])
    shapes = shapes + [gains.shape] * 3
    return pl.pallas_call(
        functools.partial(update_kernel, widths, sizes),
        in_specs=[vmem] * len(operands),
        out_specs=[vmem] * len(shapes),
        out_shape=[jax.ShapeDtypeStruct(item, jnp.float32) for item in shapes],
        name="update",
    )(*operands)


def swap(value, mask):
    count = lax.axis_size("dp") * lax.axis_size("fsdp")
    return lax.ppermute(value, ("dp", "fsdp"), [(place, place ^ mask) for place in range(count)])


def device_index():
    return lax.axis_index("dp") * lax.axis_size("fsdp") + lax.axis_index("fsdp")


def step_masks(step):
    masks = []
    for digit in range(1, 1 << len(step)):
        masks.append(sum(1 << bit for at, bit in enumerate(step[::-1]) if (digit >> at) & 1))
    return masks


def tie(*values):
    return lax.optimization_barrier(values)


def behind(value, *ahead):
    return lax.optimization_barrier((value,) + ahead)[0]


class Gather:
    def __init__(self, piece, steps):
        self.held, self.steps, self.at = piece[None], steps, 0

    def send(self):
        self.others = tuple(swap(self.held, mask) for mask in step_masks(self.steps[self.at]))

    def join(self):
        step = self.steps[self.at]
        pieces = [self.held] + list(self.others)
        for at, bit in enumerate(step[::-1]):
            upper = (device_index() >> bit) & 1 == 1
            pieces = [
                jnp.where(upper, pieces[place ^ (1 << at)], pieces[place])
                for place in range(len(pieces))
            ]
        self.held = jnp.concatenate(pieces)
        self.at += 1


class Scatter:
    def __init__(self, sent, kept, steps):
        self.sent, self.kept, self.steps, self.at = (sent,), kept, steps, 0

    def send(self):
        masks = step_masks(self.steps[self.at])
        self.others = tuple(swap(sent, mask) for sent, mask in zip(self.sent, masks))

    def join(self):
        self.at += 1
        step = self.steps[self.at] if self.at < len(self.steps) else ()
        count = 1 << len(step)
        own = 0
        for bit in step:
            own = 2 * own + ((device_index() >> bit) & 1)
        shape = (count, self.kept.shape[0] // count) + self.kept.shape[1:]
        terms = [item.reshape(shape) for item in (self.kept,) + self.others]

        def pick(digit):
            total = None
            for term in terms:
                part = lax.dynamic_index_in_dim(term, own ^ digit, 0, keepdims=False)
                part = part.astype(jnp.float32)
                total = part if total is None else total + part
            return total

        self.sent = tuple(pick(digit).astype(jnp.bfloat16) for digit in range(1, count))
        self.kept = pick(0)


def sum_packets(packet, group, inner_bits):
    masks = step_masks(group)
    others = [swap(packet, mask) for mask in masks]
    inner, outer = packet[:INNER_ROWS], packet[EDGE:]
    common = [packet[INNER_ROWS:EDGE]]
    inner, outer = [inner], [outer]
    for mask, other in zip(masks, others):
        common.append(other[INNER_ROWS:EDGE])
        if mask >> inner_bits << inner_bits == mask:
            inner.append(other[:INNER_ROWS])
        if mask >> inner_bits == 0:
            outer.append(other[EDGE:])
    tree = lambda items: (
        items[0] if len(items) == 1 else tree(
            [items[at] + items[at + 1] for at in range(0, len(items), 2)]
        )
    )
    return jnp.concatenate([tree(inner), tree(common), tree(outer)])


def merged(parts):
    whole = Scatter(None, jnp.concatenate([part.kept for part in parts], axis=2), parts[0].steps)
    whole.sent = tuple(
        jnp.concatenate(pieces, axis=2) for pieces in zip(*[part.sent for part in parts])
    )
    whole.at = parts[0].at
    return whole


def shards(
    latents,
    targets,
    horizon,
    memory_valid,
    embed,
    qkv_weight,
    out_weight,
    up_weight,
    down_weight,
    head_weight,
    gains,
    embed_rows,
    embed_cols,
    qkv_rows,
    qkv_cols,
    out_rows,
    out_cols,
    up_rows,
    up_cols,
    down_rows,
    down_cols,
    head_rows,
    head_cols,
    gain_second,
):
    samples = latents.shape[0]
    sizes = (lax.axis_size("dp"), lax.axis_size("fsdp"))
    highest = (sizes[0] * sizes[1]).bit_length() - 1
    gather_steps = [(bit,) for bit in reversed(range(3, highest))] + [(2, 1), (0,)]
    scatter_steps = gather_steps[::-1]
    mesh_plan = (sizes[0], sizes[1], gather_steps)
    core = (lax.axis_index("fsdp") & 1).astype(jnp.int32).reshape(1)

    out_turned = jnp.swapaxes(out_weight, 1, 2)
    down_turned = jnp.swapaxes(down_weight, 1, 2)
    masters = [qkv_weight, out_turned, up_weight, down_turned, embed.T, head_weight]
    widths = [qkv_weight.shape[2], out_weight.shape[2], up_weight.shape[2], down_weight.shape[1]]
    widths = widths + [embed.shape[0], head_weight.shape[1]]
    att_widths, ffn_widths = widths[0:2], widths[2:4]
    chunk_widths = [
        att_widths + widths[4:5],
        ffn_widths + att_widths,
        ffn_widths + att_widths + ffn_widths + widths[5:6],
    ]
    chunks = [Gather(piece, gather_steps) for piece in run_pack(masters, chunk_widths)]
    first, second, third = chunks
    latent_rows = latents.transpose(0, 2, 1)
    target_rows = targets.transpose(0, 2, 1)
    shared = (gains, memory_valid, core)
    back_shared = (gains, core)

    count = len(gather_steps)
    flat = lambda item: item if item.ndim == 2 else item.reshape(1, -1)
    inner = [flat(item) for item in (qkv_rows, out_rows, up_rows, down_cols, embed_cols, head_rows)]
    outer = [flat(item) for item in (qkv_cols, out_cols, up_cols, down_rows, embed_rows, head_cols)]
    row_stats = [inner[at] if ROW_IS_INNER[at] else outer[at] for at in range(6)]
    first_row = run_first(masters, row_stats)
    for at in range(count - 1):
        for chunk in chunks:
            chunk.send()
        if at == 0:
            first.others, first_row = tie(first.others, first_row)
        for chunk in chunks[: 2 if at == count - 2 else 3]:
            chunk.join()
            if at == count - 3 and chunk is first:
                first.held, third.held = tie(first.held, third.held)
    first.send()
    (other,) = first.others
    held, other, second.held = tie(first.held, other, second.held)
    second.send()
    kept = [run_forward(0, chunk_widths[0], mesh_plan, latent_rows, held, other, *shared)]
    middle, (other,) = tie(kept[0][1], second.others)
    kept.append(
        run_forward(1, chunk_widths[1], mesh_plan, middle, second.held, other, *shared)
    )
    middle, third.others = tie(kept[1][1], third.others)
    third.join()
    third.send()
    (other,) = third.others
    dmiddle, sent, held, gain_middle, loss, counted = run_middle(
        chunk_widths[2],
        mesh_plan,
        middle,
        third.held,
        other,
        target_rows,
        gains,
        memory_valid,
        horizon,
        core,
    )
    pair = Scatter(sent, held, scatter_steps)
    pair.send()
    pair.join()
    like = first.held
    before = (kept[0][1], kept[1][6], kept[1][8], kept[1][7])
    dmiddle, pair.sent = tie(dmiddle, pair.sent)
    pair.send()
    dmiddle, sent, held, gain_one = run_backward(
        1, chunk_widths[1], mesh_plan, like, kept[1], dmiddle, *back_shared, before
    )
    dmiddle, sent, held, pair.others = tie(dmiddle, sent, held, pair.others)
    one = Scatter(sent, held, scatter_steps)
    one.send()
    pair.join()
    one.join()
    dmiddle, pair.sent, one.sent = tie(dmiddle, pair.sent, one.sent)
    one.send()
    pair.send()
    sent, held, gain_zero = run_backward(
        0, chunk_widths[0], mesh_plan, like, kept[0], dmiddle, *back_shared, latent_rows
    )
    sent, held, pair.others, one.others = tie(sent, held, pair.others, one.others)
    zero = Scatter(sent, held, scatter_steps)
    zero.send()
    one.join()
    one.send()
    pair.join()
    zero.join()
    one.others = behind(one.others, zero.sent)
    zero.send()
    one.join()
    early = merged([pair, one])
    while early.at < count:
        early.send()
        zero.others = behind(zero.others, early.sent)
        early.join()
    raw_early = early.kept[0]

    packet = run_early(
        widths, raw_early, first_row, [gain_middle, gain_one], loss, counted
    )
    while zero.at < count:
        zero.join()
        if zero.at < count:
            zero.send()
    raw_late = zero.kept[0]
    packet = run_late(widths, packet, raw_late, gain_zero)
    inner_bits = sizes[1].bit_length() - 1
    rest = list(range(3, highest))
    groups = [(0,), (2, 1)] + [tuple(rest[at : at + 2][::-1]) for at in range(0, len(rest), 2)]
    for group in groups:
        packet = sum_packets(packet, group, inner_bits)
    results = run_update(
        widths, sizes, packet, raw_early, raw_late, masters, inner, outer, gains, gain_second
    )
    results = list(results)
    for at in range(3):
        results[at] = results[at].reshape(())
    for at in (3, 4, 11, 12, 19, 20):
        results[at] = jnp.swapaxes(results[at], -1, -2)
    for at in (5, 6, 25, 26):
        results[at] = results[at].reshape(-1)
    return tuple(results)


def solution(mesh):
    return jax.shard_map(
        shards,
        mesh=mesh,
        in_specs=(
            P(("dp", "fsdp"), None, None),
            P(("dp", "fsdp"), None, None),
            P(("dp", "fsdp")),
            P(("dp", "fsdp")),
            P("dp", "fsdp"),
            P(None, "fsdp", "dp"),
            P(None, "fsdp", "dp"),
            P(None, "fsdp", "dp"),
            P(None, "dp", "fsdp"),
            P("fsdp", "dp"),
            P(),
            P("dp"),
            P("fsdp"),
            P(None, "fsdp"),
            P(None, "dp"),
            P(None, "fsdp"),
            P(None, "dp"),
            P(None, "fsdp"),
            P(None, "dp"),
            P(None, "dp"),
            P(None, "fsdp"),
            P("fsdp"),
            P("dp"),
            P(),
        ),
        out_specs=(
            P(),
            P(),
            P(),
            P("dp", "fsdp"),
            P("dp", "fsdp"),
            P("dp"),
            P("fsdp"),
            P(None, "fsdp", "dp"),
            P(None, "fsdp", "dp"),
            P(None, "fsdp"),
            P(None, "dp"),
            P(None, "fsdp", "dp"),
            P(None, "fsdp", "dp"),
            P(None, "fsdp"),
            P(None, "dp"),
            P(None, "fsdp", "dp"),
            P(None, "fsdp", "dp"),
            P(None, "fsdp"),
            P(None, "dp"),
            P(None, "dp", "fsdp"),
            P(None, "dp", "fsdp"),
            P(None, "dp"),
            P(None, "fsdp"),
            P("fsdp", "dp"),
            P("fsdp", "dp"),
            P("fsdp"),
            P("dp"),
            P(),
            P(),
            P(),
        ),
        check_vma=False,
    )
```

```python
import functools

import jax
import jax.numpy as jnp
from jax import lax
from jax.experimental import pallas as pl
from jax.experimental.pallas import tpu as pltpu
from jax.sharding import PartitionSpec as P

D = 256
HEADS = 8
HEAD = D // HEADS
FF = 1024
CATS = 32
CLASSES = 32
LAYERS = 3
SEG = 48
MEM = 48
CTX = 96
VOCAB = 1024
GROUP = 8
WIDE_GROUP = 8
ROWS = GROUP * CTX
HALF = D // 2
VMEM_BYTES = 24 * 1024 * 1024
MIDDLE_BYTES = 43 * 1024 * 1024

decay_two = 0.9
step_rate = 0.3
clip_limit = 0.05
tiny_term = 1e-30
norm_eps = 1e-06
masked_score = -1e30
log2_e = 1.4426950408889634
score_scale = HEAD ** (-0.5)
gelu_one = 0.7978845608028654
gelu_two = 0.044715


def dot_nn(left, right):
    return lax.dot_general(
        left, right, (((1,), (0,)), ((), ())), preferred_element_type=jnp.float32
    )


def dot_nt(left, right):
    return lax.dot_general(
        left, right, (((1,), (1,)), ((), ())), preferred_element_type=jnp.float32
    )


def dot_tn(left, right):
    return lax.dot_general(
        left, right, (((0,), (0,)), ((), ())), preferred_element_type=jnp.float32
    )


def inverse_rms(values):
    return lax.rsqrt(jnp.mean(values * values, axis=-1, keepdims=True) + norm_eps)


def rms_back(values, inverse, gain_row, upstream):
    normed = values * inverse
    scaled = upstream * gain_row
    inner = jnp.mean(scaled * normed, axis=-1, keepdims=True)
    return (
        inverse * (scaled - normed * inner),
        jnp.sum(upstream * normed, axis=0, keepdims=True),
    )


def head_masks():
    lane = lax.broadcasted_iota(jnp.int32, (1, D // 2), 1) // HEAD
    return [lane == head for head in range(HEADS // 2)]


def expand_heads(rows, masks):
    return jnp.concatenate([rows * mask.astype(rows.dtype) for mask in masks], axis=0)


def collapse_heads(spread, rows, masks):
    product = dot_tn(spread, rows)
    queries = product.shape[0] // len(masks)
    taken = product[(len(masks) - 1) * queries :]
    for at, mask in enumerate(masks[:-1]):
        taken = jnp.where(mask, product[at * queries : (at + 1) * queries], taken)
    return taken


def half_of(part, side):
    start = part * D + side * HALF
    return slice(start, start + HALF)


def fill_bias(bias_ref):
    spread = bias_ref.shape[2]
    queries = spread // (HEADS // 2)
    key_at = lax.broadcasted_iota(jnp.int32, (CTX, spread), 0)
    query_at = lax.broadcasted_iota(jnp.int32, (CTX, spread), 1) % queries + (CTX - queries)
    later = key_at > query_at
    crosses = (query_at >= MEM) & (key_at < MEM)
    bias_ref[0] = jnp.where(later | crosses, masked_score, 0.0)
    bias_ref[1] = jnp.where(later, masked_score, 0.0)


def block_place(device, steps):
    place, weight = 0, 1
    for step in steps[:-1]:
        digit = 0
        for bit in step:
            digit = 2 * digit + ((device >> bit) & 1)
        place += digit * weight
        weight <<= len(step)
    return place


def place_weights(targets, own_ref, other_ref, core, widths, mesh_plan, start=0):
    outer_count, inner_count, steps = mesh_plan
    rows = own_ref.shape[1]
    for high in range(inner_count // 2):
        for source, side in ((own_ref, core), (other_ref, 1 - core)):
            here = pl.ds(pl.multiple_of((2 * high + side) * rows, rows), rows)
            at = start
            for (target, column), width in zip(targets, widths):
                block = [
                    source[
                        block_place(outer * inner_count + 2 * high, steps), :, at : at + width
                    ]
                    for outer in range(outer_count)
                ]
                target[here, column : column + width * outer_count] = jnp.concatenate(
                    block, axis=1
                )
                at += width


def write_blocks(send_ref, keep_ref, sum_ref, core, widths, mesh_plan, start=0):
    outer_count, inner_count, steps = mesh_plan
    rows = keep_ref.shape[1]
    for high in range(inner_count // 2):
        for target, side in ((keep_ref, core), (send_ref, 1 - core)):
            here = pl.ds(pl.multiple_of((2 * high + side) * rows, rows), rows)
            taken = sum_ref[here, :]
            for outer in range(outer_count):
                block, column = [], 0
                for width in widths:
                    block.append(taken[:, column + outer * width : column + (outer + 1) * width])
                    column += width * outer_count
                place = block_place(outer * inner_count + 2 * high, steps)
                target[place, :, start : start + sum(widths)] = jnp.concatenate(
                    block, axis=1
                ).astype(target.dtype)


def one_hot_rows(latent_ref, hot_ref, first):
    spot = lax.broadcasted_iota(jnp.int32, (CATS, VOCAB), 1) // CLASSES
    group = lax.broadcasted_iota(jnp.int32, (CATS, VOCAB), 0)
    spreader = jnp.where(spot == group, 1.0, 0.0).astype(jnp.bfloat16)
    classes = (lax.broadcasted_iota(jnp.int32, (1, VOCAB), 1) % CLASSES).astype(jnp.float32)
    for sample in range(GROUP):
        drawn = dot_tn(latent_ref[sample].astype(jnp.float32).astype(jnp.bfloat16), spreader)
        hot_ref[pl.ds(first + sample * CTX, CTX), :] = jnp.where(
            drawn == classes, 1.0, 0.0
        ).astype(jnp.bfloat16)


def tail_rows(values, queries):
    if queries == CTX:
        return values
    return jnp.concatenate(
        [
            values[(sample + 1) * CTX - queries : (sample + 1) * CTX]
            for sample in range(values.shape[0] // CTX)
        ],
        axis=0,
    )


def attend_forward(step, hidden, gain_row, weight_ref, valid_ref, bias_ref, masks, refs):
    middle_ref, qkv_ref, mix_ref, chance_ref = refs
    queries = chance_ref.shape[3] // (HEADS // 2)
    group = hidden.shape[0] // CTX
    normed = (hidden * inverse_rms(hidden) * gain_row).astype(jnp.bfloat16)
    qkv_ref[...] = dot_nn(normed, weight_ref[:, 0 : 3 * D]).astype(jnp.bfloat16)
    units = [(sample, side) for sample in range(group) for side in range(2)]
    scores = []
    for sample, side in units:
        rows = slice(sample * CTX, (sample + 1) * CTX)
        tail = slice((sample + 1) * CTX - queries, (sample + 1) * CTX)
        spread = expand_heads(qkv_ref[tail, half_of(0, side)], masks)
        scores.append(dot_nt(qkv_ref[rows, half_of(1, side)], spread))
    for (sample, side), score in zip(units, scores):
        score = score + bias_ref[valid_ref[step * group + sample]]
        peak = jnp.max(score, axis=0, keepdims=True)
        exponent = jnp.exp2((score - peak) * (score_scale * log2_e))
        total = jnp.sum(exponent, axis=0, keepdims=True)
        chance_ref[sample, side] = (exponent * (1.0 / total)).astype(jnp.bfloat16)
    for sample, side in units:
        rows = slice(sample * CTX, (sample + 1) * CTX)
        mix_ref[sample * queries : (sample + 1) * queries, half_of(0, side)] = collapse_heads(
            chance_ref[sample, side], qkv_ref[rows, half_of(2, side)], masks
        ).astype(jnp.bfloat16)
    middle_ref[...] = tail_rows(hidden, queries) + dot_nn(
        mix_ref[...], weight_ref[:, 3 * D : 4 * D]
    )


def gelu_parts(value):
    square = value * value
    share = 0.5 + 0.5 * jnp.tanh(value * (gelu_one + (gelu_one * gelu_two) * square))
    active = value * share
    bent = active * (1.0 - share)
    return active, share + bent * (2.0 * gelu_one + (6.0 * gelu_one * gelu_two) * square)


def feed_forward(middle, gain_row, weight_ref, inner_ref, slope_ref):
    normed = (middle * inverse_rms(middle) * gain_row).astype(jnp.bfloat16)
    for part in range(FF // D):
        columns = slice(part * D, (part + 1) * D)
        inner = dot_nn(normed, weight_ref[:, columns])
        for sample in range(middle.shape[0] // CTX):
            rows = slice(sample * CTX, (sample + 1) * CTX)
            active, slope = gelu_parts(inner[rows])
            inner_ref[rows, columns] = active.astype(jnp.bfloat16)
            slope_ref[rows, columns] = slope.astype(jnp.bfloat16)
    return middle + dot_nt(inner_ref[...], weight_ref[:, FF : 2 * FF])


def feed_back(here, upstream, middle, gain_row, weight_ref, slope_ref, refs):
    normed_ref, dinner_ref, dout_ref = refs
    dout = upstream.astype(jnp.bfloat16)
    dout_ref[here(0, middle.shape[0]), :] = dout
    inverse = inverse_rms(middle)
    normed_ref[here(0, middle.shape[0]), :] = (middle * inverse * gain_row).astype(jnp.bfloat16)
    for part in range(FF // D):
        columns = slice(part * D, (part + 1) * D)
        dact = dot_nn(dout, weight_ref[:, FF + part * D : FF + (part + 1) * D])
        dinner_ref[here(0, middle.shape[0]), columns] = (
            dact * slope_ref[:, columns].astype(jnp.float32)
        ).astype(jnp.bfloat16)
    dnormed = dot_nt(dinner_ref[here(0, middle.shape[0]), :], weight_ref[:, 0:FF])
    through, gain_part = rms_back(middle, inverse, gain_row, dnormed)
    return upstream + through, gain_part


def attend_back(step, here, saved, dmiddle, gain_row, weight_ref, masks, refs):
    hidden, qkv_ref, mix_ref, chance_ref = saved
    normed_ref, dmiddle_ref, dqkv_ref, mixes_ref = refs
    group = hidden.shape[0] // CTX
    queries = chance_ref.shape[3] // (HEADS // 2)
    short = here(0, group * queries, queries)
    dattend = dmiddle.astype(jnp.bfloat16)
    dmiddle_ref[short, :] = dattend
    mixes_ref[short, :] = mix_ref[...]
    dmix = dot_nt(dattend, weight_ref[:, 3 * D : 4 * D]).astype(jnp.bfloat16)
    units = [(sample, side) for sample in range(group) for side in range(2)]
    slopes, dchances, dscores = [], [], []
    for sample, side in units:
        rows = slice(sample * CTX, (sample + 1) * CTX)
        slopes.append(
            expand_heads(
                dmix[sample * queries : (sample + 1) * queries, half_of(0, side)], masks
            )
        )
        dchances.append(dot_nt(qkv_ref[rows, half_of(2, side)], slopes[-1]))
    for (sample, side), dchance in zip(units, dchances):
        chance = chance_ref[sample, side].astype(jnp.float32)
        weighed = chance * dchance
        dscores.append(
            (weighed - chance * jnp.sum(weighed, axis=0, keepdims=True)).astype(jnp.bfloat16)
        )
    for at, (sample, side) in enumerate(units):
        rows = slice(sample * CTX, (sample + 1) * CTX)
        tail = slice((sample + 1) * CTX - queries, (sample + 1) * CTX)
        there = here(sample * CTX, CTX)
        spread = expand_heads(qkv_ref[tail, half_of(0, side)], masks)
        keys = qkv_ref[rows, half_of(1, side)]
        dvalues = dot_nn(chance_ref[sample, side], slopes[at])
        dkeys = dot_nn(dscores[at], spread) * score_scale
        dqueries = (collapse_heads(dscores[at], keys, masks) * score_scale).astype(jnp.bfloat16)
        if queries < CTX:
            nothing = jnp.zeros((CTX - queries, HALF), jnp.bfloat16)
            dqueries = jnp.concatenate([nothing, dqueries], axis=0)
        dqkv_ref[there, half_of(0, side)] = dqueries
        dqkv_ref[there, half_of(1, side)] = dkeys.astype(jnp.bfloat16)
        dqkv_ref[there, half_of(2, side)] = dvalues.astype(jnp.bfloat16)
    inverse = inverse_rms(hidden)
    normed_ref[here(0, hidden.shape[0]), :] = (hidden * inverse * gain_row).astype(jnp.bfloat16)
    dnormed = dot_nt(dqkv_ref[here(0, hidden.shape[0]), :], weight_ref[:, 0 : 3 * D])
    through, gain_part = rms_back(hidden, inverse, gain_row, dnormed)
    if queries < CTX:
        nothing = jnp.zeros((CTX - queries, D), jnp.float32)
        pieces = []
        for sample in range(group):
            pieces = pieces + [nothing, dmiddle[sample * queries : (sample + 1) * queries]]
        dmiddle = jnp.concatenate(pieces, axis=0)
    return dmiddle + through, gain_part


def row_spec(width, rows=ROWS):
    return pl.BlockSpec((rows, width), lambda step: (step, 0))


def chance_spec(queries):
    return pl.BlockSpec((GROUP, 2, CTX, HEADS // 2 * queries), lambda step: (step, 0, 0, 0))


def latent_spec():
    return pl.BlockSpec((GROUP, CATS, CTX), lambda step: (step, 0, 0))


def whole_spec(shape):
    return pl.BlockSpec(shape, lambda step: (0,) * len(shape))


def in_hbm(item):
    return pltpu.with_memory_space_constraint(item, pltpu.HBM)


def smem_spec():
    return pl.BlockSpec(memory_space=pltpu.SMEM)


def forward_kernel(layer, widths, mesh_plan, source_ref, own_ref, other_ref, gains_ref, valid_ref, core_ref, *refs):
    entry_ref, att_ref, before_ref = refs[0], refs[5], refs[6]
    bias_ref = refs[7] if layer == 0 else refs[9]
    step = pl.program_id(0)

    @pl.when(step == 0)
    def _():
        fill_bias(bias_ref)
        att = [(att_ref, 0), (att_ref, 3 * D)]
        before = [(before_ref, 0)] if layer == 0 else [(before_ref, 0), (before_ref, FF)]
        targets = att + before if layer == 0 else before + att
        place_weights(targets, own_ref, other_ref, core_ref[0], widths[: len(targets)], mesh_plan)

    if layer == 0:
        one_hot_rows(source_ref, refs[8], 0)
        hidden = dot_nt(refs[8][...], before_ref[...])
    else:
        gain_ffn = gains_ref[LAYERS + layer - 1 : LAYERS + layer, :]
        hidden = feed_forward(source_ref[...], gain_ffn, before_ref, refs[7], refs[8])
    entry_ref[...] = hidden
    attend_forward(
        step,
        hidden,
        gains_ref[layer : layer + 1, :],
        att_ref,
        valid_ref,
        bias_ref,
        head_masks(),
        refs[1:5],
    )


def run_forward(layer, widths, mesh_plan, source, own, other, gains, valid, core):
    tokens = valid.shape[0] * CTX
    f32, b16 = jnp.float32, jnp.bfloat16
    chances = HEADS // 2 * CTX
    outs = [
        (pltpu.HBM((tokens, D), f32), row_spec(D)),
        (pltpu.HBM((tokens, D), f32), row_spec(D)),
        (pltpu.HBM((tokens, 3 * D), b16), row_spec(3 * D)),
        (pltpu.HBM((tokens, D), b16), row_spec(D)),
        (pltpu.HBM((tokens // CTX, 2, CTX, chances), b16), chance_spec(CTX)),
        (pltpu.HBM((D, 4 * D), b16), whole_spec((D, 4 * D))),
    ]
    scratch = [pltpu.VMEM((2, CTX, chances), f32)]
    if layer == 0:
        scratch = [pltpu.VMEM((D, VOCAB), b16)] + scratch + [pltpu.VMEM((ROWS, VOCAB), b16)]
        source_spec = latent_spec()
    else:
        source_spec = row_spec(D)
        outs.append((pltpu.HBM((D, 2 * FF), b16), whole_spec((D, 2 * FF))))
        outs = outs + [(pltpu.HBM((tokens, FF), b16), row_spec(FF))] * 2
        source = in_hbm(source)
    return pl.pallas_call(
        functools.partial(forward_kernel, layer, widths, mesh_plan),
        grid=(tokens // ROWS,),
        in_specs=[
            source_spec,
            whole_spec(own.shape),
            whole_spec(other.shape),
            whole_spec(gains.shape),
            smem_spec(),
            smem_spec(),
        ],
        out_specs=[spec for _, spec in outs],
        out_shape=[item for item, _ in outs],
        scratch_shapes=scratch,
        compiler_params=pltpu.CompilerParams(vmem_limit_bytes=VMEM_BYTES),
        cost_estimate=pl.CostEstimate(
            flops=2 * tokens * D * 12 * D,
            bytes_accessed=tokens * D * 16 + D * 12 * D * 4,
            transcendentals=tokens * (FF + HEADS * CTX),
        ),
        name="forward_part",
    )(source, own, other, gains, valid, core)


def middle_kernel(widths, mesh_plan, *refs):
    source_ref, own_ref, other_ref, drawn_ref, gains_ref, valid_ref, horizon_ref, core_ref = refs[:8]
    out_ref, send_ref, keep_ref, gain_ref, loss_ref, count_ref = refs[8:14]
    bias_ref, weight_one_ref, att_ref, weight_two_ref, head_ref, turned_ref = refs[14:20]
    entry_ref, qkv_ref, mix_ref, chance_ref, middle_two_ref, inner_one_ref, slope_one_ref = refs[20:27]
    inner_ref, slope_ref, last_ref, dmiddle_ref, sum_ref, targets_ref, counted_ref = refs[27:34]
    normed_long, dattend_ref, dqkv_long, mixes_ref, normed_two_long, dinner_long, dout_long = refs[34:]
    tokens = middle_two_ref.shape[0]
    final_ref = normed_long.at[0:tokens]
    dlogits_ref = dqkv_long.at[0:VOCAB]
    normed_ref = normed_two_long.at[0:tokens]
    dinner_ref = dinner_long.at[0:tokens]
    dout_ref = dout_long.at[0:tokens]
    groups = source_ref.shape[0] // (WIDE_GROUP * CTX)
    masks = head_masks()
    gain_att = gains_ref[LAYERS - 1 : LAYERS, :]
    gain_before = gains_ref[2 * LAYERS - 2 : 2 * LAYERS - 1, :]
    gain_ffn = gains_ref[2 * LAYERS - 1 : 2 * LAYERS, :]
    gain_final = gains_ref[2 * LAYERS : 2 * LAYERS + 1, :]
    fill_bias(bias_ref)
    place_weights(
        [
            (weight_one_ref, 0),
            (weight_one_ref, FF),
            (att_ref, 0),
            (att_ref, 3 * D),
            (weight_two_ref, 0),
            (weight_two_ref, FF),
            (head_ref, 0),
        ],
        own_ref,
        other_ref,
        core_ref[0],
        widths,
        mesh_plan,
    )

    def rows_of(group, unit=CTX):
        return pl.ds(pl.multiple_of(group * (WIDE_GROUP * unit), WIDE_GROUP * unit), WIDE_GROUP * unit)

    def forward(group, carry):
        rows, short = rows_of(group), rows_of(group, SEG)
        hidden = feed_forward(
            source_ref[rows, :],
            gain_before,
            weight_one_ref,
            inner_one_ref.at[rows],
            slope_one_ref.at[rows],
        )
        entry_ref[rows, :] = hidden
        attend_forward(
            group,
            hidden,
            gain_att,
            att_ref,
            valid_ref,
            bias_ref,
            masks,
            (
                middle_two_ref.at[short],
                qkv_ref.at[rows],
                mix_ref.at[short],
                chance_ref.at[pl.ds(group * WIDE_GROUP, WIDE_GROUP)],
            ),
        )
        return carry

    lax.fori_loop(0, groups, forward, 0)
    turned_ref[...] = head_ref[...].T
    samples = tokens // SEG
    targets_ref[...] = jnp.concatenate([drawn_ref[at] for at in range(samples)], axis=1)
    position = lax.broadcasted_iota(jnp.int32, (1, SEG), 1)
    counted_ref[...] = jnp.concatenate(
        [jnp.where(position < horizon_ref[at], 1.0, 0.0) for at in range(samples)], axis=1
    )
    count_ref[...] = jnp.sum(counted_ref[...], axis=1, keepdims=True)
    for block in range(tokens // ROWS):
        rows = slice(block * ROWS, (block + 1) * ROWS)
        middle = middle_two_ref[rows, :]
        normed = (middle * inverse_rms(middle) * gain_ffn).astype(jnp.bfloat16)
        normed_ref[rows, :] = normed
        for part in range(FF // D):
            columns = slice(part * D, (part + 1) * D)
            inner = dot_nn(normed, weight_two_ref[:, columns])
            for piece in range(GROUP):
                there = slice(block * ROWS + piece * CTX, block * ROWS + (piece + 1) * CTX)
                active, slope = gelu_parts(inner[piece * CTX : (piece + 1) * CTX])
                inner_ref[there, columns] = active.astype(jnp.bfloat16)
                slope_ref[there, columns] = slope.astype(jnp.bfloat16)
        last = middle + dot_nt(inner_ref[rows, :], weight_two_ref[:, FF : 2 * FF])
        last_ref[rows, :] = last
        final_ref[rows, :] = (last * inverse_rms(last) * gain_final).astype(jnp.bfloat16)
    span = D
    loss = jnp.zeros((1, span), jnp.float32)
    spots = lax.broadcasted_iota(jnp.int32, (CLASSES, span), 0)
    for part in range(tokens // span):
        columns = slice(part * span, (part + 1) * span)
        counted = counted_ref[0:1, columns]
        final = final_ref[columns, :]
        for quarter in range(VOCAB // D):
            logits = dot_nt(turned_ref[quarter * D : (quarter + 1) * D, :], final)
            for inside in range(D // CLASSES):
                group = quarter * (D // CLASSES) + inside
                values = logits[inside * CLASSES : (inside + 1) * CLASSES]
                shifted = values - jnp.max(values, axis=0, keepdims=True)
                exponent = jnp.exp2(shifted * log2_e)
                total = jnp.sum(exponent, axis=0, keepdims=True)
                hot = spots == targets_ref[group : group + 1, columns]
                chosen = jnp.sum(jnp.where(hot, shifted, 0.0), axis=0, keepdims=True)
                loss = loss + counted * (jnp.log(total) - chosen)
                chance = exponent * (1.0 / total)
                slope = (chance - jnp.where(hot, 1.0, 0.0)) * counted
                dlogits_ref[group * CLASSES : (group + 1) * CLASSES, columns] = slope.astype(
                    jnp.bfloat16
                )
    loss_ref[...] = jnp.sum(loss, axis=1, keepdims=True)
    sum_ref[:, 2 * FF : 2 * FF + VOCAB] = dot_nt(final_ref[...].T, dlogits_ref[...])
    dfinal = dot_nn(head_ref[...], dlogits_ref[...]).T
    last = last_ref[...]
    dlast, gain_part = rms_back(last, inverse_rms(last), gain_final, dfinal)
    gain_ref[1:2, :] = gain_part
    last_ref[...] = dlast
    gain_sum = jnp.zeros((1, D), jnp.float32)
    for block in range(tokens // ROWS):
        rows = slice(block * ROWS, (block + 1) * ROWS)
        upstream = last_ref[rows, :]
        dout = upstream.astype(jnp.bfloat16)
        dout_ref[rows, :] = dout
        for part in range(FF // D):
            columns = slice(part * D, (part + 1) * D)
            dact = dot_nn(dout, weight_two_ref[:, FF + part * D : FF + (part + 1) * D])
            dinner_ref[rows, columns] = (dact * slope_ref[rows, columns].astype(jnp.float32)).astype(jnp.bfloat16)
        dnormed = dot_nt(dinner_ref[rows, :], weight_two_ref[:, 0:FF])
        middle = middle_two_ref[rows, :]
        through, gain_part = rms_back(middle, inverse_rms(middle), gain_ffn, dnormed)
        gain_sum = gain_sum + gain_part
        dmiddle_ref[rows, :] = upstream + through
    gain_ref[0:1, :] = gain_sum
    sum_ref[:, 0:FF] = dot_nn(normed_ref[...].T, dinner_ref[...])
    sum_ref[:, FF : 2 * FF] = dot_nn(dout_ref[...].T, inner_ref[...])
    write_blocks(send_ref, keep_ref, sum_ref, core_ref[0], widths[4:], mesh_plan)
    gain_ref[2:4, :] = jnp.zeros((2, D), jnp.float32)

    def backward(group, carry):
        rows, short = rows_of(group), rows_of(group, SEG)

        def here(start, length, unit=CTX):
            return pl.ds(pl.multiple_of(group * (WIDE_GROUP * unit) + start, 16), length)

        dentry, gain_part = attend_back(
            group,
            here,
            (
                entry_ref[rows, :],
                qkv_ref.at[rows],
                mix_ref.at[short],
                chance_ref.at[pl.ds(group * WIDE_GROUP, WIDE_GROUP)],
            ),
            dmiddle_ref[short, :],
            gain_att,
            att_ref,
            masks,
            (normed_long, dattend_ref, dqkv_long, mixes_ref),
        )
        gain_ref[2:3, :] += gain_part
        dbefore, gain_part = feed_back(
            here,
            dentry,
            source_ref[rows, :],
            gain_before,
            weight_one_ref,
            slope_one_ref.at[rows],
            (normed_two_long, dinner_long, dout_long),
        )
        out_ref[rows, :] = dbefore
        gain_ref[3:4, :] += gain_part
        return carry

    lax.fori_loop(0, groups, backward, 0)
    column = 0
    for left, right in [
        (normed_two_long, dinner_long),
        (dout_long, inner_one_ref),
        (normed_long, dqkv_long),
        (mixes_ref, dattend_ref),
    ]:
        wide = right.shape[1]
        sum_ref[:, column : column + wide] = dot_nn(left[...].T, right[...])
        column += wide
    write_blocks(
        send_ref, keep_ref, sum_ref, core_ref[0], widths[:4], mesh_plan, sum(widths[4:])
    )


def block_outs(own, widths):
    shape = jax.ShapeDtypeStruct
    blocks = own.shape[:2] + (sum(widths),)
    return [shape(blocks, jnp.bfloat16)] * 2


def run_middle(widths, mesh_plan, source, own, other, targets, gains, valid, horizon, core):
    tokens = source.shape[0]
    short = tokens // CTX * SEG
    samples = tokens // CTX
    chances = HEADS // 2 * SEG
    f32, b16 = jnp.float32, jnp.bfloat16
    shape = jax.ShapeDtypeStruct
    vmem = pl.BlockSpec(memory_space=pltpu.VMEM)
    return pl.pallas_call(
        functools.partial(middle_kernel, widths, mesh_plan),
        in_specs=[vmem] * 5 + [smem_spec()] * 3,
        out_specs=[vmem] * 6,
        out_shape=[pltpu.HBM((tokens, D), f32)]
        + block_outs(own, widths)
        + [pltpu.HBM((4, D), f32), shape((1, 1), f32), shape((1, 1), f32)],
        scratch_shapes=[
            pltpu.VMEM((2, CTX, chances), f32),
            pltpu.VMEM((D, 2 * FF), b16),
            pltpu.VMEM((D, 4 * D), b16),
            pltpu.VMEM((D, 2 * FF), b16),
            pltpu.VMEM((D, VOCAB), b16),
            pltpu.VMEM((VOCAB, D), b16),
            pltpu.VMEM((tokens, D), f32),
            pltpu.VMEM((tokens, 3 * D), b16),
            pltpu.VMEM((short, D), b16),
            pltpu.VMEM((samples, 2, CTX, chances), b16),
            pltpu.VMEM((short, D), f32),
            pltpu.VMEM((tokens, FF), b16),
            pltpu.VMEM((tokens, FF), b16),
            pltpu.VMEM((short, FF), b16),
            pltpu.VMEM((short, FF), b16),
            pltpu.VMEM((short, D), f32),
            pltpu.VMEM((short, D), f32),
            pltpu.VMEM((D, 2 * FF + max(4 * D, VOCAB)), f32),
            pltpu.VMEM((CATS, short), jnp.int32),
            pltpu.VMEM((1, short), f32),
            pltpu.VMEM((tokens, D), b16),
            pltpu.VMEM((short, D), b16),
            pltpu.VMEM((tokens, 3 * D), b16),
            pltpu.VMEM((short, D), b16),
            pltpu.VMEM((tokens, D), b16),
            pltpu.VMEM((tokens, FF), b16),
            pltpu.VMEM((tokens, D), b16),
        ],
        compiler_params=pltpu.CompilerParams(vmem_limit_bytes=MIDDLE_BYTES + (0 if own.shape[1] >= 64 else VMEM_BYTES // 2)),
        cost_estimate=pl.CostEstimate(
            flops=6 * tokens * D * 8 * FF,
            bytes_accessed=tokens * D * 8 + D * 6 * FF * 10,
            transcendentals=2 * tokens * (FF + VOCAB),
        ),
        name="middle_part",
    )(source, own, other, targets, gains, valid, horizon, core)


def backward_kernel(layer, widths, mesh_plan, *refs):
    entry_ref, qkv_ref, mix_ref, chance_ref, dmiddle_ref, att_ref, gains_ref, core_ref = refs[:8]
    if layer == 0:
        latent_ref, send_ref, keep_ref, gain_ref = refs[8:12]
        att_kept, before_kept, sum_ref = refs[12:16], refs[16:18], refs[18]
    else:
        before_ref, ffn_ref, slope_ref, inner_hbm, out_ref, send_ref, keep_ref, gain_ref = refs[8:16]
        att_kept, before_kept, sum_ref = refs[16:20], refs[20:23], refs[23]
        inner_ref, inner_sem = refs[24:26]
        copy = pltpu.make_async_copy(inner_hbm, inner_ref, inner_sem)
    step = pl.program_id(0)

    def here(start, length, unit=CTX):
        base = step * (GROUP * unit)
        return pl.ds(pl.multiple_of(base + start, 16), length)

    @pl.when(step == 0)
    def _():
        gain_ref[...] = jnp.zeros_like(gain_ref)
        if layer > 0:
            copy.start()

    dentry, gain_part = attend_back(
        step,
        here,
        (entry_ref[...], qkv_ref, mix_ref, chance_ref),
        dmiddle_ref[...],
        gains_ref[layer : layer + 1, :],
        att_ref,
        head_masks(),
        att_kept,
    )
    gain_ref[0:1, :] += gain_part
    if layer == 0:
        before_kept[0][here(0, ROWS), :] = dentry.astype(jnp.bfloat16)
        one_hot_rows(latent_ref, before_kept[1], pl.multiple_of(step * ROWS, ROWS))
    else:
        dbefore, gain_part = feed_back(
            here,
            dentry,
            before_ref[...],
            gains_ref[LAYERS + layer - 1 : LAYERS + layer, :],
            ffn_ref,
            slope_ref,
            before_kept,
        )
        out_ref[...] = dbefore
        gain_ref[1:2, :] += gain_part

    @pl.when(step == pl.num_programs(0) - 1)
    def _():
        normed_ref, dattend_ref, dqkv_ref, mixes_ref = att_kept
        att = [(normed_ref, dqkv_ref), (mixes_ref, dattend_ref)]
        if layer == 0:
            pairs = att + [(before_kept[0], before_kept[1])]
        else:
            copy.wait()
            normed_two_ref, dinner_ref, dout_ref = before_kept
            pairs = [(normed_two_ref, dinner_ref), (dout_ref, inner_ref)] + att
        column = 0
        for left, right in pairs:
            wide = right.shape[1]
            sum_ref[:, column : column + wide] = dot_nn(left[...].T, right[...])
            column += wide
        write_blocks(send_ref, keep_ref, sum_ref, core_ref[0], widths, mesh_plan)


def run_backward(layer, widths, mesh_plan, blocks_like, saved, dmiddle, gains, core, before):
    entry, _, qkv, mix, chance, weights = [in_hbm(item) for item in saved[:6]]
    dmiddle = in_hbm(dmiddle)
    if layer > 0:
        before = [in_hbm(item) for item in before]
    tokens = entry.shape[0]
    queries = chance.shape[3] // (HEADS // 2)
    short = tokens // CTX * queries
    f32, b16 = jnp.float32, jnp.bfloat16
    shape = jax.ShapeDtypeStruct
    in_specs = [
        row_spec(D),
        row_spec(3 * D),
        row_spec(D, GROUP * queries),
        chance_spec(queries),
        row_spec(D, GROUP * queries),
        whole_spec(weights.shape),
        whole_spec(gains.shape),
        smem_spec(),
    ]
    operands = [entry, qkv, mix, chance, dmiddle, weights, gains, core]
    blocks = block_outs(blocks_like, widths)
    outs = [(item, whole_spec(item.shape)) for item in blocks]
    outs.append((pltpu.HBM((2, D), f32), whole_spec((2, D))))
    scratch = [
        pltpu.VMEM((tokens, D), b16),
        pltpu.VMEM((short, D), b16),
        pltpu.VMEM((tokens, 3 * D), b16),
        pltpu.VMEM((short, D), b16),
    ]
    if layer == 0:
        in_specs.append(latent_spec())
        operands.append(before)
        scratch = scratch + [pltpu.VMEM((tokens, D), b16), pltpu.VMEM((tokens, VOCAB), b16)]
        wide = 4 * D + VOCAB
    else:
        in_specs = in_specs + [row_spec(D), whole_spec(before[1].shape), row_spec(FF)]
        in_specs.append(pl.BlockSpec(memory_space=pl.ANY))
        operands = operands + list(before)
        outs.insert(0, (pltpu.HBM((tokens, D), f32), row_spec(D)))
        scratch = scratch + [
            pltpu.VMEM((tokens, D), b16),
            pltpu.VMEM((tokens, FF), b16),
            pltpu.VMEM((tokens, D), b16),
        ]
        wide = 4 * D + 2 * FF
    scratch.append(pltpu.VMEM((D, wide), f32))
    if layer > 0:
        scratch = scratch + [pltpu.VMEM((tokens, FF), b16), pltpu.SemaphoreType.DMA]
    return pl.pallas_call(
        functools.partial(backward_kernel, layer, widths, mesh_plan),
        grid=(tokens // ROWS,),
        in_specs=in_specs,
        out_specs=[spec for _, spec in outs],
        out_shape=[item for item, _ in outs],
        scratch_shapes=scratch,
        compiler_params=pltpu.CompilerParams(vmem_limit_bytes=VMEM_BYTES * 3 // 2),
        cost_estimate=pl.CostEstimate(
            flops=6 * tokens * D * wide,
            bytes_accessed=tokens * D * 24 + D * wide * 6,
            transcendentals=tokens * FF,
        ),
        name="backward_part",
    )(*operands)


def pack_kernel(*refs):
    qkv_ref, out_ref, up_ref, down_ref, embed_ref, head_ref = refs[:6]
    low = lambda value: value.astype(jnp.bfloat16)
    att = [[low(qkv_ref[at]), low(out_ref[at].T)] for at in range(LAYERS)]
    ffn = [[low(up_ref[at]), low(down_ref[at])] for at in range(LAYERS)]
    pieces = [
        att[0] + [low(embed_ref[...])],
        ffn[0] + att[1],
        ffn[1] + att[2] + ffn[2] + [low(head_ref[...])],
    ]
    for target, piece in zip(refs[6:], pieces):
        target[...] = jnp.concatenate(piece, axis=1)


def run_pack(masters, chunk_widths):
    vmem = pl.BlockSpec(memory_space=pltpu.VMEM)
    rows = masters[0].shape[1]
    return pl.pallas_call(
        pack_kernel,
        in_specs=[vmem] * 6,
        out_specs=[vmem] * 3,
        out_shape=[
            jax.ShapeDtypeStruct((rows, sum(widths)), jnp.bfloat16) for widths in chunk_widths
        ],
        name="pack",
    )(*masters)


def matrix_plan(widths):
    order = [
        (2, 2), (3, 2), (5, 0), (2, 1), (3, 1), (0, 2), (1, 2),
        (2, 0), (3, 0), (0, 1), (1, 1), (0, 0), (1, 0), (4, 0),
    ]
    plan, column = {}, 0
    for which, layer in order:
        plan[(which, layer)] = (column, widths[which])
        column += widths[which]
    return plan, column


def matrix_list():
    return [(which, layer) for which in range(4) for layer in range(LAYERS)] + [(4, 0), (5, 0)]


MATRICES = 4 * LAYERS + 2
LANES = 128
INNER_ROWS = 16
COMMON_ROWS = 16
ROW_IS_INNER = [True, True, True, False, False, True]


def master_of(masters, which, layer):
    if which == 1:
        return masters[1][layer].T
    return masters[which][layer] if which < 4 else masters[which][...]


def old_row(refs, which, layer):
    return refs[which][layer : layer + 1, :] if which < 4 else refs[which][...]


LATE = [(0, 0), (1, 0), (4, 0)]
EDGE = INNER_ROWS + COMMON_ROWS


def whole_sum(value):
    return jnp.sum(jnp.sum(value, axis=1, keepdims=True), axis=0, keepdims=True)


def square_sums(raw, chosen, plan, first):
    square = raw * raw
    rows = square.shape[0]
    inner, entries = [], []
    for item in matrix_list():
        if item in chosen:
            column, width = plan[item]
            part = square[:, column - first : column - first + width]
            inner.append(jnp.sum(part, axis=1, keepdims=True))
        else:
            inner.append(jnp.zeros((rows, 1), jnp.float32))
        entries.append(jnp.sum(inner[-1], axis=0, keepdims=True))
    inner.append(jnp.zeros((rows, LANES - MATRICES), jnp.float32))
    return jnp.concatenate(inner, axis=1).T, entries, jnp.sum(square, axis=0, keepdims=True)


def store_row(target_ref, row, values):
    total = values.shape[1]
    for at, start in enumerate(range(0, total, LANES)):
        stop = min(start + LANES, total)
        target_ref[row + at : row + at + 1, 0 : stop - start] = values[:, start:stop]


def load_row(source_ref, row, total):
    return jnp.concatenate(
        [
            source_ref[row + at : row + at + 1, 0 : min(LANES, total - start)]
            for at, start in enumerate(range(0, total, LANES))
        ],
        axis=1,
    )


def late_row(widths):
    _, total = matrix_plan(widths)
    late = sum(widths[which] for which, _ in LATE)
    return EDGE + -(-(total - late) // LANES)


def packet_rows(widths):
    late = sum(widths[which] for which, _ in LATE)
    return -(-(late_row(widths) + -(-late // LANES)) // 8) * 8


def first_kernel(*refs):
    masters, row_refs, row_ref = refs[0:6], refs[6:12], refs[12]
    weights, row_sums = [], []
    for which, layer in matrix_list():
        master = masters[which][layer] if which < 4 else masters[which][...]
        weights.append(whole_sum(master * master))
        row_sums.append(whole_sum(old_row(row_refs, which, layer)))
    nothing = lambda count: [jnp.zeros((1, count), jnp.float32)]
    pieces = nothing(2) + weights + nothing(MATRICES) + row_sums
    row_ref[...] = jnp.concatenate(pieces + nothing(LANES - 2 - 3 * MATRICES), axis=1)


def run_first(masters, rows):
    vmem = pl.BlockSpec(memory_space=pltpu.VMEM)
    return pl.pallas_call(
        first_kernel,
        in_specs=[vmem] * 12,
        out_specs=vmem,
        out_shape=jax.ShapeDtypeStruct((1, LANES), jnp.float32),
        name="first_statistics",
    )(*masters, *rows)


def early_kernel(widths, *refs):
    raw_ref, row_ref, gains_at, loss_ref, count_ref, packet_ref = (
        refs[0],
        refs[1],
        refs[2:4],
        refs[4],
        refs[5],
        refs[6],
    )
    plan, _ = matrix_plan(widths)
    chosen = [item for item in matrix_list() if item not in LATE]
    inner, entries, outer = square_sums(raw_ref[...], chosen, plan, 0)
    packet_ref[...] = jnp.zeros_like(packet_ref)
    packet_ref[0:INNER_ROWS, 0 : inner.shape[1]] = inner[0:INNER_ROWS, :]
    last, one = [ref[...] for ref in gains_at]
    gain = jnp.concatenate(
        [jnp.zeros((1, D), jnp.float32), one[0:1], last[2:3], one[1:2], last[3:4], last[0:2]],
        axis=0,
    )
    nothing = lambda count: [jnp.zeros((1, count), jnp.float32)]
    scalars = [loss_ref[...], count_ref[...]] + nothing(MATRICES) + entries
    scalars = scalars + nothing(LANES - 2 - 2 * MATRICES)
    at = INNER_ROWS
    packet_ref[at : at + 7, :] = gain[:, 0:LANES]
    packet_ref[at + 7 : at + 8, :] = row_ref[...] + jnp.concatenate(scalars, axis=1)
    packet_ref[at + 8 : at + 15, :] = gain[:, LANES:]
    store_row(packet_ref, EDGE, outer)


def late_kernel(widths, early_ref, raw_ref, gain_ref, packet_ref):
    plan, total = matrix_plan(widths)
    inner, entries, outer = square_sums(raw_ref[...], LATE, plan, total - raw_ref.shape[1])
    packet_ref[...] = early_ref[...]
    packet_ref[0:INNER_ROWS, 0 : inner.shape[1]] += inner[0:INNER_ROWS, :]
    at = INNER_ROWS
    packet_ref[at : at + 1, :] = gain_ref[0:1, 0:LANES]
    packet_ref[at + 8 : at + 9, :] = gain_ref[0:1, LANES:]
    before = jnp.zeros((1, 2 + MATRICES), jnp.float32)
    behind = jnp.zeros((1, LANES - 2 - 2 * MATRICES), jnp.float32)
    packet_ref[at + 7 : at + 8, :] += jnp.concatenate([before] + entries + [behind], axis=1)
    store_row(packet_ref, late_row(widths), outer)


def run_early(widths, raw, row, gain_parts, loss, count):
    vmem = pl.BlockSpec(memory_space=pltpu.VMEM)
    operands = [raw, row] + gain_parts + [loss, count]
    return pl.pallas_call(
        functools.partial(early_kernel, widths),
        in_specs=[vmem] * len(operands),
        out_specs=vmem,
        out_shape=jax.ShapeDtypeStruct((packet_rows(widths), LANES), jnp.float32),
        name="early_statistics",
    )(*operands)


def run_late(widths, packet, raw, gain_part):
    vmem = pl.BlockSpec(memory_space=pltpu.VMEM)
    return pl.pallas_call(
        functools.partial(late_kernel, widths),
        in_specs=[vmem] * 3,
        out_specs=vmem,
        out_shape=jax.ShapeDtypeStruct(packet.shape, jnp.float32),
        name="late_statistics",
    )(packet, raw, gain_part)


def update_kernel(widths, sizes, *refs):
    packet_ref, raw_early, raw_late = refs[:3]
    masters, inner_refs, outer_refs = refs[3:9], refs[9:15], refs[15:21]
    gains_ref, second_ref = refs[21:23]
    outs = refs[23:]
    outer_count, inner_count = sizes
    plan, total = matrix_plan(widths)
    rows = raw_early.shape[0]
    at = INNER_ROWS
    scalars = packet_ref[at + 7 : at + 8, :]
    pick = lambda at: scalars[:, at : at + 1]
    gain_sum = jnp.concatenate(
        [packet_ref[at : at + 7, :], packet_ref[at + 8 : at + 15, :]], axis=1
    )
    gain_square = jnp.sum(jnp.sum(gain_sum * gain_sum, axis=1, keepdims=True), axis=0, keepdims=True)
    square_total = gain_square
    for at in range(MATRICES):
        square_total = square_total + pick(2 + MATRICES + at)
    count_total = pick(1)
    norm_value = jnp.sqrt(square_total) / count_total
    scaling = jnp.minimum(1.0, clip_limit / norm_value) / count_total
    square_scale = scaling * scaling
    early = raw_early.shape[1]
    outer_early = load_row(packet_ref, EDGE, early)
    outer_late = load_row(packet_ref, late_row(widths), total - early)
    inner_new = []
    for at, (which, layer) in enumerate(matrix_list()):
        outer_length = widths[which] * outer_count
        inner_new.append(
            decay_two * old_row(inner_refs, which, layer)
            + (1 - decay_two)
            * (square_scale * packet_ref[at : at + 1, 0:rows] / outer_length + tiny_term)
        )
    stacked = jnp.concatenate(inner_new, axis=0)
    stacked = jnp.concatenate([stacked, jnp.ones((LANES - MATRICES, rows), jnp.float32)], axis=0)
    if rows < LANES:
        stacked = jnp.concatenate([stacked, jnp.ones((LANES, LANES - rows), jnp.float32)], axis=1)
    turned = lax.rsqrt(stacked).T
    outs[0][...] = pick(0)
    outs[1][...] = count_total
    outs[2][...] = norm_value
    first_out = {4: 3, 0: 7, 1: 11, 2: 15, 3: 19, 5: 23}
    for at, (which, layer) in enumerate(matrix_list()):
        column, width = plan[(which, layer)]
        outer_length, inner_length = width * outer_count, rows * inner_count
        row_length = inner_length if ROW_IS_INNER[which] else outer_length
        copies = outer_count if ROW_IS_INNER[which] else inner_count
        entries = outer_length * inner_length
        if column < early:
            raw = raw_early[:, column : column + width]
            outer_total = outer_early[:, column : column + width]
        else:
            raw = raw_late[:, column - early : column - early + width]
            outer_total = outer_late[:, column - early : column - early + width]
        outer_new = decay_two * old_row(outer_refs, which, layer) + (1 - decay_two) * (
            square_scale * outer_total / inner_length + tiny_term
        )
        mean_rows = decay_two * (pick(2 + 2 * MATRICES + at) / (copies * row_length)) + (
            1 - decay_two
        ) * (square_scale * pick(2 + MATRICES + at) / entries + tiny_term)
        factor = step_rate * jnp.sqrt(pick(2 + at) / entries) * jnp.sqrt(mean_rows)
        grad = raw * scaling
        updated = master_of(masters, which, layer) - grad * (
            turned[0:rows, at : at + 1] * (factor * lax.rsqrt(outer_new))
        )
        first = first_out[which]
        row_new, column_new = (
            (inner_new[at], outer_new) if ROW_IS_INNER[which] else (outer_new, inner_new[at])
        )
        if which < 4:
            if which == 1:
                updated, grad = updated.T, grad.T
            outs[first][layer] = updated
            outs[first + 1][layer] = grad
            outs[first + 2][layer : layer + 1, :] = row_new
            outs[first + 3][layer : layer + 1, :] = column_new
        else:
            outs[first][...] = updated
            outs[first + 1][...] = grad
            outs[first + 2][...] = row_new
            outs[first + 3][...] = column_new
    gain_grad = gain_sum * scaling
    second_new = decay_two * second_ref[...] + (1 - decay_two) * (gain_grad * gain_grad + tiny_term)
    gains = gains_ref[...]
    spread = jnp.sqrt(jnp.mean(gains * gains, axis=-1, keepdims=True))
    outs[27][...] = gains - step_rate * spread * gain_grad * lax.rsqrt(second_new)
    outs[28][...] = gain_grad
    outs[29][...] = second_new


def run_update(widths, sizes, packet, raw_early, raw_late, masters, inner, outer, gains, second):
    vmem = pl.BlockSpec(memory_space=pltpu.VMEM)
    operands = [packet, raw_early, raw_late] + masters + inner + outer + [gains, second]
    shapes = [(1, 1)] * 3
    for which in [4, 0, 1, 2, 3, 5]:
        shapes = shapes + [masters[which].shape] * 2
        pair = [inner[which].shape, outer[which].shape]
        shapes = shapes + (pair if ROW_IS_INNER[which] else pair[::-1])
    shapes = shapes + [gains.shape] * 3
    return pl.pallas_call(
        functools.partial(update_kernel, widths, sizes),
        in_specs=[vmem] * len(operands),
        out_specs=[vmem] * len(shapes),
        out_shape=[jax.ShapeDtypeStruct(item, jnp.float32) for item in shapes],
        name="update",
    )(*operands)


def swap(value, mask):
    count = lax.axis_size("dp") * lax.axis_size("fsdp")
    return lax.ppermute(value, ("dp", "fsdp"), [(place, place ^ mask) for place in range(count)])


def device_index():
    return lax.axis_index("dp") * lax.axis_size("fsdp") + lax.axis_index("fsdp")


def step_masks(step):
    masks = []
    for digit in range(1, 1 << len(step)):
        masks.append(sum(1 << bit for at, bit in enumerate(step[::-1]) if (digit >> at) & 1))
    return masks


def tie(*values):
    return lax.optimization_barrier(values)


def behind(value, *ahead):
    return lax.optimization_barrier((value,) + ahead)[0]


class Gather:
    def __init__(self, piece, steps):
        self.held, self.steps, self.at = piece[None], steps, 0

    def send(self):
        self.others = tuple(swap(self.held, mask) for mask in step_masks(self.steps[self.at]))

    def join(self):
        step = self.steps[self.at]
        pieces = [self.held] + list(self.others)
        for at, bit in enumerate(step[::-1]):
            upper = (device_index() >> bit) & 1 == 1
            pieces = [
                jnp.where(upper, pieces[place ^ (1 << at)], pieces[place])
                for place in range(len(pieces))
            ]
        self.held = jnp.concatenate(pieces)
        self.at += 1


class Scatter:
    def __init__(self, sent, kept, steps):
        self.sent, self.kept, self.steps, self.at = (sent,), kept, steps, 0

    def send(self):
        masks = step_masks(self.steps[self.at])
        self.others = tuple(swap(sent, mask) for sent, mask in zip(self.sent, masks))

    def join(self):
        self.at += 1
        step = self.steps[self.at] if self.at < len(self.steps) else ()
        count = 1 << len(step)
        own = 0
        for bit in step:
            own = 2 * own + ((device_index() >> bit) & 1)
        shape = (count, self.kept.shape[0] // count) + self.kept.shape[1:]
        terms = [item.reshape(shape) for item in (self.kept,) + self.others]

        def pick(digit):
            total = None
            for term in terms:
                part = lax.dynamic_index_in_dim(term, own ^ digit, 0, keepdims=False)
                part = part.astype(jnp.float32)
                total = part if total is None else total + part
            return total

        self.sent = tuple(pick(digit).astype(jnp.bfloat16) for digit in range(1, count))
        self.kept = pick(0)


def sum_packets(packet, group, inner_bits):
    masks = step_masks(group)
    others = [swap(packet, mask) for mask in masks]
    inner, outer = packet[:INNER_ROWS], packet[EDGE:]
    common = [packet[INNER_ROWS:EDGE]]
    inner, outer = [inner], [outer]
    for mask, other in zip(masks, others):
        common.append(other[INNER_ROWS:EDGE])
        if mask >> inner_bits << inner_bits == mask:
            inner.append(other[:INNER_ROWS])
        if mask >> inner_bits == 0:
            outer.append(other[EDGE:])
    tree = lambda items: (
        items[0] if len(items) == 1 else tree(
            [items[at] + items[at + 1] for at in range(0, len(items), 2)]
        )
    )
    return jnp.concatenate([tree(inner), tree(common), tree(outer)])


def merged(parts):
    whole = Scatter(None, jnp.concatenate([part.kept for part in parts], axis=2), parts[0].steps)
    whole.sent = tuple(
        jnp.concatenate(pieces, axis=2) for pieces in zip(*[part.sent for part in parts])
    )
    whole.at = parts[0].at
    return whole


def shards(
    latents,
    targets,
    horizon,
    memory_valid,
    embed,
    qkv_weight,
    out_weight,
    up_weight,
    down_weight,
    head_weight,
    gains,
    embed_rows,
    embed_cols,
    qkv_rows,
    qkv_cols,
    out_rows,
    out_cols,
    up_rows,
    up_cols,
    down_rows,
    down_cols,
    head_rows,
    head_cols,
    gain_second,
):
    samples = latents.shape[0]
    sizes = (lax.axis_size("dp"), lax.axis_size("fsdp"))
    highest = (sizes[0] * sizes[1]).bit_length() - 1
    gather_steps = [(bit,) for bit in reversed(range(3, highest))] + [(2, 1), (0,)]
    scatter_steps = gather_steps[::-1]
    mesh_plan = (sizes[0], sizes[1], gather_steps)
    core = (lax.axis_index("fsdp") & 1).astype(jnp.int32).reshape(1)

    out_turned = jnp.swapaxes(out_weight, 1, 2)
    down_turned = jnp.swapaxes(down_weight, 1, 2)
    masters = [qkv_weight, out_turned, up_weight, down_turned, embed.T, head_weight]
    widths = [qkv_weight.shape[2], out_weight.shape[2], up_weight.shape[2], down_weight.shape[1]]
    widths = widths + [embed.shape[0], head_weight.shape[1]]
    att_widths, ffn_widths = widths[0:2], widths[2:4]
    chunk_widths = [
        att_widths + widths[4:5],
        ffn_widths + att_widths,
        ffn_widths + att_widths + ffn_widths + widths[5:6],
    ]
    chunks = [Gather(piece, gather_steps) for piece in run_pack(masters, chunk_widths)]
    first, second, third = chunks
    latent_rows = latents.transpose(0, 2, 1)
    target_rows = targets.transpose(0, 2, 1)
    shared = (gains, memory_valid, core)
    back_shared = (gains, core)

    count = len(gather_steps)
    flat = lambda item: item if item.ndim == 2 else item.reshape(1, -1)
    inner = [flat(item) for item in (qkv_rows, out_rows, up_rows, down_cols, embed_cols, head_rows)]
    outer = [flat(item) for item in (qkv_cols, out_cols, up_cols, down_rows, embed_rows, head_cols)]
    row_stats = [inner[at] if ROW_IS_INNER[at] else outer[at] for at in range(6)]
    first_row = run_first(masters, row_stats)
    for at in range(count - 1):
        for chunk in chunks:
            chunk.send()
        if at == 0:
            first.others, first_row = tie(first.others, first_row)
        for chunk in chunks[: 2 if at == count - 2 else 3]:
            chunk.join()
            if at == count - 3 and chunk is first:
                first.held, third.held = tie(first.held, third.held)
    first.send()
    (other,) = first.others
    held, other, second.held = tie(first.held, other, second.held)
    second.send()
    kept = [run_forward(0, chunk_widths[0], mesh_plan, latent_rows, held, other, *shared)]
    middle, (other,) = tie(kept[0][1], second.others)
    kept.append(
        run_forward(1, chunk_widths[1], mesh_plan, middle, second.held, other, *shared)
    )
    middle, third.others = tie(kept[1][1], third.others)
    third.join()
    third.send()
    (other,) = third.others
    dmiddle, sent, held, gain_middle, loss, counted = run_middle(
        chunk_widths[2],
        mesh_plan,
        middle,
        third.held,
        other,
        target_rows,
        gains,
        memory_valid,
        horizon,
        core,
    )
    pair = Scatter(sent, held, scatter_steps)
    pair.send()
    pair.join()
    like = first.held
    before = (kept[0][1], kept[1][6], kept[1][8], kept[1][7])
    dmiddle, pair.sent = tie(dmiddle, pair.sent)
    pair.send()
    dmiddle, sent, held, gain_one = run_backward(
        1, chunk_widths[1], mesh_plan, like, kept[1], dmiddle, *back_shared, before
    )
    dmiddle, sent, held, pair.others = tie(dmiddle, sent, held, pair.others)
    one = Scatter(sent, held, scatter_steps)
    one.send()
    pair.join()
    one.join()
    dmiddle, pair.sent, one.sent = tie(dmiddle, pair.sent, one.sent)
    one.send()
    pair.send()
    sent, held, gain_zero = run_backward(
        0, chunk_widths[0], mesh_plan, like, kept[0], dmiddle, *back_shared, latent_rows
    )
    sent, held, pair.others, one.others = tie(sent, held, pair.others, one.others)
    zero = Scatter(sent, held, scatter_steps)
    zero.send()
    one.join()
    one.send()
    pair.join()
    zero.join()
    one.others = behind(one.others, zero.sent)
    zero.send()
    one.join()
    early = merged([pair, one])
    while early.at < count:
        early.send()
        if early.at == count - 1:
            zero.join()
            zero.send()
        zero.others, early.others = tie(zero.others, early.others)
        early.join()
    raw_early = early.kept[0]

    packet = run_early(
        widths, raw_early, first_row, [gain_middle, gain_one], loss, counted
    )
    while zero.at < count:
        zero.join()
        if zero.at < count:
            zero.send()
    raw_late = zero.kept[0]
    packet = run_late(widths, packet, raw_late, gain_zero)
    inner_bits = sizes[1].bit_length() - 1
    rest = list(range(3, highest))
    groups = [(0,), (2, 1)] + [tuple(rest[at : at + 2][::-1]) for at in range(0, len(rest), 2)]
    for group in groups:
        packet = sum_packets(packet, group, inner_bits)
    results = run_update(
        widths, sizes, packet, raw_early, raw_late, masters, inner, outer, gains, gain_second
    )
    results = list(results)
    for at in range(3):
        results[at] = results[at].reshape(())
    for at in (3, 4, 11, 12, 19, 20):
        results[at] = jnp.swapaxes(results[at], -1, -2)
    for at in (5, 6, 25, 26):
        results[at] = results[at].reshape(-1)
    return tuple(results)


def solution(mesh):
    return jax.shard_map(
        shards,
        mesh=mesh,
        in_specs=(
            P(("dp", "fsdp"), None, None),
            P(("dp", "fsdp"), None, None),
            P(("dp", "fsdp")),
            P(("dp", "fsdp")),
            P("dp", "fsdp"),
            P(None, "fsdp", "dp"),
            P(None, "fsdp", "dp"),
            P(None, "fsdp", "dp"),
            P(None, "dp", "fsdp"),
            P("fsdp", "dp"),
            P(),
            P("dp"),
            P("fsdp"),
            P(None, "fsdp"),
            P(None, "dp"),
            P(None, "fsdp"),
            P(None, "dp"),
            P(None, "fsdp"),
            P(None, "dp"),
            P(None, "dp"),
            P(None, "fsdp"),
            P("fsdp"),
            P("dp"),
            P(),
        ),
        out_specs=(
            P(),
            P(),
            P(),
            P("dp", "fsdp"),
            P("dp", "fsdp"),
            P("dp"),
            P("fsdp"),
            P(None, "fsdp", "dp"),
            P(None, "fsdp", "dp"),
            P(None, "fsdp"),
            P(None, "dp"),
            P(None, "fsdp", "dp"),
            P(None, "fsdp", "dp"),
            P(None, "fsdp"),
            P(None, "dp"),
            P(None, "fsdp", "dp"),
            P(None, "fsdp", "dp"),
            P(None, "fsdp"),
            P(None, "dp"),
            P(None, "dp", "fsdp"),
            P(None, "dp", "fsdp"),
            P(None, "dp"),
            P(None, "fsdp"),
            P("fsdp", "dp"),
            P("fsdp", "dp"),
            P("fsdp"),
            P("dp"),
            P(),
            P(),
            P(),
        ),
        check_vma=False,
    )
```

```python
import functools

import jax
import jax.numpy as jnp
from jax import lax
from jax.experimental import pallas as pl
from jax.experimental.pallas import tpu as pltpu
from jax.sharding import PartitionSpec as P

D = 256
HEADS = 8
HEAD = D // HEADS
FF = 1024
CATS = 32
CLASSES = 32
LAYERS = 3
SEG = 48
MEM = 48
CTX = 96
VOCAB = 1024
GROUP = 4
WIDE_GROUP = 8
ROWS = GROUP * CTX
HALF = D // 2
VMEM_BYTES = 24 * 1024 * 1024
MIDDLE_BYTES = 43 * 1024 * 1024

decay_two = 0.9
step_rate = 0.3
clip_limit = 0.05
tiny_term = 1e-30
norm_eps = 1e-06
masked_score = -1e30
log2_e = 1.4426950408889634
score_scale = HEAD ** (-0.5)
gelu_one = 0.7978845608028654
gelu_two = 0.044715


def dot_nn(left, right):
    return lax.dot_general(
        left, right, (((1,), (0,)), ((), ())), preferred_element_type=jnp.float32
    )


def dot_nt(left, right):
    return lax.dot_general(
        left, right, (((1,), (1,)), ((), ())), preferred_element_type=jnp.float32
    )


def dot_tn(left, right):
    return lax.dot_general(
        left, right, (((0,), (0,)), ((), ())), preferred_element_type=jnp.float32
    )


def inverse_rms(values):
    return lax.rsqrt(jnp.mean(values * values, axis=-1, keepdims=True) + norm_eps)


def rms_back(values, inverse, gain_row, upstream):
    normed = values * inverse
    scaled = upstream * gain_row
    inner = jnp.mean(scaled * normed, axis=-1, keepdims=True)
    return (
        inverse * (scaled - normed * inner),
        jnp.sum(upstream * normed, axis=0, keepdims=True),
    )


def head_masks():
    lane = lax.broadcasted_iota(jnp.int32, (1, D // 2), 1) // HEAD
    return [lane == head for head in range(HEADS // 2)]


def expand_heads(rows, masks):
    return jnp.concatenate([rows * mask.astype(rows.dtype) for mask in masks], axis=0)


def collapse_heads(spread, rows, masks):
    product = dot_tn(spread, rows)
    queries = product.shape[0] // len(masks)
    taken = product[(len(masks) - 1) * queries :]
    for at, mask in enumerate(masks[:-1]):
        taken = jnp.where(mask, product[at * queries : (at + 1) * queries], taken)
    return taken


def half_of(part, side):
    start = part * D + side * HALF
    return slice(start, start + HALF)


def fill_bias(bias_ref):
    spread = bias_ref.shape[2]
    queries = spread // (HEADS // 2)
    key_at = lax.broadcasted_iota(jnp.int32, (CTX, spread), 0)
    query_at = lax.broadcasted_iota(jnp.int32, (CTX, spread), 1) % queries + (CTX - queries)
    later = key_at > query_at
    crosses = (query_at >= MEM) & (key_at < MEM)
    bias_ref[0] = jnp.where(later | crosses, masked_score, 0.0)
    bias_ref[1] = jnp.where(later, masked_score, 0.0)


def block_place(device, steps):
    place, weight = 0, 1
    for step in steps[:-1]:
        digit = 0
        for bit in step:
            digit = 2 * digit + ((device >> bit) & 1)
        place += digit * weight
        weight <<= len(step)
    return place


def place_weights(targets, own_ref, other_ref, core, widths, mesh_plan, start=0):
    outer_count, inner_count, steps = mesh_plan
    rows = own_ref.shape[1]
    for high in range(inner_count // 2):
        for source, side in ((own_ref, core), (other_ref, 1 - core)):
            here = pl.ds(pl.multiple_of((2 * high + side) * rows, rows), rows)
            at = start
            for (target, column), width in zip(targets, widths):
                block = [
                    source[
                        block_place(outer * inner_count + 2 * high, steps), :, at : at + width
                    ]
                    for outer in range(outer_count)
                ]
                target[here, column : column + width * outer_count] = jnp.concatenate(
                    block, axis=1
                )
                at += width


def write_blocks(send_ref, keep_ref, sum_ref, core, widths, mesh_plan, start=0):
    outer_count, inner_count, steps = mesh_plan
    rows = keep_ref.shape[1]
    for high in range(inner_count // 2):
        for target, side in ((keep_ref, core), (send_ref, 1 - core)):
            here = pl.ds(pl.multiple_of((2 * high + side) * rows, rows), rows)
            taken = sum_ref[here, :]
            for outer in range(outer_count):
                block, column = [], 0
                for width in widths:
                    block.append(taken[:, column + outer * width : column + (outer + 1) * width])
                    column += width * outer_count
                place = block_place(outer * inner_count + 2 * high, steps)
                target[place, :, start : start + sum(widths)] = jnp.concatenate(
                    block, axis=1
                ).astype(target.dtype)


def one_hot_rows(latent_ref, hot_ref, first):
    spot = lax.broadcasted_iota(jnp.int32, (CATS, VOCAB), 1) // CLASSES
    group = lax.broadcasted_iota(jnp.int32, (CATS, VOCAB), 0)
    spreader = jnp.where(spot == group, 1.0, 0.0).astype(jnp.bfloat16)
    classes = (lax.broadcasted_iota(jnp.int32, (1, VOCAB), 1) % CLASSES).astype(jnp.float32)
    for sample in range(latent_ref.shape[0]):
        drawn = dot_tn(latent_ref[sample].astype(jnp.float32).astype(jnp.bfloat16), spreader)
        hot_ref[pl.ds(first + sample * CTX, CTX), :] = jnp.where(
            drawn == classes, 1.0, 0.0
        ).astype(jnp.bfloat16)


def tail_rows(values, queries):
    if queries == CTX:
        return values
    return jnp.concatenate(
        [
            values[(sample + 1) * CTX - queries : (sample + 1) * CTX]
            for sample in range(values.shape[0] // CTX)
        ],
        axis=0,
    )


def attend_forward(step, hidden, gain_row, weight_ref, valid_ref, bias_ref, masks, refs):
    middle_ref, qkv_ref, mix_ref, chance_ref = refs
    queries = chance_ref.shape[3] // (HEADS // 2)
    group = hidden.shape[0] // CTX
    normed = (hidden * inverse_rms(hidden) * gain_row).astype(jnp.bfloat16)
    qkv_ref[...] = dot_nn(normed, weight_ref[:, 0 : 3 * D]).astype(jnp.bfloat16)
    units = [(sample, side) for sample in range(group) for side in range(2)]
    scores = []
    for sample, side in units:
        rows = slice(sample * CTX, (sample + 1) * CTX)
        tail = slice((sample + 1) * CTX - queries, (sample + 1) * CTX)
        spread = expand_heads(qkv_ref[tail, half_of(0, side)], masks)
        scores.append(dot_nt(qkv_ref[rows, half_of(1, side)], spread))
    for (sample, side), score in zip(units, scores):
        score = score + bias_ref[valid_ref[step * group + sample]]
        peak = jnp.max(score, axis=0, keepdims=True)
        exponent = jnp.exp2((score - peak) * (score_scale * log2_e))
        total = jnp.sum(exponent, axis=0, keepdims=True)
        chance_ref[sample, side] = (exponent * (1.0 / total)).astype(jnp.bfloat16)
    for sample, side in units:
        rows = slice(sample * CTX, (sample + 1) * CTX)
        mix_ref[sample * queries : (sample + 1) * queries, half_of(0, side)] = collapse_heads(
            chance_ref[sample, side], qkv_ref[rows, half_of(2, side)], masks
        ).astype(jnp.bfloat16)
    middle_ref[...] = tail_rows(hidden, queries) + dot_nn(
        mix_ref[...], weight_ref[:, 3 * D : 4 * D]
    )


def gelu_parts(value):
    square = value * value
    share = 0.5 + 0.5 * jnp.tanh(value * (gelu_one + (gelu_one * gelu_two) * square))
    active = value * share
    bent = active * (1.0 - share)
    return active, share + bent * (2.0 * gelu_one + (6.0 * gelu_one * gelu_two) * square)


def feed_forward(middle, gain_row, weight_ref, inner_ref, slope_ref):
    normed = (middle * inverse_rms(middle) * gain_row).astype(jnp.bfloat16)
    for part in range(FF // D):
        columns = slice(part * D, (part + 1) * D)
        inner = dot_nn(normed, weight_ref[:, columns])
        for sample in range(middle.shape[0] // CTX):
            rows = slice(sample * CTX, (sample + 1) * CTX)
            active, slope = gelu_parts(inner[rows])
            inner_ref[rows, columns] = active.astype(jnp.bfloat16)
            slope_ref[rows, columns] = slope.astype(jnp.bfloat16)
    return middle + dot_nt(inner_ref[...], weight_ref[:, FF : 2 * FF])


def feed_back(here, upstream, middle, gain_row, weight_ref, slope_ref, refs, turned_ref=None):
    normed_ref, dinner_ref, dout_ref = refs
    dout = upstream.astype(jnp.bfloat16)
    dout_ref[here(0, middle.shape[0]), :] = dout
    inverse = inverse_rms(middle)
    normed_ref[here(0, middle.shape[0]), :] = (middle * inverse * gain_row).astype(jnp.bfloat16)
    for part in range(FF // D):
        columns = slice(part * D, (part + 1) * D)
        dact = dot_nn(dout, weight_ref[:, FF + part * D : FF + (part + 1) * D])
        dinner_ref[here(0, middle.shape[0]), columns] = (
            dact * slope_ref[:, columns].astype(jnp.float32)
        ).astype(jnp.bfloat16)
    dinner = dinner_ref[here(0, middle.shape[0]), :]
    if turned_ref is None:
        dnormed = dot_nt(dinner, weight_ref[:, 0:FF])
    else:
        dnormed = dot_nn(dinner, turned_ref[...])
    through, gain_part = rms_back(middle, inverse, gain_row, dnormed)
    return upstream + through, gain_part


def attend_back(step, here, saved, dmiddle, gain_row, weight_ref, masks, refs, turned_ref=None):
    hidden, qkv_ref, mix_ref, chance_ref = saved
    normed_ref, dmiddle_ref, dqkv_ref, mixes_ref = refs
    group = hidden.shape[0] // CTX
    queries = chance_ref.shape[3] // (HEADS // 2)
    short = here(0, group * queries, queries)
    dattend = dmiddle.astype(jnp.bfloat16)
    dmiddle_ref[short, :] = dattend
    mixes_ref[short, :] = mix_ref[...]
    if turned_ref is None:
        dmix = dot_nt(dattend, weight_ref[:, 3 * D : 4 * D]).astype(jnp.bfloat16)
    else:
        dmix = dot_nn(dattend, turned_ref[3 * D : 4 * D, :]).astype(jnp.bfloat16)
    units = [(sample, side) for sample in range(group) for side in range(2)]
    slopes, dchances, dscores = [], [], []
    for sample, side in units:
        rows = slice(sample * CTX, (sample + 1) * CTX)
        slopes.append(
            expand_heads(
                dmix[sample * queries : (sample + 1) * queries, half_of(0, side)], masks
            )
        )
        dchances.append(dot_nt(qkv_ref[rows, half_of(2, side)], slopes[-1]))
    for (sample, side), dchance in zip(units, dchances):
        chance = chance_ref[sample, side].astype(jnp.float32)
        weighed = chance * dchance
        dscores.append(
            (weighed - chance * jnp.sum(weighed, axis=0, keepdims=True)).astype(jnp.bfloat16)
        )
    for at, (sample, side) in enumerate(units):
        rows = slice(sample * CTX, (sample + 1) * CTX)
        tail = slice((sample + 1) * CTX - queries, (sample + 1) * CTX)
        there = here(sample * CTX, CTX)
        spread = expand_heads(qkv_ref[tail, half_of(0, side)], masks)
        keys = qkv_ref[rows, half_of(1, side)]
        dvalues = dot_nn(chance_ref[sample, side], slopes[at])
        dkeys = dot_nn(dscores[at], spread) * score_scale
        dqueries = (collapse_heads(dscores[at], keys, masks) * score_scale).astype(jnp.bfloat16)
        if queries < CTX:
            nothing = jnp.zeros((CTX - queries, HALF), jnp.bfloat16)
            dqueries = jnp.concatenate([nothing, dqueries], axis=0)
        dqkv_ref[there, half_of(0, side)] = dqueries
        dqkv_ref[there, half_of(1, side)] = dkeys.astype(jnp.bfloat16)
        dqkv_ref[there, half_of(2, side)] = dvalues.astype(jnp.bfloat16)
    inverse = inverse_rms(hidden)
    normed_ref[here(0, hidden.shape[0]), :] = (hidden * inverse * gain_row).astype(jnp.bfloat16)
    dqkv = dqkv_ref[here(0, hidden.shape[0]), :]
    if turned_ref is None:
        dnormed = dot_nt(dqkv, weight_ref[:, 0 : 3 * D])
    else:
        dnormed = dot_nn(dqkv, turned_ref[0 : 3 * D, :])
    through, gain_part = rms_back(hidden, inverse, gain_row, dnormed)
    if queries < CTX:
        nothing = jnp.zeros((CTX - queries, D), jnp.float32)
        pieces = []
        for sample in range(group):
            pieces = pieces + [nothing, dmiddle[sample * queries : (sample + 1) * queries]]
        dmiddle = jnp.concatenate(pieces, axis=0)
    return dmiddle + through, gain_part


def row_spec(width, group=GROUP, unit=CTX):
    return pl.BlockSpec((group * unit, width), lambda step: (step, 0))


def chance_spec(queries, group=GROUP):
    return pl.BlockSpec((group, 2, CTX, HEADS // 2 * queries), lambda step: (step, 0, 0, 0))


def latent_spec(group=GROUP):
    return pl.BlockSpec((group, CATS, CTX), lambda step: (step, 0, 0))


def whole_spec(shape):
    return pl.BlockSpec(shape, lambda step: (0,) * len(shape))


def in_hbm(item):
    return pltpu.with_memory_space_constraint(item, pltpu.HBM)


def smem_spec():
    return pl.BlockSpec(memory_space=pltpu.SMEM)


def forward_kernel(layer, widths, mesh_plan, source_ref, own_ref, other_ref, gains_ref, valid_ref, core_ref, *refs):
    entry_ref, att_ref, before_ref = refs[0], refs[5], refs[6]
    bias_ref = refs[7] if layer == 0 else refs[9]
    step = pl.program_id(0)

    @pl.when(step == 0)
    def _():
        fill_bias(bias_ref)
        att = [(att_ref, 0), (att_ref, 3 * D)]
        before = [(before_ref, 0)] if layer == 0 else [(before_ref, 0), (before_ref, FF)]
        targets = att + before if layer == 0 else before + att
        place_weights(targets, own_ref, other_ref, core_ref[0], widths[: len(targets)], mesh_plan)

    if layer == 0:
        one_hot_rows(source_ref, refs[8], 0)
        hidden = dot_nt(refs[8][...], before_ref[...])
    else:
        gain_ffn = gains_ref[LAYERS + layer - 1 : LAYERS + layer, :]
        hidden = feed_forward(source_ref[...], gain_ffn, before_ref, refs[7], refs[8])
    entry_ref[...] = hidden
    attend_forward(
        step,
        hidden,
        gains_ref[layer : layer + 1, :],
        att_ref,
        valid_ref,
        bias_ref,
        head_masks(),
        refs[1:5],
    )


def run_forward(layer, widths, mesh_plan, source, own, other, gains, valid, core):
    tokens = valid.shape[0] * CTX
    f32, b16 = jnp.float32, jnp.bfloat16
    chances = HEADS // 2 * CTX
    group = WIDE_GROUP if layer == 0 else GROUP
    outs = [
        (pltpu.HBM((tokens, D), f32), row_spec(D, group)),
        (pltpu.HBM((tokens, D), f32), row_spec(D, group)),
        (pltpu.HBM((tokens, 3 * D), b16), row_spec(3 * D, group)),
        (pltpu.HBM((tokens, D), b16), row_spec(D, group)),
        (pltpu.HBM((tokens // CTX, 2, CTX, chances), b16), chance_spec(CTX, group)),
        (pltpu.HBM((D, 4 * D), b16), whole_spec((D, 4 * D))),
    ]
    scratch = [pltpu.VMEM((2, CTX, chances), f32)]
    if layer == 0:
        scratch = [pltpu.VMEM((D, VOCAB), b16)] + scratch + [pltpu.VMEM((group * CTX, VOCAB), b16)]
        source_spec = latent_spec(group)
    else:
        source_spec = row_spec(D, group)
        outs.append((pltpu.HBM((D, 2 * FF), b16), whole_spec((D, 2 * FF))))
        outs = outs + [(pltpu.HBM((tokens, FF), b16), row_spec(FF, group))] * 2
        source = in_hbm(source)
    return pl.pallas_call(
        functools.partial(forward_kernel, layer, widths, mesh_plan),
        grid=(tokens // (group * CTX),),
        in_specs=[
            source_spec,
            whole_spec(own.shape),
            whole_spec(other.shape),
            whole_spec(gains.shape),
            smem_spec(),
            smem_spec(),
        ],
        out_specs=[spec for _, spec in outs],
        out_shape=[item for item, _ in outs],
        scratch_shapes=scratch,
        compiler_params=pltpu.CompilerParams(vmem_limit_bytes=VMEM_BYTES),
        cost_estimate=pl.CostEstimate(
            flops=2 * tokens * D * 12 * D,
            bytes_accessed=tokens * D * 16 + D * 12 * D * 4,
            transcendentals=tokens * (FF + HEADS * CTX),
        ),
        name="forward_part",
    )(source, own, other, gains, valid, core)


def middle_kernel(widths, mesh_plan, *refs):
    source_ref, own_ref, other_ref, drawn_ref, gains_ref, valid_ref, horizon_ref, core_ref = refs[:8]
    out_ref, send_ref, keep_ref, gain_ref, loss_ref, count_ref = refs[8:14]
    bias_ref, weight_one_ref, att_ref, weight_two_ref, head_ref, turned_ref = refs[14:20]
    entry_ref, qkv_ref, mix_ref, chance_ref, middle_two_ref, inner_one_ref, slope_one_ref = refs[20:27]
    inner_ref, slope_ref, last_ref, dmiddle_ref, sum_ref, targets_ref, counted_ref = refs[27:34]
    normed_long, dattend_ref, dqkv_long, mixes_ref, normed_two_long, dinner_long, dout_long = refs[34:]
    tokens = middle_two_ref.shape[0]
    final_ref = normed_long.at[0:tokens]
    dlogits_ref = dqkv_long.at[0:VOCAB]
    normed_ref = normed_two_long.at[0:tokens]
    dinner_ref = dinner_long.at[0:tokens]
    dout_ref = dout_long.at[0:tokens]
    groups = source_ref.shape[0] // (WIDE_GROUP * CTX)
    masks = head_masks()
    gain_att = gains_ref[LAYERS - 1 : LAYERS, :]
    gain_before = gains_ref[2 * LAYERS - 2 : 2 * LAYERS - 1, :]
    gain_ffn = gains_ref[2 * LAYERS - 1 : 2 * LAYERS, :]
    gain_final = gains_ref[2 * LAYERS : 2 * LAYERS + 1, :]
    fill_bias(bias_ref)
    place_weights(
        [
            (weight_one_ref, 0),
            (weight_one_ref, FF),
            (att_ref, 0),
            (att_ref, 3 * D),
            (weight_two_ref, 0),
            (weight_two_ref, FF),
            (head_ref, 0),
        ],
        own_ref,
        other_ref,
        core_ref[0],
        widths,
        mesh_plan,
    )

    def rows_of(group, unit=CTX):
        return pl.ds(pl.multiple_of(group * (WIDE_GROUP * unit), WIDE_GROUP * unit), WIDE_GROUP * unit)

    def forward(group, carry):
        rows, short = rows_of(group), rows_of(group, SEG)
        hidden = feed_forward(
            source_ref[rows, :],
            gain_before,
            weight_one_ref,
            inner_one_ref.at[rows],
            slope_one_ref.at[rows],
        )
        entry_ref[rows, :] = hidden
        attend_forward(
            group,
            hidden,
            gain_att,
            att_ref,
            valid_ref,
            bias_ref,
            masks,
            (
                middle_two_ref.at[short],
                qkv_ref.at[rows],
                mix_ref.at[short],
                chance_ref.at[pl.ds(group * WIDE_GROUP, WIDE_GROUP)],
            ),
        )
        return carry

    lax.fori_loop(0, groups, forward, 0)
    turned_ref[...] = head_ref[...].T
    samples = tokens // SEG
    targets_ref[...] = jnp.concatenate([drawn_ref[at] for at in range(samples)], axis=1)
    position = lax.broadcasted_iota(jnp.int32, (1, SEG), 1)
    counted_ref[...] = jnp.concatenate(
        [jnp.where(position < horizon_ref[at], 1.0, 0.0) for at in range(samples)], axis=1
    )
    count_ref[...] = jnp.sum(counted_ref[...], axis=1, keepdims=True)
    for block in range(tokens // ROWS):
        rows = slice(block * ROWS, (block + 1) * ROWS)
        middle = middle_two_ref[rows, :]
        normed = (middle * inverse_rms(middle) * gain_ffn).astype(jnp.bfloat16)
        normed_ref[rows, :] = normed
        for part in range(FF // D):
            columns = slice(part * D, (part + 1) * D)
            inner = dot_nn(normed, weight_two_ref[:, columns])
            for piece in range(GROUP):
                there = slice(block * ROWS + piece * CTX, block * ROWS + (piece + 1) * CTX)
                active, slope = gelu_parts(inner[piece * CTX : (piece + 1) * CTX])
                inner_ref[there, columns] = active.astype(jnp.bfloat16)
                slope_ref[there, columns] = slope.astype(jnp.bfloat16)
        last = middle + dot_nt(inner_ref[rows, :], weight_two_ref[:, FF : 2 * FF])
        last_ref[rows, :] = last
        final_ref[rows, :] = (last * inverse_rms(last) * gain_final).astype(jnp.bfloat16)
    span = D
    loss = jnp.zeros((1, span), jnp.float32)
    spots = lax.broadcasted_iota(jnp.int32, (CLASSES, span), 0)
    for part in range(tokens // span):
        columns = slice(part * span, (part + 1) * span)
        counted = counted_ref[0:1, columns]
        final = final_ref[columns, :]
        for quarter in range(VOCAB // D):
            logits = dot_nt(turned_ref[quarter * D : (quarter + 1) * D, :], final)
            for inside in range(D // CLASSES):
                group = quarter * (D // CLASSES) + inside
                values = logits[inside * CLASSES : (inside + 1) * CLASSES]
                shifted = values - jnp.max(values, axis=0, keepdims=True)
                exponent = jnp.exp2(shifted * log2_e)
                total = jnp.sum(exponent, axis=0, keepdims=True)
                hot = spots == targets_ref[group : group + 1, columns]
                chosen = jnp.sum(jnp.where(hot, shifted, 0.0), axis=0, keepdims=True)
                loss = loss + counted * (jnp.log(total) - chosen)
                chance = exponent * (1.0 / total)
                slope = (chance - jnp.where(hot, 1.0, 0.0)) * counted
                dlogits_ref[group * CLASSES : (group + 1) * CLASSES, columns] = slope.astype(
                    jnp.bfloat16
                )
    loss_ref[...] = jnp.sum(loss, axis=1, keepdims=True)
    sum_ref[:, 2 * FF : 2 * FF + VOCAB] = dot_nt(final_ref[...].T, dlogits_ref[...])
    dfinal = dot_nn(head_ref[...], dlogits_ref[...]).T
    last = last_ref[...]
    dlast, gain_part = rms_back(last, inverse_rms(last), gain_final, dfinal)
    gain_ref[1:2, :] = gain_part
    last_ref[...] = dlast
    gain_sum = jnp.zeros((1, D), jnp.float32)
    for block in range(tokens // ROWS):
        rows = slice(block * ROWS, (block + 1) * ROWS)
        upstream = last_ref[rows, :]
        dout = upstream.astype(jnp.bfloat16)
        dout_ref[rows, :] = dout
        for part in range(FF // D):
            columns = slice(part * D, (part + 1) * D)
            dact = dot_nn(dout, weight_two_ref[:, FF + part * D : FF + (part + 1) * D])
            dinner_ref[rows, columns] = (dact * slope_ref[rows, columns].astype(jnp.float32)).astype(jnp.bfloat16)
        dnormed = dot_nt(dinner_ref[rows, :], weight_two_ref[:, 0:FF])
        middle = middle_two_ref[rows, :]
        through, gain_part = rms_back(middle, inverse_rms(middle), gain_ffn, dnormed)
        gain_sum = gain_sum + gain_part
        dmiddle_ref[rows, :] = upstream + through
    gain_ref[0:1, :] = gain_sum
    sum_ref[:, 0:FF] = dot_nn(normed_ref[...].T, dinner_ref[...])
    sum_ref[:, FF : 2 * FF] = dot_nn(dout_ref[...].T, inner_ref[...])
    write_blocks(send_ref, keep_ref, sum_ref, core_ref[0], widths[4:], mesh_plan)
    gain_ref[2:4, :] = jnp.zeros((2, D), jnp.float32)

    def backward(group, carry):
        rows, short = rows_of(group), rows_of(group, SEG)

        def here(start, length, unit=CTX):
            return pl.ds(pl.multiple_of(group * (WIDE_GROUP * unit) + start, 16), length)

        dentry, gain_part = attend_back(
            group,
            here,
            (
                entry_ref[rows, :],
                qkv_ref.at[rows],
                mix_ref.at[short],
                chance_ref.at[pl.ds(group * WIDE_GROUP, WIDE_GROUP)],
            ),
            dmiddle_ref[short, :],
            gain_att,
            att_ref,
            masks,
            (normed_long, dattend_ref, dqkv_long, mixes_ref),
        )
        gain_ref[2:3, :] += gain_part
        dbefore, gain_part = feed_back(
            here,
            dentry,
            source_ref[rows, :],
            gain_before,
            weight_one_ref,
            slope_one_ref.at[rows],
            (normed_two_long, dinner_long, dout_long),
        )
        out_ref[rows, :] = dbefore
        gain_ref[3:4, :] += gain_part
        return carry

    lax.fori_loop(0, groups, backward, 0)
    column = 0
    for left, right in [
        (normed_two_long, dinner_long),
        (dout_long, inner_one_ref),
        (normed_long, dqkv_long),
        (mixes_ref, dattend_ref),
    ]:
        wide = right.shape[1]
        sum_ref[:, column : column + wide] = dot_nn(left[...].T, right[...])
        column += wide
    write_blocks(
        send_ref, keep_ref, sum_ref, core_ref[0], widths[:4], mesh_plan, sum(widths[4:])
    )


def block_outs(own, widths):
    shape = jax.ShapeDtypeStruct
    blocks = own.shape[:2] + (sum(widths),)
    return [shape(blocks, jnp.bfloat16)] * 2


def run_middle(widths, mesh_plan, source, own, other, targets, gains, valid, horizon, core):
    tokens = source.shape[0]
    short = tokens // CTX * SEG
    samples = tokens // CTX
    chances = HEADS // 2 * SEG
    f32, b16 = jnp.float32, jnp.bfloat16
    shape = jax.ShapeDtypeStruct
    vmem = pl.BlockSpec(memory_space=pltpu.VMEM)
    return pl.pallas_call(
        functools.partial(middle_kernel, widths, mesh_plan),
        in_specs=[vmem] * 5 + [smem_spec()] * 3,
        out_specs=[vmem] * 6,
        out_shape=[pltpu.HBM((tokens, D), f32)]
        + block_outs(own, widths)
        + [pltpu.HBM((4, D), f32), shape((1, 1), f32), shape((1, 1), f32)],
        scratch_shapes=[
            pltpu.VMEM((2, CTX, chances), f32),
            pltpu.VMEM((D, 2 * FF), b16),
            pltpu.VMEM((D, 4 * D), b16),
            pltpu.VMEM((D, 2 * FF), b16),
            pltpu.VMEM((D, VOCAB), b16),
            pltpu.VMEM((VOCAB, D), b16),
            pltpu.VMEM((tokens, D), f32),
            pltpu.VMEM((tokens, 3 * D), b16),
            pltpu.VMEM((short, D), b16),
            pltpu.VMEM((samples, 2, CTX, chances), b16),
            pltpu.VMEM((short, D), f32),
            pltpu.VMEM((tokens, FF), b16),
            pltpu.VMEM((tokens, FF), b16),
            pltpu.VMEM((short, FF), b16),
            pltpu.VMEM((short, FF), b16),
            pltpu.VMEM((short, D), f32),
            pltpu.VMEM((short, D), f32),
            pltpu.VMEM((D, 2 * FF + max(4 * D, VOCAB)), f32),
            pltpu.VMEM((CATS, short), jnp.int32),
            pltpu.VMEM((1, short), f32),
            pltpu.VMEM((tokens, D), b16),
            pltpu.VMEM((short, D), b16),
            pltpu.VMEM((tokens, 3 * D), b16),
            pltpu.VMEM((short, D), b16),
            pltpu.VMEM((tokens, D), b16),
            pltpu.VMEM((tokens, FF), b16),
            pltpu.VMEM((tokens, D), b16),
        ],
        compiler_params=pltpu.CompilerParams(vmem_limit_bytes=MIDDLE_BYTES + (0 if own.shape[1] >= 64 else VMEM_BYTES // 2)),
        cost_estimate=pl.CostEstimate(
            flops=6 * tokens * D * 8 * FF,
            bytes_accessed=tokens * D * 8 + D * 6 * FF * 10,
            transcendentals=2 * tokens * (FF + VOCAB),
        ),
        name="middle_part",
    )(source, own, other, targets, gains, valid, horizon, core)


def backward_kernel(layer, widths, mesh_plan, *refs):
    entry_ref, qkv_ref, mix_ref, chance_ref, dmiddle_ref, att_ref, gains_ref, core_ref = refs[:8]
    if layer == 0:
        latent_ref, send_ref, keep_ref, gain_ref = refs[8:12]
        att_kept, before_kept, sum_ref = refs[12:16], refs[16:18], refs[18]
    else:
        before_ref, ffn_ref, slope_ref, inner_hbm, out_ref, send_ref, keep_ref, gain_ref = refs[8:16]
        att_kept, before_kept, sum_ref = refs[16:20], refs[20:23], refs[23]
        inner_ref, inner_sem, turned_att_ref, turned_up_ref = refs[24:28]
        copy = pltpu.make_async_copy(inner_hbm, inner_ref, inner_sem)
    step = pl.program_id(0)

    def here(start, length, unit=CTX):
        base = step * (GROUP * unit)
        return pl.ds(pl.multiple_of(base + start, 16), length)

    @pl.when(step == 0)
    def _():
        gain_ref[...] = jnp.zeros_like(gain_ref)
        if layer > 0:
            copy.start()
            turned_att_ref[...] = att_ref[...].T
            turned_up_ref[...] = ffn_ref[:, 0:FF].T

    dentry, gain_part = attend_back(
        step,
        here,
        (entry_ref[...], qkv_ref, mix_ref, chance_ref),
        dmiddle_ref[...],
        gains_ref[layer : layer + 1, :],
        att_ref,
        head_masks(),
        att_kept,
        turned_att_ref if layer > 0 else None,
    )
    gain_ref[0:1, :] += gain_part
    if layer == 0:
        before_kept[0][here(0, ROWS), :] = dentry.astype(jnp.bfloat16)
        one_hot_rows(latent_ref, before_kept[1], pl.multiple_of(step * ROWS, ROWS))
    else:
        dbefore, gain_part = feed_back(
            here,
            dentry,
            before_ref[...],
            gains_ref[LAYERS + layer - 1 : LAYERS + layer, :],
            ffn_ref,
            slope_ref,
            before_kept,
            turned_up_ref,
        )
        out_ref[...] = dbefore
        gain_ref[1:2, :] += gain_part

    @pl.when(step == pl.num_programs(0) - 1)
    def _():
        normed_ref, dattend_ref, dqkv_ref, mixes_ref = att_kept
        att = [(normed_ref, dqkv_ref), (mixes_ref, dattend_ref)]
        if layer == 0:
            pairs = att + [(before_kept[0], before_kept[1])]
        else:
            copy.wait()
            normed_two_ref, dinner_ref, dout_ref = before_kept
            pairs = [(normed_two_ref, dinner_ref), (dout_ref, inner_ref)] + att
        column = 0
        for left, right in pairs:
            wide = right.shape[1]
            sum_ref[:, column : column + wide] = dot_nn(left[...].T, right[...])
            column += wide
        write_blocks(send_ref, keep_ref, sum_ref, core_ref[0], widths, mesh_plan)


def run_backward(layer, widths, mesh_plan, blocks_like, saved, dmiddle, gains, core, before):
    entry, _, qkv, mix, chance, weights = [in_hbm(item) for item in saved[:6]]
    dmiddle = in_hbm(dmiddle)
    if layer > 0:
        before = [in_hbm(item) for item in before]
    tokens = entry.shape[0]
    queries = chance.shape[3] // (HEADS // 2)
    short = tokens // CTX * queries
    f32, b16 = jnp.float32, jnp.bfloat16
    shape = jax.ShapeDtypeStruct
    in_specs = [
        row_spec(D),
        row_spec(3 * D),
        row_spec(D, GROUP, queries),
        chance_spec(queries),
        row_spec(D, GROUP, queries),
        whole_spec(weights.shape),
        whole_spec(gains.shape),
        smem_spec(),
    ]
    operands = [entry, qkv, mix, chance, dmiddle, weights, gains, core]
    blocks = block_outs(blocks_like, widths)
    outs = [(item, whole_spec(item.shape)) for item in blocks]
    outs.append((pltpu.HBM((2, D), f32), whole_spec((2, D))))
    scratch = [
        pltpu.VMEM((tokens, D), b16),
        pltpu.VMEM((short, D), b16),
        pltpu.VMEM((tokens, 3 * D), b16),
        pltpu.VMEM((short, D), b16),
    ]
    if layer == 0:
        in_specs.append(latent_spec())
        operands.append(before)
        scratch = scratch + [pltpu.VMEM((tokens, D), b16), pltpu.VMEM((tokens, VOCAB), b16)]
        wide = 4 * D + VOCAB
    else:
        in_specs = in_specs + [row_spec(D), whole_spec(before[1].shape), row_spec(FF)]
        in_specs.append(pl.BlockSpec(memory_space=pl.ANY))
        operands = operands + list(before)
        outs.insert(0, (pltpu.HBM((tokens, D), f32), row_spec(D)))
        scratch = scratch + [
            pltpu.VMEM((tokens, D), b16),
            pltpu.VMEM((tokens, FF), b16),
            pltpu.VMEM((tokens, D), b16),
        ]
        wide = 4 * D + 2 * FF
    scratch.append(pltpu.VMEM((D, wide), f32))
    if layer > 0:
        scratch = scratch + [pltpu.VMEM((tokens, FF), b16), pltpu.SemaphoreType.DMA]
        scratch = scratch + [pltpu.VMEM((4 * D, D), b16), pltpu.VMEM((FF, D), b16)]
    return pl.pallas_call(
        functools.partial(backward_kernel, layer, widths, mesh_plan),
        grid=(tokens // ROWS,),
        in_specs=in_specs,
        out_specs=[spec for _, spec in outs],
        out_shape=[item for item, _ in outs],
        scratch_shapes=scratch,
        compiler_params=pltpu.CompilerParams(vmem_limit_bytes=VMEM_BYTES * 3 // 2),
        cost_estimate=pl.CostEstimate(
            flops=6 * tokens * D * wide,
            bytes_accessed=tokens * D * 24 + D * wide * 6,
            transcendentals=tokens * FF,
        ),
        name="backward_part",
    )(*operands)


def pack_kernel(*refs):
    qkv_ref, out_ref, up_ref, down_ref, embed_ref, head_ref = refs[:6]
    low = lambda value: value.astype(jnp.bfloat16)
    att = [[low(qkv_ref[at]), low(out_ref[at].T)] for at in range(LAYERS)]
    ffn = [[low(up_ref[at]), low(down_ref[at])] for at in range(LAYERS)]
    pieces = [
        att[0] + [low(embed_ref[...])],
        ffn[0] + att[1],
        ffn[1] + att[2] + ffn[2] + [low(head_ref[...])],
    ]
    for target, piece in zip(refs[6:], pieces):
        target[...] = jnp.concatenate(piece, axis=1)


def run_pack(masters, chunk_widths):
    vmem = pl.BlockSpec(memory_space=pltpu.VMEM)
    rows = masters[0].shape[1]
    return pl.pallas_call(
        pack_kernel,
        in_specs=[vmem] * 6,
        out_specs=[vmem] * 3,
        out_shape=[
            jax.ShapeDtypeStruct((rows, sum(widths)), jnp.bfloat16) for widths in chunk_widths
        ],
        name="pack",
    )(*masters)


def matrix_plan(widths):
    order = [
        (2, 2), (3, 2), (5, 0), (2, 1), (3, 1), (0, 2), (1, 2),
        (2, 0), (3, 0), (0, 1), (1, 1), (0, 0), (1, 0), (4, 0),
    ]
    plan, column = {}, 0
    for which, layer in order:
        plan[(which, layer)] = (column, widths[which])
        column += widths[which]
    return plan, column


def matrix_list():
    return [(which, layer) for which in range(4) for layer in range(LAYERS)] + [(4, 0), (5, 0)]


MATRICES = 4 * LAYERS + 2
LANES = 128
INNER_ROWS = 16
COMMON_ROWS = 16
ROW_IS_INNER = [True, True, True, False, False, True]


def master_of(masters, which, layer):
    if which == 1:
        return masters[1][layer].T
    return masters[which][layer] if which < 4 else masters[which][...]


def old_row(refs, which, layer):
    return refs[which][layer : layer + 1, :] if which < 4 else refs[which][...]


LATE = [(0, 0), (1, 0), (4, 0)]
EDGE = INNER_ROWS + COMMON_ROWS


def whole_sum(value):
    return jnp.sum(jnp.sum(value, axis=1, keepdims=True), axis=0, keepdims=True)


def square_sums(raw, chosen, plan, first):
    square = raw * raw
    rows = square.shape[0]
    inner, entries = [], []
    for item in matrix_list():
        if item in chosen:
            column, width = plan[item]
            part = square[:, column - first : column - first + width]
            inner.append(jnp.sum(part, axis=1, keepdims=True))
        else:
            inner.append(jnp.zeros((rows, 1), jnp.float32))
        entries.append(jnp.sum(inner[-1], axis=0, keepdims=True))
    inner.append(jnp.zeros((rows, LANES - MATRICES), jnp.float32))
    return jnp.concatenate(inner, axis=1).T, entries, jnp.sum(square, axis=0, keepdims=True)


def store_row(target_ref, row, values):
    total = values.shape[1]
    for at, start in enumerate(range(0, total, LANES)):
        stop = min(start + LANES, total)
        target_ref[row + at : row + at + 1, 0 : stop - start] = values[:, start:stop]


def load_row(source_ref, row, total):
    return jnp.concatenate(
        [
            source_ref[row + at : row + at + 1, 0 : min(LANES, total - start)]
            for at, start in enumerate(range(0, total, LANES))
        ],
        axis=1,
    )


def late_row(widths):
    _, total = matrix_plan(widths)
    late = sum(widths[which] for which, _ in LATE)
    return EDGE + -(-(total - late) // LANES)


def packet_rows(widths):
    late = sum(widths[which] for which, _ in LATE)
    return -(-(late_row(widths) + -(-late // LANES)) // 8) * 8


def first_kernel(*refs):
    masters, row_refs, row_ref = refs[0:6], refs[6:12], refs[12]
    weights, row_sums = [], []
    for which, layer in matrix_list():
        master = masters[which][layer] if which < 4 else masters[which][...]
        weights.append(whole_sum(master * master))
        row_sums.append(whole_sum(old_row(row_refs, which, layer)))
    nothing = lambda count: [jnp.zeros((1, count), jnp.float32)]
    pieces = nothing(2) + weights + nothing(MATRICES) + row_sums
    row_ref[...] = jnp.concatenate(pieces + nothing(LANES - 2 - 3 * MATRICES), axis=1)


def run_first(masters, rows):
    vmem = pl.BlockSpec(memory_space=pltpu.VMEM)
    return pl.pallas_call(
        first_kernel,
        in_specs=[vmem] * 12,
        out_specs=vmem,
        out_shape=jax.ShapeDtypeStruct((1, LANES), jnp.float32),
        name="first_statistics",
    )(*masters, *rows)


def early_kernel(widths, *refs):
    raw_ref, row_ref, gains_at, loss_ref, count_ref, packet_ref = (
        refs[0],
        refs[1],
        refs[2:4],
        refs[4],
        refs[5],
        refs[6],
    )
    plan, _ = matrix_plan(widths)
    chosen = [item for item in matrix_list() if item not in LATE]
    inner, entries, outer = square_sums(raw_ref[...], chosen, plan, 0)
    packet_ref[...] = jnp.zeros_like(packet_ref)
    packet_ref[0:INNER_ROWS, 0 : inner.shape[1]] = inner[0:INNER_ROWS, :]
    last, one = [ref[...] for ref in gains_at]
    gain = jnp.concatenate(
        [jnp.zeros((1, D), jnp.float32), one[0:1], last[2:3], one[1:2], last[3:4], last[0:2]],
        axis=0,
    )
    nothing = lambda count: [jnp.zeros((1, count), jnp.float32)]
    scalars = [loss_ref[...], count_ref[...]] + nothing(MATRICES) + entries
    scalars = scalars + nothing(LANES - 2 - 2 * MATRICES)
    at = INNER_ROWS
    packet_ref[at : at + 7, :] = gain[:, 0:LANES]
    packet_ref[at + 7 : at + 8, :] = row_ref[...] + jnp.concatenate(scalars, axis=1)
    packet_ref[at + 8 : at + 15, :] = gain[:, LANES:]
    store_row(packet_ref, EDGE, outer)


def late_kernel(widths, early_ref, kept_ref, other_ref, gain_ref, packet_ref, raw_ref):
    plan, total = matrix_plan(widths)
    raw = kept_ref[0] + other_ref[0].astype(jnp.float32)
    raw_ref[...] = raw
    inner, entries, outer = square_sums(raw, LATE, plan, total - raw.shape[1])
    packet_ref[...] = early_ref[...]
    packet_ref[0:INNER_ROWS, 0 : inner.shape[1]] += inner[0:INNER_ROWS, :]
    at = INNER_ROWS
    packet_ref[at : at + 1, :] = gain_ref[0:1, 0:LANES]
    packet_ref[at + 8 : at + 9, :] = gain_ref[0:1, LANES:]
    before = jnp.zeros((1, 2 + MATRICES), jnp.float32)
    behind = jnp.zeros((1, LANES - 2 - 2 * MATRICES), jnp.float32)
    packet_ref[at + 7 : at + 8, :] += jnp.concatenate([before] + entries + [behind], axis=1)
    store_row(packet_ref, late_row(widths), outer)


def run_early(widths, raw, row, gain_parts, loss, count):
    vmem = pl.BlockSpec(memory_space=pltpu.VMEM)
    operands = [raw, row] + gain_parts + [loss, count]
    return pl.pallas_call(
        functools.partial(early_kernel, widths),
        in_specs=[vmem] * len(operands),
        out_specs=vmem,
        out_shape=jax.ShapeDtypeStruct((packet_rows(widths), LANES), jnp.float32),
        name="early_statistics",
    )(*operands)


def run_late(widths, packet, kept, other, gain_part):
    vmem = pl.BlockSpec(memory_space=pltpu.VMEM)
    shape = jax.ShapeDtypeStruct
    return pl.pallas_call(
        functools.partial(late_kernel, widths),
        in_specs=[vmem] * 4,
        out_specs=[vmem] * 2,
        out_shape=[shape(packet.shape, jnp.float32), shape(kept.shape[1:], jnp.float32)],
        name="late_statistics",
    )(packet, kept, other, gain_part)


def update_kernel(widths, sizes, *refs):
    packet_ref, raw_early, raw_late = refs[:3]
    masters, inner_refs, outer_refs = refs[3:9], refs[9:15], refs[15:21]
    gains_ref, second_ref = refs[21:23]
    outs = refs[23:]
    outer_count, inner_count = sizes
    plan, total = matrix_plan(widths)
    rows = raw_early.shape[0]
    at = INNER_ROWS
    scalars = packet_ref[at + 7 : at + 8, :]
    pick = lambda at: scalars[:, at : at + 1]
    gain_sum = jnp.concatenate(
        [packet_ref[at : at + 7, :], packet_ref[at + 8 : at + 15, :]], axis=1
    )
    gain_square = jnp.sum(jnp.sum(gain_sum * gain_sum, axis=1, keepdims=True), axis=0, keepdims=True)
    square_total = gain_square
    for at in range(MATRICES):
        square_total = square_total + pick(2 + MATRICES + at)
    count_total = pick(1)
    norm_value = jnp.sqrt(square_total) / count_total
    scaling = jnp.minimum(1.0, clip_limit / norm_value) / count_total
    square_scale = scaling * scaling
    early = raw_early.shape[1]
    outer_early = load_row(packet_ref, EDGE, early)
    outer_late = load_row(packet_ref, late_row(widths), total - early)
    inner_new = []
    for at, (which, layer) in enumerate(matrix_list()):
        outer_length = widths[which] * outer_count
        inner_new.append(
            decay_two * old_row(inner_refs, which, layer)
            + (1 - decay_two)
            * (square_scale * packet_ref[at : at + 1, 0:rows] / outer_length + tiny_term)
        )
    stacked = jnp.concatenate(inner_new, axis=0)
    stacked = jnp.concatenate([stacked, jnp.ones((LANES - MATRICES, rows), jnp.float32)], axis=0)
    if rows < LANES:
        stacked = jnp.concatenate([stacked, jnp.ones((LANES, LANES - rows), jnp.float32)], axis=1)
    turned = lax.rsqrt(stacked).T
    outs[0][...] = pick(0)
    outs[1][...] = count_total
    outs[2][...] = norm_value
    first_out = {4: 3, 0: 7, 1: 11, 2: 15, 3: 19, 5: 23}
    for at, (which, layer) in enumerate(matrix_list()):
        column, width = plan[(which, layer)]
        outer_length, inner_length = width * outer_count, rows * inner_count
        row_length = inner_length if ROW_IS_INNER[which] else outer_length
        copies = outer_count if ROW_IS_INNER[which] else inner_count
        entries = outer_length * inner_length
        if column < early:
            raw = raw_early[:, column : column + width]
            outer_total = outer_early[:, column : column + width]
        else:
            raw = raw_late[:, column - early : column - early + width]
            outer_total = outer_late[:, column - early : column - early + width]
        outer_new = decay_two * old_row(outer_refs, which, layer) + (1 - decay_two) * (
            square_scale * outer_total / inner_length + tiny_term
        )
        mean_rows = decay_two * (pick(2 + 2 * MATRICES + at) / (copies * row_length)) + (
            1 - decay_two
        ) * (square_scale * pick(2 + MATRICES + at) / entries + tiny_term)
        factor = step_rate * jnp.sqrt(pick(2 + at) / entries) * jnp.sqrt(mean_rows)
        grad = raw * scaling
        updated = master_of(masters, which, layer) - grad * (
            turned[0:rows, at : at + 1] * (factor * lax.rsqrt(outer_new))
        )
        first = first_out[which]
        row_new, column_new = (
            (inner_new[at], outer_new) if ROW_IS_INNER[which] else (outer_new, inner_new[at])
        )
        if which < 4:
            if which == 1:
                updated, grad = updated.T, grad.T
            outs[first][layer] = updated
            outs[first + 1][layer] = grad
            outs[first + 2][layer : layer + 1, :] = row_new
            outs[first + 3][layer : layer + 1, :] = column_new
        else:
            outs[first][...] = updated
            outs[first + 1][...] = grad
            outs[first + 2][...] = row_new
            outs[first + 3][...] = column_new
    gain_grad = gain_sum * scaling
    second_new = decay_two * second_ref[...] + (1 - decay_two) * (gain_grad * gain_grad + tiny_term)
    gains = gains_ref[...]
    spread = jnp.sqrt(jnp.mean(gains * gains, axis=-1, keepdims=True))
    outs[27][...] = gains - step_rate * spread * gain_grad * lax.rsqrt(second_new)
    outs[28][...] = gain_grad
    outs[29][...] = second_new


def run_update(widths, sizes, packet, raw_early, raw_late, masters, inner, outer, gains, second):
    vmem = pl.BlockSpec(memory_space=pltpu.VMEM)
    operands = [packet, raw_early, raw_late] + masters + inner + outer + [gains, second]
    shapes = [(1, 1)] * 3
    for which in [4, 0, 1, 2, 3, 5]:
        shapes = shapes + [masters[which].shape] * 2
        pair = [inner[which].shape, outer[which].shape]
        shapes = shapes + (pair if ROW_IS_INNER[which] else pair[::-1])
    shapes = shapes + [gains.shape] * 3
    return pl.pallas_call(
        functools.partial(update_kernel, widths, sizes),
        in_specs=[vmem] * len(operands),
        out_specs=[vmem] * len(shapes),
        out_shape=[jax.ShapeDtypeStruct(item, jnp.float32) for item in shapes],
        name="update",
    )(*operands)


def swap(value, mask):
    count = lax.axis_size("dp") * lax.axis_size("fsdp")
    return lax.ppermute(value, ("dp", "fsdp"), [(place, place ^ mask) for place in range(count)])


def device_index():
    return lax.axis_index("dp") * lax.axis_size("fsdp") + lax.axis_index("fsdp")


def step_masks(step):
    masks = []
    for digit in range(1, 1 << len(step)):
        masks.append(sum(1 << bit for at, bit in enumerate(step[::-1]) if (digit >> at) & 1))
    return masks


def tie(*values):
    return lax.optimization_barrier(values)


def behind(value, *ahead):
    return lax.optimization_barrier((value,) + ahead)[0]


class Gather:
    def __init__(self, piece, steps):
        self.held, self.steps, self.at = piece[None], steps, 0

    def send(self):
        self.others = tuple(swap(self.held, mask) for mask in step_masks(self.steps[self.at]))

    def join(self):
        step = self.steps[self.at]
        pieces = [self.held] + list(self.others)
        for at, bit in enumerate(step[::-1]):
            upper = (device_index() >> bit) & 1 == 1
            pieces = [
                jnp.where(upper, pieces[place ^ (1 << at)], pieces[place])
                for place in range(len(pieces))
            ]
        self.held = jnp.concatenate(pieces)
        self.at += 1


class Scatter:
    def __init__(self, sent, kept, steps):
        self.sent, self.kept, self.steps, self.at = (sent,), kept, steps, 0

    def send(self):
        masks = step_masks(self.steps[self.at])
        self.others = tuple(swap(sent, mask) for sent, mask in zip(self.sent, masks))

    def join(self):
        self.at += 1
        step = self.steps[self.at] if self.at < len(self.steps) else ()
        count = 1 << len(step)
        own = 0
        for bit in step:
            own = 2 * own + ((device_index() >> bit) & 1)
        shape = (count, self.kept.shape[0] // count) + self.kept.shape[1:]
        terms = [item.reshape(shape) for item in (self.kept,) + self.others]

        def pick(digit):
            total = None
            for term in terms:
                part = lax.dynamic_index_in_dim(term, own ^ digit, 0, keepdims=False)
                part = part.astype(jnp.float32)
                total = part if total is None else total + part
            return total

        self.sent = tuple(pick(digit).astype(jnp.bfloat16) for digit in range(1, count))
        self.kept = pick(0)


def sum_packets(packet, group, inner_bits):
    masks = step_masks(group)
    others = [swap(packet, mask) for mask in masks]
    inner, outer = packet[:INNER_ROWS], packet[EDGE:]
    common = [packet[INNER_ROWS:EDGE]]
    inner, outer = [inner], [outer]
    for mask, other in zip(masks, others):
        common.append(other[INNER_ROWS:EDGE])
        if mask >> inner_bits << inner_bits == mask:
            inner.append(other[:INNER_ROWS])
        if mask >> inner_bits == 0:
            outer.append(other[EDGE:])
    tree = lambda items: (
        items[0] if len(items) == 1 else tree(
            [items[at] + items[at + 1] for at in range(0, len(items), 2)]
        )
    )
    return jnp.concatenate([tree(inner), tree(common), tree(outer)])


def merged(parts):
    whole = Scatter(None, jnp.concatenate([part.kept for part in parts], axis=2), parts[0].steps)
    whole.sent = tuple(
        jnp.concatenate(pieces, axis=2) for pieces in zip(*[part.sent for part in parts])
    )
    whole.at = parts[0].at
    return whole


def shards(
    latents,
    targets,
    horizon,
    memory_valid,
    embed,
    qkv_weight,
    out_weight,
    up_weight,
    down_weight,
    head_weight,
    gains,
    embed_rows,
    embed_cols,
    qkv_rows,
    qkv_cols,
    out_rows,
    out_cols,
    up_rows,
    up_cols,
    down_rows,
    down_cols,
    head_rows,
    head_cols,
    gain_second,
):
    samples = latents.shape[0]
    sizes = (lax.axis_size("dp"), lax.axis_size("fsdp"))
    highest = (sizes[0] * sizes[1]).bit_length() - 1
    gather_steps = [(bit,) for bit in reversed(range(3, highest))] + [(2, 1), (0,)]
    scatter_steps = gather_steps[::-1]
    mesh_plan = (sizes[0], sizes[1], gather_steps)
    core = (lax.axis_index("fsdp") & 1).astype(jnp.int32).reshape(1)

    out_turned = jnp.swapaxes(out_weight, 1, 2)
    down_turned = jnp.swapaxes(down_weight, 1, 2)
    masters = [qkv_weight, out_turned, up_weight, down_turned, embed.T, head_weight]
    widths = [qkv_weight.shape[2], out_weight.shape[2], up_weight.shape[2], down_weight.shape[1]]
    widths = widths + [embed.shape[0], head_weight.shape[1]]
    att_widths, ffn_widths = widths[0:2], widths[2:4]
    chunk_widths = [
        att_widths + widths[4:5],
        ffn_widths + att_widths,
        ffn_widths + att_widths + ffn_widths + widths[5:6],
    ]
    chunks = [Gather(piece, gather_steps) for piece in run_pack(masters, chunk_widths)]
    first, second, third = chunks
    latent_rows = latents.transpose(0, 2, 1)
    target_rows = targets.transpose(0, 2, 1)
    shared = (gains, memory_valid, core)
    back_shared = (gains, core)

    count = len(gather_steps)
    flat = lambda item: item if item.ndim == 2 else item.reshape(1, -1)
    inner = [flat(item) for item in (qkv_rows, out_rows, up_rows, down_cols, embed_cols, head_rows)]
    outer = [flat(item) for item in (qkv_cols, out_cols, up_cols, down_rows, embed_rows, head_cols)]
    row_stats = [inner[at] if ROW_IS_INNER[at] else outer[at] for at in range(6)]
    first_row = run_first(masters, row_stats)
    for at in range(count - 1):
        for chunk in chunks:
            chunk.send()
        if at == count - 2:
            second.others, first_row = tie(second.others, first_row)
        for chunk in chunks[: 2 if at == count - 2 else 3]:
            chunk.join()
            if at == count - 3 and chunk is first:
                first.held, third.held = tie(first.held, third.held)
    first.send()
    (other,) = first.others
    held, other, second.held = tie(first.held, other, second.held)
    second.send()
    kept = [run_forward(0, chunk_widths[0], mesh_plan, latent_rows, held, other, *shared)]
    middle, (other,) = tie(kept[0][1], second.others)
    kept.append(
        run_forward(1, chunk_widths[1], mesh_plan, middle, second.held, other, *shared)
    )
    middle, third.others = tie(kept[1][1], third.others)
    third.join()
    third.send()
    (other,) = third.others
    dmiddle, sent, held, gain_middle, loss, counted = run_middle(
        chunk_widths[2],
        mesh_plan,
        middle,
        third.held,
        other,
        target_rows,
        gains,
        memory_valid,
        horizon,
        core,
    )
    pair = Scatter(sent, held, scatter_steps)
    pair.send()
    pair.join()
    like = first.held
    before = (kept[0][1], kept[1][6], kept[1][8], kept[1][7])
    dmiddle, pair.sent = tie(dmiddle, pair.sent)
    pair.send()
    dmiddle, sent, held, gain_one = run_backward(
        1, chunk_widths[1], mesh_plan, like, kept[1], dmiddle, *back_shared, before
    )
    dmiddle, sent, held, pair.others = tie(dmiddle, sent, held, pair.others)
    one = Scatter(sent, held, scatter_steps)
    one.send()
    pair.join()
    one.join()
    dmiddle, pair.sent, one.sent = tie(dmiddle, pair.sent, one.sent)
    one.send()
    pair.send()
    sent, held, gain_zero = run_backward(
        0, chunk_widths[0], mesh_plan, like, kept[0], dmiddle, *back_shared, latent_rows
    )
    sent, held, pair.others, one.others = tie(sent, held, pair.others, one.others)
    zero = Scatter(sent, held, scatter_steps)
    zero.send()
    one.join()
    one.send()
    pair.join()
    zero.join()
    one.others = behind(one.others, zero.sent)
    zero.send()
    one.join()
    early = merged([pair, one])
    while early.at < count:
        early.send()
        if early.at == count - 1:
            zero.join()
            zero.send()
        zero.others, early.others = tie(zero.others, early.others)
        early.join()
    raw_early = early.kept[0]

    packet = run_early(
        widths, raw_early, first_row, [gain_middle, gain_one], loss, counted
    )
    while zero.at < count - 1:
        zero.join()
        zero.send()
    packet, raw_late = run_late(widths, packet, zero.kept, zero.others[0], gain_zero)
    inner_bits = sizes[1].bit_length() - 1
    rest = list(range(3, highest))
    groups = [(0,), (2, 1)] + [tuple(rest[at : at + 2][::-1]) for at in range(0, len(rest), 2)]
    for group in groups:
        packet = sum_packets(packet, group, inner_bits)
    results = run_update(
        widths, sizes, packet, raw_early, raw_late, masters, inner, outer, gains, gain_second
    )
    results = list(results)
    for at in range(3):
        results[at] = results[at].reshape(())
    for at in (3, 4, 11, 12, 19, 20):
        results[at] = jnp.swapaxes(results[at], -1, -2)
    for at in (5, 6, 25, 26):
        results[at] = results[at].reshape(-1)
    return tuple(results)


def solution(mesh):
    return jax.shard_map(
        shards,
        mesh=mesh,
        in_specs=(
            P(("dp", "fsdp"), None, None),
            P(("dp", "fsdp"), None, None),
            P(("dp", "fsdp")),
            P(("dp", "fsdp")),
            P("dp", "fsdp"),
            P(None, "fsdp", "dp"),
            P(None, "fsdp", "dp"),
            P(None, "fsdp", "dp"),
            P(None, "dp", "fsdp"),
            P("fsdp", "dp"),
            P(),
            P("dp"),
            P("fsdp"),
            P(None, "fsdp"),
            P(None, "dp"),
            P(None, "fsdp"),
            P(None, "dp"),
            P(None, "fsdp"),
            P(None, "dp"),
            P(None, "dp"),
            P(None, "fsdp"),
            P("fsdp"),
            P("dp"),
            P(),
        ),
        out_specs=(
            P(),
            P(),
            P(),
            P("dp", "fsdp"),
            P("dp", "fsdp"),
            P("dp"),
            P("fsdp"),
            P(None, "fsdp", "dp"),
            P(None, "fsdp", "dp"),
            P(None, "fsdp"),
            P(None, "dp"),
            P(None, "fsdp", "dp"),
            P(None, "fsdp", "dp"),
            P(None, "fsdp"),
            P(None, "dp"),
            P(None, "fsdp", "dp"),
            P(None, "fsdp", "dp"),
            P(None, "fsdp"),
            P(None, "dp"),
            P(None, "dp", "fsdp"),
            P(None, "dp", "fsdp"),
            P(None, "dp"),
            P(None, "fsdp"),
            P("fsdp", "dp"),
            P("fsdp", "dp"),
            P("fsdp"),
            P("dp"),
            P(),
            P(),
            P(),
        ),
        check_vma=False,
    )
```

```python
import functools

import jax
import jax.numpy as jnp
from jax import lax
from jax.experimental import pallas as pl
from jax.experimental.pallas import tpu as pltpu
from jax.sharding import PartitionSpec as P

D = 256
HEADS = 8
HEAD = D // HEADS
FF = 1024
CATS = 32
CLASSES = 32
LAYERS = 3
SEG = 48
MEM = 48
CTX = 96
VOCAB = 1024
GROUP = 4
WIDE_GROUP = 8
ROWS = GROUP * CTX
HALF = D // 2
VMEM_BYTES = 24 * 1024 * 1024
MIDDLE_BYTES = 43 * 1024 * 1024

decay_two = 0.9
step_rate = 0.3
clip_limit = 0.05
tiny_term = 1e-30
norm_eps = 1e-06
masked_score = -1e30
log2_e = 1.4426950408889634
score_scale = HEAD ** (-0.5)
gelu_one = 0.7978845608028654
gelu_two = 0.044715


def dot_nn(left, right):
    return lax.dot_general(
        left, right, (((1,), (0,)), ((), ())), preferred_element_type=jnp.float32
    )


def dot_nt(left, right):
    return lax.dot_general(
        left, right, (((1,), (1,)), ((), ())), preferred_element_type=jnp.float32
    )


def dot_tn(left, right):
    return lax.dot_general(
        left, right, (((0,), (0,)), ((), ())), preferred_element_type=jnp.float32
    )


def inverse_rms(values):
    return lax.rsqrt(jnp.mean(values * values, axis=-1, keepdims=True) + norm_eps)


def rms_back(values, inverse, gain_row, upstream):
    normed = values * inverse
    scaled = upstream * gain_row
    inner = jnp.mean(scaled * normed, axis=-1, keepdims=True)
    return (
        inverse * (scaled - normed * inner),
        jnp.sum(upstream * normed, axis=0, keepdims=True),
    )


def head_masks():
    lane = lax.broadcasted_iota(jnp.int32, (1, D // 2), 1) // HEAD
    return [lane == head for head in range(HEADS // 2)]


def expand_heads(rows, masks):
    return jnp.concatenate([rows * mask.astype(rows.dtype) for mask in masks], axis=0)


def collapse_heads(spread, rows, masks):
    product = dot_tn(spread, rows)
    queries = product.shape[0] // len(masks)
    taken = product[(len(masks) - 1) * queries :]
    for at, mask in enumerate(masks[:-1]):
        taken = jnp.where(mask, product[at * queries : (at + 1) * queries], taken)
    return taken


def half_of(part, side):
    start = part * D + side * HALF
    return slice(start, start + HALF)


def fill_bias(bias_ref):
    spread = bias_ref.shape[2]
    queries = spread // (HEADS // 2)
    key_at = lax.broadcasted_iota(jnp.int32, (CTX, spread), 0)
    query_at = lax.broadcasted_iota(jnp.int32, (CTX, spread), 1) % queries + (CTX - queries)
    later = key_at > query_at
    crosses = (query_at >= MEM) & (key_at < MEM)
    bias_ref[0] = jnp.where(later | crosses, masked_score, 0.0)
    bias_ref[1] = jnp.where(later, masked_score, 0.0)


def block_place(device, steps):
    place, weight = 0, 1
    for step in steps[:-1]:
        digit = 0
        for bit in step:
            digit = 2 * digit + ((device >> bit) & 1)
        place += digit * weight
        weight <<= len(step)
    return place


def place_weights(targets, own_ref, other_ref, core, widths, mesh_plan, start=0):
    outer_count, inner_count, steps = mesh_plan
    rows = own_ref.shape[1]
    for high in range(inner_count // 2):
        for source, side in ((own_ref, core), (other_ref, 1 - core)):
            here = pl.ds(pl.multiple_of((2 * high + side) * rows, rows), rows)
            at = start
            for (target, column), width in zip(targets, widths):
                block = [
                    source[
                        block_place(outer * inner_count + 2 * high, steps), :, at : at + width
                    ]
                    for outer in range(outer_count)
                ]
                target[here, column : column + width * outer_count] = jnp.concatenate(
                    block, axis=1
                )
                at += width


def write_blocks(send_ref, keep_ref, sum_ref, core, widths, mesh_plan, start=0):
    outer_count, inner_count, steps = mesh_plan
    rows = keep_ref.shape[1]
    for high in range(inner_count // 2):
        for target, side in ((keep_ref, core), (send_ref, 1 - core)):
            here = pl.ds(pl.multiple_of((2 * high + side) * rows, rows), rows)
            taken = sum_ref[here, :]
            for outer in range(outer_count):
                block, column = [], 0
                for width in widths:
                    block.append(taken[:, column + outer * width : column + (outer + 1) * width])
                    column += width * outer_count
                place = block_place(outer * inner_count + 2 * high, steps)
                target[place, :, start : start + sum(widths)] = jnp.concatenate(
                    block, axis=1
                ).astype(target.dtype)


def one_hot_rows(latent_ref, hot_ref, first):
    spot = lax.broadcasted_iota(jnp.int32, (CATS, VOCAB), 1) // CLASSES
    group = lax.broadcasted_iota(jnp.int32, (CATS, VOCAB), 0)
    spreader = jnp.where(spot == group, 1.0, 0.0).astype(jnp.bfloat16)
    classes = (lax.broadcasted_iota(jnp.int32, (1, VOCAB), 1) % CLASSES).astype(jnp.float32)
    for sample in range(latent_ref.shape[0]):
        drawn = dot_tn(latent_ref[sample].astype(jnp.float32).astype(jnp.bfloat16), spreader)
        hot_ref[pl.ds(first + sample * CTX, CTX), :] = jnp.where(
            drawn == classes, 1.0, 0.0
        ).astype(jnp.bfloat16)


def tail_rows(values, queries):
    if queries == CTX:
        return values
    return jnp.concatenate(
        [
            values[(sample + 1) * CTX - queries : (sample + 1) * CTX]
            for sample in range(values.shape[0] // CTX)
        ],
        axis=0,
    )


def attend_forward(step, hidden, gain_row, weight_ref, valid_ref, bias_ref, masks, refs):
    middle_ref, qkv_ref, mix_ref, chance_ref = refs
    queries = chance_ref.shape[3] // (HEADS // 2)
    group = hidden.shape[0] // CTX
    normed = (hidden * inverse_rms(hidden) * gain_row).astype(jnp.bfloat16)
    qkv_ref[...] = dot_nn(normed, weight_ref[:, 0 : 3 * D]).astype(jnp.bfloat16)
    units = [(sample, side) for sample in range(group) for side in range(2)]
    scores = []
    for sample, side in units:
        rows = slice(sample * CTX, (sample + 1) * CTX)
        tail = slice((sample + 1) * CTX - queries, (sample + 1) * CTX)
        spread = expand_heads(qkv_ref[tail, half_of(0, side)], masks)
        scores.append(dot_nt(qkv_ref[rows, half_of(1, side)], spread))
    for (sample, side), score in zip(units, scores):
        score = score + bias_ref[valid_ref[step * group + sample]]
        peak = jnp.max(score, axis=0, keepdims=True)
        exponent = jnp.exp2((score - peak) * (score_scale * log2_e))
        total = jnp.sum(exponent, axis=0, keepdims=True)
        chance_ref[sample, side] = (exponent * (1.0 / total)).astype(jnp.bfloat16)
    for sample, side in units:
        rows = slice(sample * CTX, (sample + 1) * CTX)
        mix_ref[sample * queries : (sample + 1) * queries, half_of(0, side)] = collapse_heads(
            chance_ref[sample, side], qkv_ref[rows, half_of(2, side)], masks
        ).astype(jnp.bfloat16)
    middle_ref[...] = tail_rows(hidden, queries) + dot_nn(
        mix_ref[...], weight_ref[:, 3 * D : 4 * D]
    )


def gelu_parts(value):
    square = value * value
    share = 0.5 + 0.5 * jnp.tanh(value * (gelu_one + (gelu_one * gelu_two) * square))
    active = value * share
    bent = active * (1.0 - share)
    return active, share + bent * (2.0 * gelu_one + (6.0 * gelu_one * gelu_two) * square)


def feed_forward(middle, gain_row, weight_ref, inner_ref, slope_ref):
    normed = (middle * inverse_rms(middle) * gain_row).astype(jnp.bfloat16)
    for part in range(FF // D):
        columns = slice(part * D, (part + 1) * D)
        inner = dot_nn(normed, weight_ref[:, columns])
        for sample in range(middle.shape[0] // CTX):
            rows = slice(sample * CTX, (sample + 1) * CTX)
            active, slope = gelu_parts(inner[rows])
            inner_ref[rows, columns] = active.astype(jnp.bfloat16)
            slope_ref[rows, columns] = slope.astype(jnp.bfloat16)
    return middle + dot_nt(inner_ref[...], weight_ref[:, FF : 2 * FF])


def feed_back(here, upstream, middle, gain_row, weight_ref, slope_ref, refs):
    normed_ref, dinner_ref, dout_ref = refs
    dout = upstream.astype(jnp.bfloat16)
    dout_ref[here(0, middle.shape[0]), :] = dout
    inverse = inverse_rms(middle)
    normed_ref[here(0, middle.shape[0]), :] = (middle * inverse * gain_row).astype(jnp.bfloat16)
    for part in range(FF // D):
        columns = slice(part * D, (part + 1) * D)
        dact = dot_nn(dout, weight_ref[:, FF + part * D : FF + (part + 1) * D])
        dinner_ref[here(0, middle.shape[0]), columns] = (
            dact * slope_ref[:, columns].astype(jnp.float32)
        ).astype(jnp.bfloat16)
    dnormed = dot_nt(dinner_ref[here(0, middle.shape[0]), :], weight_ref[:, 0:FF])
    through, gain_part = rms_back(middle, inverse, gain_row, dnormed)
    return upstream + through, gain_part


def attend_back(step, here, saved, dmiddle, gain_row, weight_ref, masks, refs):
    hidden, qkv_ref, mix_ref, chance_ref = saved
    normed_ref, dmiddle_ref, dqkv_ref, mixes_ref = refs
    group = hidden.shape[0] // CTX
    queries = chance_ref.shape[3] // (HEADS // 2)
    short = here(0, group * queries, queries)
    dattend = dmiddle.astype(jnp.bfloat16)
    dmiddle_ref[short, :] = dattend
    mixes_ref[short, :] = mix_ref[...]
    dmix = dot_nt(dattend, weight_ref[:, 3 * D : 4 * D]).astype(jnp.bfloat16)
    units = [(sample, side) for sample in range(group) for side in range(2)]
    slopes, dchances, dscores = [], [], []
    for sample, side in units:
        rows = slice(sample * CTX, (sample + 1) * CTX)
        slopes.append(
            expand_heads(
                dmix[sample * queries : (sample + 1) * queries, half_of(0, side)], masks
            )
        )
        dchances.append(dot_nt(qkv_ref[rows, half_of(2, side)], slopes[-1]))
    for (sample, side), dchance in zip(units, dchances):
        chance = chance_ref[sample, side].astype(jnp.float32)
        weighed = chance * dchance
        dscores.append(
            (weighed - chance * jnp.sum(weighed, axis=0, keepdims=True)).astype(jnp.bfloat16)
        )
    for at, (sample, side) in enumerate(units):
        rows = slice(sample * CTX, (sample + 1) * CTX)
        tail = slice((sample + 1) * CTX - queries, (sample + 1) * CTX)
        there = here(sample * CTX, CTX)
        spread = expand_heads(qkv_ref[tail, half_of(0, side)], masks)
        keys = qkv_ref[rows, half_of(1, side)]
        dvalues = dot_nn(chance_ref[sample, side], slopes[at])
        dkeys = dot_nn(dscores[at], spread) * score_scale
        dqueries = (collapse_heads(dscores[at], keys, masks) * score_scale).astype(jnp.bfloat16)
        if queries < CTX:
            nothing = jnp.zeros((CTX - queries, HALF), jnp.bfloat16)
            dqueries = jnp.concatenate([nothing, dqueries], axis=0)
        dqkv_ref[there, half_of(0, side)] = dqueries
        dqkv_ref[there, half_of(1, side)] = dkeys.astype(jnp.bfloat16)
        dqkv_ref[there, half_of(2, side)] = dvalues.astype(jnp.bfloat16)
    inverse = inverse_rms(hidden)
    normed_ref[here(0, hidden.shape[0]), :] = (hidden * inverse * gain_row).astype(jnp.bfloat16)
    dnormed = dot_nt(dqkv_ref[here(0, hidden.shape[0]), :], weight_ref[:, 0 : 3 * D])
    through, gain_part = rms_back(hidden, inverse, gain_row, dnormed)
    if queries < CTX:
        nothing = jnp.zeros((CTX - queries, D), jnp.float32)
        pieces = []
        for sample in range(group):
            pieces = pieces + [nothing, dmiddle[sample * queries : (sample + 1) * queries]]
        dmiddle = jnp.concatenate(pieces, axis=0)
    return dmiddle + through, gain_part


def row_spec(width, group=GROUP, unit=CTX):
    return pl.BlockSpec((group * unit, width), lambda step: (step, 0))


def chance_spec(queries, group=GROUP):
    return pl.BlockSpec((group, 2, CTX, HEADS // 2 * queries), lambda step: (step, 0, 0, 0))


def latent_spec(group=GROUP):
    return pl.BlockSpec((group, CATS, CTX), lambda step: (step, 0, 0))


def whole_spec(shape):
    return pl.BlockSpec(shape, lambda step: (0,) * len(shape))


def in_hbm(item):
    return pltpu.with_memory_space_constraint(item, pltpu.HBM)


def smem_spec():
    return pl.BlockSpec(memory_space=pltpu.SMEM)


def forward_kernel(layer, widths, mesh_plan, source_ref, own_ref, other_ref, gains_ref, valid_ref, core_ref, *refs):
    entry_ref, att_ref, before_ref = refs[0], refs[5], refs[6]
    bias_ref = refs[7] if layer == 0 else refs[9]
    step = pl.program_id(0)

    @pl.when(step == 0)
    def _():
        fill_bias(bias_ref)
        att = [(att_ref, 0), (att_ref, 3 * D)]
        before = [(before_ref, 0)] if layer == 0 else [(before_ref, 0), (before_ref, FF)]
        targets = att + before if layer == 0 else before + att
        place_weights(targets, own_ref, other_ref, core_ref[0], widths[: len(targets)], mesh_plan)

    if layer == 0:
        one_hot_rows(source_ref, refs[8], 0)
        hidden = dot_nt(refs[8][...], before_ref[...])
    else:
        gain_ffn = gains_ref[LAYERS + layer - 1 : LAYERS + layer, :]
        hidden = feed_forward(source_ref[...], gain_ffn, before_ref, refs[7], refs[8])
    entry_ref[...] = hidden
    attend_forward(
        step,
        hidden,
        gains_ref[layer : layer + 1, :],
        att_ref,
        valid_ref,
        bias_ref,
        head_masks(),
        refs[1:5],
    )


def run_forward(layer, widths, mesh_plan, source, own, other, gains, valid, core):
    tokens = valid.shape[0] * CTX
    f32, b16 = jnp.float32, jnp.bfloat16
    chances = HEADS // 2 * CTX
    group = WIDE_GROUP if layer == 0 else GROUP
    outs = [
        (pltpu.HBM((tokens, D), f32), row_spec(D, group)),
        (pltpu.HBM((tokens, D), f32), row_spec(D, group)),
        (pltpu.HBM((tokens, 3 * D), b16), row_spec(3 * D, group)),
        (pltpu.HBM((tokens, D), b16), row_spec(D, group)),
        (pltpu.HBM((tokens // CTX, 2, CTX, chances), b16), chance_spec(CTX, group)),
        (pltpu.HBM((D, 4 * D), b16), whole_spec((D, 4 * D))),
    ]
    scratch = [pltpu.VMEM((2, CTX, chances), f32)]
    if layer == 0:
        scratch = [pltpu.VMEM((D, VOCAB), b16)] + scratch + [pltpu.VMEM((group * CTX, VOCAB), b16)]
        source_spec = latent_spec(group)
    else:
        source_spec = row_spec(D, group)
        outs.append((pltpu.HBM((D, 2 * FF), b16), whole_spec((D, 2 * FF))))
        outs = outs + [(pltpu.HBM((tokens, FF), b16), row_spec(FF, group))] * 2
        source = in_hbm(source)
    return pl.pallas_call(
        functools.partial(forward_kernel, layer, widths, mesh_plan),
        grid=(tokens // (group * CTX),),
        in_specs=[
            source_spec,
            whole_spec(own.shape),
            whole_spec(other.shape),
            whole_spec(gains.shape),
            smem_spec(),
            smem_spec(),
        ],
        out_specs=[spec for _, spec in outs],
        out_shape=[item for item, _ in outs],
        scratch_shapes=scratch,
        compiler_params=pltpu.CompilerParams(vmem_limit_bytes=VMEM_BYTES),
        cost_estimate=pl.CostEstimate(
            flops=2 * tokens * D * 12 * D,
            bytes_accessed=tokens * D * 16 + D * 12 * D * 4,
            transcendentals=tokens * (FF + HEADS * CTX),
        ),
        name="forward_part",
    )(source, own, other, gains, valid, core)


def middle_kernel(widths, mesh_plan, *refs):
    source_ref, own_ref, other_ref, drawn_ref, gains_ref, valid_ref, horizon_ref, core_ref = refs[:8]
    out_ref, send_ref, keep_ref, gain_ref, loss_ref, count_ref = refs[8:14]
    bias_ref, weight_one_ref, att_ref, weight_two_ref, head_ref, turned_ref = refs[14:20]
    entry_ref, qkv_ref, mix_ref, chance_ref, middle_two_ref, inner_one_ref, slope_one_ref = refs[20:27]
    inner_ref, slope_ref, last_ref, dmiddle_ref, sum_ref, targets_ref, counted_ref = refs[27:34]
    normed_long, dattend_ref, dqkv_long, mixes_ref, normed_two_long, dinner_long, dout_long = refs[34:]
    tokens = middle_two_ref.shape[0]
    final_ref = normed_long.at[0:tokens]
    dlogits_ref = dqkv_long.at[0:VOCAB]
    normed_ref = normed_two_long.at[0:tokens]
    dinner_ref = dinner_long.at[0:tokens]
    dout_ref = dout_long.at[0:tokens]
    groups = source_ref.shape[0] // (WIDE_GROUP * CTX)
    masks = head_masks()
    gain_att = gains_ref[LAYERS - 1 : LAYERS, :]
    gain_before = gains_ref[2 * LAYERS - 2 : 2 * LAYERS - 1, :]
    gain_ffn = gains_ref[2 * LAYERS - 1 : 2 * LAYERS, :]
    gain_final = gains_ref[2 * LAYERS : 2 * LAYERS + 1, :]
    fill_bias(bias_ref)
    place_weights(
        [
            (weight_one_ref, 0),
            (weight_one_ref, FF),
            (att_ref, 0),
            (att_ref, 3 * D),
            (weight_two_ref, 0),
            (weight_two_ref, FF),
            (head_ref, 0),
        ],
        own_ref,
        other_ref,
        core_ref[0],
        widths,
        mesh_plan,
    )

    def rows_of(group, unit=CTX):
        return pl.ds(pl.multiple_of(group * (WIDE_GROUP * unit), WIDE_GROUP * unit), WIDE_GROUP * unit)

    def forward(group, carry):
        rows, short = rows_of(group), rows_of(group, SEG)
        hidden = feed_forward(
            source_ref[rows, :],
            gain_before,
            weight_one_ref,
            inner_one_ref.at[rows],
            slope_one_ref.at[rows],
        )
        entry_ref[rows, :] = hidden
        attend_forward(
            group,
            hidden,
            gain_att,
            att_ref,
            valid_ref,
            bias_ref,
            masks,
            (
                middle_two_ref.at[short],
                qkv_ref.at[rows],
                mix_ref.at[short],
                chance_ref.at[pl.ds(group * WIDE_GROUP, WIDE_GROUP)],
            ),
        )
        return carry

    lax.fori_loop(0, groups, forward, 0)
    turned_ref[...] = head_ref[...].T
    samples = tokens // SEG
    targets_ref[...] = jnp.concatenate([drawn_ref[at] for at in range(samples)], axis=1)
    position = lax.broadcasted_iota(jnp.int32, (1, SEG), 1)
    counted_ref[...] = jnp.concatenate(
        [jnp.where(position < horizon_ref[at], 1.0, 0.0) for at in range(samples)], axis=1
    )
    count_ref[...] = jnp.sum(counted_ref[...], axis=1, keepdims=True)
    for block in range(tokens // ROWS):
        rows = slice(block * ROWS, (block + 1) * ROWS)
        middle = middle_two_ref[rows, :]
        normed = (middle * inverse_rms(middle) * gain_ffn).astype(jnp.bfloat16)
        normed_ref[rows, :] = normed
        for part in range(FF // D):
            columns = slice(part * D, (part + 1) * D)
            inner = dot_nn(normed, weight_two_ref[:, columns])
            for piece in range(GROUP):
                there = slice(block * ROWS + piece * CTX, block * ROWS + (piece + 1) * CTX)
                active, slope = gelu_parts(inner[piece * CTX : (piece + 1) * CTX])
                inner_ref[there, columns] = active.astype(jnp.bfloat16)
                slope_ref[there, columns] = slope.astype(jnp.bfloat16)
        last = middle + dot_nt(inner_ref[rows, :], weight_two_ref[:, FF : 2 * FF])
        last_ref[rows, :] = last
        final_ref[rows, :] = (last * inverse_rms(last) * gain_final).astype(jnp.bfloat16)
    span = D
    loss = jnp.zeros((1, span), jnp.float32)
    spots = lax.broadcasted_iota(jnp.int32, (CLASSES, span), 0)
    for part in range(tokens // span):
        columns = slice(part * span, (part + 1) * span)
        counted = counted_ref[0:1, columns]
        final = final_ref[columns, :]
        for quarter in range(VOCAB // D):
            logits = dot_nt(turned_ref[quarter * D : (quarter + 1) * D, :], final)
            for inside in range(D // CLASSES):
                group = quarter * (D // CLASSES) + inside
                values = logits[inside * CLASSES : (inside + 1) * CLASSES]
                shifted = values - jnp.max(values, axis=0, keepdims=True)
                exponent = jnp.exp2(shifted * log2_e)
                total = jnp.sum(exponent, axis=0, keepdims=True)
                hot = spots == targets_ref[group : group + 1, columns]
                chosen = jnp.sum(jnp.where(hot, shifted, 0.0), axis=0, keepdims=True)
                loss = loss + counted * (jnp.log(total) - chosen)
                chance = exponent * (1.0 / total)
                slope = (chance - jnp.where(hot, 1.0, 0.0)) * counted
                dlogits_ref[group * CLASSES : (group + 1) * CLASSES, columns] = slope.astype(
                    jnp.bfloat16
                )
    loss_ref[...] = jnp.sum(loss, axis=1, keepdims=True)
    sum_ref[:, 2 * FF : 2 * FF + VOCAB] = dot_nt(final_ref[...].T, dlogits_ref[...])
    dfinal = dot_nn(head_ref[...], dlogits_ref[...]).T
    last = last_ref[...]
    dlast, gain_part = rms_back(last, inverse_rms(last), gain_final, dfinal)
    gain_ref[1:2, :] = gain_part
    last_ref[...] = dlast
    gain_sum = jnp.zeros((1, D), jnp.float32)
    for block in range(tokens // ROWS):
        rows = slice(block * ROWS, (block + 1) * ROWS)
        upstream = last_ref[rows, :]
        dout = upstream.astype(jnp.bfloat16)
        dout_ref[rows, :] = dout
        for part in range(FF // D):
            columns = slice(part * D, (part + 1) * D)
            dact = dot_nn(dout, weight_two_ref[:, FF + part * D : FF + (part + 1) * D])
            dinner_ref[rows, columns] = (dact * slope_ref[rows, columns].astype(jnp.float32)).astype(jnp.bfloat16)
        dnormed = dot_nt(dinner_ref[rows, :], weight_two_ref[:, 0:FF])
        middle = middle_two_ref[rows, :]
        through, gain_part = rms_back(middle, inverse_rms(middle), gain_ffn, dnormed)
        gain_sum = gain_sum + gain_part
        dmiddle_ref[rows, :] = upstream + through
    gain_ref[0:1, :] = gain_sum
    sum_ref[:, 0:FF] = dot_nn(normed_ref[...].T, dinner_ref[...])
    sum_ref[:, FF : 2 * FF] = dot_nn(dout_ref[...].T, inner_ref[...])
    write_blocks(send_ref, keep_ref, sum_ref, core_ref[0], widths[4:], mesh_plan)
    gain_ref[2:4, :] = jnp.zeros((2, D), jnp.float32)

    def backward(group, carry):
        rows, short = rows_of(group), rows_of(group, SEG)

        def here(start, length, unit=CTX):
            return pl.ds(pl.multiple_of(group * (WIDE_GROUP * unit) + start, 16), length)

        dentry, gain_part = attend_back(
            group,
            here,
            (
                entry_ref[rows, :],
                qkv_ref.at[rows],
                mix_ref.at[short],
                chance_ref.at[pl.ds(group * WIDE_GROUP, WIDE_GROUP)],
            ),
            dmiddle_ref[short, :],
            gain_att,
            att_ref,
            masks,
            (normed_long, dattend_ref, dqkv_long, mixes_ref),
        )
        gain_ref[2:3, :] += gain_part
        dbefore, gain_part = feed_back(
            here,
            dentry,
            source_ref[rows, :],
            gain_before,
            weight_one_ref,
            slope_one_ref.at[rows],
            (normed_two_long, dinner_long, dout_long),
        )
        out_ref[rows, :] = dbefore
        gain_ref[3:4, :] += gain_part
        return carry

    lax.fori_loop(0, groups, backward, 0)
    column = 0
    for left, right in [
        (normed_two_long, dinner_long),
        (dout_long, inner_one_ref),
        (normed_long, dqkv_long),
        (mixes_ref, dattend_ref),
    ]:
        wide = right.shape[1]
        sum_ref[:, column : column + wide] = dot_nn(left[...].T, right[...])
        column += wide
    write_blocks(
        send_ref, keep_ref, sum_ref, core_ref[0], widths[:4], mesh_plan, sum(widths[4:])
    )


def block_outs(own, widths):
    shape = jax.ShapeDtypeStruct
    blocks = own.shape[:2] + (sum(widths),)
    return [shape(blocks, jnp.bfloat16)] * 2


def run_middle(widths, mesh_plan, source, own, other, targets, gains, valid, horizon, core):
    tokens = source.shape[0]
    short = tokens // CTX * SEG
    samples = tokens // CTX
    chances = HEADS // 2 * SEG
    f32, b16 = jnp.float32, jnp.bfloat16
    shape = jax.ShapeDtypeStruct
    vmem = pl.BlockSpec(memory_space=pltpu.VMEM)
    return pl.pallas_call(
        functools.partial(middle_kernel, widths, mesh_plan),
        in_specs=[vmem] * 5 + [smem_spec()] * 3,
        out_specs=[vmem] * 6,
        out_shape=[pltpu.HBM((tokens, D), f32)]
        + block_outs(own, widths)
        + [pltpu.HBM((4, D), f32), shape((1, 1), f32), shape((1, 1), f32)],
        scratch_shapes=[
            pltpu.VMEM((2, CTX, chances), f32),
            pltpu.VMEM((D, 2 * FF), b16),
            pltpu.VMEM((D, 4 * D), b16),
            pltpu.VMEM((D, 2 * FF), b16),
            pltpu.VMEM((D, VOCAB), b16),
            pltpu.VMEM((VOCAB, D), b16),
            pltpu.VMEM((tokens, D), f32),
            pltpu.VMEM((tokens, 3 * D), b16),
            pltpu.VMEM((short, D), b16),
            pltpu.VMEM((samples, 2, CTX, chances), b16),
            pltpu.VMEM((short, D), f32),
            pltpu.VMEM((tokens, FF), b16),
            pltpu.VMEM((tokens, FF), b16),
            pltpu.VMEM((short, FF), b16),
            pltpu.VMEM((short, FF), b16),
            pltpu.VMEM((short, D), f32),
            pltpu.VMEM((short, D), f32),
            pltpu.VMEM((D, 2 * FF + max(4 * D, VOCAB)), f32),
            pltpu.VMEM((CATS, short), jnp.int32),
            pltpu.VMEM((1, short), f32),
            pltpu.VMEM((tokens, D), b16),
            pltpu.VMEM((short, D), b16),
            pltpu.VMEM((tokens, 3 * D), b16),
            pltpu.VMEM((short, D), b16),
            pltpu.VMEM((tokens, D), b16),
            pltpu.VMEM((tokens, FF), b16),
            pltpu.VMEM((tokens, D), b16),
        ],
        compiler_params=pltpu.CompilerParams(vmem_limit_bytes=MIDDLE_BYTES + (0 if own.shape[1] >= 64 else VMEM_BYTES // 2)),
        cost_estimate=pl.CostEstimate(
            flops=6 * tokens * D * 8 * FF,
            bytes_accessed=tokens * D * 8 + D * 6 * FF * 10,
            transcendentals=2 * tokens * (FF + VOCAB),
        ),
        name="middle_part",
    )(source, own, other, targets, gains, valid, horizon, core)


def backward_kernel(layer, widths, mesh_plan, *refs):
    entry_ref, qkv_ref, mix_ref, chance_ref, dmiddle_ref, att_ref, gains_ref, core_ref = refs[:8]
    if layer == 0:
        latent_ref, send_ref, keep_ref, gain_ref = refs[8:12]
        att_kept, before_kept, sum_ref = refs[12:16], refs[16:18], refs[18]
    else:
        before_ref, ffn_ref, slope_ref, inner_hbm, out_ref, send_ref, keep_ref, gain_ref = refs[8:16]
        att_kept, before_kept, sum_ref = refs[16:20], refs[20:23], refs[23]
        inner_ref, inner_sem = refs[24:26]
        copy = pltpu.make_async_copy(inner_hbm, inner_ref, inner_sem)
    step = pl.program_id(0)

    def here(start, length, unit=CTX):
        base = step * (GROUP * unit)
        return pl.ds(pl.multiple_of(base + start, 16), length)

    @pl.when(step == 0)
    def _():
        gain_ref[...] = jnp.zeros_like(gain_ref)
        if layer > 0:
            copy.start()

    dentry, gain_part = attend_back(
        step,
        here,
        (entry_ref[...], qkv_ref, mix_ref, chance_ref),
        dmiddle_ref[...],
        gains_ref[layer : layer + 1, :],
        att_ref,
        head_masks(),
        att_kept,
    )
    gain_ref[0:1, :] += gain_part
    if layer == 0:
        before_kept[0][here(0, ROWS), :] = dentry.astype(jnp.bfloat16)
        one_hot_rows(latent_ref, before_kept[1], pl.multiple_of(step * ROWS, ROWS))
    else:
        dbefore, gain_part = feed_back(
            here,
            dentry,
            before_ref[...],
            gains_ref[LAYERS + layer - 1 : LAYERS + layer, :],
            ffn_ref,
            slope_ref,
            before_kept,
        )
        out_ref[...] = dbefore
        gain_ref[1:2, :] += gain_part

    @pl.when(step == pl.num_programs(0) - 1)
    def _():
        normed_ref, dattend_ref, dqkv_ref, mixes_ref = att_kept
        att = [(normed_ref, dqkv_ref), (mixes_ref, dattend_ref)]
        if layer == 0:
            pairs = att + [(before_kept[0], before_kept[1])]
        else:
            copy.wait()
            normed_two_ref, dinner_ref, dout_ref = before_kept
            pairs = [(normed_two_ref, dinner_ref), (dout_ref, inner_ref)] + att
        column = 0
        for left, right in pairs:
            wide = right.shape[1]
            sum_ref[:, column : column + wide] = dot_nn(left[...].T, right[...])
            column += wide
        write_blocks(send_ref, keep_ref, sum_ref, core_ref[0], widths, mesh_plan)


def run_backward(layer, widths, mesh_plan, blocks_like, saved, dmiddle, gains, core, before):
    entry, _, qkv, mix, chance, weights = [in_hbm(item) for item in saved[:6]]
    dmiddle = in_hbm(dmiddle)
    if layer > 0:
        before = [in_hbm(item) for item in before]
    tokens = entry.shape[0]
    queries = chance.shape[3] // (HEADS // 2)
    short = tokens // CTX * queries
    f32, b16 = jnp.float32, jnp.bfloat16
    shape = jax.ShapeDtypeStruct
    in_specs = [
        row_spec(D),
        row_spec(3 * D),
        row_spec(D, GROUP, queries),
        chance_spec(queries),
        row_spec(D, GROUP, queries),
        whole_spec(weights.shape),
        whole_spec(gains.shape),
        smem_spec(),
    ]
    operands = [entry, qkv, mix, chance, dmiddle, weights, gains, core]
    blocks = block_outs(blocks_like, widths)
    outs = [(item, whole_spec(item.shape)) for item in blocks]
    outs.append((pltpu.HBM((2, D), f32), whole_spec((2, D))))
    scratch = [
        pltpu.VMEM((tokens, D), b16),
        pltpu.VMEM((short, D), b16),
        pltpu.VMEM((tokens, 3 * D), b16),
        pltpu.VMEM((short, D), b16),
    ]
    if layer == 0:
        in_specs.append(latent_spec())
        operands.append(before)
        scratch = scratch + [pltpu.VMEM((tokens, D), b16), pltpu.VMEM((tokens, VOCAB), b16)]
        wide = 4 * D + VOCAB
    else:
        in_specs = in_specs + [row_spec(D), whole_spec(before[1].shape), row_spec(FF)]
        in_specs.append(pl.BlockSpec(memory_space=pl.ANY))
        operands = operands + list(before)
        outs.insert(0, (pltpu.HBM((tokens, D), f32), row_spec(D)))
        scratch = scratch + [
            pltpu.VMEM((tokens, D), b16),
            pltpu.VMEM((tokens, FF), b16),
            pltpu.VMEM((tokens, D), b16),
        ]
        wide = 4 * D + 2 * FF
    scratch.append(pltpu.VMEM((D, wide), f32))
    if layer > 0:
        scratch = scratch + [pltpu.VMEM((tokens, FF), b16), pltpu.SemaphoreType.DMA]
    return pl.pallas_call(
        functools.partial(backward_kernel, layer, widths, mesh_plan),
        grid=(tokens // ROWS,),
        in_specs=in_specs,
        out_specs=[spec for _, spec in outs],
        out_shape=[item for item, _ in outs],
        scratch_shapes=scratch,
        compiler_params=pltpu.CompilerParams(vmem_limit_bytes=VMEM_BYTES * 3 // 2),
        cost_estimate=pl.CostEstimate(
            flops=6 * tokens * D * wide,
            bytes_accessed=tokens * D * 24 + D * wide * 6,
            transcendentals=tokens * FF,
        ),
        name="backward_part",
    )(*operands)


def pack_kernel(*refs):
    qkv_ref, out_ref, up_ref, down_ref, embed_ref, head_ref = refs[:6]
    low = lambda value: value.astype(jnp.bfloat16)
    att = [[low(qkv_ref[at]), low(out_ref[at].T)] for at in range(LAYERS)]
    ffn = [[low(up_ref[at]), low(down_ref[at])] for at in range(LAYERS)]
    pieces = [
        att[0] + [low(embed_ref[...])],
        ffn[0] + att[1],
        ffn[1] + att[2] + ffn[2] + [low(head_ref[...])],
    ]
    for target, piece in zip(refs[6:], pieces):
        target[...] = jnp.concatenate(piece, axis=1)


def run_pack(masters, chunk_widths):
    vmem = pl.BlockSpec(memory_space=pltpu.VMEM)
    rows = masters[0].shape[1]
    return pl.pallas_call(
        pack_kernel,
        in_specs=[vmem] * 6,
        out_specs=[vmem] * 3,
        out_shape=[
            jax.ShapeDtypeStruct((rows, sum(widths)), jnp.bfloat16) for widths in chunk_widths
        ],
        name="pack",
    )(*masters)


def matrix_plan(widths):
    order = [
        (2, 2), (3, 2), (5, 0), (2, 1), (3, 1), (0, 2), (1, 2),
        (2, 0), (3, 0), (0, 1), (1, 1), (0, 0), (1, 0), (4, 0),
    ]
    plan, column = {}, 0
    for which, layer in order:
        plan[(which, layer)] = (column, widths[which])
        column += widths[which]
    return plan, column


def matrix_list():
    return [(which, layer) for which in range(4) for layer in range(LAYERS)] + [(4, 0), (5, 0)]


MATRICES = 4 * LAYERS + 2
LANES = 128
INNER_ROWS = 16
COMMON_ROWS = 16
ROW_IS_INNER = [True, True, True, False, False, True]


def master_of(masters, which, layer):
    if which == 1:
        return masters[1][layer].T
    return masters[which][layer] if which < 4 else masters[which][...]


def old_row(refs, which, layer):
    return refs[which][layer : layer + 1, :] if which < 4 else refs[which][...]


LATE = [(0, 0), (1, 0), (4, 0)]
EDGE = INNER_ROWS + COMMON_ROWS


def whole_sum(value):
    return jnp.sum(jnp.sum(value, axis=1, keepdims=True), axis=0, keepdims=True)


def square_sums(raw, chosen, plan, first):
    square = raw * raw
    rows = square.shape[0]
    inner, entries = [], []
    for item in matrix_list():
        if item in chosen:
            column, width = plan[item]
            part = square[:, column - first : column - first + width]
            inner.append(jnp.sum(part, axis=1, keepdims=True))
        else:
            inner.append(jnp.zeros((rows, 1), jnp.float32))
        entries.append(jnp.sum(inner[-1], axis=0, keepdims=True))
    inner.append(jnp.zeros((rows, LANES - MATRICES), jnp.float32))
    return jnp.concatenate(inner, axis=1).T, entries, jnp.sum(square, axis=0, keepdims=True)


def store_row(target_ref, row, values):
    total = values.shape[1]
    for at, start in enumerate(range(0, total, LANES)):
        stop = min(start + LANES, total)
        target_ref[row + at : row + at + 1, 0 : stop - start] = values[:, start:stop]


def load_row(source_ref, row, total):
    return jnp.concatenate(
        [
            source_ref[row + at : row + at + 1, 0 : min(LANES, total - start)]
            for at, start in enumerate(range(0, total, LANES))
        ],
        axis=1,
    )


def late_row(widths):
    _, total = matrix_plan(widths)
    late = sum(widths[which] for which, _ in LATE)
    return EDGE + -(-(total - late) // LANES)


def packet_rows(widths):
    late = sum(widths[which] for which, _ in LATE)
    return -(-(late_row(widths) + -(-late // LANES)) // 8) * 8


def first_kernel(*refs):
    masters, row_refs, row_ref = refs[0:6], refs[6:12], refs[12]
    weights, row_sums = [], []
    for which, layer in matrix_list():
        master = masters[which][layer] if which < 4 else masters[which][...]
        weights.append(whole_sum(master * master))
        row_sums.append(whole_sum(old_row(row_refs, which, layer)))
    nothing = lambda count: [jnp.zeros((1, count), jnp.float32)]
    pieces = nothing(2) + weights + nothing(MATRICES) + row_sums
    row_ref[...] = jnp.concatenate(pieces + nothing(LANES - 2 - 3 * MATRICES), axis=1)


def run_first(masters, rows):
    vmem = pl.BlockSpec(memory_space=pltpu.VMEM)
    return pl.pallas_call(
        first_kernel,
        in_specs=[vmem] * 12,
        out_specs=vmem,
        out_shape=jax.ShapeDtypeStruct((1, LANES), jnp.float32),
        name="first_statistics",
    )(*masters, *rows)


def early_kernel(widths, *refs):
    raw_ref, row_ref, gains_at, loss_ref, count_ref, packet_ref = (
        refs[0],
        refs[1],
        refs[2:4],
        refs[4],
        refs[5],
        refs[6],
    )
    plan, _ = matrix_plan(widths)
    chosen = [item for item in matrix_list() if item not in LATE]
    inner, entries, outer = square_sums(raw_ref[...], chosen, plan, 0)
    packet_ref[...] = jnp.zeros_like(packet_ref)
    packet_ref[0:INNER_ROWS, 0 : inner.shape[1]] = inner[0:INNER_ROWS, :]
    last, one = [ref[...] for ref in gains_at]
    gain = jnp.concatenate(
        [jnp.zeros((1, D), jnp.float32), one[0:1], last[2:3], one[1:2], last[3:4], last[0:2]],
        axis=0,
    )
    nothing = lambda count: [jnp.zeros((1, count), jnp.float32)]
    scalars = [loss_ref[...], count_ref[...]] + nothing(MATRICES) + entries
    scalars = scalars + nothing(LANES - 2 - 2 * MATRICES)
    at = INNER_ROWS
    packet_ref[at : at + 7, :] = gain[:, 0:LANES]
    packet_ref[at + 7 : at + 8, :] = row_ref[...] + jnp.concatenate(scalars, axis=1)
    packet_ref[at + 8 : at + 15, :] = gain[:, LANES:]
    store_row(packet_ref, EDGE, outer)


def late_kernel(widths, early_ref, raw_ref, gain_ref, packet_ref):
    plan, total = matrix_plan(widths)
    inner, entries, outer = square_sums(raw_ref[...], LATE, plan, total - raw_ref.shape[1])
    packet_ref[...] = early_ref[...]
    packet_ref[0:INNER_ROWS, 0 : inner.shape[1]] += inner[0:INNER_ROWS, :]
    at = INNER_ROWS
    packet_ref[at : at + 1, :] = gain_ref[0:1, 0:LANES]
    packet_ref[at + 8 : at + 9, :] = gain_ref[0:1, LANES:]
    before = jnp.zeros((1, 2 + MATRICES), jnp.float32)
    behind = jnp.zeros((1, LANES - 2 - 2 * MATRICES), jnp.float32)
    packet_ref[at + 7 : at + 8, :] += jnp.concatenate([before] + entries + [behind], axis=1)
    store_row(packet_ref, late_row(widths), outer)


def run_early(widths, raw, row, gain_parts, loss, count):
    vmem = pl.BlockSpec(memory_space=pltpu.VMEM)
    operands = [raw, row] + gain_parts + [loss, count]
    return pl.pallas_call(
        functools.partial(early_kernel, widths),
        in_specs=[vmem] * len(operands),
        out_specs=vmem,
        out_shape=jax.ShapeDtypeStruct((packet_rows(widths), LANES), jnp.float32),
        name="early_statistics",
    )(*operands)


def run_late(widths, packet, raw, gain_part):
    vmem = pl.BlockSpec(memory_space=pltpu.VMEM)
    return pl.pallas_call(
        functools.partial(late_kernel, widths),
        in_specs=[vmem] * 3,
        out_specs=vmem,
        out_shape=jax.ShapeDtypeStruct(packet.shape, jnp.float32),
        name="late_statistics",
    )(packet, raw, gain_part)


def update_kernel(widths, sizes, *refs):
    packet_ref, raw_early, raw_late = refs[:3]
    masters, inner_refs, outer_refs = refs[3:9], refs[9:15], refs[15:21]
    gains_ref, second_ref = refs[21:23]
    outs = refs[23:]
    outer_count, inner_count = sizes
    plan, total = matrix_plan(widths)
    rows = raw_early.shape[0]
    at = INNER_ROWS
    scalars = packet_ref[at + 7 : at + 8, :]
    pick = lambda at: scalars[:, at : at + 1]
    gain_sum = jnp.concatenate(
        [packet_ref[at : at + 7, :], packet_ref[at + 8 : at + 15, :]], axis=1
    )
    gain_square = jnp.sum(jnp.sum(gain_sum * gain_sum, axis=1, keepdims=True), axis=0, keepdims=True)
    square_total = gain_square
    for at in range(MATRICES):
        square_total = square_total + pick(2 + MATRICES + at)
    count_total = pick(1)
    norm_value = jnp.sqrt(square_total) / count_total
    scaling = jnp.minimum(1.0, clip_limit / norm_value) / count_total
    square_scale = scaling * scaling
    early = raw_early.shape[1]
    outer_early = load_row(packet_ref, EDGE, early)
    outer_late = load_row(packet_ref, late_row(widths), total - early)
    inner_new = []
    for at, (which, layer) in enumerate(matrix_list()):
        outer_length = widths[which] * outer_count
        inner_new.append(
            decay_two * old_row(inner_refs, which, layer)
            + (1 - decay_two)
            * (square_scale * packet_ref[at : at + 1, 0:rows] / outer_length + tiny_term)
        )
    stacked = jnp.concatenate(inner_new, axis=0)
    stacked = jnp.concatenate([stacked, jnp.ones((LANES - MATRICES, rows), jnp.float32)], axis=0)
    if rows < LANES:
        stacked = jnp.concatenate([stacked, jnp.ones((LANES, LANES - rows), jnp.float32)], axis=1)
    turned = lax.rsqrt(stacked).T
    outs[0][...] = pick(0)
    outs[1][...] = count_total
    outs[2][...] = norm_value
    first_out = {4: 3, 0: 7, 1: 11, 2: 15, 3: 19, 5: 23}
    for at, (which, layer) in enumerate(matrix_list()):
        column, width = plan[(which, layer)]
        outer_length, inner_length = width * outer_count, rows * inner_count
        row_length = inner_length if ROW_IS_INNER[which] else outer_length
        copies = outer_count if ROW_IS_INNER[which] else inner_count
        entries = outer_length * inner_length
        if column < early:
            raw = raw_early[:, column : column + width]
            outer_total = outer_early[:, column : column + width]
        else:
            raw = raw_late[:, column - early : column - early + width]
            outer_total = outer_late[:, column - early : column - early + width]
        outer_new = decay_two * old_row(outer_refs, which, layer) + (1 - decay_two) * (
            square_scale * outer_total / inner_length + tiny_term
        )
        mean_rows = decay_two * (pick(2 + 2 * MATRICES + at) / (copies * row_length)) + (
            1 - decay_two
        ) * (square_scale * pick(2 + MATRICES + at) / entries + tiny_term)
        factor = step_rate * jnp.sqrt(pick(2 + at) / entries) * jnp.sqrt(mean_rows)
        grad = raw * scaling
        updated = master_of(masters, which, layer) - grad * (
            turned[0:rows, at : at + 1] * (factor * lax.rsqrt(outer_new))
        )
        first = first_out[which]
        row_new, column_new = (
            (inner_new[at], outer_new) if ROW_IS_INNER[which] else (outer_new, inner_new[at])
        )
        if which < 4:
            if which == 1:
                updated, grad = updated.T, grad.T
            outs[first][layer] = updated
            outs[first + 1][layer] = grad
            outs[first + 2][layer : layer + 1, :] = row_new
            outs[first + 3][layer : layer + 1, :] = column_new
        else:
            outs[first][...] = updated
            outs[first + 1][...] = grad
            outs[first + 2][...] = row_new
            outs[first + 3][...] = column_new
    gain_grad = gain_sum * scaling
    second_new = decay_two * second_ref[...] + (1 - decay_two) * (gain_grad * gain_grad + tiny_term)
    gains = gains_ref[...]
    spread = jnp.sqrt(jnp.mean(gains * gains, axis=-1, keepdims=True))
    outs[27][...] = gains - step_rate * spread * gain_grad * lax.rsqrt(second_new)
    outs[28][...] = gain_grad
    outs[29][...] = second_new


def run_update(widths, sizes, packet, raw_early, raw_late, masters, inner, outer, gains, second):
    vmem = pl.BlockSpec(memory_space=pltpu.VMEM)
    operands = [packet, raw_early, raw_late] + masters + inner + outer + [gains, second]
    shapes = [(1, 1)] * 3
    for which in [4, 0, 1, 2, 3, 5]:
        shapes = shapes + [masters[which].shape] * 2
        pair = [inner[which].shape, outer[which].shape]
        shapes = shapes + (pair if ROW_IS_INNER[which] else pair[::-1])
    shapes = shapes + [gains.shape] * 3
    return pl.pallas_call(
        functools.partial(update_kernel, widths, sizes),
        in_specs=[vmem] * len(operands),
        out_specs=[vmem] * len(shapes),
        out_shape=[jax.ShapeDtypeStruct(item, jnp.float32) for item in shapes],
        name="update",
    )(*operands)


def swap(value, mask):
    count = lax.axis_size("dp") * lax.axis_size("fsdp")
    return lax.ppermute(value, ("dp", "fsdp"), [(place, place ^ mask) for place in range(count)])


def device_index():
    return lax.axis_index("dp") * lax.axis_size("fsdp") + lax.axis_index("fsdp")


def step_masks(step):
    masks = []
    for digit in range(1, 1 << len(step)):
        masks.append(sum(1 << bit for at, bit in enumerate(step[::-1]) if (digit >> at) & 1))
    return masks


def tie(*values):
    return lax.optimization_barrier(values)


def behind(value, *ahead):
    return lax.optimization_barrier((value,) + ahead)[0]


class Gather:
    def __init__(self, piece, steps):
        self.held, self.steps, self.at = piece[None], steps, 0

    def send(self):
        self.others = tuple(swap(self.held, mask) for mask in step_masks(self.steps[self.at]))

    def join(self):
        step = self.steps[self.at]
        pieces = [self.held] + list(self.others)
        for at, bit in enumerate(step[::-1]):
            upper = (device_index() >> bit) & 1 == 1
            pieces = [
                jnp.where(upper, pieces[place ^ (1 << at)], pieces[place])
                for place in range(len(pieces))
            ]
        self.held = jnp.concatenate(pieces)
        self.at += 1


class Scatter:
    def __init__(self, sent, kept, steps):
        self.sent, self.kept, self.steps, self.at = (sent,), kept, steps, 0

    def send(self):
        masks = step_masks(self.steps[self.at])
        self.others = tuple(swap(sent, mask) for sent, mask in zip(self.sent, masks))

    def join(self):
        self.at += 1
        step = self.steps[self.at] if self.at < len(self.steps) else ()
        count = 1 << len(step)
        own = 0
        for bit in step:
            own = 2 * own + ((device_index() >> bit) & 1)
        shape = (count, self.kept.shape[0] // count) + self.kept.shape[1:]
        terms = [item.reshape(shape) for item in (self.kept,) + self.others]

        def pick(digit):
            total = None
            for term in terms:
                part = lax.dynamic_index_in_dim(term, own ^ digit, 0, keepdims=False)
                part = part.astype(jnp.float32)
                total = part if total is None else total + part
            return total

        self.sent = tuple(pick(digit).astype(jnp.bfloat16) for digit in range(1, count))
        self.kept = pick(0)


def sum_packets(packet, group, inner_bits):
    row = lax.broadcasted_iota(jnp.int32, packet.shape, 0)
    terms = [packet]
    for mask in step_masks(group):
        first = 0 if mask >> inner_bits << inner_bits == mask else INNER_ROWS
        stop = packet.shape[0] if mask >> inner_bits == 0 else EDGE
        terms.append(jnp.where((row >= first) & (row < stop), swap(packet, mask), 0.0))
    while len(terms) > 1:
        terms = [terms[at] + terms[at + 1] for at in range(0, len(terms), 2)]
    return terms[0]


def merged(parts):
    whole = Scatter(None, jnp.concatenate([part.kept for part in parts], axis=2), parts[0].steps)
    whole.sent = tuple(
        jnp.concatenate(pieces, axis=2) for pieces in zip(*[part.sent for part in parts])
    )
    whole.at = parts[0].at
    return whole


def shards(
    latents,
    targets,
    horizon,
    memory_valid,
    embed,
    qkv_weight,
    out_weight,
    up_weight,
    down_weight,
    head_weight,
    gains,
    embed_rows,
    embed_cols,
    qkv_rows,
    qkv_cols,
    out_rows,
    out_cols,
    up_rows,
    up_cols,
    down_rows,
    down_cols,
    head_rows,
    head_cols,
    gain_second,
):
    samples = latents.shape[0]
    sizes = (lax.axis_size("dp"), lax.axis_size("fsdp"))
    highest = (sizes[0] * sizes[1]).bit_length() - 1
    gather_steps = [(bit,) for bit in reversed(range(3, highest))] + [(2, 1), (0,)]
    scatter_steps = gather_steps[::-1]
    mesh_plan = (sizes[0], sizes[1], gather_steps)
    core = (lax.axis_index("fsdp") & 1).astype(jnp.int32).reshape(1)

    out_turned = jnp.swapaxes(out_weight, 1, 2)
    down_turned = jnp.swapaxes(down_weight, 1, 2)
    masters = [qkv_weight, out_turned, up_weight, down_turned, embed.T, head_weight]
    widths = [qkv_weight.shape[2], out_weight.shape[2], up_weight.shape[2], down_weight.shape[1]]
    widths = widths + [embed.shape[0], head_weight.shape[1]]
    att_widths, ffn_widths = widths[0:2], widths[2:4]
    chunk_widths = [
        att_widths + widths[4:5],
        ffn_widths + att_widths,
        ffn_widths + att_widths + ffn_widths + widths[5:6],
    ]
    chunks = [Gather(piece, gather_steps) for piece in run_pack(masters, chunk_widths)]
    first, second, third = chunks
    latent_rows = latents.transpose(0, 2, 1)
    target_rows = targets.transpose(0, 2, 1)
    shared = (gains, memory_valid, core)
    back_shared = (gains, core)

    count = len(gather_steps)
    flat = lambda item: item if item.ndim == 2 else item.reshape(1, -1)
    inner = [flat(item) for item in (qkv_rows, out_rows, up_rows, down_cols, embed_cols, head_rows)]
    outer = [flat(item) for item in (qkv_cols, out_cols, up_cols, down_rows, embed_rows, head_cols)]
    row_stats = [inner[at] if ROW_IS_INNER[at] else outer[at] for at in range(6)]
    first_row = run_first(masters, row_stats)
    for at in range(count - 1):
        for chunk in chunks:
            chunk.send()
        if at == 0:
            first.others, first_row = tie(first.others, first_row)
        for chunk in chunks[: 2 if at == count - 2 else 3]:
            chunk.join()
            if at == count - 3 and chunk is first:
                first.held, third.held = tie(first.held, third.held)
    first.send()
    (other,) = first.others
    held, other, second.held = tie(first.held, other, second.held)
    second.send()
    kept = [run_forward(0, chunk_widths[0], mesh_plan, latent_rows, held, other, *shared)]
    middle, (other,) = tie(kept[0][1], second.others)
    kept.append(
        run_forward(1, chunk_widths[1], mesh_plan, middle, second.held, other, *shared)
    )
    middle, third.others = tie(kept[1][1], third.others)
    third.join()
    third.send()
    (other,) = third.others
    dmiddle, sent, held, gain_middle, loss, counted = run_middle(
        chunk_widths[2],
        mesh_plan,
        middle,
        third.held,
        other,
        target_rows,
        gains,
        memory_valid,
        horizon,
        core,
    )
    pair = Scatter(sent, held, scatter_steps)
    pair.send()
    pair.join()
    like = first.held
    before = (kept[0][1], kept[1][6], kept[1][8], kept[1][7])
    dmiddle, pair.sent = tie(dmiddle, pair.sent)
    pair.send()
    dmiddle, sent, held, gain_one = run_backward(
        1, chunk_widths[1], mesh_plan, like, kept[1], dmiddle, *back_shared, before
    )
    dmiddle, sent, held, pair.others = tie(dmiddle, sent, held, pair.others)
    one = Scatter(sent, held, scatter_steps)
    one.send()
    pair.join()
    one.join()
    dmiddle, pair.sent, one.sent = tie(dmiddle, pair.sent, one.sent)
    one.send()
    pair.send()
    sent, held, gain_zero = run_backward(
        0, chunk_widths[0], mesh_plan, like, kept[0], dmiddle, *back_shared, latent_rows
    )
    sent, held, pair.others, one.others = tie(sent, held, pair.others, one.others)
    zero = Scatter(sent, held, scatter_steps)
    zero.send()
    one.join()
    one.send()
    pair.join()
    zero.join()
    one.others = behind(one.others, zero.sent)
    zero.send()
    one.join()
    early = merged([pair, one])
    while early.at < count:
        early.send()
        if early.at == count - 1:
            zero.join()
            zero.send()
        zero.others, early.others = tie(zero.others, early.others)
        early.join()
    raw_early = early.kept[0]

    packet = run_early(
        widths, raw_early, first_row, [gain_middle, gain_one], loss, counted
    )
    while zero.at < count:
        zero.join()
        if zero.at < count:
            zero.send()
    raw_late = zero.kept[0]
    packet = run_late(widths, packet, raw_late, gain_zero)
    inner_bits = sizes[1].bit_length() - 1
    rest = list(range(3, highest))
    groups = [(0,), (2, 1)] + [tuple(rest[at : at + 2][::-1]) for at in range(0, len(rest), 2)]
    for group in groups:
        packet = sum_packets(packet, group, inner_bits)
    results = run_update(
        widths, sizes, packet, raw_early, raw_late, masters, inner, outer, gains, gain_second
    )
    results = list(results)
    for at in range(3):
        results[at] = results[at].reshape(())
    for at in (3, 4, 11, 12, 19, 20):
        results[at] = jnp.swapaxes(results[at], -1, -2)
    for at in (5, 6, 25, 26):
        results[at] = results[at].reshape(-1)
    return tuple(results)


def solution(mesh):
    return jax.shard_map(
        shards,
        mesh=mesh,
        in_specs=(
            P(("dp", "fsdp"), None, None),
            P(("dp", "fsdp"), None, None),
            P(("dp", "fsdp")),
            P(("dp", "fsdp")),
            P("dp", "fsdp"),
            P(None, "fsdp", "dp"),
            P(None, "fsdp", "dp"),
            P(None, "fsdp", "dp"),
            P(None, "dp", "fsdp"),
            P("fsdp", "dp"),
            P(),
            P("dp"),
            P("fsdp"),
            P(None, "fsdp"),
            P(None, "dp"),
            P(None, "fsdp"),
            P(None, "dp"),
            P(None, "fsdp"),
            P(None, "dp"),
            P(None, "dp"),
            P(None, "fsdp"),
            P("fsdp"),
            P("dp"),
            P(),
        ),
        out_specs=(
            P(),
            P(),
            P(),
            P("dp", "fsdp"),
            P("dp", "fsdp"),
            P("dp"),
            P("fsdp"),
            P(None, "fsdp", "dp"),
            P(None, "fsdp", "dp"),
            P(None, "fsdp"),
            P(None, "dp"),
            P(None, "fsdp", "dp"),
            P(None, "fsdp", "dp"),
            P(None, "fsdp"),
            P(None, "dp"),
            P(None, "fsdp", "dp"),
            P(None, "fsdp", "dp"),
            P(None, "fsdp"),
            P(None, "dp"),
            P(None, "dp", "fsdp"),
            P(None, "dp", "fsdp"),
            P(None, "dp"),
            P(None, "fsdp"),
            P("fsdp", "dp"),
            P("fsdp", "dp"),
            P("fsdp"),
            P("dp"),
            P(),
            P(),
            P(),
        ),
        check_vma=False,
    )
```

```python
import functools

import jax
import jax.numpy as jnp
from jax import lax
from jax.experimental import pallas as pl
from jax.experimental.pallas import tpu as pltpu
from jax.sharding import PartitionSpec as P

D = 256
HEADS = 8
HEAD = D // HEADS
FF = 1024
CATS = 32
CLASSES = 32
LAYERS = 3
SEG = 48
MEM = 48
CTX = 96
VOCAB = 1024
GROUP = 4
WIDE_GROUP = 8
ROWS = GROUP * CTX
HALF = D // 2
VMEM_BYTES = 24 * 1024 * 1024
MIDDLE_BYTES = 43 * 1024 * 1024

decay_two = 0.9
step_rate = 0.3
clip_limit = 0.05
tiny_term = 1e-30
norm_eps = 1e-06
masked_score = -1e30
log2_e = 1.4426950408889634
score_scale = HEAD ** (-0.5)
gelu_one = 0.7978845608028654
gelu_two = 0.044715


def dot_nn(left, right):
    return lax.dot_general(
        left, right, (((1,), (0,)), ((), ())), preferred_element_type=jnp.float32
    )


def dot_nt(left, right):
    return lax.dot_general(
        left, right, (((1,), (1,)), ((), ())), preferred_element_type=jnp.float32
    )


def dot_tn(left, right):
    return lax.dot_general(
        left, right, (((0,), (0,)), ((), ())), preferred_element_type=jnp.float32
    )


def inverse_rms(values):
    return lax.rsqrt(jnp.mean(values * values, axis=-1, keepdims=True) + norm_eps)


def rms_back(values, inverse, gain_row, upstream):
    normed = values * inverse
    scaled = upstream * gain_row
    inner = jnp.mean(scaled * normed, axis=-1, keepdims=True)
    return (
        inverse * (scaled - normed * inner),
        jnp.sum(upstream * normed, axis=0, keepdims=True),
    )


def head_masks():
    lane = lax.broadcasted_iota(jnp.int32, (1, D // 2), 1) // HEAD
    return [lane == head for head in range(HEADS // 2)]


def expand_heads(rows, masks):
    return jnp.concatenate([rows * mask.astype(rows.dtype) for mask in masks], axis=0)


def collapse_heads(spread, rows, masks):
    product = dot_tn(spread, rows)
    queries = product.shape[0] // len(masks)
    taken = product[(len(masks) - 1) * queries :]
    for at, mask in enumerate(masks[:-1]):
        taken = jnp.where(mask, product[at * queries : (at + 1) * queries], taken)
    return taken


def half_of(part, side):
    start = part * D + side * HALF
    return slice(start, start + HALF)


def fill_bias(bias_ref):
    spread = bias_ref.shape[2]
    queries = spread // (HEADS // 2)
    key_at = lax.broadcasted_iota(jnp.int32, (CTX, spread), 0)
    query_at = lax.broadcasted_iota(jnp.int32, (CTX, spread), 1) % queries + (CTX - queries)
    later = key_at > query_at
    crosses = (query_at >= MEM) & (key_at < MEM)
    bias_ref[0] = jnp.where(later | crosses, masked_score, 0.0)
    bias_ref[1] = jnp.where(later, masked_score, 0.0)


def block_place(device, steps):
    place, weight = 0, 1
    for step in steps[:-1]:
        digit = 0
        for bit in step:
            digit = 2 * digit + ((device >> bit) & 1)
        place += digit * weight
        weight <<= len(step)
    return place


def place_weights(targets, own_ref, other_ref, core, widths, mesh_plan, start=0):
    outer_count, inner_count, steps = mesh_plan
    rows = own_ref.shape[1]
    for high in range(inner_count // 2):
        for source, side in ((own_ref, core), (other_ref, 1 - core)):
            here = pl.ds(pl.multiple_of((2 * high + side) * rows, rows), rows)
            at = start
            for (target, column), width in zip(targets, widths):
                block = [
                    source[
                        block_place(outer * inner_count + 2 * high, steps), :, at : at + width
                    ]
                    for outer in range(outer_count)
                ]
                target[here, column : column + width * outer_count] = jnp.concatenate(
                    block, axis=1
                )
                at += width


def write_blocks(send_ref, keep_ref, sum_ref, core, widths, mesh_plan, start=0):
    outer_count, inner_count, steps = mesh_plan
    rows = keep_ref.shape[1]
    for high in range(inner_count // 2):
        for target, side in ((keep_ref, core), (send_ref, 1 - core)):
            here = pl.ds(pl.multiple_of((2 * high + side) * rows, rows), rows)
            taken = sum_ref[here, :]
            for outer in range(outer_count):
                block, column = [], 0
                for width in widths:
                    block.append(taken[:, column + outer * width : column + (outer + 1) * width])
                    column += width * outer_count
                place = block_place(outer * inner_count + 2 * high, steps)
                target[place, :, start : start + sum(widths)] = jnp.concatenate(
                    block, axis=1
                ).astype(target.dtype)


def one_hot_rows(latent_ref, hot_ref, first):
    spot = lax.broadcasted_iota(jnp.int32, (CATS, VOCAB), 1) // CLASSES
    group = lax.broadcasted_iota(jnp.int32, (CATS, VOCAB), 0)
    spreader = jnp.where(spot == group, 1.0, 0.0).astype(jnp.bfloat16)
    classes = (lax.broadcasted_iota(jnp.int32, (1, VOCAB), 1) % CLASSES).astype(jnp.float32)
    for sample in range(latent_ref.shape[0]):
        drawn = dot_tn(latent_ref[sample].astype(jnp.float32).astype(jnp.bfloat16), spreader)
        hot_ref[pl.ds(first + sample * CTX, CTX), :] = jnp.where(
            drawn == classes, 1.0, 0.0
        ).astype(jnp.bfloat16)


def tail_rows(values, queries):
    if queries == CTX:
        return values
    return jnp.concatenate(
        [
            values[(sample + 1) * CTX - queries : (sample + 1) * CTX]
            for sample in range(values.shape[0] // CTX)
        ],
        axis=0,
    )


def attend_forward(step, hidden, gain_row, weight_ref, valid_ref, bias_ref, masks, refs):
    middle_ref, qkv_ref, mix_ref, chance_ref = refs
    queries = chance_ref.shape[3] // (HEADS // 2)
    group = hidden.shape[0] // CTX
    normed = (hidden * inverse_rms(hidden) * gain_row).astype(jnp.bfloat16)
    qkv_ref[...] = dot_nn(normed, weight_ref[:, 0 : 3 * D]).astype(jnp.bfloat16)
    units = [(sample, side) for sample in range(group) for side in range(2)]
    scores = []
    for sample, side in units:
        rows = slice(sample * CTX, (sample + 1) * CTX)
        tail = slice((sample + 1) * CTX - queries, (sample + 1) * CTX)
        spread = expand_heads(qkv_ref[tail, half_of(0, side)], masks)
        scores.append(dot_nt(qkv_ref[rows, half_of(1, side)], spread))
    for (sample, side), score in zip(units, scores):
        score = score + bias_ref[valid_ref[step * group + sample]]
        peak = jnp.max(score, axis=0, keepdims=True)
        exponent = jnp.exp2((score - peak) * (score_scale * log2_e))
        total = jnp.sum(exponent, axis=0, keepdims=True)
        chance_ref[sample, side] = (exponent * (1.0 / total)).astype(jnp.bfloat16)
    for sample, side in units:
        rows = slice(sample * CTX, (sample + 1) * CTX)
        mix_ref[sample * queries : (sample + 1) * queries, half_of(0, side)] = collapse_heads(
            chance_ref[sample, side], qkv_ref[rows, half_of(2, side)], masks
        ).astype(jnp.bfloat16)
    middle_ref[...] = tail_rows(hidden, queries) + dot_nn(
        mix_ref[...], weight_ref[:, 3 * D : 4 * D]
    )


def gelu_parts(value):
    square = value * value
    share = 0.5 + 0.5 * jnp.tanh(value * (gelu_one + (gelu_one * gelu_two) * square))
    active = value * share
    bent = active * (1.0 - share)
    return active, share + bent * (2.0 * gelu_one + (6.0 * gelu_one * gelu_two) * square)


def feed_forward(middle, gain_row, weight_ref, inner_ref, slope_ref):
    normed = (middle * inverse_rms(middle) * gain_row).astype(jnp.bfloat16)
    for part in range(FF // D):
        columns = slice(part * D, (part + 1) * D)
        inner = dot_nn(normed, weight_ref[:, columns])
        for sample in range(middle.shape[0] // CTX):
            rows = slice(sample * CTX, (sample + 1) * CTX)
            active, slope = gelu_parts(inner[rows])
            inner_ref[rows, columns] = active.astype(jnp.bfloat16)
            slope_ref[rows, columns] = slope.astype(jnp.bfloat16)
    return middle + dot_nt(inner_ref[...], weight_ref[:, FF : 2 * FF])


def feed_back(here, upstream, middle, gain_row, weight_ref, slope_ref, refs):
    normed_ref, dinner_ref, dout_ref = refs
    dout = upstream.astype(jnp.bfloat16)
    dout_ref[here(0, middle.shape[0]), :] = dout
    inverse = inverse_rms(middle)
    normed_ref[here(0, middle.shape[0]), :] = (middle * inverse * gain_row).astype(jnp.bfloat16)
    for part in range(FF // D):
        columns = slice(part * D, (part + 1) * D)
        dact = dot_nn(dout, weight_ref[:, FF + part * D : FF + (part + 1) * D])
        dinner_ref[here(0, middle.shape[0]), columns] = (
            dact * slope_ref[:, columns].astype(jnp.float32)
        ).astype(jnp.bfloat16)
    dnormed = dot_nt(dinner_ref[here(0, middle.shape[0]), :], weight_ref[:, 0:FF])
    through, gain_part = rms_back(middle, inverse, gain_row, dnormed)
    return upstream + through, gain_part


def attend_back(step, here, saved, dmiddle, gain_row, weight_ref, masks, refs):
    hidden, qkv_ref, mix_ref, chance_ref = saved
    normed_ref, dmiddle_ref, dqkv_ref, mixes_ref = refs
    group = hidden.shape[0] // CTX
    queries = chance_ref.shape[3] // (HEADS // 2)
    short = here(0, group * queries, queries)
    dattend = dmiddle.astype(jnp.bfloat16)
    dmiddle_ref[short, :] = dattend
    mixes_ref[short, :] = mix_ref[...]
    dmix = dot_nt(dattend, weight_ref[:, 3 * D : 4 * D]).astype(jnp.bfloat16)
    units = [(sample, side) for sample in range(group) for side in range(2)]
    slopes, dchances, dscores = [], [], []
    for sample, side in units:
        rows = slice(sample * CTX, (sample + 1) * CTX)
        slopes.append(
            expand_heads(
                dmix[sample * queries : (sample + 1) * queries, half_of(0, side)], masks
            )
        )
        dchances.append(dot_nt(qkv_ref[rows, half_of(2, side)], slopes[-1]))
    for (sample, side), dchance in zip(units, dchances):
        chance = chance_ref[sample, side].astype(jnp.float32)
        weighed = chance * dchance
        dscores.append(
            (weighed - chance * jnp.sum(weighed, axis=0, keepdims=True)).astype(jnp.bfloat16)
        )
    for at, (sample, side) in enumerate(units):
        rows = slice(sample * CTX, (sample + 1) * CTX)
        tail = slice((sample + 1) * CTX - queries, (sample + 1) * CTX)
        there = here(sample * CTX, CTX)
        spread = expand_heads(qkv_ref[tail, half_of(0, side)], masks)
        keys = qkv_ref[rows, half_of(1, side)]
        dvalues = dot_nn(chance_ref[sample, side], slopes[at])
        dkeys = dot_nn(dscores[at], spread) * score_scale
        dqueries = (collapse_heads(dscores[at], keys, masks) * score_scale).astype(jnp.bfloat16)
        if queries < CTX:
            nothing = jnp.zeros((CTX - queries, HALF), jnp.bfloat16)
            dqueries = jnp.concatenate([nothing, dqueries], axis=0)
        dqkv_ref[there, half_of(0, side)] = dqueries
        dqkv_ref[there, half_of(1, side)] = dkeys.astype(jnp.bfloat16)
        dqkv_ref[there, half_of(2, side)] = dvalues.astype(jnp.bfloat16)
    inverse = inverse_rms(hidden)
    normed_ref[here(0, hidden.shape[0]), :] = (hidden * inverse * gain_row).astype(jnp.bfloat16)
    dnormed = dot_nt(dqkv_ref[here(0, hidden.shape[0]), :], weight_ref[:, 0 : 3 * D])
    through, gain_part = rms_back(hidden, inverse, gain_row, dnormed)
    if queries < CTX:
        nothing = jnp.zeros((CTX - queries, D), jnp.float32)
        pieces = []
        for sample in range(group):
            pieces = pieces + [nothing, dmiddle[sample * queries : (sample + 1) * queries]]
        dmiddle = jnp.concatenate(pieces, axis=0)
    return dmiddle + through, gain_part


def row_spec(width, group=GROUP, unit=CTX):
    return pl.BlockSpec((group * unit, width), lambda step: (step, 0))


def chance_spec(queries, group=GROUP):
    return pl.BlockSpec((group, 2, CTX, HEADS // 2 * queries), lambda step: (step, 0, 0, 0))


def latent_spec(group=GROUP):
    return pl.BlockSpec((group, CATS, CTX), lambda step: (step, 0, 0))


def whole_spec(shape):
    return pl.BlockSpec(shape, lambda step: (0,) * len(shape))


def in_hbm(item):
    return pltpu.with_memory_space_constraint(item, pltpu.HBM)


def smem_spec():
    return pl.BlockSpec(memory_space=pltpu.SMEM)


def forward_kernel(layer, widths, mesh_plan, source_ref, own_ref, other_ref, gains_ref, valid_ref, core_ref, *refs):
    entry_ref, att_ref, before_ref = refs[0], refs[5], refs[6]
    bias_ref = refs[7] if layer == 0 else refs[9]
    step = pl.program_id(0)

    @pl.when(step == 0)
    def _():
        fill_bias(bias_ref)
        att = [(att_ref, 0), (att_ref, 3 * D)]
        before = [(before_ref, 0)] if layer == 0 else [(before_ref, 0), (before_ref, FF)]
        targets = att + before if layer == 0 else before + att
        place_weights(targets, own_ref, other_ref, core_ref[0], widths[: len(targets)], mesh_plan)

    if layer == 0:
        one_hot_rows(source_ref, refs[8], 0)
        hidden = dot_nt(refs[8][...], before_ref[...])
    else:
        gain_ffn = gains_ref[LAYERS + layer - 1 : LAYERS + layer, :]
        hidden = feed_forward(source_ref[...], gain_ffn, before_ref, refs[7], refs[8])
    entry_ref[...] = hidden
    attend_forward(
        step,
        hidden,
        gains_ref[layer : layer + 1, :],
        att_ref,
        valid_ref,
        bias_ref,
        head_masks(),
        refs[1:5],
    )


def run_forward(layer, widths, mesh_plan, source, own, other, gains, valid, core):
    tokens = valid.shape[0] * CTX
    f32, b16 = jnp.float32, jnp.bfloat16
    chances = HEADS // 2 * CTX
    group = WIDE_GROUP if layer == 0 else GROUP
    outs = [
        (pltpu.HBM((tokens, D), f32), row_spec(D, group)),
        (pltpu.HBM((tokens, D), f32), row_spec(D, group)),
        (pltpu.HBM((tokens, 3 * D), b16), row_spec(3 * D, group)),
        (pltpu.HBM((tokens, D), b16), row_spec(D, group)),
        (pltpu.HBM((tokens // CTX, 2, CTX, chances), b16), chance_spec(CTX, group)),
        (pltpu.HBM((D, 4 * D), b16), whole_spec((D, 4 * D))),
    ]
    scratch = [pltpu.VMEM((2, CTX, chances), f32)]
    if layer == 0:
        scratch = [pltpu.VMEM((D, VOCAB), b16)] + scratch + [pltpu.VMEM((group * CTX, VOCAB), b16)]
        source_spec = latent_spec(group)
    else:
        source_spec = row_spec(D, group)
        outs.append((pltpu.HBM((D, 2 * FF), b16), whole_spec((D, 2 * FF))))
        outs = outs + [(pltpu.HBM((tokens, FF), b16), row_spec(FF, group))] * 2
        source = in_hbm(source)
    return pl.pallas_call(
        functools.partial(forward_kernel, layer, widths, mesh_plan),
        grid=(tokens // (group * CTX),),
        in_specs=[
            source_spec,
            whole_spec(own.shape),
            whole_spec(other.shape),
            whole_spec(gains.shape),
            smem_spec(),
            smem_spec(),
        ],
        out_specs=[spec for _, spec in outs],
        out_shape=[item for item, _ in outs],
        scratch_shapes=scratch,
        compiler_params=pltpu.CompilerParams(vmem_limit_bytes=VMEM_BYTES),
        cost_estimate=pl.CostEstimate(
            flops=2 * tokens * D * 12 * D,
            bytes_accessed=tokens * D * 16 + D * 12 * D * 4,
            transcendentals=tokens * (FF + HEADS * CTX),
        ),
        name="forward_part",
    )(source, own, other, gains, valid, core)


def middle_kernel(widths, mesh_plan, *refs):
    source_ref, own_ref, other_ref, drawn_ref, gains_ref, valid_ref, horizon_ref, core_ref = refs[:8]
    out_ref, send_ref, keep_ref, gain_ref, loss_ref, count_ref = refs[8:14]
    bias_ref, weight_one_ref, att_ref, weight_two_ref, head_ref, turned_ref = refs[14:20]
    entry_ref, qkv_ref, mix_ref, chance_ref, middle_two_ref, inner_one_ref, slope_one_ref = refs[20:27]
    inner_ref, slope_ref, last_ref, dmiddle_ref, sum_ref, targets_ref, counted_ref = refs[27:34]
    normed_long, dattend_ref, dqkv_long, mixes_ref, normed_two_long, dinner_long, dout_long = refs[34:]
    tokens = middle_two_ref.shape[0]
    final_ref = normed_long.at[0:tokens]
    dlogits_ref = dqkv_long.at[0:VOCAB]
    normed_ref = normed_two_long.at[0:tokens]
    dinner_ref = dinner_long.at[0:tokens]
    dout_ref = dout_long.at[0:tokens]
    groups = source_ref.shape[0] // (WIDE_GROUP * CTX)
    masks = head_masks()
    gain_att = gains_ref[LAYERS - 1 : LAYERS, :]
    gain_before = gains_ref[2 * LAYERS - 2 : 2 * LAYERS - 1, :]
    gain_ffn = gains_ref[2 * LAYERS - 1 : 2 * LAYERS, :]
    gain_final = gains_ref[2 * LAYERS : 2 * LAYERS + 1, :]
    fill_bias(bias_ref)
    place_weights(
        [
            (weight_one_ref, 0),
            (weight_one_ref, FF),
            (att_ref, 0),
            (att_ref, 3 * D),
            (weight_two_ref, 0),
            (weight_two_ref, FF),
            (head_ref, 0),
        ],
        own_ref,
        other_ref,
        core_ref[0],
        widths,
        mesh_plan,
    )

    def rows_of(group, unit=CTX):
        return pl.ds(pl.multiple_of(group * (WIDE_GROUP * unit), WIDE_GROUP * unit), WIDE_GROUP * unit)

    def forward(group, carry):
        rows, short = rows_of(group), rows_of(group, SEG)
        hidden = feed_forward(
            source_ref[rows, :],
            gain_before,
            weight_one_ref,
            inner_one_ref.at[rows],
            slope_one_ref.at[rows],
        )
        entry_ref[rows, :] = hidden
        attend_forward(
            group,
            hidden,
            gain_att,
            att_ref,
            valid_ref,
            bias_ref,
            masks,
            (
                middle_two_ref.at[short],
                qkv_ref.at[rows],
                mix_ref.at[short],
                chance_ref.at[pl.ds(group * WIDE_GROUP, WIDE_GROUP)],
            ),
        )
        return carry

    lax.fori_loop(0, groups, forward, 0)
    turned_ref[...] = head_ref[...].T
    samples = tokens // SEG
    targets_ref[...] = jnp.concatenate([drawn_ref[at] for at in range(samples)], axis=1)
    position = lax.broadcasted_iota(jnp.int32, (1, SEG), 1)
    counted_ref[...] = jnp.concatenate(
        [jnp.where(position < horizon_ref[at], 1.0, 0.0) for at in range(samples)], axis=1
    )
    count_ref[...] = jnp.sum(counted_ref[...], axis=1, keepdims=True)
    for block in range(tokens // ROWS):
        rows = slice(block * ROWS, (block + 1) * ROWS)
        middle = middle_two_ref[rows, :]
        normed = (middle * inverse_rms(middle) * gain_ffn).astype(jnp.bfloat16)
        normed_ref[rows, :] = normed
        for part in range(FF // D):
            columns = slice(part * D, (part + 1) * D)
            inner = dot_nn(normed, weight_two_ref[:, columns])
            for piece in range(GROUP):
                there = slice(block * ROWS + piece * CTX, block * ROWS + (piece + 1) * CTX)
                active, slope = gelu_parts(inner[piece * CTX : (piece + 1) * CTX])
                inner_ref[there, columns] = active.astype(jnp.bfloat16)
                slope_ref[there, columns] = slope.astype(jnp.bfloat16)
        last = middle + dot_nt(inner_ref[rows, :], weight_two_ref[:, FF : 2 * FF])
        last_ref[rows, :] = last
        final_ref[rows, :] = (last * inverse_rms(last) * gain_final).astype(jnp.bfloat16)
    span = D
    loss = jnp.zeros((1, span), jnp.float32)
    spots = lax.broadcasted_iota(jnp.int32, (CLASSES, span), 0)
    for part in range(tokens // span):
        columns = slice(part * span, (part + 1) * span)
        counted = counted_ref[0:1, columns]
        final = final_ref[columns, :]
        for quarter in range(VOCAB // D):
            logits = dot_nt(turned_ref[quarter * D : (quarter + 1) * D, :], final)
            for inside in range(D // CLASSES):
                group = quarter * (D // CLASSES) + inside
                values = logits[inside * CLASSES : (inside + 1) * CLASSES]
                shifted = values - jnp.max(values, axis=0, keepdims=True)
                exponent = jnp.exp2(shifted * log2_e)
                total = jnp.sum(exponent, axis=0, keepdims=True)
                hot = spots == targets_ref[group : group + 1, columns]
                chosen = jnp.sum(jnp.where(hot, shifted, 0.0), axis=0, keepdims=True)
                loss = loss + counted * (jnp.log(total) - chosen)
                chance = exponent * (1.0 / total)
                slope = (chance - jnp.where(hot, 1.0, 0.0)) * counted
                dlogits_ref[group * CLASSES : (group + 1) * CLASSES, columns] = slope.astype(
                    jnp.bfloat16
                )
    loss_ref[...] = jnp.sum(loss, axis=1, keepdims=True)
    sum_ref[:, 2 * FF : 2 * FF + VOCAB] = dot_nt(final_ref[...].T, dlogits_ref[...])
    dfinal = dot_nn(head_ref[...], dlogits_ref[...]).T
    last = last_ref[...]
    dlast, gain_part = rms_back(last, inverse_rms(last), gain_final, dfinal)
    gain_ref[1:2, :] = gain_part
    last_ref[...] = dlast
    gain_sum = jnp.zeros((1, D), jnp.float32)
    for block in range(tokens // ROWS):
        rows = slice(block * ROWS, (block + 1) * ROWS)
        upstream = last_ref[rows, :]
        dout = upstream.astype(jnp.bfloat16)
        dout_ref[rows, :] = dout
        for part in range(FF // D):
            columns = slice(part * D, (part + 1) * D)
            dact = dot_nn(dout, weight_two_ref[:, FF + part * D : FF + (part + 1) * D])
            dinner_ref[rows, columns] = (dact * slope_ref[rows, columns].astype(jnp.float32)).astype(jnp.bfloat16)
        dnormed = dot_nt(dinner_ref[rows, :], weight_two_ref[:, 0:FF])
        middle = middle_two_ref[rows, :]
        through, gain_part = rms_back(middle, inverse_rms(middle), gain_ffn, dnormed)
        gain_sum = gain_sum + gain_part
        dmiddle_ref[rows, :] = upstream + through
    gain_ref[0:1, :] = gain_sum
    sum_ref[:, 0:FF] = dot_nn(normed_ref[...].T, dinner_ref[...])
    sum_ref[:, FF : 2 * FF] = dot_nn(dout_ref[...].T, inner_ref[...])
    write_blocks(send_ref, keep_ref, sum_ref, core_ref[0], widths[4:], mesh_plan)
    gain_ref[2:4, :] = jnp.zeros((2, D), jnp.float32)

    def backward(group, carry):
        rows, short = rows_of(group), rows_of(group, SEG)

        def here(start, length, unit=CTX):
            return pl.ds(pl.multiple_of(group * (WIDE_GROUP * unit) + start, 16), length)

        dentry, gain_part = attend_back(
            group,
            here,
            (
                entry_ref[rows, :],
                qkv_ref.at[rows],
                mix_ref.at[short],
                chance_ref.at[pl.ds(group * WIDE_GROUP, WIDE_GROUP)],
            ),
            dmiddle_ref[short, :],
            gain_att,
            att_ref,
            masks,
            (normed_long, dattend_ref, dqkv_long, mixes_ref),
        )
        gain_ref[2:3, :] += gain_part
        dbefore, gain_part = feed_back(
            here,
            dentry,
            source_ref[rows, :],
            gain_before,
            weight_one_ref,
            slope_one_ref.at[rows],
            (normed_two_long, dinner_long, dout_long),
        )
        out_ref[rows, :] = dbefore
        gain_ref[3:4, :] += gain_part
        return carry

    lax.fori_loop(0, groups, backward, 0)
    column = 0
    for left, right in [
        (normed_two_long, dinner_long),
        (dout_long, inner_one_ref),
        (normed_long, dqkv_long),
        (mixes_ref, dattend_ref),
    ]:
        wide = right.shape[1]
        sum_ref[:, column : column + wide] = dot_nn(left[...].T, right[...])
        column += wide
    write_blocks(
        send_ref, keep_ref, sum_ref, core_ref[0], widths[:4], mesh_plan, sum(widths[4:])
    )


def block_outs(own, widths):
    shape = jax.ShapeDtypeStruct
    blocks = own.shape[:2] + (sum(widths),)
    return [shape(blocks, jnp.bfloat16)] * 2


def run_middle(widths, mesh_plan, source, own, other, targets, gains, valid, horizon, core):
    tokens = source.shape[0]
    short = tokens // CTX * SEG
    samples = tokens // CTX
    chances = HEADS // 2 * SEG
    f32, b16 = jnp.float32, jnp.bfloat16
    shape = jax.ShapeDtypeStruct
    vmem = pl.BlockSpec(memory_space=pltpu.VMEM)
    return pl.pallas_call(
        functools.partial(middle_kernel, widths, mesh_plan),
        in_specs=[vmem] * 5 + [smem_spec()] * 3,
        out_specs=[vmem] * 6,
        out_shape=[pltpu.HBM((tokens, D), f32)]
        + block_outs(own, widths)
        + [pltpu.HBM((4, D), f32), shape((1, 1), f32), shape((1, 1), f32)],
        scratch_shapes=[
            pltpu.VMEM((2, CTX, chances), f32),
            pltpu.VMEM((D, 2 * FF), b16),
            pltpu.VMEM((D, 4 * D), b16),
            pltpu.VMEM((D, 2 * FF), b16),
            pltpu.VMEM((D, VOCAB), b16),
            pltpu.VMEM((VOCAB, D), b16),
            pltpu.VMEM((tokens, D), f32),
            pltpu.VMEM((tokens, 3 * D), b16),
            pltpu.VMEM((short, D), b16),
            pltpu.VMEM((samples, 2, CTX, chances), b16),
            pltpu.VMEM((short, D), f32),
            pltpu.VMEM((tokens, FF), b16),
            pltpu.VMEM((tokens, FF), b16),
            pltpu.VMEM((short, FF), b16),
            pltpu.VMEM((short, FF), b16),
            pltpu.VMEM((short, D), f32),
            pltpu.VMEM((short, D), f32),
            pltpu.VMEM((D, 2 * FF + max(4 * D, VOCAB)), f32),
            pltpu.VMEM((CATS, short), jnp.int32),
            pltpu.VMEM((1, short), f32),
            pltpu.VMEM((tokens, D), b16),
            pltpu.VMEM((short, D), b16),
            pltpu.VMEM((tokens, 3 * D), b16),
            pltpu.VMEM((short, D), b16),
            pltpu.VMEM((tokens, D), b16),
            pltpu.VMEM((tokens, FF), b16),
            pltpu.VMEM((tokens, D), b16),
        ],
        compiler_params=pltpu.CompilerParams(vmem_limit_bytes=MIDDLE_BYTES + (0 if own.shape[1] >= 64 else VMEM_BYTES // 2)),
        cost_estimate=pl.CostEstimate(
            flops=6 * tokens * D * 8 * FF,
            bytes_accessed=tokens * D * 8 + D * 6 * FF * 10,
            transcendentals=2 * tokens * (FF + VOCAB),
        ),
        name="middle_part",
    )(source, own, other, targets, gains, valid, horizon, core)


def backward_kernel(layer, widths, mesh_plan, *refs):
    entry_ref, qkv_ref, mix_ref, chance_ref, dmiddle_ref, att_ref, gains_ref, core_ref = refs[:8]
    if layer == 0:
        latent_ref, send_ref, keep_ref, gain_ref = refs[8:12]
        att_kept, before_kept, sum_ref = refs[12:16], refs[16:18], refs[18]
    else:
        before_ref, ffn_ref, slope_ref, inner_hbm, out_ref, send_ref, keep_ref, gain_ref = refs[8:16]
        att_kept, before_kept, sum_ref = refs[16:20], refs[20:23], refs[23]
        inner_ref, inner_sem = refs[24:26]
        copy = pltpu.make_async_copy(inner_hbm, inner_ref, inner_sem)
    step = pl.program_id(0)

    def here(start, length, unit=CTX):
        base = step * (GROUP * unit)
        return pl.ds(pl.multiple_of(base + start, 16), length)

    @pl.when(step == 0)
    def _():
        gain_ref[...] = jnp.zeros_like(gain_ref)
        if layer > 0:
            copy.start()

    dentry, gain_part = attend_back(
        step,
        here,
        (entry_ref[...], qkv_ref, mix_ref, chance_ref),
        dmiddle_ref[...],
        gains_ref[layer : layer + 1, :],
        att_ref,
        head_masks(),
        att_kept,
    )
    gain_ref[0:1, :] += gain_part
    if layer == 0:
        before_kept[0][here(0, ROWS), :] = dentry.astype(jnp.bfloat16)
        one_hot_rows(latent_ref, before_kept[1], pl.multiple_of(step * ROWS, ROWS))
    else:
        dbefore, gain_part = feed_back(
            here,
            dentry,
            before_ref[...],
            gains_ref[LAYERS + layer - 1 : LAYERS + layer, :],
            ffn_ref,
            slope_ref,
            before_kept,
        )
        out_ref[...] = dbefore
        gain_ref[1:2, :] += gain_part

    @pl.when(step == pl.num_programs(0) - 1)
    def _():
        normed_ref, dattend_ref, dqkv_ref, mixes_ref = att_kept
        att = [(normed_ref, dqkv_ref), (mixes_ref, dattend_ref)]
        if layer == 0:
            pairs = att + [(before_kept[0], before_kept[1])]
        else:
            copy.wait()
            normed_two_ref, dinner_ref, dout_ref = before_kept
            pairs = [(normed_two_ref, dinner_ref), (dout_ref, inner_ref)] + att
        column = 0
        for left, right in pairs:
            wide = right.shape[1]
            sum_ref[:, column : column + wide] = dot_nn(left[...].T, right[...])
            column += wide
        write_blocks(send_ref, keep_ref, sum_ref, core_ref[0], widths, mesh_plan)


def run_backward(layer, widths, mesh_plan, blocks_like, saved, dmiddle, gains, core, before):
    entry, _, qkv, mix, chance = [in_hbm(item) for item in saved[:5]]
    weights = saved[5]
    if layer > 0:
        dmiddle = in_hbm(dmiddle)
        before = [in_hbm(before[0]), before[1]] + [in_hbm(item) for item in before[2:]]
    tokens = entry.shape[0]
    queries = chance.shape[3] // (HEADS // 2)
    short = tokens // CTX * queries
    f32, b16 = jnp.float32, jnp.bfloat16
    shape = jax.ShapeDtypeStruct
    in_specs = [
        row_spec(D),
        row_spec(3 * D),
        row_spec(D, GROUP, queries),
        chance_spec(queries),
        row_spec(D, GROUP, queries),
        whole_spec(weights.shape),
        whole_spec(gains.shape),
        smem_spec(),
    ]
    operands = [entry, qkv, mix, chance, dmiddle, weights, gains, core]
    blocks = block_outs(blocks_like, widths)
    outs = [(item, whole_spec(item.shape)) for item in blocks]
    outs.append((pltpu.HBM((2, D), f32), whole_spec((2, D))))
    scratch = [
        pltpu.VMEM((tokens, D), b16),
        pltpu.VMEM((short, D), b16),
        pltpu.VMEM((tokens, 3 * D), b16),
        pltpu.VMEM((short, D), b16),
    ]
    if layer == 0:
        in_specs.append(latent_spec())
        operands.append(before)
        scratch = scratch + [pltpu.VMEM((tokens, D), b16), pltpu.VMEM((tokens, VOCAB), b16)]
        wide = 4 * D + VOCAB
    else:
        in_specs = in_specs + [row_spec(D), whole_spec(before[1].shape), row_spec(FF)]
        in_specs.append(pl.BlockSpec(memory_space=pl.ANY))
        operands = operands + list(before)
        outs.insert(0, (shape((tokens, D), f32), row_spec(D)))
        scratch = scratch + [
            pltpu.VMEM((tokens, D), b16),
            pltpu.VMEM((tokens, FF), b16),
            pltpu.VMEM((tokens, D), b16),
        ]
        wide = 4 * D + 2 * FF
    scratch.append(pltpu.VMEM((D, wide), f32))
    if layer > 0:
        scratch = scratch + [pltpu.VMEM((tokens, FF), b16), pltpu.SemaphoreType.DMA]
    return pl.pallas_call(
        functools.partial(backward_kernel, layer, widths, mesh_plan),
        grid=(tokens // ROWS,),
        in_specs=in_specs,
        out_specs=[spec for _, spec in outs],
        out_shape=[item for item, _ in outs],
        scratch_shapes=scratch,
        compiler_params=pltpu.CompilerParams(vmem_limit_bytes=VMEM_BYTES * 3 // 2),
        cost_estimate=pl.CostEstimate(
            flops=6 * tokens * D * wide,
            bytes_accessed=tokens * D * 24 + D * wide * 6,
            transcendentals=tokens * FF,
        ),
        name="backward_part",
    )(*operands)


def pack_kernel(*refs):
    qkv_ref, out_ref, up_ref, down_ref, embed_ref, head_ref = refs[:6]
    low = lambda value: value.astype(jnp.bfloat16)
    att = [[low(qkv_ref[at]), low(out_ref[at].T)] for at in range(LAYERS)]
    ffn = [[low(up_ref[at]), low(down_ref[at])] for at in range(LAYERS)]
    pieces = [
        att[0] + [low(embed_ref[...])],
        ffn[0] + att[1],
        ffn[1] + att[2] + ffn[2] + [low(head_ref[...])],
    ]
    for target, piece in zip(refs[6:], pieces):
        target[...] = jnp.concatenate(piece, axis=1)


def run_pack(masters, chunk_widths):
    vmem = pl.BlockSpec(memory_space=pltpu.VMEM)
    rows = masters[0].shape[1]
    return pl.pallas_call(
        pack_kernel,
        in_specs=[vmem] * 6,
        out_specs=[vmem] * 3,
        out_shape=[
            jax.ShapeDtypeStruct((rows, sum(widths)), jnp.bfloat16) for widths in chunk_widths
        ],
        name="pack",
    )(*masters)


def matrix_plan(widths):
    order = [
        (2, 2), (3, 2), (5, 0), (2, 1), (3, 1), (0, 2), (1, 2),
        (2, 0), (3, 0), (0, 1), (1, 1), (0, 0), (1, 0), (4, 0),
    ]
    plan, column = {}, 0
    for which, layer in order:
        plan[(which, layer)] = (column, widths[which])
        column += widths[which]
    return plan, column


def matrix_list():
    return [(which, layer) for which in range(4) for layer in range(LAYERS)] + [(4, 0), (5, 0)]


MATRICES = 4 * LAYERS + 2
LANES = 128
INNER_ROWS = 16
COMMON_ROWS = 16
ROW_IS_INNER = [True, True, True, False, False, True]


def master_of(masters, which, layer):
    if which == 1:
        return masters[1][layer].T
    return masters[which][layer] if which < 4 else masters[which][...]


def old_row(refs, which, layer):
    return refs[which][layer : layer + 1, :] if which < 4 else refs[which][...]


LATE = [(0, 0), (1, 0), (4, 0)]
EDGE = INNER_ROWS + COMMON_ROWS


def whole_sum(value):
    return jnp.sum(jnp.sum(value, axis=1, keepdims=True), axis=0, keepdims=True)


def square_sums(raw, chosen, plan, first):
    square = raw * raw
    rows = square.shape[0]
    inner, entries = [], []
    for item in matrix_list():
        if item in chosen:
            column, width = plan[item]
            part = square[:, column - first : column - first + width]
            inner.append(jnp.sum(part, axis=1, keepdims=True))
        else:
            inner.append(jnp.zeros((rows, 1), jnp.float32))
        entries.append(jnp.sum(inner[-1], axis=0, keepdims=True))
    inner.append(jnp.zeros((rows, LANES - MATRICES), jnp.float32))
    return jnp.concatenate(inner, axis=1).T, entries, jnp.sum(square, axis=0, keepdims=True)


def store_row(target_ref, row, values):
    total = values.shape[1]
    for at, start in enumerate(range(0, total, LANES)):
        stop = min(start + LANES, total)
        target_ref[row + at : row + at + 1, 0 : stop - start] = values[:, start:stop]


def load_row(source_ref, row, total):
    return jnp.concatenate(
        [
            source_ref[row + at : row + at + 1, 0 : min(LANES, total - start)]
            for at, start in enumerate(range(0, total, LANES))
        ],
        axis=1,
    )


def late_row(widths):
    _, total = matrix_plan(widths)
    late = sum(widths[which] for which, _ in LATE)
    return EDGE + -(-(total - late) // LANES)


def packet_rows(widths):
    late = sum(widths[which] for which, _ in LATE)
    return -(-(late_row(widths) + -(-late // LANES)) // 8) * 8


def first_kernel(*refs):
    masters, row_refs, row_ref = refs[0:6], refs[6:12], refs[12]
    weights, row_sums = [], []
    for which, layer in matrix_list():
        master = masters[which][layer] if which < 4 else masters[which][...]
        weights.append(whole_sum(master * master))
        row_sums.append(whole_sum(old_row(row_refs, which, layer)))
    nothing = lambda count: [jnp.zeros((1, count), jnp.float32)]
    pieces = nothing(2) + weights + nothing(MATRICES) + row_sums
    row_ref[...] = jnp.concatenate(pieces + nothing(LANES - 2 - 3 * MATRICES), axis=1)


def run_first(masters, rows):
    vmem = pl.BlockSpec(memory_space=pltpu.VMEM)
    return pl.pallas_call(
        first_kernel,
        in_specs=[vmem] * 12,
        out_specs=vmem,
        out_shape=jax.ShapeDtypeStruct((1, LANES), jnp.float32),
        name="first_statistics",
    )(*masters, *rows)


def early_kernel(widths, *refs):
    raw_ref, row_ref, gains_at, loss_ref, count_ref, packet_ref = (
        refs[0],
        refs[1],
        refs[2:4],
        refs[4],
        refs[5],
        refs[6],
    )
    plan, _ = matrix_plan(widths)
    chosen = [item for item in matrix_list() if item not in LATE]
    inner, entries, outer = square_sums(raw_ref[...], chosen, plan, 0)
    packet_ref[...] = jnp.zeros_like(packet_ref)
    packet_ref[0:INNER_ROWS, 0 : inner.shape[1]] = inner[0:INNER_ROWS, :]
    last, one = [ref[...] for ref in gains_at]
    gain = jnp.concatenate(
        [jnp.zeros((1, D), jnp.float32), one[0:1], last[2:3], one[1:2], last[3:4], last[0:2]],
        axis=0,
    )
    nothing = lambda count: [jnp.zeros((1, count), jnp.float32)]
    scalars = [loss_ref[...], count_ref[...]] + nothing(MATRICES) + entries
    scalars = scalars + nothing(LANES - 2 - 2 * MATRICES)
    at = INNER_ROWS
    packet_ref[at : at + 7, :] = gain[:, 0:LANES]
    packet_ref[at + 7 : at + 8, :] = row_ref[...] + jnp.concatenate(scalars, axis=1)
    packet_ref[at + 8 : at + 15, :] = gain[:, LANES:]
    store_row(packet_ref, EDGE, outer)


def late_kernel(widths, early_ref, raw_ref, gain_ref, packet_ref):
    plan, total = matrix_plan(widths)
    inner, entries, outer = square_sums(raw_ref[...], LATE, plan, total - raw_ref.shape[1])
    packet_ref[...] = early_ref[...]
    packet_ref[0:INNER_ROWS, 0 : inner.shape[1]] += inner[0:INNER_ROWS, :]
    at = INNER_ROWS
    packet_ref[at : at + 1, :] = gain_ref[0:1, 0:LANES]
    packet_ref[at + 8 : at + 9, :] = gain_ref[0:1, LANES:]
    before = jnp.zeros((1, 2 + MATRICES), jnp.float32)
    behind = jnp.zeros((1, LANES - 2 - 2 * MATRICES), jnp.float32)
    packet_ref[at + 7 : at + 8, :] += jnp.concatenate([before] + entries + [behind], axis=1)
    store_row(packet_ref, late_row(widths), outer)


def run_early(widths, raw, row, gain_parts, loss, count):
    vmem = pl.BlockSpec(memory_space=pltpu.VMEM)
    operands = [raw, row] + gain_parts + [loss, count]
    return pl.pallas_call(
        functools.partial(early_kernel, widths),
        in_specs=[vmem] * len(operands),
        out_specs=vmem,
        out_shape=jax.ShapeDtypeStruct((packet_rows(widths), LANES), jnp.float32),
        name="early_statistics",
    )(*operands)


def run_late(widths, packet, raw, gain_part):
    vmem = pl.BlockSpec(memory_space=pltpu.VMEM)
    return pl.pallas_call(
        functools.partial(late_kernel, widths),
        in_specs=[vmem] * 3,
        out_specs=vmem,
        out_shape=jax.ShapeDtypeStruct(packet.shape, jnp.float32),
        name="late_statistics",
    )(packet, raw, gain_part)


def update_kernel(widths, sizes, *refs):
    packet_ref, raw_early, raw_late = refs[:3]
    masters, inner_refs, outer_refs = refs[3:9], refs[9:15], refs[15:21]
    gains_ref, second_ref = refs[21:23]
    outs = refs[23:]
    outer_count, inner_count = sizes
    plan, total = matrix_plan(widths)
    rows = raw_early.shape[0]
    at = INNER_ROWS
    scalars = packet_ref[at + 7 : at + 8, :]
    pick = lambda at: scalars[:, at : at + 1]
    gain_sum = jnp.concatenate(
        [packet_ref[at : at + 7, :], packet_ref[at + 8 : at + 15, :]], axis=1
    )
    gain_square = jnp.sum(jnp.sum(gain_sum * gain_sum, axis=1, keepdims=True), axis=0, keepdims=True)
    square_total = gain_square
    for at in range(MATRICES):
        square_total = square_total + pick(2 + MATRICES + at)
    count_total = pick(1)
    norm_value = jnp.sqrt(square_total) / count_total
    scaling = jnp.minimum(1.0, clip_limit / norm_value) / count_total
    square_scale = scaling * scaling
    early = raw_early.shape[1]
    outer_early = load_row(packet_ref, EDGE, early)
    outer_late = load_row(packet_ref, late_row(widths), total - early)
    inner_new = []
    for at, (which, layer) in enumerate(matrix_list()):
        outer_length = widths[which] * outer_count
        inner_new.append(
            decay_two * old_row(inner_refs, which, layer)
            + (1 - decay_two)
            * (square_scale * packet_ref[at : at + 1, 0:rows] / outer_length + tiny_term)
        )
    stacked = jnp.concatenate(inner_new, axis=0)
    stacked = jnp.concatenate([stacked, jnp.ones((LANES - MATRICES, rows), jnp.float32)], axis=0)
    if rows < LANES:
        stacked = jnp.concatenate([stacked, jnp.ones((LANES, LANES - rows), jnp.float32)], axis=1)
    turned = lax.rsqrt(stacked).T
    outs[0][...] = pick(0)
    outs[1][...] = count_total
    outs[2][...] = norm_value
    first_out = {4: 3, 0: 7, 1: 11, 2: 15, 3: 19, 5: 23}
    for at, (which, layer) in enumerate(matrix_list()):
        column, width = plan[(which, layer)]
        outer_length, inner_length = width * outer_count, rows * inner_count
        row_length = inner_length if ROW_IS_INNER[which] else outer_length
        copies = outer_count if ROW_IS_INNER[which] else inner_count
        entries = outer_length * inner_length
        if column < early:
            raw = raw_early[:, column : column + width]
            outer_total = outer_early[:, column : column + width]
        else:
            raw = raw_late[:, column - early : column - early + width]
            outer_total = outer_late[:, column - early : column - early + width]
        outer_new = decay_two * old_row(outer_refs, which, layer) + (1 - decay_two) * (
            square_scale * outer_total / inner_length + tiny_term
        )
        mean_rows = decay_two * (pick(2 + 2 * MATRICES + at) / (copies * row_length)) + (
            1 - decay_two
        ) * (square_scale * pick(2 + MATRICES + at) / entries + tiny_term)
        factor = step_rate * jnp.sqrt(pick(2 + at) / entries) * jnp.sqrt(mean_rows)
        grad = raw * scaling
        updated = master_of(masters, which, layer) - grad * (
            turned[0:rows, at : at + 1] * (factor * lax.rsqrt(outer_new))
        )
        first = first_out[which]
        row_new, column_new = (
            (inner_new[at], outer_new) if ROW_IS_INNER[which] else (outer_new, inner_new[at])
        )
        if which < 4:
            if which == 1:
                updated, grad = updated.T, grad.T
            outs[first][layer] = updated
            outs[first + 1][layer] = grad
            outs[first + 2][layer : layer + 1, :] = row_new
            outs[first + 3][layer : layer + 1, :] = column_new
        else:
            outs[first][...] = updated
            outs[first + 1][...] = grad
            outs[first + 2][...] = row_new
            outs[first + 3][...] = column_new
    gain_grad = gain_sum * scaling
    second_new = decay_two * second_ref[...] + (1 - decay_two) * (gain_grad * gain_grad + tiny_term)
    gains = gains_ref[...]
    spread = jnp.sqrt(jnp.mean(gains * gains, axis=-1, keepdims=True))
    outs[27][...] = gains - step_rate * spread * gain_grad * lax.rsqrt(second_new)
    outs[28][...] = gain_grad
    outs[29][...] = second_new


def run_update(widths, sizes, packet, raw_early, raw_late, masters, inner, outer, gains, second):
    vmem = pl.BlockSpec(memory_space=pltpu.VMEM)
    operands = [packet, raw_early, raw_late] + masters + inner + outer + [gains, second]
    shapes = [(1, 1)] * 3
    for which in [4, 0, 1, 2, 3, 5]:
        shapes = shapes + [masters[which].shape] * 2
        pair = [inner[which].shape, outer[which].shape]
        shapes = shapes + (pair if ROW_IS_INNER[which] else pair[::-1])
    shapes = shapes + [gains.shape] * 3
    return pl.pallas_call(
        functools.partial(update_kernel, widths, sizes),
        in_specs=[vmem] * len(operands),
        out_specs=[vmem] * len(shapes),
        out_shape=[jax.ShapeDtypeStruct(item, jnp.float32) for item in shapes],
        name="update",
    )(*operands)


def swap(value, mask):
    count = lax.axis_size("dp") * lax.axis_size("fsdp")
    return lax.ppermute(value, ("dp", "fsdp"), [(place, place ^ mask) for place in range(count)])


def device_index():
    return lax.axis_index("dp") * lax.axis_size("fsdp") + lax.axis_index("fsdp")


def step_masks(step):
    masks = []
    for digit in range(1, 1 << len(step)):
        masks.append(sum(1 << bit for at, bit in enumerate(step[::-1]) if (digit >> at) & 1))
    return masks


def tie(*values):
    return lax.optimization_barrier(values)


def behind(value, *ahead):
    return lax.optimization_barrier((value,) + ahead)[0]


class Gather:
    def __init__(self, piece, steps):
        self.held, self.steps, self.at = piece[None], steps, 0

    def send(self):
        self.others = tuple(swap(self.held, mask) for mask in step_masks(self.steps[self.at]))

    def join(self):
        step = self.steps[self.at]
        pieces = [self.held] + list(self.others)
        for at, bit in enumerate(step[::-1]):
            upper = (device_index() >> bit) & 1 == 1
            pieces = [
                jnp.where(upper, pieces[place ^ (1 << at)], pieces[place])
                for place in range(len(pieces))
            ]
        self.held = jnp.concatenate(pieces)
        self.at += 1


class Scatter:
    def __init__(self, sent, kept, steps):
        self.sent, self.kept, self.steps, self.at = (sent,), kept, steps, 0

    def send(self):
        masks = step_masks(self.steps[self.at])
        self.others = tuple(swap(sent, mask) for sent, mask in zip(self.sent, masks))

    def join(self):
        self.at += 1
        step = self.steps[self.at] if self.at < len(self.steps) else ()
        count = 1 << len(step)
        own = 0
        for bit in step:
            own = 2 * own + ((device_index() >> bit) & 1)
        shape = (count, self.kept.shape[0] // count) + self.kept.shape[1:]
        terms = [item.reshape(shape) for item in (self.kept,) + self.others]

        def pick(digit):
            total = None
            for term in terms:
                part = lax.dynamic_index_in_dim(term, own ^ digit, 0, keepdims=False)
                part = part.astype(jnp.float32)
                total = part if total is None else total + part
            return total

        self.sent = tuple(pick(digit).astype(jnp.bfloat16) for digit in range(1, count))
        self.kept = pick(0)


def sum_packets(packet, group, inner_bits):
    row = lax.broadcasted_iota(jnp.int32, packet.shape, 0)
    terms = [packet]
    for mask in step_masks(group):
        first = 0 if mask >> inner_bits << inner_bits == mask else INNER_ROWS
        stop = packet.shape[0] if mask >> inner_bits == 0 else EDGE
        terms.append(jnp.where((row >= first) & (row < stop), swap(packet, mask), 0.0))
    while len(terms) > 1:
        terms = [terms[at] + terms[at + 1] for at in range(0, len(terms), 2)]
    return terms[0]


def merged(parts):
    whole = Scatter(None, jnp.concatenate([part.kept for part in parts], axis=2), parts[0].steps)
    whole.sent = tuple(
        jnp.concatenate(pieces, axis=2) for pieces in zip(*[part.sent for part in parts])
    )
    whole.at = parts[0].at
    return whole


def shards(
    latents,
    targets,
    horizon,
    memory_valid,
    embed,
    qkv_weight,
    out_weight,
    up_weight,
    down_weight,
    head_weight,
    gains,
    embed_rows,
    embed_cols,
    qkv_rows,
    qkv_cols,
    out_rows,
    out_cols,
    up_rows,
    up_cols,
    down_rows,
    down_cols,
    head_rows,
    head_cols,
    gain_second,
):
    samples = latents.shape[0]
    sizes = (lax.axis_size("dp"), lax.axis_size("fsdp"))
    highest = (sizes[0] * sizes[1]).bit_length() - 1
    gather_steps = [(bit,) for bit in reversed(range(3, highest))] + [(2, 1), (0,)]
    scatter_steps = gather_steps[::-1]
    mesh_plan = (sizes[0], sizes[1], gather_steps)
    core = (lax.axis_index("fsdp") & 1).astype(jnp.int32).reshape(1)

    out_turned = jnp.swapaxes(out_weight, 1, 2)
    down_turned = jnp.swapaxes(down_weight, 1, 2)
    masters = [qkv_weight, out_turned, up_weight, down_turned, embed.T, head_weight]
    widths = [qkv_weight.shape[2], out_weight.shape[2], up_weight.shape[2], down_weight.shape[1]]
    widths = widths + [embed.shape[0], head_weight.shape[1]]
    att_widths, ffn_widths = widths[0:2], widths[2:4]
    chunk_widths = [
        att_widths + widths[4:5],
        ffn_widths + att_widths,
        ffn_widths + att_widths + ffn_widths + widths[5:6],
    ]
    chunks = [Gather(piece, gather_steps) for piece in run_pack(masters, chunk_widths)]
    first, second, third = chunks
    latent_rows = latents.transpose(0, 2, 1)
    target_rows = targets.transpose(0, 2, 1)
    shared = (gains, memory_valid, core)
    back_shared = (gains, core)

    count = len(gather_steps)
    flat = lambda item: item if item.ndim == 2 else item.reshape(1, -1)
    inner = [flat(item) for item in (qkv_rows, out_rows, up_rows, down_cols, embed_cols, head_rows)]
    outer = [flat(item) for item in (qkv_cols, out_cols, up_cols, down_rows, embed_rows, head_cols)]
    row_stats = [inner[at] if ROW_IS_INNER[at] else outer[at] for at in range(6)]
    first_row = run_first(masters, row_stats)
    for at in range(count - 1):
        for chunk in chunks:
            chunk.send()
        if at == 0:
            first.others, first_row = tie(first.others, first_row)
        for chunk in chunks[: 2 if at == count - 2 else 3]:
            chunk.join()
            if at == count - 3 and chunk is first:
                first.held, third.held = tie(first.held, third.held)
    first.send()
    (other,) = first.others
    held, other, second.held = tie(first.held, other, second.held)
    second.send()
    kept = [run_forward(0, chunk_widths[0], mesh_plan, latent_rows, held, other, *shared)]
    middle, (other,) = tie(kept[0][1], second.others)
    kept.append(
        run_forward(1, chunk_widths[1], mesh_plan, middle, second.held, other, *shared)
    )
    middle, third.others = tie(kept[1][1], third.others)
    third.join()
    third.send()
    (other,) = third.others
    dmiddle, sent, held, gain_middle, loss, counted = run_middle(
        chunk_widths[2],
        mesh_plan,
        middle,
        third.held,
        other,
        target_rows,
        gains,
        memory_valid,
        horizon,
        core,
    )
    pair = Scatter(sent, held, scatter_steps)
    pair.send()
    pair.join()
    like = first.held
    before = (kept[0][1], kept[1][6], kept[1][8], kept[1][7])
    dmiddle, pair.sent = tie(dmiddle, pair.sent)
    pair.send()
    dmiddle, sent, held, gain_one = run_backward(
        1, chunk_widths[1], mesh_plan, like, kept[1], dmiddle, *back_shared, before
    )
    dmiddle, sent, held, pair.others = tie(dmiddle, sent, held, pair.others)
    one = Scatter(sent, held, scatter_steps)
    one.send()
    pair.join()
    one.join()
    dmiddle, pair.sent, one.sent = tie(dmiddle, pair.sent, one.sent)
    one.send()
    pair.send()
    sent, held, gain_zero = run_backward(
        0, chunk_widths[0], mesh_plan, like, kept[0], dmiddle, *back_shared, latent_rows
    )
    sent, held, pair.others, one.others = tie(sent, held, pair.others, one.others)
    zero = Scatter(sent, held, scatter_steps)
    zero.send()
    one.join()
    one.send()
    pair.join()
    zero.join()
    one.others = behind(one.others, zero.sent)
    zero.send()
    one.join()
    early = merged([pair, one])
    while early.at < count:
        early.send()
        if early.at == count - 1:
            zero.join()
            zero.send()
        zero.others, early.others = tie(zero.others, early.others)
        early.join()
    raw_early = early.kept[0]

    packet = run_early(
        widths, raw_early, first_row, [gain_middle, gain_one], loss, counted
    )
    while zero.at < count:
        zero.join()
        if zero.at < count:
            zero.send()
    raw_late = zero.kept[0]
    packet = run_late(widths, packet, raw_late, gain_zero)
    inner_bits = sizes[1].bit_length() - 1
    rest = list(range(3, highest))
    groups = [(0,), (2, 1)] + [tuple(rest[at : at + 2][::-1]) for at in range(0, len(rest), 2)]
    for group in groups:
        packet = sum_packets(packet, group, inner_bits)
    results = run_update(
        widths, sizes, packet, raw_early, raw_late, masters, inner, outer, gains, gain_second
    )
    results = list(results)
    for at in range(3):
        results[at] = results[at].reshape(())
    for at in (3, 4, 11, 12, 19, 20):
        results[at] = jnp.swapaxes(results[at], -1, -2)
    for at in (5, 6, 25, 26):
        results[at] = results[at].reshape(-1)
    return tuple(results)


def solution(mesh):
    return jax.shard_map(
        shards,
        mesh=mesh,
        in_specs=(
            P(("dp", "fsdp"), None, None),
            P(("dp", "fsdp"), None, None),
            P(("dp", "fsdp")),
            P(("dp", "fsdp")),
            P("dp", "fsdp"),
            P(None, "fsdp", "dp"),
            P(None, "fsdp", "dp"),
            P(None, "fsdp", "dp"),
            P(None, "dp", "fsdp"),
            P("fsdp", "dp"),
            P(),
            P("dp"),
            P("fsdp"),
            P(None, "fsdp"),
            P(None, "dp"),
            P(None, "fsdp"),
            P(None, "dp"),
            P(None, "fsdp"),
            P(None, "dp"),
            P(None, "dp"),
            P(None, "fsdp"),
            P("fsdp"),
            P("dp"),
            P(),
        ),
        out_specs=(
            P(),
            P(),
            P(),
            P("dp", "fsdp"),
            P("dp", "fsdp"),
            P("dp"),
            P("fsdp"),
            P(None, "fsdp", "dp"),
            P(None, "fsdp", "dp"),
            P(None, "fsdp"),
            P(None, "dp"),
            P(None, "fsdp", "dp"),
            P(None, "fsdp", "dp"),
            P(None, "fsdp"),
            P(None, "dp"),
            P(None, "fsdp", "dp"),
            P(None, "fsdp", "dp"),
            P(None, "fsdp"),
            P(None, "dp"),
            P(None, "dp", "fsdp"),
            P(None, "dp", "fsdp"),
            P(None, "dp"),
            P(None, "fsdp"),
            P("fsdp", "dp"),
            P("fsdp", "dp"),
            P("fsdp"),
            P("dp"),
            P(),
            P(),
            P(),
        ),
        check_vma=False,
    )
```
